32 devices in a mesh: fsdp: 4 (over z), context: 4 (over y, x), tensor: 2 (over core).
Axes of the slice: x: 2, y: 2, z: 4, core: 2. Of those that a mesh axis runs over, the one named last changes fastest.
Arguments:
- tokens: bfloat16 [10240, 2048], P(('fsdp', 'context')), may hold values from -6 to 6
- cotangent: bfloat16 [10240, 2048], P(('fsdp', 'context')), may hold values from -6 to 6
- attn_gain: bfloat16 [2048], P(('fsdp', 'context')), may hold values from 0.099609375 to 1.8984375
- w_query: bfloat16 [2048, 2048], P(('fsdp', 'context'), 'tensor'), may hold values from -0.5 to 0.5
- w_key: bfloat16 [2048, 512], P(('fsdp', 'context'), 'tensor'), may hold values from -0.5 to 0.5
- w_value: bfloat16 [2048, 512], P(('fsdp', 'context'), 'tensor'), may hold values from -0.125 to 0.125
- w_out: bfloat16 [2048, 2048], P('tensor', ('fsdp', 'context')), may hold values from -1 to 1
- ffn_gain: bfloat16 [2048], P(('fsdp', 'context')), may hold values from 0.099609375 to 1.8984375
- w_gate: bfloat16 [2048, 8192], P(('fsdp', 'context'), 'tensor'), may hold values from -0.125 to 0.125
- w_up: bfloat16 [2048, 8192], P(('fsdp', 'context'), 'tensor'), may hold values from -0.125 to 0.125
- w_down: bfloat16 [8192, 2048], P('tensor', ('fsdp', 'context')), may hold values from -0.25 to 0.25
- piece_segment: int32 [4, 20], P('fsdp'), may hold values from 0 to 12, as said below
- piece_parent: int32 [4, 20], P('fsdp'), may hold values from -1 to 4, as said below
- piece_start: int32 [4, 20], P('fsdp'), may hold values from 0 to 1152, as said below
Outputs:
- output: bfloat16 [10240, 2048], P(('fsdp', 'context'))
- grad_tokens: float32 [10240, 2048], P(('fsdp', 'context'))
- grad_attn_gain: float32 [2048], P(('fsdp', 'context'))
- grad_query: float32 [2048, 2048], P(('fsdp', 'context'), 'tensor')
- grad_key: float32 [2048, 512], P(('fsdp', 'context'), 'tensor')
- grad_value: float32 [2048, 512], P(('fsdp', 'context'), 'tensor')
- grad_out: float32 [2048, 2048], P('tensor', ('fsdp', 'context'))
- grad_ffn_gain: float32 [2048], P(('fsdp', 'context'))
- grad_gate: float32 [2048, 8192], P(('fsdp', 'context'), 'tensor')
- grad_up: float32 [2048, 8192], P(('fsdp', 'context'), 'tensor')
- grad_down: float32 [8192, 2048], P('tensor', ('fsdp', 'context'))
The draws below stay inside these ranges and needn't reach their ends.
Inputs may be any that keep to these rules, and one draw needn't show every extreme that they name: `piece_segment`: tree t's trunk is segment 13 t, its branches 13 t + 1 to 13 t + 4, its leaves 13 t + 5 to 13 t + 12, leaves 13 t + 5 + 2 b and 13 t + 6 + 2 b under branch 13 t + 1 + b. Within each row (one fsdp group) every tree 0 to 0 has 20 pieces: 8 trunk pieces, and 1 pieces for each of four branches and eight leaves. Pieces are placed in any order; one tree of each group has a trunk piece first on every device of the context axis. `piece_parent`: the trunk's segment for a branch's pieces, the branch's for a leaf's, -1 for trunk pieces. `piece_start`: trunk pieces start at multiples of 128 below 1024, branch pieces at 1024 + multiples of 128, leaf pieces at 1152 + multiples of 128; the pieces of one segment cover its positions once.
All inputs are finite; a program needn't handle non-finite values.
Results may differ from the reference program's by a relative error of at most 0.019.
Values may be sent and summed in bfloat16 or wider, within the bound.
A program may use at most 320 MiB of HBM per device.

```python
import jax
import jax.numpy as jnp
from jax import lax

D = 2048
HEADS = 32
KV_HEADS = 8
HEAD = 64
FF = 8192
SEG = 128
TREES_GROUP = 1
PIECE = 128
GROUP_PIECES = 20
GROUP_TOK = 2560
TOKENS = 10240
N_FSDP = 4
N_CONTEXT = 4


def tree_layout(key):
    per_tree = 5 * N_CONTEXT
    group_size = TREES_GROUP * per_tree
    per_dev = 5 * TREES_GROUP
    piece_span = SEG // PIECE

    def one_group(group_key):
        key_star, key_perm = jax.random.split(group_key)
        spanning = jax.random.randint(key_star, (), 0, TREES_GROUP)
        piece_id = jnp.arange(group_size, dtype=jnp.int32)
        tree_id = piece_id // per_tree
        within = piece_id % per_tree
        special = (tree_id == spanning) & (within < N_CONTEXT)
        shuffled = jax.random.permutation(key_perm, group_size).astype(jnp.int32)
        ranking = jnp.where(special, group_size + within, shuffled)
        ordering = jnp.argsort(ranking, stable=True).astype(jnp.int32)
        slot_id = jnp.arange(group_size, dtype=jnp.int32)
        device = slot_id // per_dev
        local_slot = slot_id % per_dev
        rest_index = jnp.clip(device * (per_dev - 1) + local_slot - 1, 0, group_size - N_CONTEXT - 1)
        chosen = jnp.where(local_slot == 0, ordering[jnp.clip(group_size - N_CONTEXT + device, 0, group_size - 1)], ordering[rest_index])
        chosen_tree = chosen // per_tree
        chosen_within = chosen % per_tree
        segment_index = chosen_within // piece_span
        piece_offset = chosen_within % piece_span
        local_segment = jnp.where(segment_index < 8, 0, segment_index - 7)
        local_parent = jnp.where(segment_index < 8, -1, jnp.where(segment_index < 12, 0, 1 + (segment_index - 12) // 2))
        start_pos = jnp.where(segment_index < 8, chosen_within * PIECE, jnp.where(segment_index < 12, 8 * SEG + piece_offset * PIECE, 9 * SEG + piece_offset * PIECE))
        segment_id = chosen_tree * 13 + local_segment
        parent_id = jnp.where(local_parent < 0, -1, chosen_tree * 13 + local_parent)
        return (segment_id.astype(jnp.int32), parent_id.astype(jnp.int32), start_pos.astype(jnp.int32))
    group_keys = jax.random.split(key, N_FSDP)
    return jax.vmap(one_group)(group_keys)


def draw_piece_segment(key, part):
    return tree_layout(key)[0]


def draw_piece_parent(key, part):
    return tree_layout(key)[1]


def draw_piece_start(key, part):
    return tree_layout(key)[2]


def steps_of(stream_key, extent, shards, least, high):
    level = 1.0
    for axis_at, blocks in shards:
        steps = jax.random.uniform(jax.random.fold_in(jax.random.fold_in(stream_key, 6), axis_at), (blocks,), jnp.float32, least / len(shards), high / len(shards))
        level = level * jnp.repeat(jnp.exp(steps), extent[axis_at] // blocks).reshape((-1,) + (1,) * (len(extent) - 1 - axis_at))
    return level


def scatter_about(rng, extent, spread, bound, cuts=(), kind=jnp.bfloat16):
    values = jax.random.normal(rng, extent, jnp.float32) * spread
    if len(cuts) > 0:
        values = steps_of(rng, extent, cuts, -0.22, 0.18) * values
    return jnp.clip(values, min=-bound, max=bound).astype(kind)


def setup_inputs(seed: int = 0) -> dict:
    seeds = jax.random.split(jax.random.key(seed), 15)
    return {
        "tokens": scatter_about(seeds[0], (TOKENS, D), 1.0, 6.0, ((0, 16),)),
        "cotangent": scatter_about(seeds[1], (TOKENS, D), 1.0, 6.0, ((0, 16),)),
        "attn_gain": jnp.clip(1.0 + 0.18 * jax.random.normal(seeds[2], (D,), jnp.float32), 0.099609375, 1.8984375).astype(jnp.bfloat16),
        "w_query": scatter_about(seeds[3], (D, HEADS * HEAD), (D // 16) ** -0.5, 0.5, ((0, 16), (1, 2))),
        "w_key": scatter_about(seeds[4], (D, KV_HEADS * HEAD), (D // 16) ** -0.5, 0.5, ((0, 16), (1, 2))),
        "w_value": scatter_about(seeds[5], (D, KV_HEADS * HEAD), D ** -0.5, 0.125, ((0, 16), (1, 2))),
        "w_out": scatter_about(seeds[6], (HEADS * HEAD, D), (HEADS * HEAD // 64) ** -0.5, 1.0, ((0, 2), (1, 16))),
        "ffn_gain": jnp.clip(1.0 + 0.18 * jax.random.normal(seeds[7], (D,), jnp.float32), 0.099609375, 1.8984375).astype(jnp.bfloat16),
        "w_gate": scatter_about(seeds[8], (D, FF), D ** -0.5, 0.125, ((0, 16), (1, 2))),
        "w_up": scatter_about(seeds[9], (D, FF), D ** -0.5, 0.125, ((0, 16), (1, 2))),
        "w_down": scatter_about(seeds[10], (FF, D), (FF // 16) ** -0.5, 0.25, ((0, 2), (1, 16))),
        "piece_segment": draw_piece_segment(jax.random.fold_in(seeds[14], 71), 0),
        "piece_parent": draw_piece_parent(jax.random.fold_in(seeds[14], 71), 0),
        "piece_start": draw_piece_start(jax.random.fold_in(seeds[14], 71), 0),
    }


@jax.custom_vjp
def low(v):
    return lax.optimization_barrier(v.astype(jnp.bfloat16)).astype(jnp.float32)

@jax.custom_vjp
def low_back(v):
    return v

def low_keep(v):
    return (low(v), None)

def low_pass(kept, grad):
    return (grad,)

def back_keep(v):
    return (v, None)

def back_low(kept, grad):
    return (low(grad),)
low.defvjp(low_keep, low_pass)
low_back.defvjp(back_keep, back_low)
epsilon = 1e-05
rope_base = 10000000.0
residual_scale = 0.22
score_scale = 0.015625
masked_score = -1e+30

def matmul_high(left_side, right_side):
    return jnp.dot(left_side, right_side, precision=lax.Precision.HIGHEST, preferred_element_type=jnp.float32)

def rms_norm(residual_in, gain_vector):
    inv_root = lax.rsqrt(lax.optimization_barrier(jnp.mean(residual_in * residual_in, axis=-1, keepdims=True)) + epsilon)
    return residual_in * inv_root * gain_vector

def rope_tables(positions, head_width):
    frequency = rope_base ** (-(jnp.arange(head_width // 2).astype(jnp.float32) * 2.0) / head_width)
    angles = positions.astype(jnp.float32)[:, None] * frequency[None, :]
    angles = jnp.concatenate([angles, angles], axis=-1)
    return (jnp.cos(angles), jnp.sin(angles))

def rotate_pairs(values, cosine_table, sine_table):
    half_width = values.shape[-1] // 2
    turned = jnp.concatenate([-values[..., half_width:], values[..., :half_width]], axis=-1)
    return values * cosine_table[:, None, :] + turned * sine_table[:, None, :]

def visible_mask(tree_query, segment_query, parent_query, position_query, tree_key, segment_key, position_key):
    same_tree = tree_query[:, None] == tree_key[None, :]
    on_path = (position_key[None, :] < 8 * SEG) | (segment_query[:, None] == segment_key[None, :]) | (parent_query[:, None] == segment_key[None, :])
    causal = position_key[None, :] <= position_query[:, None]
    return same_tree & on_path & causal

def group_attention(operands):
    queries, key_vectors, values, tree_ids, segments, parents, positions = operands
    visible = visible_mask(tree_ids, segments, parents, positions, tree_ids, segments, positions)

    def head_attention(head_operands):
        query_head, key_head, value_head = head_operands
        scores = low_back(score_scale * matmul_high(query_head, key_head.T))
        scores = jnp.where(visible, scores, masked_score)
        weights = low(jax.nn.softmax(scores, axis=-1))
        return matmul_high(weights, value_head)
    repeat_count = queries.shape[1] // key_vectors.shape[1]
    keys_full = jnp.repeat(key_vectors, repeat_count, axis=1)
    values_full = jnp.repeat(values, repeat_count, axis=1)
    outputs = lax.map(jax.checkpoint(head_attention), (jnp.transpose(queries, (1, 0, 2)), jnp.transpose(keys_full, (1, 0, 2)), jnp.transpose(values_full, (1, 0, 2))))
    return jnp.transpose(outputs, (1, 0, 2))

def reference(tokens, cotangent, attn_gain, w_query, w_key, w_value, w_out, ffn_gain, w_gate, w_up, w_down, piece_segment, piece_parent, piece_start):
    offsets = jnp.tile(jnp.arange(PIECE, dtype=jnp.int32), GROUP_PIECES)
    positions = jnp.repeat(piece_start, PIECE, axis=1) + offsets[None, :]
    segments = jnp.repeat(piece_segment, PIECE, axis=1)
    tree_ids = segments // 13
    parents = jnp.repeat(piece_parent, PIECE, axis=1)
    cosine_table, sine_table = rope_tables(positions.reshape(TOKENS), HEAD)

    def forward(residual_in, attn_scale, query_w, key_w, value_w, out_w, ffn_scale, gate_w, up_w, down_w):
        normed = low(rms_norm(residual_in, attn_scale))
        query_raw = low_back(matmul_high(normed, query_w))
        key_raw = low_back(matmul_high(normed, key_w))
        value_raw = low_back(matmul_high(normed, value_w))
        queries = low(rotate_pairs(query_raw.reshape(TOKENS, HEADS, HEAD), cosine_table, sine_table))
        key_vectors = low(rotate_pairs(key_raw.reshape(TOKENS, KV_HEADS, HEAD), cosine_table, sine_table))
        values = low(value_raw).reshape(TOKENS, KV_HEADS, HEAD)
        attended = lax.map(group_attention, (queries.reshape(N_FSDP, GROUP_TOK, HEADS, HEAD), key_vectors.reshape(N_FSDP, GROUP_TOK, KV_HEADS, HEAD), values.reshape(N_FSDP, GROUP_TOK, KV_HEADS, HEAD), tree_ids, segments, parents, positions))
        attended = low(low_back(attended.reshape(TOKENS, HEADS * HEAD)))
        branch = low_back(matmul_high(attended, out_w))
        middle = residual_in + residual_scale * branch
        normed_ffn = low(rms_norm(middle, ffn_scale))
        gate_proj = low_back(matmul_high(normed_ffn, gate_w))
        up_proj = low_back(matmul_high(normed_ffn, up_w))
        hidden = low(jax.nn.silu(gate_proj) * up_proj)
        ffn_out = low_back(matmul_high(hidden, down_w))
        return middle + residual_scale * ffn_out
    inputs = tuple((argument.astype(jnp.float32) for argument in (tokens, attn_gain, w_query, w_key, w_value, w_out, ffn_gain, w_gate, w_up, w_down)))
    result, pullback = jax.vjp(forward, *inputs)
    gradients = pullback(cotangent.astype(jnp.float32))
    return (result.astype(jnp.bfloat16), gradients[0], gradients[1], gradients[2], gradients[3], gradients[4], gradients[5], gradients[6], gradients[7], gradients[8], gradients[9])
```

```python
import functools

import jax
import jax.numpy as jnp
from jax import lax
from jax.experimental import pallas as pl
from jax.experimental.pallas import tpu as pltpu
from jax.sharding import PartitionSpec as P

HEAD = 64
SEG = 128
TRUNK = 8 * SEG
BRANCHES = 4
LEAVES = 8
GROUP = TRUNK + (BRANCHES + LEAVES) * SEG
DEPTH = TRUNK + 2 * SEG
TILE = 2 * SEG

epsilon = 1e-05
rope_base = 10000000.0
residual_scale = 0.22
score_scale = 0.015625
masked_score = -1e30

FIRST = (((0,), (0,)), ((), ()))
LAST = (((1,), (1,)), ((), ()))
PLAIN = (((1,), (0,)), ((), ()))


def dot(left_side, right_side, dims=PLAIN):
    return lax.dot_general(left_side, right_side, dims, preferred_element_type=jnp.float32)


def rope_tables():
    frequency = rope_base ** (-(jnp.arange(HEAD // 2).astype(jnp.float32) * 2.0) / HEAD)
    angles = jnp.arange(DEPTH).astype(jnp.float32)[:, None] * frequency[None, :]
    sine = jnp.sin(angles)
    cosine = jnp.cos(angles)
    return (
        jnp.concatenate([cosine] * 4, axis=-1),
        jnp.concatenate([-sine, sine, -sine, sine], axis=-1),
    )


def lanes(values):
    return lax.broadcasted_iota(jnp.int32, values.shape, 1)


def swap_halves(values):
    return jnp.where(
        lanes(values) % HEAD < HEAD // 2,
        pltpu.roll(values, 128 - HEAD // 2, 1),
        pltpu.roll(values, HEAD // 2, 1),
    )


def only_head(values, head):
    return jnp.where(lanes(values) // HEAD == head, values, jnp.zeros_like(values))


def query_tiles(work):
    for j in range(TRUNK // TILE):
        prefix = [(0, j * TILE, False)] if j else []
        work(j * TILE, prefix + [(j * TILE, TILE, True)], False)

    def branch(i, carry):
        row = pl.multiple_of(TRUNK + i * TILE, TILE)
        work(row, [(0, TRUNK, False), (row, TILE, True)], True)
        return carry

    lax.fori_loop(0, BRANCHES * SEG // TILE, branch, 0)

    def leaf(i, carry):
        row = pl.multiple_of(TRUNK + BRANCHES * SEG + i * TILE, TILE)
        parent = pl.multiple_of(TRUNK + i * SEG, SEG)
        work(row, [(0, TRUNK, False), (parent, SEG, False), (row, TILE, True)], True)
        return carry

    lax.fori_loop(0, LEAVES * SEG // TILE, leaf, 0)


def visible_scores(keys, query, own, one_segment):
    scores = dot(keys, query, LAST)
    if not own:
        return scores
    key_at = lax.broadcasted_iota(jnp.int32, scores.shape, 0)
    query_at = lax.broadcasted_iota(jnp.int32, scores.shape, 1)
    seen = key_at <= query_at
    if one_segment:
        seen = seen & (key_at // SEG == query_at // SEG)
    return jnp.where(seen, scores, masked_score)


def attention_forward_kernel(
    to_ref, start_ref, raw_ref, cos_ref, sin_ref, out_ref, q_ref, k_ref, v_ref, log_ref, held
):
    width = q_ref.shape[1]
    pieces = to_ref.shape[0]
    piece = raw_ref.shape[0] // pieces

    def place(p, carry):
        rows = pl.ds(pl.multiple_of(p * piece, piece), piece)
        to = pl.ds(pl.multiple_of(to_ref[p], piece), piece)
        at = pl.ds(pl.multiple_of(start_ref[p], piece), piece)
        cosine, sine = cos_ref[at, :], sin_ref[at, :]

        def turn(values):
            return values * cosine + swap_halves(values) * sine

        for g in range(width // 128):
            cut = slice(g * 128, g * 128 + 128)
            turned = turn(raw_ref[rows, cut]).astype(jnp.bfloat16)
            q_ref[to, cut] = turned * jnp.bfloat16(score_scale)
        pair = raw_ref[rows, width : width + 128]
        low = lanes(pair) < HEAD
        key = turn(pair)
        key = jnp.where(low, key, pltpu.roll(key, HEAD, 1)).astype(jnp.bfloat16)
        value = jnp.where(low, pltpu.roll(pair, HEAD, 1), pair).astype(jnp.bfloat16)
        for g in range(width // 128):
            cut = slice(g * 128, g * 128 + 128)
            k_ref[to, cut] = key
            v_ref[to, cut] = value
        return carry

    lax.fori_loop(0, pieces, place, 0)

    def work(row, parts, one_segment):
        rows = pl.ds(row, TILE)

        def one_head(head, carry):
            query = only_head(q_ref[rows, :], head)
            scores = [
                visible_scores(k_ref[pl.ds(first, count), :], query, own, one_segment)
                for first, count, own in parts
            ]
            largest = functools.reduce(
                jnp.maximum, [jnp.max(s, axis=0, keepdims=True) for s in scores]
            )
            exponent = [jnp.exp(s - largest) for s in scores]
            total = functools.reduce(
                jnp.add, [jnp.sum(e, axis=0, keepdims=True) for e in exponent]
            )
            inverse = 1.0 / total
            result = functools.reduce(
                jnp.add,
                [
                    dot((e * inverse).astype(jnp.bfloat16), v_ref[pl.ds(first, count), :], FIRST)
                    for e, (first, count, own) in zip(exponent, parts)
                ],
            )
            log_ref[head, :, rows] = largest + jnp.log(total)
            before = held[rows, :]
            held[rows, :] = jnp.where(
                lanes(before) // HEAD == head, result.astype(jnp.bfloat16), before
            )
            return carry

        lax.fori_loop(0, width // HEAD, one_head, 0)

    query_tiles(work)

    def back(p, carry):
        rows = pl.ds(pl.multiple_of(p * piece, piece), piece)
        to = pl.ds(pl.multiple_of(to_ref[p], piece), piece)
        out_ref[rows, :] = held[to, :]
        return carry

    lax.fori_loop(0, pieces, back, 0)


def attention_backward_kernel(
    to_ref,
    start_ref,
    grad_ref,
    q_ref,
    k_ref,
    v_ref,
    log_ref,
    cos_ref,
    sin_ref,
    out_ref,
    og_ref,
    dq_ref,
    dk_ref,
    dv_ref,
):
    width = q_ref.shape[1]
    pieces = to_ref.shape[0]
    piece = grad_ref.shape[0] // pieces

    def place(p, carry):
        rows = pl.ds(pl.multiple_of(p * piece, piece), piece)
        to = pl.ds(pl.multiple_of(to_ref[p], piece), piece)
        og_ref[to, :] = grad_ref[rows, :]
        return carry

    lax.fori_loop(0, pieces, place, 0)
    dk_ref[...] = jnp.zeros_like(dk_ref)
    dv_ref[...] = jnp.zeros_like(dv_ref)

    def work(row, parts, one_segment):
        rows = pl.ds(row, TILE)
        dq_ref[rows, :] = jnp.zeros((TILE, width), jnp.float32)

        def one_head(head, carry):
            query = only_head(q_ref[rows, :], head)
            out_grad = only_head(og_ref[rows, :], head)
            log_total = log_ref[head, :, rows]
            weights, products = [], []
            for first, count, own in parts:
                keys = pl.ds(first, count)
                scores = visible_scores(k_ref[keys, :], query, own, one_segment)
                weights.append(jnp.exp(scores - log_total))
                products.append(dot(v_ref[keys, :], out_grad, LAST))
            inner = functools.reduce(
                jnp.add,
                [jnp.sum(w * d, axis=0, keepdims=True) for w, d in zip(weights, products)],
            )
            query_grad = jnp.zeros((TILE, width), jnp.float32)
            for (first, count, own), w, d in zip(parts, weights, products):
                keys = pl.ds(first, count)
                score_grad = (w * (d - inner)).astype(jnp.bfloat16)
                dv_ref[keys, :] += dot(w.astype(jnp.bfloat16), out_grad)
                dk_ref[keys, :] += dot(score_grad, query)
                query_grad += dot(score_grad, k_ref[keys, :], FIRST)
            dq_ref[rows, :] += only_head(query_grad, head)
            return carry

        lax.fori_loop(0, width // HEAD, one_head, 0)

    query_tiles(work)

    def back(p, carry):
        rows = pl.ds(pl.multiple_of(p * piece, piece), piece)
        to = pl.ds(pl.multiple_of(to_ref[p], piece), piece)
        at = pl.ds(pl.multiple_of(start_ref[p], piece), piece)
        cosine, sine = cos_ref[at, :], sin_ref[at, :]

        def turn_back(values):
            return values * cosine - swap_halves(values) * sine

        def over_heads(ref):
            total = functools.reduce(
                jnp.add, [ref[to, g * 128 : g * 128 + 128] for g in range(width // 128)]
            )
            return total + pltpu.roll(total, HEAD, 1)

        for g in range(width // 128):
            cut = slice(g * 128, g * 128 + 128)
            turned = turn_back(score_scale * dq_ref[to, cut])
            out_ref[rows, cut] = turned.astype(jnp.bfloat16)
        key = turn_back(over_heads(dk_ref))
        value = over_heads(dv_ref)
        pair = jnp.where(lanes(key) < HEAD, key, value)
        out_ref[rows, width : width + 128] = pair.astype(jnp.bfloat16)
        return carry

    lax.fori_loop(0, pieces, back, 0)


SMEM = pl.BlockSpec(memory_space=pltpu.SMEM)
VMEM = pl.BlockSpec(memory_space=pltpu.VMEM)
VMEM_LIMIT = 48 * 1024 * 1024


def attention_cost(width, products):
    flops = products * 2 * GROUP * (GROUP * 2 // 5) * width
    return pl.CostEstimate(
        flops=flops, bytes_accessed=16 * GROUP * width, transcendentals=GROUP * GROUP * width // 128
    )


def attention_forward(places, starts, raw, tables):
    width = raw.shape[1] - 2 * HEAD
    rows = raw.shape[0]
    kept = jax.ShapeDtypeStruct((rows, width), jnp.bfloat16)
    return pl.pallas_call(
        attention_forward_kernel,
        out_shape=[kept] * 4 + [jax.ShapeDtypeStruct((width // HEAD, 1, rows), jnp.float32)],
        in_specs=[SMEM, SMEM, VMEM, VMEM, VMEM],
        out_specs=[VMEM] * 5,
        scratch_shapes=[pltpu.VMEM((rows, width), jnp.bfloat16)],
        compiler_params=pltpu.CompilerParams(vmem_limit_bytes=VMEM_LIMIT),
        cost_estimate=attention_cost(width, 4),
        name="attention_forward",
    )(places, starts, raw, *tables)


def attention_backward(places, starts, out_grad, kept, tables):
    rows, width = out_grad.shape
    return pl.pallas_call(
        attention_backward_kernel,
        out_shape=jax.ShapeDtypeStruct((rows, width + 2 * HEAD), jnp.bfloat16),
        in_specs=[SMEM, SMEM] + [VMEM] * 7,
        out_specs=VMEM,
        scratch_shapes=[
            pltpu.VMEM((rows, width), jnp.bfloat16),
            pltpu.VMEM((rows, width), jnp.float32),
            pltpu.VMEM((rows, width), jnp.float32),
            pltpu.VMEM((rows, width), jnp.float32),
        ],
        compiler_params=pltpu.CompilerParams(vmem_limit_bytes=VMEM_LIMIT),
        cost_estimate=attention_cost(width, 10),
        name="attention_backward",
    )(places, starts, out_grad, *kept, *tables)


def norm_backward(gradient, normed, inv_root):
    return inv_root * (gradient - normed * jnp.mean(gradient * normed, axis=-1, keepdims=True))


def inverse_root(values):
    return lax.rsqrt(jnp.mean(values * values, axis=-1, keepdims=True) + epsilon)


PLANE = ("context", "tensor")


def gather_rows(values):
    return lax.all_gather(values, PLANE, axis=0, tiled=True)


def scatter_rows(partial):
    return lax.psum_scatter(
        partial.astype(jnp.bfloat16), PLANE, scatter_dimension=0, tiled=True
    ).astype(jnp.float32)


def local(
    tokens,
    cotangent,
    attn_gain,
    w_query,
    w_key,
    w_value,
    w_out,
    ffn_gain,
    w_gate,
    w_up,
    w_down,
    piece_segment,
    piece_parent,
    piece_start,
):
    groups = lax.axis_size("context")
    cores = lax.axis_size("tensor")
    depth = w_query.shape[0]
    kv_count = w_key.shape[1] // HEAD
    sharing = groups // kv_count
    share = tokens.shape[0] // cores
    first_row = lax.axis_index("tensor") * share

    def my_rows(values):
        return lax.dynamic_slice_in_dim(values, first_row, share, 0)

    def blocks(weight):
        return jnp.transpose(weight.reshape(depth, groups, -1), (1, 0, 2))

    def kv_blocks(weight):
        return jnp.repeat(jnp.transpose(weight.reshape(depth, kv_count, HEAD), (1, 0, 2)), sharing, 0)

    def spread(weight_blocks):
        mine = lax.all_to_all(weight_blocks, "context", 0, 0)
        mine = mine.reshape(groups * depth, -1)
        return lax.all_gather(mine, "fsdp", axis=0, tiled=True)

    gains = jnp.stack([attn_gain, ffn_gain], axis=1)
    gains = jnp.broadcast_to(jnp.pad(gains, ((0, 0), (0, 126))), (groups, depth, 128))
    packed = spread(
        jnp.concatenate(
            [blocks(w_query), kv_blocks(w_key), kv_blocks(w_value), blocks(w_out.T), gains], axis=2
        )
    )
    width = w_query.shape[1] // groups
    qkv_full = packed[:, : width + 2 * HEAD]
    out_full = packed[:, width + 2 * HEAD : 2 * width + 2 * HEAD]
    gains_full = packed[:, 2 * width + 2 * HEAD :].astype(jnp.float32)
    attn_scale, ffn_scale = gains_full[:, 0], gains_full[:, 1]
    gate_full = spread(blocks(w_gate))
    up_full = spread(blocks(w_up))
    down_full = spread(blocks(w_down.T))

    segment, starts = piece_segment[0] % 13, piece_start[0]
    places = jnp.where(
        segment == 0,
        starts,
        jnp.where(
            segment <= BRANCHES,
            starts + (segment - 1) * SEG,
            starts + (segment - 1 - BRANCHES) * SEG + (BRANCHES - 1) * SEG,
        ),
    )
    tables = rope_tables()

    inputs_full = gather_rows(my_rows(tokens)).astype(jnp.float32)
    hidden_first = (inputs_full * inverse_root(inputs_full) * attn_scale).astype(jnp.bfloat16)
    residual_in = my_rows(tokens).astype(jnp.float32)
    grad_result = my_rows(cotangent).astype(jnp.float32)
    ffn_grad = gather_rows((residual_scale * grad_result).astype(jnp.bfloat16))

    raw = dot(hidden_first, qkv_full)
    attended, *kept = attention_forward(places, starts, raw, tables)
    branch = scatter_rows(dot(attended, out_full, LAST))
    middle = residual_in + residual_scale * branch
    norm_second = inverse_root(middle)
    normed_second = middle * norm_second
    hidden_second = gather_rows((normed_second * ffn_scale).astype(jnp.bfloat16))

    gate_proj = dot(hidden_second, gate_full)
    up_proj = dot(hidden_second, up_full)
    sigmoid_gate = jax.nn.sigmoid(gate_proj)
    silu_gate = gate_proj * sigmoid_gate
    hidden = (silu_gate * up_proj).astype(jnp.bfloat16)
    grad_hidden = dot(ffn_grad, down_full)
    silu_slope = sigmoid_gate * (1.0 + gate_proj * (1.0 - sigmoid_gate))
    grad_gate_proj = (grad_hidden * up_proj * silu_slope).astype(jnp.bfloat16)
    grad_up_proj = (grad_hidden * silu_gate).astype(jnp.bfloat16)
    grad_second = scatter_rows(
        dot(grad_gate_proj, gate_full, LAST) + dot(grad_up_proj, up_full, LAST)
    )
    ffn_out = scatter_rows(dot(hidden, down_full, LAST))
    result = (middle + residual_scale * ffn_out).astype(jnp.bfloat16)
    result = lax.all_gather(result, "tensor", axis=0, tiled=True)

    def collect(gradient):
        mine = lax.psum_scatter(
            gradient.astype(jnp.bfloat16), "fsdp", scatter_dimension=0, tiled=True
        )
        return lax.all_to_all(mine.reshape(groups, depth, -1), "context", 0, 0)

    def columns(gradient):
        return jnp.transpose(gradient, (1, 0, 2)).reshape(depth, -1).astype(jnp.float32)

    grad_down = collect(dot(ffn_grad, hidden, FIRST))
    grad_gate = collect(dot(hidden_second, grad_gate_proj, FIRST))
    grad_up = collect(dot(hidden_second, grad_up_proj, FIRST))

    grad_ffn_gain = jnp.sum(grad_second * normed_second, axis=0)
    grad_middle = grad_result + norm_backward(grad_second * ffn_scale, normed_second, norm_second)
    attn_grad = gather_rows((residual_scale * grad_middle).astype(jnp.bfloat16))
    grad_attended = dot(attn_grad, out_full).astype(jnp.bfloat16)
    back = attention_backward(places, starts, grad_attended, kept, tables)
    grad_first = scatter_rows(dot(back, qkv_full, LAST))
    grad_attn = collect(
        jnp.concatenate([dot(hidden_first, back, FIRST), dot(attn_grad, attended, FIRST)], axis=1)
    )
    norm_first = inverse_root(residual_in)
    normed_first = residual_in * norm_first
    grad_attn_gain = jnp.sum(grad_first * normed_first, axis=0)
    grad_tokens = grad_middle + norm_backward(grad_first * attn_scale, normed_first, norm_first)
    grad_tokens = lax.all_gather(grad_tokens, "tensor", axis=0, tiled=True)

    gain_grads = lax.psum(
        jnp.stack([grad_attn_gain, grad_ffn_gain]), ("fsdp", "context", "tensor")
    )
    rank = lax.axis_index("fsdp") * groups + lax.axis_index("context")
    gain_grads = lax.dynamic_slice_in_dim(gain_grads, rank * depth, depth, 1)

    def kv_columns(gradient):
        gradient = gradient.astype(jnp.float32).reshape(kv_count, sharing, depth, HEAD)
        return jnp.transpose(jnp.sum(gradient, axis=1), (1, 0, 2)).reshape(depth, -1)

    return (
        result,
        grad_tokens,
        gain_grads[0],
        columns(grad_attn[:, :, :width]),
        kv_columns(grad_attn[:, :, width : width + HEAD]),
        kv_columns(grad_attn[:, :, width + HEAD : width + 2 * HEAD]),
        columns(grad_attn[:, :, width + 2 * HEAD :]).T,
        gain_grads[1],
        columns(grad_gate),
        columns(grad_up),
        columns(grad_down).T,
    )


ROWS = ("fsdp", "context")


def solution(mesh):
    return jax.shard_map(
        local,
        mesh=mesh,
        in_specs=(
            P(ROWS, None),
            P(ROWS, None),
            P(ROWS),
            P(ROWS, "tensor"),
            P(ROWS, "tensor"),
            P(ROWS, "tensor"),
            P("tensor", ROWS),
            P(ROWS),
            P(ROWS, "tensor"),
            P(ROWS, "tensor"),
            P("tensor", ROWS),
            P("fsdp", None),
            P("fsdp", None),
            P("fsdp", None),
        ),
        out_specs=(
            P(ROWS, None),
            P(ROWS, None),
            P(ROWS),
            P(ROWS, "tensor"),
            P(ROWS, "tensor"),
            P(ROWS, "tensor"),
            P("tensor", ROWS),
            P(ROWS),
            P(ROWS, "tensor"),
            P(ROWS, "tensor"),
            P("tensor", ROWS),
        ),
        check_vma=False,
    )
```

```python
import functools

import jax
import jax.numpy as jnp
from jax import lax
from jax.experimental import pallas as pl
from jax.experimental.pallas import tpu as pltpu
from jax.sharding import PartitionSpec as P

HEAD = 64
SEG = 128
TRUNK = 8 * SEG
BRANCHES = 4
LEAVES = 8
GROUP = TRUNK + (BRANCHES + LEAVES) * SEG
DEPTH = TRUNK + 2 * SEG
TILE = 2 * SEG

epsilon = 1e-05
rope_base = 10000000.0
residual_scale = 0.22
score_scale = 0.015625
masked_score = -1e30

FIRST = (((0,), (0,)), ((), ()))
LAST = (((1,), (1,)), ((), ()))
PLAIN = (((1,), (0,)), ((), ()))


def dot(left_side, right_side, dims=PLAIN):
    return lax.dot_general(left_side, right_side, dims, preferred_element_type=jnp.float32)


def rope_tables():
    frequency = rope_base ** (-(jnp.arange(HEAD // 2).astype(jnp.float32) * 2.0) / HEAD)
    angles = jnp.arange(DEPTH).astype(jnp.float32)[:, None] * frequency[None, :]
    sine = jnp.sin(angles)
    cosine = jnp.cos(angles)
    return (
        jnp.concatenate([cosine] * 4, axis=-1),
        jnp.concatenate([-sine, sine, -sine, sine], axis=-1),
    )


def lanes(values):
    return lax.broadcasted_iota(jnp.int32, values.shape, 1)


def swap_halves(values):
    return jnp.where(
        lanes(values) % HEAD < HEAD // 2,
        pltpu.roll(values, 128 - HEAD // 2, 1),
        pltpu.roll(values, HEAD // 2, 1),
    )


def only_head(values, head):
    return jnp.where(lanes(values) // HEAD == head, values, jnp.zeros_like(values))


def query_tiles(work):
    for j in range(TRUNK // TILE):
        prefix = [(0, j * TILE, False)] if j else []
        work(j * TILE, prefix + [(j * TILE, TILE, True)], False)

    def branch(i, carry):
        row = pl.multiple_of(TRUNK + i * TILE, TILE)
        work(row, [(0, TRUNK, False), (row, TILE, True)], True)
        return carry

    lax.fori_loop(0, BRANCHES * SEG // TILE, branch, 0)

    def leaf(i, carry):
        row = pl.multiple_of(TRUNK + BRANCHES * SEG + i * TILE, TILE)
        parent = pl.multiple_of(TRUNK + i * SEG, SEG)
        work(row, [(0, TRUNK, False), (parent, SEG, False), (row, TILE, True)], True)
        return carry

    lax.fori_loop(0, LEAVES * SEG // TILE, leaf, 0)


def visible_scores(keys, query, own, one_segment):
    scores = dot(keys, query, LAST)
    if not own:
        return scores
    key_at = lax.broadcasted_iota(jnp.int32, scores.shape, 0)
    query_at = lax.broadcasted_iota(jnp.int32, scores.shape, 1)
    seen = key_at <= query_at
    if one_segment:
        seen = seen & (key_at // SEG == query_at // SEG)
    return jnp.where(seen, scores, masked_score)


def attention_forward_kernel(
    to_ref, start_ref, raw_ref, cos_ref, sin_ref, out_ref, q_ref, k_ref, v_ref, log_ref, held
):
    width = q_ref.shape[1]
    pieces = to_ref.shape[0]
    piece = raw_ref.shape[0] // pieces

    def place(p, carry):
        rows = pl.ds(pl.multiple_of(p * piece, piece), piece)
        to = pl.ds(pl.multiple_of(to_ref[p], piece), piece)
        at = pl.ds(pl.multiple_of(start_ref[p], piece), piece)
        cosine, sine = cos_ref[at, :], sin_ref[at, :]

        def turn(values):
            return values * cosine + swap_halves(values) * sine

        for g in range(width // 128):
            cut = slice(g * 128, g * 128 + 128)
            turned = turn(raw_ref[rows, cut]).astype(jnp.bfloat16)
            q_ref[to, cut] = turned * jnp.bfloat16(score_scale)
        pair = raw_ref[rows, width : width + 128]
        low = lanes(pair) < HEAD
        key = turn(pair)
        key = jnp.where(low, key, pltpu.roll(key, HEAD, 1)).astype(jnp.bfloat16)
        value = jnp.where(low, pltpu.roll(pair, HEAD, 1), pair).astype(jnp.bfloat16)
        for g in range(width // 128):
            cut = slice(g * 128, g * 128 + 128)
            k_ref[to, cut] = key
            v_ref[to, cut] = value
        return carry

    lax.fori_loop(0, pieces, place, 0)

    def work(row, parts, one_segment):
        rows = pl.ds(row, TILE)

        def one_head(head, carry):
            query = only_head(q_ref[rows, :], head)
            scores = [
                visible_scores(k_ref[pl.ds(first, count), :], query, own, one_segment)
                for first, count, own in parts
            ]
            largest = functools.reduce(
                jnp.maximum, [jnp.max(s, axis=0, keepdims=True) for s in scores]
            )
            exponent = [jnp.exp(s - largest) for s in scores]
            total = functools.reduce(
                jnp.add, [jnp.sum(e, axis=0, keepdims=True) for e in exponent]
            )
            inverse = 1.0 / total
            result = functools.reduce(
                jnp.add,
                [
                    dot((e * inverse).astype(jnp.bfloat16), v_ref[pl.ds(first, count), :], FIRST)
                    for e, (first, count, own) in zip(exponent, parts)
                ],
            )
            log_ref[head, :, rows] = largest + jnp.log(total)
            before = held[rows, :]
            held[rows, :] = jnp.where(
                lanes(before) // HEAD == head, result.astype(jnp.bfloat16), before
            )
            return carry

        lax.fori_loop(0, width // HEAD, one_head, 0)

    query_tiles(work)

    def back(p, carry):
        rows = pl.ds(pl.multiple_of(p * piece, piece), piece)
        to = pl.ds(pl.multiple_of(to_ref[p], piece), piece)
        out_ref[rows, :] = held[to, :]
        return carry

    lax.fori_loop(0, pieces, back, 0)


def attention_backward_kernel(
    to_ref,
    start_ref,
    grad_ref,
    q_ref,
    k_ref,
    v_ref,
    log_ref,
    cos_ref,
    sin_ref,
    out_ref,
    og_ref,
    dq_ref,
    dk_ref,
    dv_ref,
):
    width = q_ref.shape[1]
    pieces = to_ref.shape[0]
    piece = grad_ref.shape[0] // pieces

    def place(p, carry):
        rows = pl.ds(pl.multiple_of(p * piece, piece), piece)
        to = pl.ds(pl.multiple_of(to_ref[p], piece), piece)
        og_ref[to, :] = grad_ref[rows, :]
        return carry

    lax.fori_loop(0, pieces, place, 0)
    dk_ref[...] = jnp.zeros_like(dk_ref)
    dv_ref[...] = jnp.zeros_like(dv_ref)

    def work(row, parts, one_segment):
        rows = pl.ds(row, TILE)
        dq_ref[rows, :] = jnp.zeros((TILE, width), jnp.float32)

        def one_head(head, carry):
            query = only_head(q_ref[rows, :], head)
            out_grad = only_head(og_ref[rows, :], head)
            log_total = log_ref[head, :, rows]
            weights, products = [], []
            for first, count, own in parts:
                keys = pl.ds(first, count)
                scores = visible_scores(k_ref[keys, :], query, own, one_segment)
                weights.append(jnp.exp(scores - log_total))
                products.append(dot(v_ref[keys, :], out_grad, LAST))
            inner = functools.reduce(
                jnp.add,
                [jnp.sum(w * d, axis=0, keepdims=True) for w, d in zip(weights, products)],
            )
            query_grad = jnp.zeros((TILE, width), jnp.float32)
            for (first, count, own), w, d in zip(parts, weights, products):
                keys = pl.ds(first, count)
                score_grad = (w * (d - inner)).astype(jnp.bfloat16)
                dv_ref[keys, :] += dot(w.astype(jnp.bfloat16), out_grad)
                dk_ref[keys, :] += dot(score_grad, query)
                query_grad += dot(score_grad, k_ref[keys, :], FIRST)
            dq_ref[rows, :] += only_head(query_grad, head)
            return carry

        lax.fori_loop(0, width // HEAD, one_head, 0)

    query_tiles(work)

    def back(p, carry):
        rows = pl.ds(pl.multiple_of(p * piece, piece), piece)
        to = pl.ds(pl.multiple_of(to_ref[p], piece), piece)
        at = pl.ds(pl.multiple_of(start_ref[p], piece), piece)
        cosine, sine = cos_ref[at, :], sin_ref[at, :]

        def turn_back(values):
            return values * cosine - swap_halves(values) * sine

        def over_heads(ref):
            total = functools.reduce(
                jnp.add, [ref[to, g * 128 : g * 128 + 128] for g in range(width // 128)]
            )
            return total + pltpu.roll(total, HEAD, 1)

        for g in range(width // 128):
            cut = slice(g * 128, g * 128 + 128)
            turned = turn_back(score_scale * dq_ref[to, cut])
            out_ref[rows, cut] = turned.astype(jnp.bfloat16)
        key = turn_back(over_heads(dk_ref))
        value = over_heads(dv_ref)
        pair = jnp.where(lanes(key) < HEAD, key, value)
        out_ref[rows, width : width + 128] = pair.astype(jnp.bfloat16)
        return carry

    lax.fori_loop(0, pieces, back, 0)


SMEM = pl.BlockSpec(memory_space=pltpu.SMEM)
VMEM = pl.BlockSpec(memory_space=pltpu.VMEM)
VMEM_LIMIT = 48 * 1024 * 1024


def attention_cost(width, products):
    flops = products * 2 * GROUP * (GROUP * 2 // 5) * width
    return pl.CostEstimate(
        flops=flops, bytes_accessed=16 * GROUP * width, transcendentals=GROUP * GROUP * width // 128
    )


def attention_forward(places, starts, raw, tables):
    width = raw.shape[1] - 2 * HEAD
    rows = raw.shape[0]
    kept = jax.ShapeDtypeStruct((rows, width), jnp.bfloat16)
    return pl.pallas_call(
        attention_forward_kernel,
        out_shape=[kept] * 4 + [jax.ShapeDtypeStruct((width // HEAD, 1, rows), jnp.float32)],
        in_specs=[SMEM, SMEM, VMEM, VMEM, VMEM],
        out_specs=[VMEM] * 5,
        scratch_shapes=[pltpu.VMEM((rows, width), jnp.bfloat16)],
        compiler_params=pltpu.CompilerParams(vmem_limit_bytes=VMEM_LIMIT),
        cost_estimate=attention_cost(width, 4),
        name="attention_forward",
    )(places, starts, raw, *tables)


def attention_backward(places, starts, out_grad, kept, tables):
    rows, width = out_grad.shape
    return pl.pallas_call(
        attention_backward_kernel,
        out_shape=jax.ShapeDtypeStruct((rows, width + 2 * HEAD), jnp.bfloat16),
        in_specs=[SMEM, SMEM] + [VMEM] * 7,
        out_specs=VMEM,
        scratch_shapes=[
            pltpu.VMEM((rows, width), jnp.bfloat16),
            pltpu.VMEM((rows, width), jnp.float32),
            pltpu.VMEM((rows, width), jnp.float32),
            pltpu.VMEM((rows, width), jnp.float32),
        ],
        compiler_params=pltpu.CompilerParams(vmem_limit_bytes=VMEM_LIMIT),
        cost_estimate=attention_cost(width, 10),
        name="attention_backward",
    )(places, starts, out_grad, *kept, *tables)


MESH = pl.DeviceIdType.MESH
ANY = pl.BlockSpec(memory_space=pl.ANY)
CHUNKS = 4
SLAB = 16


def lasting(microseconds):
    return pl.CostEstimate(
        flops=0, bytes_accessed=int(microseconds * 3_000_000), transcendentals=0
    )


class Plane:
    def __init__(self, sent, landed, diagonal=False):
        self.sent, self.landed = sent, landed
        self.copies = []
        self.rank = lax.axis_index("context")
        self.core = lax.axis_index("tensor")
        self.at_x = self.rank + 1 - 2 * lax.rem(self.rank, 2)
        self.at_y = lax.rem(self.rank + 2, 4)
        self.at_both = 3 - self.rank
        self.x = {"context": self.at_x}
        self.y = {"context": self.at_y}
        self.both = {"context": self.at_both}
        self.sibling = {"tensor": 1 - self.core}
        barrier = pltpu.get_barrier_semaphore()
        partners = [self.x, self.y, self.sibling] + ([self.both] if diagonal else [])
        for partner in partners:
            pl.semaphore_signal(barrier, inc=1, device_id=partner, device_id_type=MESH)
        pl.semaphore_wait(barrier, len(partners))

    def copy(self, number, source, target, partner):
        return pltpu.make_async_remote_copy(
            src_ref=source,
            dst_ref=target,
            send_sem=self.sent.at[number],
            recv_sem=self.landed.at[number],
            device_id=partner,
            device_id_type=MESH,
        )

    def send(self, source, target, partner):
        number = len(self.copies)
        started = self.copy(number, source, target, partner)
        started.start()
        self.copies.append(started)
        return number

    def arrive(self, number, target):
        self.copy(number, target, target, self.sibling).wait_recv()

    def finish(self):
        for started in self.copies:
            started.wait_send()


def chunk(index, rows):
    return pl.ds(index * (rows // CHUNKS), rows // CHUNKS)


class Gather:
    def __init__(self, plane, block, out):
        self.plane, self.block, self.out = plane, block, out
        self.rows = block.shape[0]
        self.to_x, self.to_y, self.across = {}, {}, {}

    def start(self, k):
        p, cut = self.plane, chunk(k, self.rows)
        target = self.out.at[p.rank, p.core, cut]
        self.to_x[k] = p.send(self.block.at[cut], target, p.x)
        self.to_y[k] = p.send(self.block.at[cut], target, p.y)
        self.across[0, k] = p.send(self.block.at[cut], target, p.sibling)

    def forward(self):
        p, out = self.plane, self.out
        onward = {}
        for k in range(CHUNKS):
            cut = chunk(k, self.rows)
            from_x, from_y = out.at[p.at_x, p.core, cut], out.at[p.at_y, p.core, cut]
            p.arrive(self.to_x[k], from_x)
            if k < CHUNKS // 2:
                onward[k] = p.send(from_x, from_x, p.y)
            self.across[1, k] = p.send(from_x, from_x, p.sibling)
            p.arrive(self.to_y[k], from_y)
            if k >= CHUNKS // 2:
                onward[k] = p.send(from_y, from_y, p.x)
            self.across[2, k] = p.send(from_y, from_y, p.sibling)
        for k in range(CHUNKS):
            far = out.at[p.at_both, p.core, chunk(k, self.rows)]
            p.arrive(onward[k], far)
            self.across[3, k] = p.send(far, far, p.sibling)

    def finish(self):
        p = self.plane
        for i, rank in enumerate((p.rank, p.at_x, p.at_y, p.at_both)):
            for k in range(CHUNKS):
                p.arrive(
                    self.across[i, k], self.out.at[rank, 1 - p.core, chunk(k, self.rows)]
                )


GATHER_COPIES = CHUNKS * 8


def add_rows(target, source, first, count):
    def step(i, carry):
        rows = pl.ds(first + i * SLAB, SLAB)
        target[rows, :] = (
            target[rows, :].astype(jnp.float32) + source[rows, :].astype(jnp.float32)
        ).astype(jnp.bfloat16)
        return carry

    lax.fori_loop(0, count // SLAB, step, 0)


class Scatter:
    def __init__(self, plane, partial, held, other, near_x, near_y, far_x, far_y, local):
        p = plane
        rows = near_x.shape[0]
        half = rows // 2
        top, low = pl.ds(0, half), pl.ds(half, half)
        order = (p.at_both, p.at_x, p.at_y, p.rank)
        across, kept = [], []
        for i, rank in enumerate(order):
            across.append(p.send(partial.at[rank, 1 - p.core], other.at[i], p.sibling))
            kept.append(pltpu.make_async_copy(partial.at[rank, p.core], held.at[i], local.at[i]))
            kept[i].start()

        def pair(i):
            p.arrive(across[i], other.at[i])
            kept[i].wait()
            add_rows(held.at[i], other.at[i], 0, rows)

        pair(0)
        first = p.send(held.at[0, top], far_x, p.x)
        second = p.send(held.at[0, low], far_y, p.y)
        pair(1)
        third = p.send(held.at[1, top], near_x.at[top], p.x)
        pair(2)
        fourth = p.send(held.at[2, low], near_y.at[low], p.y)
        p.arrive(first, far_x)
        add_rows(held.at[2], far_x, 0, half)
        fifth = p.send(held.at[2, top], near_y.at[top], p.y)
        p.arrive(second, far_y)

        def step(i, carry):
            rows, at = pl.ds(half + i * SLAB, SLAB), pl.ds(i * SLAB, SLAB)
            held[1, rows, :] = (
                held[1, rows, :].astype(jnp.float32) + far_y[at, :].astype(jnp.float32)
            ).astype(jnp.bfloat16)
            return carry

        lax.fori_loop(0, half // SLAB, step, 0)
        sixth = p.send(held.at[1, low], near_x.at[low], p.x)
        pair(3)
        p.arrive(third, near_x.at[top])
        p.arrive(fourth, near_y.at[low])
        p.arrive(fifth, near_y.at[top])
        p.arrive(sixth, near_x.at[low])
        self.parts = (held.at[3], near_x, near_y)

    def rows(self, rows):
        return sum(part[rows, :].astype(jnp.float32) for part in self.parts)


SCATTER_COPIES = 4 + 6


def scatter_scratch(share, width):
    kind = jnp.bfloat16
    return [
        pltpu.VMEM((4, share, width), kind),
        pltpu.VMEM((4, share, width), kind),
        pltpu.VMEM((share, width), kind),
        pltpu.VMEM((share, width), kind),
        pltpu.VMEM((share // 2, width), kind),
        pltpu.VMEM((share // 2, width), kind),
        pltpu.SemaphoreType.DMA((4,)),
    ]


def wires(count):
    return [pltpu.SemaphoreType.DMA((count,)), pltpu.SemaphoreType.DMA((count,))]


def row_root(values):
    return lax.rsqrt(jnp.mean(values * values, axis=-1, keepdims=True) + epsilon)


def slabs(first, count, work):
    def step(i, carry):
        work(pl.ds(first + i * SLAB, SLAB))
        return carry

    lax.fori_loop(0, count // SLAB, step, 0)


def start_kernel(
    block, gate, up, down, out, gate_out, up_out, down_out, sent, landed, local
):
    p = Plane(sent, landed, diagonal=True)
    gather = Gather(p, block, out)
    mine = [pltpu.make_async_copy(block, out.at[p.rank, p.core], local.at[0])]
    for k in range(CHUNKS):
        gather.start(k)
    moves = []
    for i, (source, target) in enumerate(((gate, gate_out), (up, up_out), (down, down_out))):
        mine.append(pltpu.make_async_copy(source.at[p.rank], target.at[p.rank], local.at[i + 1]))
        for partner, rank in ((p.x, p.at_x), (p.y, p.at_y), (p.both, p.at_both)):
            number = p.send(source.at[rank], target.at[p.rank], partner)
            moves.append((number, target.at[rank]))
    for started in mine:
        started.start()
    gather.forward()
    gather.finish()
    for number, target in moves:
        p.arrive(number, target)
    p.finish()
    for started in mine:
        started.wait()


def start_plane(block, gate, up, down):
    share, width = block.shape
    full = jax.ShapeDtypeStruct((4, 2, share, width), block.dtype)
    weight = jax.ShapeDtypeStruct(gate.shape, gate.dtype)
    full, *weights = pl.pallas_call(
        start_kernel,
        out_shape=[full, weight, weight, weight],
        in_specs=[ANY] * 4,
        out_specs=[ANY] * 4,
        scratch_shapes=wires(GATHER_COPIES + 9) + [pltpu.SemaphoreType.DMA((4,))],
        compiler_params=pltpu.CompilerParams(collective_id=1, has_side_effects=True),
        cost_estimate=lasting(80),
        name="gather_tokens",
    )(block, gate, up, down)
    return full.reshape(8 * share, width), weights


def middle_kernel(
    partial, residual, gain, out, middle, sent, landed, own_copy, hidden, *scratch
):
    p = Plane(sent, landed)
    total = Scatter(p, partial, *scratch)
    share = hidden.shape[0]
    gather = Gather(p, hidden, out)

    def work(rows):
        value = residual[rows, :].astype(jnp.float32) + residual_scale * total.rows(rows)
        middle[rows, :] = value
        hidden[rows, :] = (value * row_root(value) * gain[...]).astype(jnp.bfloat16)

    for k in range(CHUNKS):
        slabs(k * (share // CHUNKS), share // CHUNKS, work)
        gather.start(k)
    mine = pltpu.make_async_copy(hidden, out.at[p.rank, p.core], own_copy)
    mine.start()
    gather.forward()
    gather.finish()
    p.finish()
    mine.wait()


def middle_plane(partial, residual, gain):
    share, width = residual.shape
    full = jax.ShapeDtypeStruct((4, 2, share, width), jnp.bfloat16)
    out, middle = pl.pallas_call(
        middle_kernel,
        out_shape=[full, jax.ShapeDtypeStruct((share, width), jnp.float32)],
        in_specs=[ANY, VMEM, VMEM],
        out_specs=[ANY, VMEM],
        scratch_shapes=wires(GATHER_COPIES + SCATTER_COPIES)
        + [pltpu.SemaphoreType.DMA, pltpu.VMEM((share, width), jnp.bfloat16)]
        + scatter_scratch(share, width),
        compiler_params=pltpu.CompilerParams(
            collective_id=2, has_side_effects=True, vmem_limit_bytes=VMEM_LIMIT
        ),
        cost_estimate=lasting(100),
        name="middle_rows",
    )(partial.reshape(full.shape), residual, gain)
    return out.reshape(8 * share, width), middle


def second_kernel(
    partial, middle, cotangent, gain, out, grad_middle, sent, landed, own_copy, hidden, *scratch
):
    p = Plane(sent, landed)
    total = Scatter(p, partial, *scratch)
    share = hidden.shape[0]
    gather = Gather(p, hidden, out)

    def work(rows):
        value = middle[rows, :]
        root = row_root(value)
        normed = value * root
        slope = total.rows(rows) * gain[...]
        mean = jnp.mean(slope * normed, axis=-1, keepdims=True)
        gradient = cotangent[rows, :].astype(jnp.float32) + root * (slope - normed * mean)
        grad_middle[rows, :] = gradient
        hidden[rows, :] = (residual_scale * gradient).astype(jnp.bfloat16)

    for k in range(CHUNKS):
        slabs(k * (share // CHUNKS), share // CHUNKS, work)
        gather.start(k)
    mine = pltpu.make_async_copy(hidden, out.at[p.rank, p.core], own_copy)
    mine.start()
    gather.forward()
    gather.finish()
    p.finish()
    mine.wait()


def second_plane(partial, middle, cotangent, gain):
    share, width = middle.shape
    full = jax.ShapeDtypeStruct((4, 2, share, width), jnp.bfloat16)
    out, grad_middle = pl.pallas_call(
        second_kernel,
        out_shape=[full, jax.ShapeDtypeStruct((share, width), jnp.float32)],
        in_specs=[ANY, VMEM, VMEM, VMEM],
        out_specs=[ANY, VMEM],
        scratch_shapes=wires(GATHER_COPIES + SCATTER_COPIES)
        + [pltpu.SemaphoreType.DMA, pltpu.VMEM((share, width), jnp.bfloat16)]
        + scatter_scratch(share, width),
        compiler_params=pltpu.CompilerParams(
            collective_id=3, has_side_effects=True, vmem_limit_bytes=VMEM_LIMIT
        ),
        cost_estimate=lasting(100),
        name="second_rows",
    )(partial.reshape(full.shape), middle, cotangent, gain)
    return out.reshape(8 * share, width), grad_middle


def last_kernel(
    partial, residual, grad_middle, gain, result, out, result_out, sent, landed, local_copy, held, *scratch
):
    p = Plane(sent, landed)
    kept = [pltpu.make_async_copy(result, result_out.at[p.core], local_copy.at[0])]
    kept[0].start()
    given = p.send(result, result_out.at[p.core], p.sibling)
    total = Scatter(p, partial, *scratch)
    share = held.shape[0]

    def work(rows):
        value = residual[rows, :].astype(jnp.float32)
        root = row_root(value)
        normed = value * root
        slope = total.rows(rows) * gain[...]
        mean = jnp.mean(slope * normed, axis=-1, keepdims=True)
        held[rows, :] = grad_middle[rows, :] + root * (slope - normed * mean)

    across = []
    for k in range(CHUNKS):
        cut = chunk(k, share)
        slabs(k * (share // CHUNKS), share // CHUNKS, work)
        across.append(p.send(held.at[cut], out.at[p.core, cut], p.sibling))
    kept.append(pltpu.make_async_copy(held, out.at[p.core], local_copy.at[1]))
    kept[1].start()
    p.arrive(given, result_out.at[1 - p.core])
    for k in range(CHUNKS):
        p.arrive(across[k], out.at[1 - p.core, chunk(k, share)])
    p.finish()
    for started in kept:
        started.wait()


def last_plane(partial, residual, grad_middle, gain, result):
    share, width = residual.shape
    out, result_out = pl.pallas_call(
        last_kernel,
        out_shape=[
            jax.ShapeDtypeStruct((2, share, width), jnp.float32),
            jax.ShapeDtypeStruct((2, share, width), jnp.bfloat16),
        ],
        in_specs=[ANY, VMEM, VMEM, VMEM, ANY],
        out_specs=[ANY, ANY],
        scratch_shapes=wires(CHUNKS + 1 + SCATTER_COPIES)
        + [pltpu.SemaphoreType.DMA((2,)), pltpu.VMEM((share, width), jnp.float32)]
        + scatter_scratch(share, width),
        compiler_params=pltpu.CompilerParams(
            collective_id=4, has_side_effects=True, vmem_limit_bytes=VMEM_LIMIT
        ),
        cost_estimate=lasting(70),
        name="last_rows",
    )(partial.reshape(4, 2, share, width), residual, grad_middle, gain, result)
    return out.reshape(2 * share, width), result_out.reshape(2 * share, width)


def context_pairs(step):
    return [(i, i ^ step) for i in range(4)]


def swap_cores(values):
    return lax.ppermute(values, "tensor", [(0, 1), (1, 0)])


def gather_beside(block):
    rank, core = lax.axis_index("context"), lax.axis_index("tensor")
    share, width = block.shape
    mine = jnp.zeros((4, share, width), block.dtype)
    for step in range(4):
        got = lax.ppermute(block, "context", context_pairs(step)) if step else block
        mine = lax.dynamic_update_slice(mine, got[None], (rank ^ step, 0, 0))
    theirs = swap_cores(mine)
    first = jnp.where(core == 0, mine, theirs)
    second = jnp.where(core == 0, theirs, mine)
    return jnp.stack([first, second], axis=1).reshape(8 * share, width)


def scatter_beside(partial, share):
    rank, core = lax.axis_index("context"), lax.axis_index("tensor")
    blocks = partial.reshape(4, 2, share, -1)
    keep = lax.dynamic_index_in_dim(blocks, core, 1, False)
    give = lax.dynamic_index_in_dim(blocks, 1 - core, 1, False)
    both = (keep.astype(jnp.float32) + swap_cores(give).astype(jnp.float32)).astype(jnp.bfloat16)
    total = lax.dynamic_index_in_dim(both, rank, 0, False).astype(jnp.float32)
    for step in range(1, 4):
        block = lax.dynamic_index_in_dim(both, rank ^ step, 0, False)
        total += lax.ppermute(block, "context", context_pairs(step)).astype(jnp.float32)
    return total


def norm_backward(gradient, normed, inv_root):
    return inv_root * (gradient - normed * jnp.mean(gradient * normed, axis=-1, keepdims=True))


def inverse_root(values):
    return lax.rsqrt(jnp.mean(values * values, axis=-1, keepdims=True) + epsilon)


PLANE = ("context", "tensor")


def gather_rows(values):
    return lax.all_gather(values, PLANE, axis=0, tiled=True)


def scatter_rows(partial):
    return lax.psum_scatter(
        partial.astype(jnp.bfloat16), PLANE, scatter_dimension=0, tiled=True
    ).astype(jnp.float32)


def local(
    tokens,
    cotangent,
    attn_gain,
    w_query,
    w_key,
    w_value,
    w_out,
    ffn_gain,
    w_gate,
    w_up,
    w_down,
    piece_segment,
    piece_parent,
    piece_start,
):
    groups = lax.axis_size("context")
    cores = lax.axis_size("tensor")
    depth = w_query.shape[0]
    kv_count = w_key.shape[1] // HEAD
    sharing = groups // kv_count
    share = tokens.shape[0] // cores
    first_row = lax.axis_index("tensor") * share

    def my_rows(values):
        return lax.dynamic_slice_in_dim(values, first_row, share, 0)

    def blocks(weight):
        return jnp.transpose(weight.reshape(depth, groups, -1), (1, 0, 2))

    def kv_blocks(weight):
        return jnp.repeat(jnp.transpose(weight.reshape(depth, kv_count, HEAD), (1, 0, 2)), sharing, 0)

    def spread(weight_blocks):
        mine = lax.all_to_all(weight_blocks, "context", 0, 0)
        mine = mine.reshape(groups * depth, -1)
        return lax.all_gather(mine, "fsdp", axis=0, tiled=True)

    gains = jnp.stack([attn_gain, ffn_gain], axis=1)
    gains = jnp.broadcast_to(jnp.pad(gains, ((0, 0), (0, 126))), (groups, depth, 128))
    packed = spread(
        jnp.concatenate(
            [blocks(w_query), kv_blocks(w_key), kv_blocks(w_value), blocks(w_out.T), gains], axis=2
        )
    )
    width = w_query.shape[1] // groups
    qkv_full = packed[:, : width + 2 * HEAD]
    out_full = packed[:, width + 2 * HEAD : 2 * width + 2 * HEAD]
    gains_full = packed[:, 2 * width + 2 * HEAD :].astype(jnp.float32)
    attn_scale, ffn_scale = gains_full[:, 0], gains_full[:, 1]
    square = groups == 4 and cores == 2
    ffn_blocks = blocks(w_gate), blocks(w_up), blocks(w_down.T)
    tokens_half, cotangent_half = my_rows(tokens), my_rows(cotangent)
    if square:
        inputs_full, ffn_blocks = start_plane(tokens_half, *ffn_blocks)
    else:
        inputs_full = gather_rows(tokens_half)
        ffn_blocks = [lax.all_to_all(w, "context", 0, 0) for w in ffn_blocks]
    gate_full, up_full, down_full = (
        lax.all_gather(w.reshape(groups * depth, -1), "fsdp", axis=0, tiled=True)
        for w in ffn_blocks
    )

    segment, starts = piece_segment[0] % 13, piece_start[0]
    places = jnp.where(
        segment == 0,
        starts,
        jnp.where(
            segment <= BRANCHES,
            starts + (segment - 1) * SEG,
            starts + (segment - 1 - BRANCHES) * SEG + (BRANCHES - 1) * SEG,
        ),
    )
    tables = rope_tables()

    inputs_full = inputs_full.astype(jnp.float32)
    hidden_first = (inputs_full * inverse_root(inputs_full) * attn_scale).astype(jnp.bfloat16)
    residual_in = tokens_half.astype(jnp.float32)
    grad_result = cotangent_half.astype(jnp.float32)
    ffn_grad = (residual_scale * grad_result).astype(jnp.bfloat16)
    ffn_grad = gather_beside(ffn_grad) if square else gather_rows(ffn_grad)

    raw = dot(hidden_first, qkv_full)
    attended, *kept = attention_forward(places, starts, raw, tables)
    branch = dot(attended, out_full, LAST).astype(jnp.bfloat16)
    if square:
        hidden_second, middle = middle_plane(branch, tokens_half, ffn_scale[None, :])
    else:
        middle = residual_in + residual_scale * scatter_rows(branch)
        hidden_second = gather_rows((middle * inverse_root(middle) * ffn_scale).astype(jnp.bfloat16))

    gate_proj = dot(hidden_second, gate_full)
    up_proj = dot(hidden_second, up_full)
    sigmoid_gate = jax.nn.sigmoid(gate_proj)
    silu_gate = gate_proj * sigmoid_gate
    hidden = (silu_gate * up_proj).astype(jnp.bfloat16)
    grad_hidden = dot(ffn_grad, down_full)
    silu_slope = sigmoid_gate * (1.0 + gate_proj * (1.0 - sigmoid_gate))
    grad_gate_proj = (grad_hidden * up_proj * silu_slope).astype(jnp.bfloat16)
    grad_up_proj = (grad_hidden * silu_gate).astype(jnp.bfloat16)
    grad_second = (
        dot(grad_gate_proj, gate_full, LAST) + dot(grad_up_proj, up_full, LAST)
    ).astype(jnp.bfloat16)
    ffn_out = dot(hidden, down_full, LAST).astype(jnp.bfloat16)
    ffn_out = scatter_beside(ffn_out, share) if square else scatter_rows(ffn_out)
    result = (middle + residual_scale * ffn_out).astype(jnp.bfloat16)

    def collect(gradient):
        mine = lax.psum_scatter(
            gradient.astype(jnp.bfloat16), "fsdp", scatter_dimension=0, tiled=True
        )
        return lax.all_to_all(mine.reshape(groups, depth, -1), "context", 0, 0)

    def columns(gradient):
        return jnp.transpose(gradient, (1, 0, 2)).reshape(depth, -1).astype(jnp.float32)

    grad_down = collect(dot(ffn_grad, hidden, FIRST))
    grad_gate = collect(dot(hidden_second, grad_gate_proj, FIRST))
    grad_up = collect(dot(hidden_second, grad_up_proj, FIRST))

    if square:
        attn_grad, grad_middle = second_plane(
            grad_second, middle, cotangent_half, ffn_scale[None, :]
        )
    else:
        root = inverse_root(middle)
        grad_middle = grad_result + norm_backward(
            scatter_rows(grad_second) * ffn_scale, middle * root, root
        )
        attn_grad = gather_rows((residual_scale * grad_middle).astype(jnp.bfloat16))
    grad_attended = dot(attn_grad, out_full).astype(jnp.bfloat16)
    back = attention_backward(places, starts, grad_attended, kept, tables)
    grad_first = dot(back, qkv_full, LAST).astype(jnp.bfloat16)
    if square:
        grad_tokens, result = last_plane(
            grad_first, tokens_half, grad_middle, attn_scale[None, :], result
        )
    else:
        root = inverse_root(residual_in)
        grad_tokens = grad_middle + norm_backward(
            scatter_rows(grad_first) * attn_scale, residual_in * root, root
        )
        grad_tokens = lax.all_gather(grad_tokens, "tensor", axis=0, tiled=True)
        result = lax.all_gather(result, "tensor", axis=0, tiled=True)
    grad_attn = collect(
        jnp.concatenate([dot(hidden_first, back, FIRST), dot(attn_grad, attended, FIRST)], axis=1)
    )
    def kv_columns(gradient):
        gradient = gradient.astype(jnp.float32).reshape(kv_count, sharing, depth, HEAD)
        return jnp.transpose(jnp.sum(gradient, axis=1), (1, 0, 2)).reshape(depth, -1)

    grad_query = columns(grad_attn[:, :, :width])
    grad_key = kv_columns(grad_attn[:, :, width : width + HEAD])
    grad_value = kv_columns(grad_attn[:, :, width + HEAD : width + 2 * HEAD])
    grad_gate, grad_up = columns(grad_gate), columns(grad_up)

    def against(*pairs):
        return sum(jnp.sum(weight.astype(jnp.float32) * g, axis=1) for weight, g in pairs)

    gain_grads = jnp.stack(
        [
            against((w_query, grad_query), (w_key, grad_key), (w_value, grad_value)),
            against((w_gate, grad_gate), (w_up, grad_up)),
        ]
    )
    gain_grads += swap_cores(gain_grads) if square else lax.psum(gain_grads, "tensor") - gain_grads
    return (
        result,
        grad_tokens,
        gain_grads[0] / attn_gain.astype(jnp.float32),
        grad_query,
        grad_key,
        grad_value,
        columns(grad_attn[:, :, width + 2 * HEAD :]).T,
        gain_grads[1] / ffn_gain.astype(jnp.float32),
        grad_gate,
        grad_up,
        columns(grad_down).T,
    )


ROWS = ("fsdp", "context")


def solution(mesh):
    return jax.shard_map(
        local,
        mesh=mesh,
        in_specs=(
            P(ROWS, None),
            P(ROWS, None),
            P(ROWS),
            P(ROWS, "tensor"),
            P(ROWS, "tensor"),
            P(ROWS, "tensor"),
            P("tensor", ROWS),
            P(ROWS),
            P(ROWS, "tensor"),
            P(ROWS, "tensor"),
            P("tensor", ROWS),
            P("fsdp", None),
            P("fsdp", None),
            P("fsdp", None),
        ),
        out_specs=(
            P(ROWS, None),
            P(ROWS, None),
            P(ROWS),
            P(ROWS, "tensor"),
            P(ROWS, "tensor"),
            P(ROWS, "tensor"),
            P("tensor", ROWS),
            P(ROWS),
            P(ROWS, "tensor"),
            P(ROWS, "tensor"),
            P("tensor", ROWS),
        ),
        check_vma=False,
    )
```

```python
import functools

import jax
import jax.numpy as jnp
from jax import lax
from jax.experimental import pallas as pl
from jax.experimental.pallas import tpu as pltpu
from jax.sharding import PartitionSpec as P

HEAD = 64
SEG = 128
TRUNK = 8 * SEG
BRANCHES = 4
LEAVES = 8
GROUP = TRUNK + (BRANCHES + LEAVES) * SEG
DEPTH = TRUNK + 2 * SEG
TILE = 2 * SEG

epsilon = 1e-05
rope_base = 10000000.0
residual_scale = 0.22
score_scale = 0.015625
masked_score = -1e30

FIRST = (((0,), (0,)), ((), ()))
LAST = (((1,), (1,)), ((), ()))
PLAIN = (((1,), (0,)), ((), ()))


def dot(left_side, right_side, dims=PLAIN):
    return lax.dot_general(left_side, right_side, dims, preferred_element_type=jnp.float32)


def rope_tables():
    frequency = rope_base ** (-(jnp.arange(HEAD // 2).astype(jnp.float32) * 2.0) / HEAD)
    angles = jnp.arange(DEPTH).astype(jnp.float32)[:, None] * frequency[None, :]
    sine = jnp.sin(angles)
    cosine = jnp.cos(angles)
    return (
        jnp.concatenate([cosine] * 4, axis=-1),
        jnp.concatenate([-sine, sine, -sine, sine], axis=-1),
    )


def lanes(values):
    return lax.broadcasted_iota(jnp.int32, values.shape, 1)


def swap_halves(values):
    return jnp.where(
        lanes(values) % HEAD < HEAD // 2,
        pltpu.roll(values, 128 - HEAD // 2, 1),
        pltpu.roll(values, HEAD // 2, 1),
    )


def only_head(values, head):
    return jnp.where(lanes(values) // HEAD == head, values, jnp.zeros_like(values))


def query_tiles(work):
    for j in range(TRUNK // TILE):
        prefix = [(0, j * TILE, False)] if j else []
        work(j * TILE, prefix + [(j * TILE, TILE, True)], False)

    def branch(i, carry):
        row = pl.multiple_of(TRUNK + i * TILE, TILE)
        work(row, [(0, TRUNK, False), (row, TILE, True)], True)
        return carry

    lax.fori_loop(0, BRANCHES * SEG // TILE, branch, 0)

    def leaf(i, carry):
        row = pl.multiple_of(TRUNK + BRANCHES * SEG + i * TILE, TILE)
        parent = pl.multiple_of(TRUNK + i * SEG, SEG)
        work(row, [(0, TRUNK, False), (parent, SEG, False), (row, TILE, True)], True)
        return carry

    lax.fori_loop(0, LEAVES * SEG // TILE, leaf, 0)


def visible_scores(keys, query, own, one_segment):
    scores = dot(keys, query, LAST)
    if not own:
        return scores
    key_at = lax.broadcasted_iota(jnp.int32, scores.shape, 0)
    query_at = lax.broadcasted_iota(jnp.int32, scores.shape, 1)
    seen = key_at <= query_at
    if one_segment:
        seen = seen & (key_at // SEG == query_at // SEG)
    return jnp.where(seen, scores, masked_score)


def turned_over(target, source):
    for first in range(0, source.shape[0], TILE):
        block = source[first : first + TILE, :128].astype(jnp.float32)
        target[:, first : first + TILE] = jnp.transpose(block)[:HEAD].astype(jnp.bfloat16)


def head_pairs(width, work):
    together = min(PAIR, width // HEAD)

    def step(i, carry):
        work([i * together + j for j in range(together)])
        return carry

    lax.fori_loop(0, width // HEAD // together, step, 0)


PAIR = 2


def attention_forward_kernel(
    to_ref, start_ref, raw_ref, cos_ref, sin_ref, out_ref, q_ref, k_ref, v_ref, log_ref,
    held, values_ref, tile_ref,
):
    width = q_ref.shape[1]
    pieces = to_ref.shape[0]
    piece = raw_ref.shape[0] // pieces

    def place(p, carry):
        rows = pl.ds(pl.multiple_of(p * piece, piece), piece)
        to = pl.ds(pl.multiple_of(to_ref[p], piece), piece)
        at = pl.ds(pl.multiple_of(start_ref[p], piece), piece)
        cosine, sine = cos_ref[at, :], sin_ref[at, :]

        def turn(values):
            return values * cosine + swap_halves(values) * sine

        for g in range(width // 128):
            cut = slice(g * 128, g * 128 + 128)
            turned = turn(raw_ref[rows, cut]).astype(jnp.bfloat16)
            q_ref[to, cut] = turned * jnp.bfloat16(score_scale)
        pair = raw_ref[rows, width : width + 128]
        low = lanes(pair) < HEAD
        key = turn(pair)
        key = jnp.where(low, key, pltpu.roll(key, HEAD, 1)).astype(jnp.bfloat16)
        value = jnp.where(low, pltpu.roll(pair, HEAD, 1), pair).astype(jnp.bfloat16)
        for g in range(width // 128):
            cut = slice(g * 128, g * 128 + 128)
            k_ref[to, cut] = key
            v_ref[to, cut] = value
        return carry

    lax.fori_loop(0, pieces, place, 0)
    turned_over(values_ref, v_ref)

    def work(row, parts, one_segment):
        rows = pl.ds(row, TILE)

        def one_head(head):
            query = only_head(q_ref[rows, :], head)
            scores = [
                visible_scores(k_ref[pl.ds(first, count), :], query, own, one_segment)
                for first, count, own in parts
            ]
            largest = functools.reduce(
                jnp.maximum, [jnp.max(s, axis=0, keepdims=True) for s in scores]
            )
            exponent = [jnp.exp(s - largest) for s in scores]
            total = functools.reduce(
                jnp.add, [jnp.sum(e, axis=0, keepdims=True) for e in exponent]
            )
            result = functools.reduce(
                jnp.add,
                [
                    dot(values_ref[:, pl.ds(first, count)], e.astype(jnp.bfloat16))
                    for e, (first, count, own) in zip(exponent, parts)
                ],
            )
            log_ref[head, :, rows] = largest + jnp.log(total)
            tile_ref[pl.ds(pl.multiple_of(head * HEAD, HEAD), HEAD), :] = result * (1.0 / total)

        def heads(together):
            for head in together:
                one_head(head)

        head_pairs(width, heads)
        held[rows, :] = jnp.transpose(tile_ref[...]).astype(jnp.bfloat16)

    query_tiles(work)

    def back(p, carry):
        rows = pl.ds(pl.multiple_of(p * piece, piece), piece)
        to = pl.ds(pl.multiple_of(to_ref[p], piece), piece)
        out_ref[rows, :] = held[to, :]
        return carry

    lax.fori_loop(0, pieces, back, 0)


def attention_backward_kernel(
    to_ref,
    start_ref,
    grad_ref,
    q_ref,
    k_ref,
    v_ref,
    log_ref,
    cos_ref,
    sin_ref,
    *rest,
):
    out_ref, og_ref, dq_ref, dk_ref, dv_ref, keys_ref, tile_ref = rest[-7:]
    width = q_ref.shape[1]
    pieces = to_ref.shape[0]
    piece = grad_ref.shape[0] // pieces

    def place(p, carry):
        rows = pl.ds(pl.multiple_of(p * piece, piece), piece)
        to = pl.ds(pl.multiple_of(to_ref[p], piece), piece)
        og_ref[to, :] = grad_ref[rows, :]
        return carry

    lax.fori_loop(0, pieces, place, 0)
    turned_over(keys_ref, k_ref)
    dk_ref[...] = jnp.zeros_like(dk_ref)
    dv_ref[...] = jnp.zeros_like(dv_ref)

    def work(row, parts, one_segment):
        rows = pl.ds(row, TILE)

        def heads(together):
            queries, out_grads, all_weights, all_grads = [], [], [], []
            for head in together:
                query = only_head(q_ref[rows, :], head)
                out_grad = only_head(og_ref[rows, :], head)
                log_total = log_ref[head, :, rows]
                weights, products = [], []
                for first, count, own in parts:
                    keys = pl.ds(first, count)
                    scores = visible_scores(k_ref[keys, :], query, own, one_segment)
                    weights.append(jnp.exp(scores - log_total))
                    products.append(dot(v_ref[keys, :], out_grad, LAST))
                inner = functools.reduce(
                    jnp.add,
                    [jnp.sum(w * d, axis=0, keepdims=True) for w, d in zip(weights, products)],
                )
                grads = [
                    (w * (d - inner)).astype(jnp.bfloat16) for w, d in zip(weights, products)
                ]
                queries.append(query)
                out_grads.append(out_grad)
                all_weights.append([w.astype(jnp.bfloat16) for w in weights])
                all_grads.append(grads)
                tile_ref[pl.ds(pl.multiple_of(head * HEAD, HEAD), HEAD), :] = functools.reduce(
                    jnp.add,
                    [
                        dot(keys_ref[:, pl.ds(first, count)], g)
                        for (first, count, own), g in zip(parts, grads)
                    ],
                )
            query = jnp.concatenate(queries, axis=0)
            out_grad = jnp.concatenate(out_grads, axis=0)
            for i, (first, count, own) in enumerate(parts):
                keys = pl.ds(first, count)
                weights = jnp.concatenate([w[i] for w in all_weights], axis=1)
                grads = jnp.concatenate([g[i] for g in all_grads], axis=1)
                dv_ref[keys, :] += dot(weights, out_grad)
                dk_ref[keys, :] += dot(grads, query)

        head_pairs(width, heads)
        dq_ref[rows, :] = jnp.transpose(tile_ref[...])

    query_tiles(work)

    def back(p, carry):
        rows = pl.ds(pl.multiple_of(p * piece, piece), piece)
        to = pl.ds(pl.multiple_of(to_ref[p], piece), piece)
        at = pl.ds(pl.multiple_of(start_ref[p], piece), piece)
        cosine, sine = cos_ref[at, :], sin_ref[at, :]

        def turn_back(values):
            return values * cosine - swap_halves(values) * sine

        def over_heads(ref):
            total = functools.reduce(
                jnp.add, [ref[to, g * 128 : g * 128 + 128] for g in range(width // 128)]
            )
            return total + pltpu.roll(total, HEAD, 1)

        for g in range(width // 128):
            cut = slice(g * 128, g * 128 + 128)
            turned = turn_back(score_scale * dq_ref[to, cut])
            out_ref[rows, cut] = turned.astype(jnp.bfloat16)
        key = turn_back(over_heads(dk_ref))
        value = over_heads(dv_ref)
        pair = jnp.where(lanes(key) < HEAD, key, value)
        out_ref[rows, width : width + 128] = pair.astype(jnp.bfloat16)
        return carry

    lax.fori_loop(0, pieces, back, 0)


SMEM = pl.BlockSpec(memory_space=pltpu.SMEM)
VMEM = pl.BlockSpec(memory_space=pltpu.VMEM)
VMEM_LIMIT = 48 * 1024 * 1024


def attention_cost(width, products):
    flops = products * 2 * GROUP * (GROUP * 2 // 5) * width
    return pl.CostEstimate(
        flops=flops, bytes_accessed=16 * GROUP * width, transcendentals=GROUP * GROUP * width // 128
    )


def attention_forward(places, starts, raw, tables):
    width = raw.shape[1] - 2 * HEAD
    rows = raw.shape[0]
    kept = jax.ShapeDtypeStruct((rows, width), jnp.bfloat16)
    return pl.pallas_call(
        attention_forward_kernel,
        out_shape=[kept] * 4 + [jax.ShapeDtypeStruct((width // HEAD, 1, rows), jnp.float32)],
        in_specs=[SMEM, SMEM, VMEM, VMEM, VMEM],
        out_specs=[VMEM] * 5,
        scratch_shapes=[
            pltpu.VMEM((rows, width), jnp.bfloat16),
            pltpu.VMEM((HEAD, rows), jnp.bfloat16),
            pltpu.VMEM((width, TILE), jnp.float32),
        ],
        compiler_params=pltpu.CompilerParams(vmem_limit_bytes=VMEM_LIMIT),
        cost_estimate=attention_cost(width, 4),
        name="attention_forward",
    )(places, starts, raw, *tables)


def attention_backward(places, starts, out_grad, kept, tables, early):
    rows, width = out_grad.shape
    return pl.pallas_call(
        attention_backward_kernel,
        out_shape=jax.ShapeDtypeStruct((rows, width + 2 * HEAD), jnp.bfloat16),
        in_specs=[SMEM, SMEM] + [VMEM] * 7 + [ANY] * len(early),
        out_specs=VMEM,
        scratch_shapes=[
            pltpu.VMEM((rows, width), jnp.bfloat16),
            pltpu.VMEM((rows, width), jnp.float32),
            pltpu.VMEM((rows, width), jnp.float32),
            pltpu.VMEM((rows, width), jnp.float32),
            pltpu.VMEM((HEAD, rows), jnp.bfloat16),
            pltpu.VMEM((width, TILE), jnp.float32),
        ],
        compiler_params=pltpu.CompilerParams(vmem_limit_bytes=VMEM_LIMIT),
        cost_estimate=attention_cost(width, 10),
        name="attention_backward",
    )(places, starts, out_grad, *kept, *tables, *early)


MESH = pl.DeviceIdType.MESH
ANY = pl.BlockSpec(memory_space=pl.ANY)
CHUNKS = 4
SLAB = 16


def lasting(microseconds):
    return pl.CostEstimate(
        flops=0, bytes_accessed=int(microseconds * 3_000_000), transcendentals=0
    )


class Plane:
    def __init__(self, sent, landed, diagonal=False):
        self.sent, self.landed = sent, landed
        self.copies = []
        self.rank = lax.axis_index("context")
        self.core = lax.axis_index("tensor")
        self.at_x = self.rank + 1 - 2 * lax.rem(self.rank, 2)
        self.at_y = lax.rem(self.rank + 2, 4)
        self.at_both = 3 - self.rank
        self.x = {"context": self.at_x}
        self.y = {"context": self.at_y}
        self.both = {"context": self.at_both}
        self.sibling = {"tensor": 1 - self.core}
        barrier = pltpu.get_barrier_semaphore()
        partners = [self.x, self.y, self.sibling] + ([self.both] if diagonal else [])
        for partner in partners:
            pl.semaphore_signal(barrier, inc=1, device_id=partner, device_id_type=MESH)
        pl.semaphore_wait(barrier, len(partners))

    def copy(self, number, source, target, partner):
        return pltpu.make_async_remote_copy(
            src_ref=source,
            dst_ref=target,
            send_sem=self.sent.at[number],
            recv_sem=self.landed.at[number],
            device_id=partner,
            device_id_type=MESH,
        )

    def send(self, source, target, partner):
        number = len(self.copies)
        started = self.copy(number, source, target, partner)
        started.start()
        self.copies.append(started)
        return number

    def arrive(self, number, target):
        self.copy(number, target, target, self.sibling).wait_recv()

    def finish(self):
        for started in self.copies:
            started.wait_send()


def chunk(index, rows):
    return pl.ds(index * (rows // CHUNKS), rows // CHUNKS)


class Gather:
    def __init__(self, plane, block, out):
        self.plane, self.block, self.out = plane, block, out
        self.rows = block.shape[0]
        self.to_x, self.to_y, self.across = {}, {}, {}

    def start(self, k):
        p, cut = self.plane, chunk(k, self.rows)
        target = self.out.at[p.rank, p.core, cut]
        self.to_x[k] = p.send(self.block.at[cut], target, p.x)
        self.to_y[k] = p.send(self.block.at[cut], target, p.y)
        self.across[0, k] = p.send(self.block.at[cut], target, p.sibling)

    def forward(self):
        p, out = self.plane, self.out
        onward = {}
        for k in range(CHUNKS):
            cut = chunk(k, self.rows)
            from_x, from_y = out.at[p.at_x, p.core, cut], out.at[p.at_y, p.core, cut]
            p.arrive(self.to_x[k], from_x)
            if k < CHUNKS // 2:
                onward[k] = p.send(from_x, from_x, p.y)
            self.across[1, k] = p.send(from_x, from_x, p.sibling)
            p.arrive(self.to_y[k], from_y)
            if k >= CHUNKS // 2:
                onward[k] = p.send(from_y, from_y, p.x)
            self.across[2, k] = p.send(from_y, from_y, p.sibling)
        for k in range(CHUNKS):
            far = out.at[p.at_both, p.core, chunk(k, self.rows)]
            p.arrive(onward[k], far)
            self.across[3, k] = p.send(far, far, p.sibling)

    def finish(self):
        p = self.plane
        for i, rank in enumerate((p.rank, p.at_x, p.at_y, p.at_both)):
            for k in range(CHUNKS):
                p.arrive(
                    self.across[i, k], self.out.at[rank, 1 - p.core, chunk(k, self.rows)]
                )


GATHER_COPIES = CHUNKS * 8


def add_rows(target, source, first, count):
    def step(i, carry):
        rows = pl.ds(first + i * SLAB, SLAB)
        target[rows, :] = (
            target[rows, :].astype(jnp.float32) + source[rows, :].astype(jnp.float32)
        ).astype(jnp.bfloat16)
        return carry

    lax.fori_loop(0, count // SLAB, step, 0)


class Scatter:
    def __init__(self, plane, partial, held, other, near_x, near_y, far_x, far_y, local):
        p = plane
        rows = near_x.shape[0]
        half = rows // 2
        top, low = pl.ds(0, half), pl.ds(half, half)
        order = (p.at_both, p.at_x, p.at_y, p.rank)
        across, kept = [], []
        for i, rank in enumerate(order):
            across.append(p.send(partial.at[rank, 1 - p.core], other.at[i], p.sibling))
            kept.append(pltpu.make_async_copy(partial.at[rank, p.core], held.at[i], local.at[i]))
            kept[i].start()

        def pair(i):
            p.arrive(across[i], other.at[i])
            kept[i].wait()
            add_rows(held.at[i], other.at[i], 0, rows)

        pair(0)
        first = p.send(held.at[0, top], far_x, p.x)
        second = p.send(held.at[0, low], far_y, p.y)
        pair(1)
        third = p.send(held.at[1, top], near_x.at[top], p.x)
        pair(2)
        fourth = p.send(held.at[2, low], near_y.at[low], p.y)
        p.arrive(first, far_x)
        add_rows(held.at[2], far_x, 0, half)
        fifth = p.send(held.at[2, top], near_y.at[top], p.y)
        p.arrive(second, far_y)

        def step(i, carry):
            rows, at = pl.ds(half + i * SLAB, SLAB), pl.ds(i * SLAB, SLAB)
            held[1, rows, :] = (
                held[1, rows, :].astype(jnp.float32) + far_y[at, :].astype(jnp.float32)
            ).astype(jnp.bfloat16)
            return carry

        lax.fori_loop(0, half // SLAB, step, 0)
        sixth = p.send(held.at[1, low], near_x.at[low], p.x)
        pair(3)
        p.arrive(third, near_x.at[top])
        p.arrive(fourth, near_y.at[low])
        p.arrive(fifth, near_y.at[top])
        p.arrive(sixth, near_x.at[low])
        self.parts = (held.at[3], near_x, near_y)

    def rows(self, rows):
        return sum(part[rows, :].astype(jnp.float32) for part in self.parts)


SCATTER_COPIES = 4 + 6


def scatter_scratch(share, width):
    kind = jnp.bfloat16
    return [
        pltpu.VMEM((4, share, width), kind),
        pltpu.VMEM((4, share, width), kind),
        pltpu.VMEM((share, width), kind),
        pltpu.VMEM((share, width), kind),
        pltpu.VMEM((share // 2, width), kind),
        pltpu.VMEM((share // 2, width), kind),
        pltpu.SemaphoreType.DMA((4,)),
    ]


def wires(count):
    return [pltpu.SemaphoreType.DMA((count,)), pltpu.SemaphoreType.DMA((count,))]


def row_root(values):
    return lax.rsqrt(jnp.mean(values * values, axis=-1, keepdims=True) + epsilon)


def slabs(first, count, work):
    def step(i, carry):
        work(pl.ds(first + i * SLAB, SLAB))
        return carry

    lax.fori_loop(0, count // SLAB, step, 0)


def start_kernel(
    block, gate, up, down, cotangent, out, gate_out, up_out, down_out, scaled, sent, landed, local
):
    p = Plane(sent, landed, diagonal=True)
    gather = Gather(p, block, out)
    columns = gate_out.shape[2]

    def part(weight, rank):
        return weight.at[:, pl.ds(pl.multiple_of(rank * columns, 128), columns)]

    mine = [pltpu.make_async_copy(block, out.at[p.rank, p.core], local.at[0])]
    for k in range(CHUNKS):
        gather.start(k)
    moves = []
    for i, (source, target) in enumerate(((gate, gate_out), (up, up_out), (down, down_out))):
        mine.append(
            pltpu.make_async_copy(part(source, p.rank), target.at[p.rank], local.at[i + 1])
        )
        for partner, rank in ((p.x, p.at_x), (p.y, p.at_y), (p.both, p.at_both)):
            number = p.send(part(source, rank), target.at[p.rank], partner)
            moves.append((number, target.at[rank]))
    for started in mine:
        started.start()

    def scale(rows):
        value = residual_scale * cotangent[rows, :].astype(jnp.float32)
        scaled[rows, :] = value.astype(jnp.bfloat16)

    slabs(0, scaled.shape[0], scale)
    gather.forward()
    gather.finish()
    for number, target in moves:
        p.arrive(number, target)
    p.finish()
    for started in mine:
        started.wait()


def start_plane(block, gate, up, down, cotangent):
    share, width = block.shape
    depth, units = gate.shape
    full = jax.ShapeDtypeStruct((4, 2, share, width), block.dtype)
    weight = jax.ShapeDtypeStruct((4, depth, units // 4), gate.dtype)
    full, *rest = pl.pallas_call(
        start_kernel,
        out_shape=[full, weight, weight, weight, jax.ShapeDtypeStruct(cotangent.shape, jnp.bfloat16)],
        in_specs=[VMEM, ANY, ANY, ANY, VMEM],
        out_specs=[ANY] * 4 + [VMEM],
        scratch_shapes=wires(GATHER_COPIES + 9) + [pltpu.SemaphoreType.DMA((4,))],
        compiler_params=pltpu.CompilerParams(
            collective_id=1, has_side_effects=True, vmem_limit_bytes=VMEM_LIMIT
        ),
        cost_estimate=lasting(80),
        name="gather_tokens",
    )(block, gate, up, down, cotangent)
    return full.reshape(8 * share, width), rest[:3], rest[3]


def middle_kernel(
    partial,
    residual,
    gain,
    beside,
    from_x,
    from_y,
    from_both,
    out,
    middle,
    beside_out,
    sent,
    landed,
    local,
    hidden,
    held_beside,
    held_blocks,
    *scratch,
):
    p = Plane(sent, landed)
    blocks = ((from_x, p.at_x), (from_y, p.at_y), (from_both, p.at_both))
    loads = [pltpu.make_async_copy(beside, held_beside, local.at[0])]
    for i, (block, rank) in enumerate(blocks):
        loads.append(pltpu.make_async_copy(block, held_blocks.at[i], local.at[i + 1]))
    for started in loads:
        started.start()
    total = Scatter(p, partial, *scratch)
    kept, across = [], []
    loads[0].wait()
    kept.append(pltpu.make_async_copy(held_beside, beside_out.at[p.rank], local.at[0]))
    kept[0].start()
    for i, (block, rank) in enumerate(blocks):
        loads[i + 1].wait()
        place = beside_out.at[rank, p.core]
        kept.append(pltpu.make_async_copy(held_blocks.at[i], place, local.at[i + 1]))
        kept[i + 1].start()
        across.append(p.send(held_blocks.at[i], place, p.sibling))
    share = hidden.shape[0]
    gather = Gather(p, hidden, out)

    def work(rows):
        value = residual[rows, :].astype(jnp.float32) + residual_scale * total.rows(rows)
        middle[rows, :] = value
        hidden[rows, :] = (value * row_root(value) * gain[...]).astype(jnp.bfloat16)

    for k in range(CHUNKS):
        slabs(k * (share // CHUNKS), share // CHUNKS, work)
        gather.start(k)
    kept.append(pltpu.make_async_copy(hidden, out.at[p.rank, p.core], local.at[4]))
    kept[4].start()
    gather.forward()
    gather.finish()
    for number, rank in zip(across, (p.at_x, p.at_y, p.at_both)):
        p.arrive(number, beside_out.at[rank, 1 - p.core])
    p.finish()
    for started in kept:
        started.wait()


def middle_plane(partial, residual, gain, beside, blocks):
    share, width = residual.shape
    full = jax.ShapeDtypeStruct((4, 2, share, width), jnp.bfloat16)
    out, middle, beside_out = pl.pallas_call(
        middle_kernel,
        out_shape=[full, jax.ShapeDtypeStruct((share, width), jnp.float32), full],
        in_specs=[ANY, VMEM, VMEM] + [ANY] * 4,
        out_specs=[ANY, VMEM, ANY],
        scratch_shapes=wires(GATHER_COPIES + SCATTER_COPIES + 3)
        + [
            pltpu.SemaphoreType.DMA((5,)),
            pltpu.VMEM((share, width), jnp.bfloat16),
            pltpu.VMEM((2, share, width), jnp.bfloat16),
            pltpu.VMEM((3, share, width), jnp.bfloat16),
        ]
        + scatter_scratch(share, width),
        compiler_params=pltpu.CompilerParams(
            collective_id=2, has_side_effects=True, vmem_limit_bytes=VMEM_LIMIT
        ),
        cost_estimate=lasting(100),
        name="middle_rows",
    )(partial.reshape(full.shape), residual, gain, beside.reshape(2, share, width), *blocks)
    return out.reshape(8 * share, width), middle, beside_out.reshape(8 * share, width)


def second_kernel(
    partial,
    other_partial,
    middle,
    cotangent,
    gain,
    early_first,
    early_second,
    out,
    grad_middle,
    pairs,
    sent,
    landed,
    local,
    hidden,
    held,
    theirs,
    *scratch,
):
    p = Plane(sent, landed)
    total = Scatter(p, partial, *scratch)
    share = hidden.shape[0]
    gather = Gather(p, hidden, out)
    order = (p.rank, p.at_x, p.at_y, p.at_both)
    kept, across = [], []
    for i, rank in enumerate(order):
        across.append(p.send(other_partial.at[rank, 1 - p.core], theirs.at[i], p.sibling))
        kept.append(
            pltpu.make_async_copy(other_partial.at[rank, p.core], held.at[i], local.at[i])
        )
        kept[i].start()

    def work(rows):
        value = middle[rows, :]
        root = row_root(value)
        normed = value * root
        slope = total.rows(rows) * gain[...]
        mean = jnp.mean(slope * normed, axis=-1, keepdims=True)
        gradient = cotangent[rows, :].astype(jnp.float32) + root * (slope - normed * mean)
        grad_middle[rows, :] = gradient
        hidden[rows, :] = (residual_scale * gradient).astype(jnp.bfloat16)

    for k in range(CHUNKS):
        slabs(k * (share // CHUNKS), share // CHUNKS, work)
        gather.start(k)
    mine = pltpu.make_async_copy(hidden, out.at[p.rank, p.core], local.at[4])
    mine.start()
    for i in range(4):
        p.arrive(across[i], theirs.at[i])
        kept[i].wait()
        add_rows(held.at[i], theirs.at[i], 0, share)
    whole = pltpu.make_async_copy(held, pairs, local.at[5])
    whole.start()
    gather.forward()
    gather.finish()
    p.finish()
    mine.wait()
    whole.wait()


def second_plane(partial, other_partial, middle, cotangent, gain, early):
    share, width = middle.shape
    full = jax.ShapeDtypeStruct((4, 2, share, width), jnp.bfloat16)
    quarter = jax.ShapeDtypeStruct((4, share, width), jnp.bfloat16)
    out, grad_middle, pairs = pl.pallas_call(
        second_kernel,
        out_shape=[full, jax.ShapeDtypeStruct((share, width), jnp.float32), quarter],
        in_specs=[ANY, ANY, VMEM, VMEM, VMEM, ANY, ANY],
        out_specs=[ANY, VMEM, ANY],
        scratch_shapes=wires(GATHER_COPIES + SCATTER_COPIES + 4)
        + [
            pltpu.SemaphoreType.DMA((6,)),
            pltpu.VMEM((share, width), jnp.bfloat16),
            pltpu.VMEM(quarter.shape, jnp.bfloat16),
            pltpu.VMEM(quarter.shape, jnp.bfloat16),
        ]
        + scatter_scratch(share, width),
        compiler_params=pltpu.CompilerParams(
            collective_id=3, has_side_effects=True, vmem_limit_bytes=VMEM_LIMIT
        ),
        cost_estimate=lasting(100),
        name="second_rows",
    )(
        partial.reshape(full.shape),
        other_partial.reshape(full.shape),
        middle,
        cotangent,
        gain,
        *early,
    )
    return out.reshape(8 * share, width), grad_middle, pairs


def last_kernel(
    partial,
    residual,
    grad_middle,
    gain,
    middle,
    ffn_own,
    ffn_x,
    ffn_y,
    ffn_both,
    out,
    result_out,
    done,
    sent,
    landed,
    local,
    held,
    result,
    *scratch,
):
    p = Plane(sent, landed)
    done[...] = jnp.zeros_like(done)
    total = Scatter(p, partial, *scratch)
    share = held.shape[0]

    def finish_result(rows):
        parts = (ffn_own, ffn_x, ffn_y, ffn_both)
        ffn = sum(part[rows, :].astype(jnp.float32) for part in parts)
        result[rows, :] = (middle[rows, :] + residual_scale * ffn).astype(jnp.bfloat16)

    slabs(0, share, finish_result)
    kept = [pltpu.make_async_copy(result, result_out.at[p.core], local.at[0])]
    kept[0].start()
    given = p.send(result, result_out.at[p.core], p.sibling)

    def work(rows):
        value = residual[rows, :].astype(jnp.float32)
        root = row_root(value)
        normed = value * root
        slope = total.rows(rows) * gain[...]
        mean = jnp.mean(slope * normed, axis=-1, keepdims=True)
        held[rows, :] = grad_middle[rows, :] + root * (slope - normed * mean)

    across = []
    for k in range(CHUNKS):
        cut = chunk(k, share)
        slabs(k * (share // CHUNKS), share // CHUNKS, work)
        across.append(p.send(held.at[cut], out.at[p.core, cut], p.sibling))
    kept.append(pltpu.make_async_copy(held, out.at[p.core], local.at[1]))
    kept[1].start()
    p.arrive(given, result_out.at[1 - p.core])
    for k in range(CHUNKS):
        p.arrive(across[k], out.at[1 - p.core, chunk(k, share)])
    p.finish()
    for started in kept:
        started.wait()


def last_plane(partial, residual, grad_middle, gain, middle, ffn_parts):
    share, width = residual.shape
    out, result_out, done = pl.pallas_call(
        last_kernel,
        out_shape=[
            jax.ShapeDtypeStruct((2, share, width), jnp.float32),
            jax.ShapeDtypeStruct((2, share, width), jnp.bfloat16),
            jax.ShapeDtypeStruct((8, 128), jnp.float32),
        ],
        in_specs=[ANY] + [VMEM] * 8,
        out_specs=[ANY, ANY, VMEM],
        scratch_shapes=wires(CHUNKS + 1 + SCATTER_COPIES)
        + [
            pltpu.SemaphoreType.DMA((2,)),
            pltpu.VMEM((share, width), jnp.float32),
            pltpu.VMEM((share, width), jnp.bfloat16),
        ]
        + scatter_scratch(share, width),
        compiler_params=pltpu.CompilerParams(
            collective_id=4, has_side_effects=True, vmem_limit_bytes=VMEM_LIMIT
        ),
        cost_estimate=lasting(70),
        name="last_rows",
    )(partial.reshape(4, 2, share, width), residual, grad_middle, gain, middle, *ffn_parts)
    return out.reshape(2 * share, width), result_out.reshape(2 * share, width), done


def exchange_kernel(blocks, *rest):
    out, sent, landed = rest[-3:]
    p = Plane(sent, landed, diagonal=True)
    moves = []
    for partner, rank in ((p.both, p.at_both), (p.x, p.at_x), (p.y, p.at_y)):
        moves.append((p.send(blocks.at[rank], out.at[p.rank], partner), out.at[rank]))
    out[p.rank] = blocks[p.rank]
    for number, target in moves:
        p.arrive(number, target)
    p.finish()


def exchange(blocks, early):
    return pl.pallas_call(
        exchange_kernel,
        out_shape=jax.ShapeDtypeStruct(blocks.shape, blocks.dtype),
        in_specs=[VMEM] + [ANY] * len(early),
        out_specs=VMEM,
        scratch_shapes=wires(3),
        compiler_params=pltpu.CompilerParams(collective_id=5, has_side_effects=True),
        cost_estimate=lasting(8),
        name="exchange_blocks",
    )(blocks, *early)


def context_pairs(step):
    return [(i, i ^ step) for i in range(4)]


def swap_cores(values):
    return lax.ppermute(values, "tensor", [(0, 1), (1, 0)])


def ffn_first_kernel(hidden, gate_w, up_w, m, gate, up):
    for j in range(gate_w.shape[1] // 256):
        cut = slice(j * 256, j * 256 + 256)
        gate_part = dot(hidden[...], gate_w[:, cut])
        up_part = dot(hidden[...], up_w[:, cut])
        gate[:, cut] = gate_part.astype(jnp.bfloat16)
        up[:, cut] = up_part.astype(jnp.bfloat16)
        sigmoid = 1.0 / (1.0 + jnp.exp(-gate_part))
        m[:, cut] = (gate_part * sigmoid * up_part).astype(jnp.bfloat16)


def ffn_second_kernel(grad, gate, up, m, gate_w, up_w, down_w, early, slopes, forward, back):
    units = gate_w.shape[1]
    for j in range(units // 256):
        cut = slice(j * 256, j * 256 + 256)
        grad_part = dot(grad[...], down_w[:, cut])
        gate_part = gate[:, cut].astype(jnp.float32)
        up_part = up[:, cut].astype(jnp.float32)
        sigmoid = 1.0 / (1.0 + jnp.exp(-gate_part))
        slope = sigmoid * (1.0 + gate_part * (1.0 - sigmoid))
        slopes[:, cut] = (grad_part * up_part * slope).astype(jnp.bfloat16)
        slopes[:, units + j * 256 : units + j * 256 + 256] = (
            grad_part * gate_part * sigmoid
        ).astype(jnp.bfloat16)
    for j in range(gate_w.shape[0] // 512):
        cut = slice(j * 512, j * 512 + 512)
        forward[:, cut] = dot(m[...], down_w[cut, :], LAST).astype(jnp.bfloat16)
        back[:, cut] = (
            dot(slopes[:, :units], gate_w[cut, :], LAST)
            + dot(slopes[:, units:], up_w[cut, :], LAST)
        ).astype(jnp.bfloat16)


def first_rows_kernel(values, gain, weight, hidden, raw):
    value = values[...].astype(jnp.float32)
    normed = (value * row_root(value) * gain[...]).astype(jnp.bfloat16)
    hidden[...] = normed
    raw[...] = dot(normed, weight[...])


def first_rows(values, gain, weight):
    count, width = values.shape
    columns = weight.shape[1]
    return pl.pallas_call(
        first_rows_kernel,
        grid=(count // ROW_TILE,),
        in_specs=[
            pl.BlockSpec((ROW_TILE, width), lambda i: (i, 0)),
            pl.BlockSpec((1, width), lambda i: (0, 0)),
            pl.BlockSpec((width, columns), lambda i: (0, 0)),
        ],
        out_specs=[
            pl.BlockSpec((ROW_TILE, width), lambda i: (i, 0)),
            pl.BlockSpec((ROW_TILE, columns), lambda i: (i, 0)),
        ],
        out_shape=[
            jax.ShapeDtypeStruct((count, width), jnp.bfloat16),
            jax.ShapeDtypeStruct((count, columns), jnp.float32),
        ],
        compiler_params=pltpu.CompilerParams(vmem_limit_bytes=VMEM_LIMIT),
        cost_estimate=lasting(12),
        name="first_rows",
    )(values, gain, weight)


def attention_weights_kernel(hidden, back, grad, attended, *early_and_out):
    out = early_and_out[-1]
    columns = back.shape[1]
    out[:, :columns] = dot(hidden[...], back[...], FIRST).astype(jnp.bfloat16)
    out[:, columns:] = dot(grad[...], attended[...], FIRST).astype(jnp.bfloat16)


def attention_weights(hidden, back, grad, attended, early):
    count, width = hidden.shape
    first, second = back.shape[1], attended.shape[1]
    tall = pl.BlockSpec((count, 512), lambda i: (0, i))
    return pl.pallas_call(
        attention_weights_kernel,
        grid=(width // 512,),
        in_specs=[
            tall,
            pl.BlockSpec((count, first), lambda i: (0, 0)),
            tall,
            pl.BlockSpec((count, second), lambda i: (0, 0)),
        ]
        + [ANY] * len(early),
        out_specs=pl.BlockSpec((512, first + second), lambda i: (i, 0)),
        out_shape=jax.ShapeDtypeStruct((width, first + second), jnp.bfloat16),
        compiler_params=pltpu.CompilerParams(vmem_limit_bytes=VMEM_LIMIT),
        cost_estimate=lasting(12),
        name="attention_weights",
    )(hidden, back, grad, attended, *early)


ROW_TILE = 256


def row_tiles(kernel, name, rows, weights, extra, widths):
    count = rows[0].shape[0]

    def tile(width):
        return pl.BlockSpec((ROW_TILE, width), lambda i: (i, 0))

    whole = [
        pl.BlockSpec(w.shape, lambda i: (0, 0), pipeline_mode=pl.Buffered(1)) for w in weights
    ]
    flops = 2 * count * sum(w.size for w in weights)
    return pl.pallas_call(
        kernel,
        grid=(count // ROW_TILE,),
        in_specs=[tile(r.shape[1]) for r in rows] + whole + [ANY] * len(extra),
        out_specs=[tile(width) for width in widths],
        out_shape=[jax.ShapeDtypeStruct((count, width), jnp.bfloat16) for width in widths],
        compiler_params=pltpu.CompilerParams(vmem_limit_bytes=56 * 1024 * 1024),
        cost_estimate=pl.CostEstimate(flops=flops, bytes_accessed=flops // 400, transcendentals=0),
        name=name,
    )(*rows, *weights, *extra)


def norm_backward(gradient, normed, inv_root):
    return inv_root * (gradient - normed * jnp.mean(gradient * normed, axis=-1, keepdims=True))


def inverse_root(values):
    return lax.rsqrt(jnp.mean(values * values, axis=-1, keepdims=True) + epsilon)


PLANE = ("context", "tensor")


def gather_rows(values):
    return lax.all_gather(values, PLANE, axis=0, tiled=True)


def scatter_rows(partial):
    return lax.psum_scatter(
        partial.astype(jnp.bfloat16), PLANE, scatter_dimension=0, tiled=True
    ).astype(jnp.float32)


def local(
    tokens,
    cotangent,
    attn_gain,
    w_query,
    w_key,
    w_value,
    w_out,
    ffn_gain,
    w_gate,
    w_up,
    w_down,
    piece_segment,
    piece_parent,
    piece_start,
):
    groups = lax.axis_size("context")
    cores = lax.axis_size("tensor")
    depth = w_query.shape[0]
    kv_count = w_key.shape[1] // HEAD
    sharing = groups // kv_count
    share = tokens.shape[0] // cores
    first_row = lax.axis_index("tensor") * share

    def my_rows(values):
        return lax.dynamic_slice_in_dim(values, first_row, share, 0)

    def blocks(weight):
        return jnp.transpose(weight.reshape(depth, groups, -1), (1, 0, 2))

    def kv_blocks(weight):
        return jnp.repeat(jnp.transpose(weight.reshape(depth, kv_count, HEAD), (1, 0, 2)), sharing, 0)

    def spread(weight_blocks):
        mine = lax.all_to_all(weight_blocks, "context", 0, 0)
        mine = mine.reshape(groups * depth, -1)
        return lax.all_gather(mine, "fsdp", axis=0, tiled=True)

    gains = jnp.stack([attn_gain, ffn_gain], axis=1)
    gains = jnp.broadcast_to(jnp.pad(gains, ((0, 0), (0, 126))), (groups, depth, 128))
    packed = spread(
        jnp.concatenate(
            [blocks(w_query), kv_blocks(w_key), kv_blocks(w_value), blocks(w_out.T), gains], axis=2
        )
    )
    width = w_query.shape[1] // groups
    qkv_full = packed[:, : width + 2 * HEAD]
    out_full = packed[:, width + 2 * HEAD : 2 * width + 2 * HEAD]
    gains_full = packed[:, 2 * width + 2 * HEAD :].astype(jnp.float32)
    attn_scale, ffn_scale = gains_full[:, 0], gains_full[:, 1]
    square = groups == 4 and cores == 2
    tokens_half, cotangent_half = my_rows(tokens), my_rows(cotangent)
    if square:
        inputs_full, ffn_blocks, ffn_grad = start_plane(
            tokens_half, w_gate, w_up, w_down.T, cotangent
        )
    else:
        inputs_full = gather_rows(tokens_half)
        ffn_grad = (residual_scale * cotangent.astype(jnp.float32)).astype(jnp.bfloat16)
        ffn_blocks = [
            lax.all_to_all(blocks(w), "context", 0, 0) for w in (w_gate, w_up, w_down.T)
        ]
    gate_full, up_full, down_full = (
        lax.all_gather(w.reshape(groups * depth, -1), "fsdp", axis=0, tiled=True)
        for w in ffn_blocks
    )

    segment, starts = piece_segment[0] % 13, piece_start[0]
    places = jnp.where(
        segment == 0,
        starts,
        jnp.where(
            segment <= BRANCHES,
            starts + (segment - 1) * SEG,
            starts + (segment - 1 - BRANCHES) * SEG + (BRANCHES - 1) * SEG,
        ),
    )
    tables = rope_tables()

    residual_in = tokens_half.astype(jnp.float32)
    grad_result = cotangent_half.astype(jnp.float32)
    my_ffn_grad = my_rows(ffn_grad)

    hidden_first, raw = first_rows(inputs_full, attn_scale[None, :], qkv_full)
    attended, *kept = attention_forward(places, starts, raw, tables)
    branch = dot(attended, out_full, LAST).astype(jnp.bfloat16)
    if square:
        ffn_grad_blocks = [
            lax.ppermute(my_ffn_grad, "context", context_pairs(step)) for step in (1, 2, 3)
        ]
        hidden_second, middle, ffn_grad = middle_plane(
            branch, tokens_half, ffn_scale[None, :], ffn_grad, ffn_grad_blocks
        )
    else:
        ffn_grad = gather_rows(my_ffn_grad)
        middle = residual_in + residual_scale * scatter_rows(branch)
        hidden_second = gather_rows((middle * inverse_root(middle) * ffn_scale).astype(jnp.bfloat16))

    units = gate_full.shape[1]
    hidden, gate_proj, up_proj = row_tiles(
        ffn_first_kernel,
        "ffn_first",
        [hidden_second],
        [gate_full, up_full],
        [],
        [units, units, units],
    )
    grad_down = dot(ffn_grad, hidden, FIRST).astype(jnp.bfloat16)
    slopes, ffn_out, grad_second = row_tiles(
        ffn_second_kernel,
        "ffn_second",
        [ffn_grad, gate_proj, up_proj, hidden],
        [gate_full, up_full, down_full],
        [grad_down],
        [2 * units, gate_full.shape[0], gate_full.shape[0]],
    )
    grad_gate_up = dot(hidden_second, slopes, FIRST).astype(jnp.bfloat16)

    def sum_groups(gradient):
        return lax.psum_scatter(gradient, "fsdp", scatter_dimension=0, tiled=True)

    def hand_back(gradient):
        return lax.all_to_all(gradient.reshape(groups, depth, -1), "context", 0, 0)

    def columns(gradient):
        return jnp.transpose(gradient, (1, 0, 2)).reshape(depth, -1).astype(jnp.float32)

    if square:
        attn_grad, grad_middle, ffn_pairs = second_plane(
            grad_second,
            ffn_out,
            middle,
            cotangent_half,
            ffn_scale[None, :],
            [grad_down, grad_gate_up],
        )
        ffn_parts = [ffn_pairs[0]] + [
            lax.ppermute(ffn_pairs[step], "context", context_pairs(step)) for step in (1, 2, 3)
        ]
    else:
        root = inverse_root(middle)
        grad_middle = grad_result + norm_backward(
            scatter_rows(grad_second) * ffn_scale, middle * root, root
        )
        attn_grad = gather_rows((residual_scale * grad_middle).astype(jnp.bfloat16))
        ffn_parts = []
    grad_attended = dot(attn_grad, out_full).astype(jnp.bfloat16)
    grad_down = sum_groups(grad_down)
    grad_gate_up = sum_groups(grad_gate_up)
    back = attention_backward(places, starts, grad_attended, kept, tables, [grad_down])
    grad_down = hand_back(grad_down)
    grad_attn = attention_weights(
        hidden_first, back, attn_grad, attended, [grad_gate_up, grad_down, *ffn_parts[1:]]
    )
    grad_attn = sum_groups(grad_attn)
    grad_gate_up = hand_back(grad_gate_up)
    grad_first = dot(back, qkv_full, LAST).astype(jnp.bfloat16)
    if square:
        grad_tokens, result, done = last_plane(
            grad_first,
            tokens_half,
            grad_middle,
            attn_scale[None, :],
            middle,
            ffn_parts,
        )
        grad_attn = exchange(
            grad_attn.reshape(groups, depth, -1), [done, grad_gate_up]
        )
    else:
        root = inverse_root(residual_in)
        grad_tokens = grad_middle + norm_backward(
            scatter_rows(grad_first) * attn_scale, residual_in * root, root
        )
        grad_tokens = lax.all_gather(grad_tokens, "tensor", axis=0, tiled=True)
        result = (middle + residual_scale * scatter_rows(ffn_out)).astype(jnp.bfloat16)
        grad_attn = hand_back(grad_attn)
        result = lax.all_gather(result, "tensor", axis=0, tiled=True)
    def kv_columns(gradient):
        gradient = gradient.astype(jnp.float32).reshape(kv_count, sharing, depth, HEAD)
        return jnp.transpose(jnp.sum(gradient, axis=1), (1, 0, 2)).reshape(depth, -1)

    grad_query = columns(grad_attn[:, :, :width])
    grad_key = kv_columns(grad_attn[:, :, width : width + HEAD])
    grad_value = kv_columns(grad_attn[:, :, width + HEAD : width + 2 * HEAD])
    grad_gate, grad_up = columns(grad_gate_up[:, :, :units]), columns(grad_gate_up[:, :, units:])

    def against(*pairs):
        return sum(jnp.sum(weight.astype(jnp.float32) * g, axis=1) for weight, g in pairs)

    gain_grads = jnp.stack(
        [
            against((w_query, grad_query), (w_key, grad_key), (w_value, grad_value)),
            against((w_gate, grad_gate), (w_up, grad_up)),
        ]
    )
    gain_grads += swap_cores(gain_grads) if square else lax.psum(gain_grads, "tensor") - gain_grads
    return (
        result,
        grad_tokens,
        gain_grads[0] / attn_gain.astype(jnp.float32),
        grad_query,
        grad_key,
        grad_value,
        columns(grad_attn[:, :, width + 2 * HEAD :]).T,
        gain_grads[1] / ffn_gain.astype(jnp.float32),
        grad_gate,
        grad_up,
        columns(grad_down).T,
    )


ROWS = ("fsdp", "context")


def solution(mesh):
    return jax.shard_map(
        local,
        mesh=mesh,
        in_specs=(
            P(ROWS, None),
            P(ROWS, None),
            P(ROWS),
            P(ROWS, "tensor"),
            P(ROWS, "tensor"),
            P(ROWS, "tensor"),
            P("tensor", ROWS),
            P(ROWS),
            P(ROWS, "tensor"),
            P(ROWS, "tensor"),
            P("tensor", ROWS),
            P("fsdp", None),
            P("fsdp", None),
            P("fsdp", None),
        ),
        out_specs=(
            P(ROWS, None),
            P(ROWS, None),
            P(ROWS),
            P(ROWS, "tensor"),
            P(ROWS, "tensor"),
            P(ROWS, "tensor"),
            P("tensor", ROWS),
            P(ROWS),
            P(ROWS, "tensor"),
            P(ROWS, "tensor"),
            P("tensor", ROWS),
        ),
        check_vma=False,
    )
```

```python
import functools

import jax
import jax.numpy as jnp
from jax import lax
from jax.experimental import pallas as pl
from jax.experimental.pallas import tpu as pltpu
from jax.sharding import PartitionSpec as P

HEAD = 64
SEG = 128
TRUNK = 8 * SEG
BRANCHES = 4
LEAVES = 8
GROUP = TRUNK + (BRANCHES + LEAVES) * SEG
DEPTH = TRUNK + 2 * SEG
TILE = 2 * SEG

epsilon = 1e-05
rope_base = 10000000.0
residual_scale = 0.22
score_scale = 0.015625
masked_score = -1e30

FIRST = (((0,), (0,)), ((), ()))
LAST = (((1,), (1,)), ((), ()))
PLAIN = (((1,), (0,)), ((), ()))


def dot(left_side, right_side, dims=PLAIN):
    return lax.dot_general(left_side, right_side, dims, preferred_element_type=jnp.float32)


def rope_tables():
    frequency = rope_base ** (-(jnp.arange(HEAD // 2).astype(jnp.float32) * 2.0) / HEAD)
    angles = jnp.arange(DEPTH).astype(jnp.float32)[:, None] * frequency[None, :]
    sine = jnp.sin(angles)
    cosine = jnp.cos(angles)
    return (
        jnp.concatenate([cosine] * 4, axis=-1),
        jnp.concatenate([-sine, sine, -sine, sine], axis=-1),
    )


def lanes(values):
    return lax.broadcasted_iota(jnp.int32, values.shape, 1)


def swap_halves(values):
    return jnp.where(
        lanes(values) % HEAD < HEAD // 2,
        pltpu.roll(values, 128 - HEAD // 2, 1),
        pltpu.roll(values, HEAD // 2, 1),
    )


def only_head(values, head):
    return jnp.where(lanes(values) // HEAD == head, values, jnp.zeros_like(values))


def query_tiles(work):
    for j in range(TRUNK // TILE):
        prefix = [(0, j * TILE, False)] if j else []
        work(j * TILE, prefix + [(j * TILE, TILE, True)], False)

    def branch(i, carry):
        row = pl.multiple_of(TRUNK + i * TILE, TILE)
        work(row, [(0, TRUNK, False), (row, TILE, True)], True)
        return carry

    lax.fori_loop(0, BRANCHES * SEG // TILE, branch, 0)

    def leaf(i, carry):
        row = pl.multiple_of(TRUNK + BRANCHES * SEG + i * TILE, TILE)
        parent = pl.multiple_of(TRUNK + i * SEG, SEG)
        work(row, [(0, TRUNK, False), (parent, SEG, False), (row, TILE, True)], True)
        return carry

    lax.fori_loop(0, LEAVES * SEG // TILE, leaf, 0)


def visible_scores(keys, query, own, one_segment):
    scores = dot(keys, query, LAST)
    if not own:
        return scores
    key_at = lax.broadcasted_iota(jnp.int32, scores.shape, 0)
    query_at = lax.broadcasted_iota(jnp.int32, scores.shape, 1)
    seen = key_at <= query_at
    if one_segment:
        seen = seen & (key_at // SEG == query_at // SEG)
    return jnp.where(seen, scores, masked_score)


def turned_over(target, source):
    for first in range(0, source.shape[0], TILE):
        block = source[first : first + TILE, :128].astype(jnp.float32)
        target[:, first : first + TILE] = jnp.transpose(block)[:HEAD].astype(jnp.bfloat16)


def head_pairs(width, work):
    together = min(PAIR, width // HEAD)

    def step(i, carry):
        work([i * together + j for j in range(together)])
        return carry

    lax.fori_loop(0, width // HEAD // together, step, 0)


PAIR = 2


def attention_forward_kernel(
    to_ref, start_ref, raw_ref, cos_ref, sin_ref, out_ref, q_ref, k_ref, v_ref, log_ref,
    held, values_ref, tile_ref,
):
    width = q_ref.shape[1]
    pieces = to_ref.shape[0]
    piece = raw_ref.shape[0] // pieces

    def place(p, carry):
        rows = pl.ds(pl.multiple_of(p * piece, piece), piece)
        to = pl.ds(pl.multiple_of(to_ref[p], piece), piece)
        at = pl.ds(pl.multiple_of(start_ref[p], piece), piece)
        cosine, sine = cos_ref[at, :], sin_ref[at, :]

        def turn(values):
            return values * cosine + swap_halves(values) * sine

        for g in range(width // 128):
            cut = slice(g * 128, g * 128 + 128)
            turned = turn(raw_ref[rows, cut]).astype(jnp.bfloat16)
            q_ref[to, cut] = turned * jnp.bfloat16(score_scale)
        pair = raw_ref[rows, width : width + 128]
        low = lanes(pair) < HEAD
        key = turn(pair)
        key = jnp.where(low, key, pltpu.roll(key, HEAD, 1)).astype(jnp.bfloat16)
        value = jnp.where(low, pltpu.roll(pair, HEAD, 1), pair).astype(jnp.bfloat16)
        for g in range(width // 128):
            cut = slice(g * 128, g * 128 + 128)
            k_ref[to, cut] = key
            v_ref[to, cut] = value
        return carry

    lax.fori_loop(0, pieces, place, 0)
    turned_over(values_ref, v_ref)

    def work(row, parts, one_segment):
        rows = pl.ds(row, TILE)

        def one_head(head):
            query = only_head(q_ref[rows, :], head)
            scores = [
                visible_scores(k_ref[pl.ds(first, count), :], query, own, one_segment)
                for first, count, own in parts
            ]
            largest = functools.reduce(
                jnp.maximum, [jnp.max(s, axis=0, keepdims=True) for s in scores]
            )
            exponent = [jnp.exp(s - largest) for s in scores]
            total = functools.reduce(
                jnp.add, [jnp.sum(e, axis=0, keepdims=True) for e in exponent]
            )
            result = functools.reduce(
                jnp.add,
                [
                    dot(values_ref[:, pl.ds(first, count)], e.astype(jnp.bfloat16))
                    for e, (first, count, own) in zip(exponent, parts)
                ],
            )
            log_ref[head, :, rows] = largest + jnp.log(total)
            tile_ref[pl.ds(pl.multiple_of(head * HEAD, HEAD), HEAD), :] = result * (1.0 / total)

        def heads(together):
            for head in together:
                one_head(head)

        head_pairs(width, heads)
        held[rows, :] = jnp.transpose(tile_ref[...]).astype(jnp.bfloat16)

    query_tiles(work)

    def back(p, carry):
        rows = pl.ds(pl.multiple_of(p * piece, piece), piece)
        to = pl.ds(pl.multiple_of(to_ref[p], piece), piece)
        out_ref[rows, :] = held[to, :]
        return carry

    lax.fori_loop(0, pieces, back, 0)


def attention_backward_kernel(
    to_ref,
    start_ref,
    grad_ref,
    q_ref,
    k_ref,
    v_ref,
    log_ref,
    cos_ref,
    sin_ref,
    *rest,
):
    out_ref, og_ref, dq_ref, dk_ref, dv_ref, keys_ref, tile_ref = rest[-7:]
    width = q_ref.shape[1]
    pieces = to_ref.shape[0]
    piece = grad_ref.shape[0] // pieces

    def place(p, carry):
        rows = pl.ds(pl.multiple_of(p * piece, piece), piece)
        to = pl.ds(pl.multiple_of(to_ref[p], piece), piece)
        og_ref[to, :] = grad_ref[rows, :]
        return carry

    lax.fori_loop(0, pieces, place, 0)
    turned_over(keys_ref, k_ref)
    dk_ref[...] = jnp.zeros_like(dk_ref)
    dv_ref[...] = jnp.zeros_like(dv_ref)

    def work(row, parts, one_segment):
        rows = pl.ds(row, TILE)

        def heads(together):
            queries, out_grads, all_weights, all_grads = [], [], [], []
            for head in together:
                query = only_head(q_ref[rows, :], head)
                out_grad = only_head(og_ref[rows, :], head)
                log_total = log_ref[head, :, rows]
                weights, products = [], []
                for first, count, own in parts:
                    keys = pl.ds(first, count)
                    scores = visible_scores(k_ref[keys, :], query, own, one_segment)
                    weights.append(jnp.exp(scores - log_total))
                    products.append(dot(v_ref[keys, :], out_grad, LAST))
                inner = functools.reduce(
                    jnp.add,
                    [jnp.sum(w * d, axis=0, keepdims=True) for w, d in zip(weights, products)],
                )
                grads = [
                    (w * (d - inner)).astype(jnp.bfloat16) for w, d in zip(weights, products)
                ]
                queries.append(query)
                out_grads.append(out_grad)
                all_weights.append([w.astype(jnp.bfloat16) for w in weights])
                all_grads.append(grads)
                tile_ref[pl.ds(pl.multiple_of(head * HEAD, HEAD), HEAD), :] = functools.reduce(
                    jnp.add,
                    [
                        dot(keys_ref[:, pl.ds(first, count)], g)
                        for (first, count, own), g in zip(parts, grads)
                    ],
                )
            query = jnp.concatenate(queries, axis=0)
            out_grad = jnp.concatenate(out_grads, axis=0)
            for i, (first, count, own) in enumerate(parts):
                keys = pl.ds(first, count)
                weights = jnp.concatenate([w[i] for w in all_weights], axis=1)
                grads = jnp.concatenate([g[i] for g in all_grads], axis=1)
                dv_ref[keys, :] += dot(weights, out_grad)
                dk_ref[keys, :] += dot(grads, query)

        head_pairs(width, heads)
        dq_ref[rows, :] = jnp.transpose(tile_ref[...])

    query_tiles(work)

    def back(p, carry):
        rows = pl.ds(pl.multiple_of(p * piece, piece), piece)
        to = pl.ds(pl.multiple_of(to_ref[p], piece), piece)
        at = pl.ds(pl.multiple_of(start_ref[p], piece), piece)
        cosine, sine = cos_ref[at, :], sin_ref[at, :]

        def turn_back(values):
            return values * cosine - swap_halves(values) * sine

        def over_heads(ref):
            total = functools.reduce(
                jnp.add, [ref[to, g * 128 : g * 128 + 128] for g in range(width // 128)]
            )
            return total + pltpu.roll(total, HEAD, 1)

        for g in range(width // 128):
            cut = slice(g * 128, g * 128 + 128)
            turned = turn_back(score_scale * dq_ref[to, cut])
            out_ref[rows, cut] = turned.astype(jnp.bfloat16)
        key = turn_back(over_heads(dk_ref))
        value = over_heads(dv_ref)
        pair = jnp.where(lanes(key) < HEAD, key, value)
        out_ref[rows, width : width + 128] = pair.astype(jnp.bfloat16)
        return carry

    lax.fori_loop(0, pieces, back, 0)


SMEM = pl.BlockSpec(memory_space=pltpu.SMEM)
VMEM = pl.BlockSpec(memory_space=pltpu.VMEM)
VMEM_LIMIT = 48 * 1024 * 1024


def attention_cost(width, products):
    flops = products * 2 * GROUP * (GROUP * 2 // 5) * width
    return pl.CostEstimate(
        flops=flops, bytes_accessed=16 * GROUP * width, transcendentals=GROUP * GROUP * width // 128
    )


def attention_forward(places, starts, raw, tables):
    width = raw.shape[1] - 2 * HEAD
    rows = raw.shape[0]
    kept = jax.ShapeDtypeStruct((rows, width), jnp.bfloat16)
    return pl.pallas_call(
        attention_forward_kernel,
        out_shape=[kept] * 4 + [jax.ShapeDtypeStruct((width // HEAD, 1, rows), jnp.float32)],
        in_specs=[SMEM, SMEM, VMEM, VMEM, VMEM],
        out_specs=[VMEM] * 5,
        scratch_shapes=[
            pltpu.VMEM((rows, width), jnp.bfloat16),
            pltpu.VMEM((HEAD, rows), jnp.bfloat16),
            pltpu.VMEM((width, TILE), jnp.float32),
        ],
        compiler_params=pltpu.CompilerParams(vmem_limit_bytes=VMEM_LIMIT),
        cost_estimate=attention_cost(width, 4),
        name="attention_forward",
    )(places, starts, raw, *tables)


def attention_backward(places, starts, out_grad, kept, tables, early):
    rows, width = out_grad.shape
    return pl.pallas_call(
        attention_backward_kernel,
        out_shape=jax.ShapeDtypeStruct((rows, width + 2 * HEAD), jnp.bfloat16),
        in_specs=[SMEM, SMEM] + [VMEM] * 7 + [ANY] * len(early),
        out_specs=VMEM,
        scratch_shapes=[
            pltpu.VMEM((rows, width), jnp.bfloat16),
            pltpu.VMEM((rows, width), jnp.float32),
            pltpu.VMEM((rows, width), jnp.float32),
            pltpu.VMEM((rows, width), jnp.float32),
            pltpu.VMEM((HEAD, rows), jnp.bfloat16),
            pltpu.VMEM((width, TILE), jnp.float32),
        ],
        compiler_params=pltpu.CompilerParams(vmem_limit_bytes=VMEM_LIMIT),
        cost_estimate=attention_cost(width, 10),
        name="attention_backward",
    )(places, starts, out_grad, *kept, *tables, *early)


MESH = pl.DeviceIdType.MESH
ANY = pl.BlockSpec(memory_space=pl.ANY)
CHUNKS = 4
SLAB = 16


def lasting(microseconds):
    return pl.CostEstimate(
        flops=0, bytes_accessed=int(microseconds * 3_000_000), transcendentals=0
    )


class Plane:
    def __init__(self, sent, landed, diagonal=False, entered=False):
        self.sent, self.landed = sent, landed
        self.copies = []
        self.rank = lax.axis_index("context")
        self.core = lax.axis_index("tensor")
        self.at_x = self.rank + 1 - 2 * lax.rem(self.rank, 2)
        self.at_y = lax.rem(self.rank + 2, 4)
        self.at_both = 3 - self.rank
        self.x = {"context": self.at_x}
        self.y = {"context": self.at_y}
        self.both = {"context": self.at_both}
        self.sibling = {"tensor": 1 - self.core}
        if entered:
            return
        barrier = pltpu.get_barrier_semaphore()
        partners = [self.x, self.y, self.sibling] + ([self.both] if diagonal else [])
        for partner in partners:
            pl.semaphore_signal(barrier, inc=1, device_id=partner, device_id_type=MESH)
        pl.semaphore_wait(barrier, len(partners))

    def copy(self, number, source, target, partner):
        return pltpu.make_async_remote_copy(
            src_ref=source,
            dst_ref=target,
            send_sem=self.sent.at[number],
            recv_sem=self.landed.at[number],
            device_id=partner,
            device_id_type=MESH,
        )

    def send(self, source, target, partner):
        number = len(self.copies)
        started = self.copy(number, source, target, partner)
        started.start()
        self.copies.append(started)
        return number

    def arrive(self, number, target):
        self.copy(number, target, target, self.sibling).wait_recv()

    def finish(self):
        for started in self.copies:
            started.wait_send()


def chunk(index, rows):
    return pl.ds(index * (rows // CHUNKS), rows // CHUNKS)


class Gather:
    def __init__(self, plane, block, out):
        self.plane, self.block, self.out = plane, block, out
        self.rows = block.shape[0]
        self.to_x, self.to_y, self.across = {}, {}, {}

    def start(self, k):
        p, cut = self.plane, chunk(k, self.rows)
        target = self.out.at[p.rank, p.core, cut]
        self.to_x[k] = p.send(self.block.at[cut], target, p.x)
        self.to_y[k] = p.send(self.block.at[cut], target, p.y)
        self.across[0, k] = p.send(self.block.at[cut], target, p.sibling)

    def forward(self):
        p, out = self.plane, self.out
        onward = {}
        for k in range(CHUNKS):
            cut = chunk(k, self.rows)
            from_x, from_y = out.at[p.at_x, p.core, cut], out.at[p.at_y, p.core, cut]
            p.arrive(self.to_x[k], from_x)
            if k < CHUNKS // 2:
                onward[k] = p.send(from_x, from_x, p.y)
            self.across[1, k] = p.send(from_x, from_x, p.sibling)
            p.arrive(self.to_y[k], from_y)
            if k >= CHUNKS // 2:
                onward[k] = p.send(from_y, from_y, p.x)
            self.across[2, k] = p.send(from_y, from_y, p.sibling)
        for k in range(CHUNKS):
            far = out.at[p.at_both, p.core, chunk(k, self.rows)]
            p.arrive(onward[k], far)
            self.across[3, k] = p.send(far, far, p.sibling)

    def finish(self):
        p = self.plane
        for i, rank in enumerate((p.rank, p.at_x, p.at_y, p.at_both)):
            for k in range(CHUNKS):
                p.arrive(
                    self.across[i, k], self.out.at[rank, 1 - p.core, chunk(k, self.rows)]
                )


GATHER_COPIES = CHUNKS * 8


def add_rows(target, source, first, count):
    def step(i, carry):
        rows = pl.ds(first + i * SLAB, SLAB)
        target[rows, :] = (
            target[rows, :].astype(jnp.float32) + source[rows, :].astype(jnp.float32)
        ).astype(jnp.bfloat16)
        return carry

    lax.fori_loop(0, count // SLAB, step, 0)


class Scatter:
    def __init__(self, plane, partial, held, other, near_x, near_y, far_x, far_y, local):
        p = self.plane = plane
        rows = near_x.shape[0]
        half = rows // 2
        halves = top, low = pl.ds(0, half), pl.ds(half, half)
        order = (p.at_both, p.at_x, p.at_y, p.rank)
        across, kept = {}, []
        for i, h in ((0, 0), (0, 1), (1, 0), (2, 0), (1, 1), (2, 1), (3, 0), (3, 1)):
            source = partial.at[order[i], 1 - p.core, halves[h]]
            across[i, h] = p.send(source, other.at[i, halves[h]], p.sibling)
        for i in range(4):
            kept.append(
                pltpu.make_async_copy(partial.at[order[i], p.core], held.at[i], local.at[i])
            )
            kept[i].start()

        def pair(i, h):
            p.arrive(across[i, h], other.at[i, halves[h]])
            add_rows(held.at[i], other.at[i], h * half, half)

        kept[0].wait()
        pair(0, 0)
        first = p.send(held.at[0, top], far_x, p.x)
        pair(0, 1)
        second = p.send(held.at[0, low], far_y, p.y)
        kept[1].wait()
        pair(1, 0)
        third = p.send(held.at[1, top], near_x.at[top], p.x)
        kept[2].wait()
        pair(2, 0)
        p.arrive(first, far_x)
        add_rows(held.at[2], far_x, 0, half)
        fourth = p.send(held.at[2, top], near_y.at[top], p.y)
        pair(1, 1)
        p.arrive(second, far_y)

        def step(i, carry):
            rows, at = pl.ds(half + i * SLAB, SLAB), pl.ds(i * SLAB, SLAB)
            held[1, rows, :] = (
                held[1, rows, :].astype(jnp.float32) + far_y[at, :].astype(jnp.float32)
            ).astype(jnp.bfloat16)
            return carry

        lax.fori_loop(0, half // SLAB, step, 0)
        fifth = p.send(held.at[1, low], near_x.at[low], p.x)
        pair(2, 1)
        sixth = p.send(held.at[2, low], near_y.at[low], p.y)
        kept[3].wait()
        pair(3, 0)
        pair(3, 1)
        self.halves = halves
        self.from_x, self.from_y = (third, fifth), (fourth, sixth)
        self.parts = (held.at[3], near_x, near_y)

    def ready(self, h):
        _, near_x, near_y = self.parts
        self.plane.arrive(self.from_x[h], near_x.at[self.halves[h]])
        self.plane.arrive(self.from_y[h], near_y.at[self.halves[h]])

    def rows(self, rows):
        return sum(part[rows, :].astype(jnp.float32) for part in self.parts)


SCATTER_COPIES = 8 + 6


def scatter_scratch(share, width):
    kind = jnp.bfloat16
    return [
        pltpu.VMEM((4, share, width), kind),
        pltpu.VMEM((4, share, width), kind),
        pltpu.VMEM((share, width), kind),
        pltpu.VMEM((share, width), kind),
        pltpu.VMEM((share // 2, width), kind),
        pltpu.VMEM((share // 2, width), kind),
        pltpu.SemaphoreType.DMA((4,)),
    ]


def wires(count):
    return [pltpu.SemaphoreType.DMA((count,)), pltpu.SemaphoreType.DMA((count,))]


def row_root(values):
    return lax.rsqrt(jnp.mean(values * values, axis=-1, keepdims=True) + epsilon)


def slabs(first, count, work):
    def step(i, carry):
        work(pl.ds(first + i * SLAB, SLAB))
        return carry

    lax.fori_loop(0, count // SLAB, step, 0)


class Exchange:
    def __init__(self, plane, source, target, local):
        p = plane
        columns = target.shape[2]

        def part(rank):
            return source.at[:, pl.ds(pl.multiple_of(rank * columns, 128), columns)]

        self.plane, self.target, self.moves = p, target, []
        self.mine = pltpu.make_async_copy(part(p.rank), target.at[p.rank], local)
        self.mine.start()
        for partner, rank in ((p.both, p.at_both), (p.x, p.at_x), (p.y, p.at_y)):
            self.moves.append((p.send(part(rank), target.at[p.rank], partner), rank))

    def finish(self):
        for number, rank in self.moves:
            self.plane.arrive(number, self.target.at[rank])
        self.mine.wait()


def start_kernel(block, gate, cotangent, out, gate_out, scaled, my_scaled, sent, landed, local):
    p = Plane(sent, landed, diagonal=True)
    gather = Gather(p, block, out)
    mine = pltpu.make_async_copy(block, out.at[p.rank, p.core], local.at[0])
    for k in range(CHUNKS):
        gather.start(k)
    exchange = Exchange(p, gate, gate_out, local.at[1])
    mine.start()
    share = block.shape[0]

    def scale(rows):
        value = residual_scale * cotangent[rows, :].astype(jnp.float32)
        scaled[rows, :] = value.astype(jnp.bfloat16)

    def keep(rows):
        from_rows = pl.ds(pl.multiple_of(p.core * share + rows.start, SLAB), SLAB)
        my_scaled[rows, :] = scaled[from_rows, :]

    slabs(0, scaled.shape[0], scale)
    slabs(0, share, keep)
    gather.forward()
    gather.finish()
    exchange.finish()
    p.finish()
    mine.wait()


def start_plane(block, gate, cotangent):
    share, width = block.shape
    depth, units = gate.shape
    return pl.pallas_call(
        start_kernel,
        out_shape=[
            jax.ShapeDtypeStruct((4, 2, share, width), block.dtype),
            jax.ShapeDtypeStruct((4, depth, units // 4), gate.dtype),
            jax.ShapeDtypeStruct(cotangent.shape, jnp.bfloat16),
            jax.ShapeDtypeStruct(block.shape, jnp.bfloat16),
        ],
        in_specs=[VMEM, ANY, VMEM],
        out_specs=[ANY, ANY, VMEM, VMEM],
        scratch_shapes=wires(GATHER_COPIES + 3) + [pltpu.SemaphoreType.DMA((2,))],
        compiler_params=pltpu.CompilerParams(
            collective_id=1, has_side_effects=True, vmem_limit_bytes=VMEM_LIMIT
        ),
        cost_estimate=lasting(60),
        name="gather_tokens",
    )(block, gate, cotangent)


def middle_kernel(
    partial,
    residual,
    gain,
    beside,
    from_x,
    from_y,
    from_both,
    out,
    middle,
    beside_out,
    sent,
    landed,
    local,
    hidden,
    held_beside,
    held_blocks,
    *scratch,
):
    p = Plane(sent, landed)
    blocks = ((from_x, p.at_x), (from_y, p.at_y), (from_both, p.at_both))
    loads = [pltpu.make_async_copy(beside, held_beside, local.at[0])]
    for i, (block, rank) in enumerate(blocks):
        loads.append(pltpu.make_async_copy(block, held_blocks.at[i], local.at[i + 1]))
    for started in loads:
        started.start()
    total = Scatter(p, partial, *scratch)
    kept, across = [], []
    loads[0].wait()
    kept.append(pltpu.make_async_copy(held_beside, beside_out.at[p.rank], local.at[0]))
    kept[0].start()
    for i, (block, rank) in enumerate(blocks):
        loads[i + 1].wait()
        place = beside_out.at[rank, p.core]
        kept.append(pltpu.make_async_copy(held_blocks.at[i], place, local.at[i + 1]))
        kept[i + 1].start()
        across.append(p.send(held_blocks.at[i], place, p.sibling))
    share = hidden.shape[0]
    gather = Gather(p, hidden, out)

    def work(rows):
        value = residual[rows, :].astype(jnp.float32) + residual_scale * total.rows(rows)
        middle[rows, :] = value
        hidden[rows, :] = (value * row_root(value) * gain[...]).astype(jnp.bfloat16)

    for k in range(CHUNKS):
        if k % (CHUNKS // 2) == 0:
            total.ready(k // (CHUNKS // 2))
        slabs(k * (share // CHUNKS), share // CHUNKS, work)
        gather.start(k)
    kept.append(pltpu.make_async_copy(hidden, out.at[p.rank, p.core], local.at[4]))
    kept[4].start()
    gather.forward()
    gather.finish()
    for number, rank in zip(across, (p.at_x, p.at_y, p.at_both)):
        p.arrive(number, beside_out.at[rank, 1 - p.core])
    p.finish()
    for started in kept:
        started.wait()


def middle_plane(partial, residual, gain, beside, blocks):
    share, width = residual.shape
    full = jax.ShapeDtypeStruct((4, 2, share, width), jnp.bfloat16)
    out, middle, beside_out = pl.pallas_call(
        middle_kernel,
        out_shape=[full, jax.ShapeDtypeStruct((share, width), jnp.float32), full],
        in_specs=[ANY, VMEM, VMEM] + [ANY] * 4,
        out_specs=[ANY, VMEM, ANY],
        scratch_shapes=wires(GATHER_COPIES + SCATTER_COPIES + 3)
        + [
            pltpu.SemaphoreType.DMA((5,)),
            pltpu.VMEM((share, width), jnp.bfloat16),
            pltpu.VMEM((2, share, width), jnp.bfloat16),
            pltpu.VMEM((3, share, width), jnp.bfloat16),
        ]
        + scatter_scratch(share, width),
        compiler_params=pltpu.CompilerParams(
            collective_id=2, has_side_effects=True, vmem_limit_bytes=VMEM_LIMIT
        ),
        cost_estimate=lasting(100),
        name="middle_rows",
    )(partial.reshape(full.shape), residual, gain, beside.reshape(2, share, width), *blocks)
    return out.reshape(8 * share, width), middle, beside_out.reshape(8 * share, width)


def second_kernel(
    partial,
    other_partial,
    middle,
    cotangent,
    gain,
    early_first,
    early_second,
    out,
    grad_middle,
    pair_own,
    pair_x,
    pair_y,
    pair_both,
    sent,
    landed,
    local,
    hidden,
    held,
    theirs,
    *scratch,
):
    p = Plane(sent, landed)
    total = Scatter(p, partial, *scratch)
    share = hidden.shape[0]
    gather = Gather(p, hidden, out)
    order = (p.rank, p.at_x, p.at_y, p.at_both)
    kept, across = [], []
    for i, rank in enumerate(order):
        across.append(p.send(other_partial.at[rank, 1 - p.core], theirs.at[i], p.sibling))
        kept.append(
            pltpu.make_async_copy(other_partial.at[rank, p.core], held.at[i], local.at[i])
        )
        kept[i].start()

    def work(rows):
        value = middle[rows, :]
        root = row_root(value)
        normed = value * root
        slope = total.rows(rows) * gain[...]
        mean = jnp.mean(slope * normed, axis=-1, keepdims=True)
        gradient = cotangent[rows, :].astype(jnp.float32) + root * (slope - normed * mean)
        grad_middle[rows, :] = gradient
        hidden[rows, :] = (residual_scale * gradient).astype(jnp.bfloat16)

    for k in range(CHUNKS):
        if k % (CHUNKS // 2) == 0:
            total.ready(k // (CHUNKS // 2))
        slabs(k * (share // CHUNKS), share // CHUNKS, work)
        gather.start(k)
    mine = pltpu.make_async_copy(hidden, out.at[p.rank, p.core], local.at[4])
    mine.start()
    for i in range(4):
        p.arrive(across[i], theirs.at[i])
        kept[i].wait()
        add_rows(held.at[i], theirs.at[i], 0, share)
        target = (pair_own, pair_x, pair_y, pair_both)[i]
        kept[i] = pltpu.make_async_copy(held.at[i], target, local.at[i])
        kept[i].start()
    gather.forward()
    gather.finish()
    p.finish()
    mine.wait()
    for started in kept:
        started.wait()


def second_plane(partial, other_partial, middle, cotangent, gain, early):
    share, width = middle.shape
    full = jax.ShapeDtypeStruct((4, 2, share, width), jnp.bfloat16)
    quarter = jax.ShapeDtypeStruct((4, share, width), jnp.bfloat16)
    out, grad_middle, *pairs = pl.pallas_call(
        second_kernel,
        out_shape=[full, jax.ShapeDtypeStruct((share, width), jnp.float32)]
        + [jax.ShapeDtypeStruct((share, width), jnp.bfloat16)] * 4,
        in_specs=[ANY, ANY, VMEM, VMEM, VMEM, ANY, ANY],
        out_specs=[ANY, VMEM] + [ANY] * 4,
        scratch_shapes=wires(GATHER_COPIES + SCATTER_COPIES + 4)
        + [
            pltpu.SemaphoreType.DMA((5,)),
            pltpu.VMEM((share, width), jnp.bfloat16),
            pltpu.VMEM(quarter.shape, jnp.bfloat16),
            pltpu.VMEM(quarter.shape, jnp.bfloat16),
        ]
        + scatter_scratch(share, width),
        compiler_params=pltpu.CompilerParams(
            collective_id=3, has_side_effects=True, vmem_limit_bytes=VMEM_LIMIT
        ),
        cost_estimate=lasting(100),
        name="second_rows",
    )(
        partial.reshape(full.shape),
        other_partial.reshape(full.shape),
        middle,
        cotangent,
        gain,
        *early,
    )
    return out.reshape(8 * share, width), grad_middle, pairs


def lane_sums(pairs):
    total = 0.0
    for a, b in pairs:
        product = a.astype(jnp.float32) * b.astype(jnp.float32)
        total += jnp.sum(product, axis=1, keepdims=True)
    return jnp.broadcast_to(total, (total.shape[0], 128))


def last_kernel(
    partial,
    residual,
    grad_middle,
    gain,
    middle,
    ffn_own,
    ffn_x,
    ffn_y,
    ffn_both,
    grads,
    gate,
    up,
    out,
    result_out,
    gain_out,
    sent,
    landed,
    local,
    held,
    result,
    sums,
    *scratch,
):
    p = Plane(sent, landed)
    total = Scatter(p, partial, *scratch)
    share = held.shape[0]

    def finish_result(rows):
        parts = (ffn_own, ffn_x, ffn_y, ffn_both)
        ffn = sum(part[rows, :].astype(jnp.float32) for part in parts)
        result[rows, :] = (middle[rows, :] + residual_scale * ffn).astype(jnp.bfloat16)

    slabs(0, share, finish_result)
    kept = [pltpu.make_async_copy(result, result_out.at[p.core], local.at[0])]
    kept[0].start()
    given = p.send(result, result_out.at[p.core], p.sibling)
    units = gate.shape[1] // 4

    def gain_rows(rows):
        pairs = []
        for c in range(4):
            columns = slice(c * units, c * units + units)
            pairs.append((grads[c, rows, :units], gate[rows, columns]))
            pairs.append((grads[c, rows, units:], up[rows, columns]))
        sums[0, rows, :] = lane_sums(pairs)

    slabs(0, gate.shape[0], gain_rows)
    swapped = p.send(sums.at[0], sums.at[1], p.sibling)

    def work(rows):
        value = residual[rows, :].astype(jnp.float32)
        root = row_root(value)
        normed = value * root
        slope = total.rows(rows) * gain[...]
        mean = jnp.mean(slope * normed, axis=-1, keepdims=True)
        held[rows, :] = grad_middle[rows, :] + root * (slope - normed * mean)

    across = []
    for k in range(CHUNKS):
        cut = chunk(k, share)
        if k % (CHUNKS // 2) == 0:
            total.ready(k // (CHUNKS // 2))
        slabs(k * (share // CHUNKS), share // CHUNKS, work)
        across.append(p.send(held.at[cut], out.at[p.core, cut], p.sibling))
    kept.append(pltpu.make_async_copy(held, out.at[p.core], local.at[1]))
    kept[1].start()
    p.arrive(swapped, sums.at[1])
    gain_out[...] = sums[0] + sums[1]
    p.arrive(given, result_out.at[1 - p.core])
    for k in range(CHUNKS):
        p.arrive(across[k], out.at[1 - p.core, chunk(k, share)])
    p.finish()
    for started in kept:
        started.wait()


def last_plane(partial, residual, grad_middle, gain, middle, ffn_parts, grads, gate, up):
    share, width = residual.shape
    out, result_out, gain_out = pl.pallas_call(
        last_kernel,
        out_shape=[
            jax.ShapeDtypeStruct((2, share, width), jnp.float32),
            jax.ShapeDtypeStruct((2, share, width), jnp.bfloat16),
            jax.ShapeDtypeStruct((gate.shape[0], 128), jnp.float32),
        ],
        in_specs=[ANY] + [VMEM] * 11,
        out_specs=[ANY, ANY, VMEM],
        scratch_shapes=wires(CHUNKS + 2 + SCATTER_COPIES)
        + [
            pltpu.SemaphoreType.DMA((2,)),
            pltpu.VMEM((share, width), jnp.float32),
            pltpu.VMEM((share, width), jnp.bfloat16),
            pltpu.VMEM((2, gate.shape[0], 128), jnp.float32),
        ]
        + scatter_scratch(share, width),
        compiler_params=pltpu.CompilerParams(
            collective_id=4, has_side_effects=True, vmem_limit_bytes=VMEM_LIMIT
        ),
        cost_estimate=lasting(70),
        name="last_rows",
    )(
        partial.reshape(4, 2, share, width),
        residual,
        grad_middle,
        gain,
        middle,
        *ffn_parts,
        grads,
        gate,
        up,
    )
    return out.reshape(2 * share, width), result_out.reshape(2 * share, width), gain_out


def qkv_columns(blocks):
    return blocks.shape[2] // 2 + HEAD


def exchange_kernel(blocks, weights, early, out, gain_out, sent, landed, sums):
    p = Plane(sent, landed, diagonal=True)
    moves = []
    for partner, rank in ((p.both, p.at_both), (p.x, p.at_x), (p.y, p.at_y)):
        moves.append((p.send(blocks.at[rank], out.at[p.rank], partner), out.at[rank]))
    out[p.rank] = blocks[p.rank]
    for number, target in moves:
        p.arrive(number, target)
    columns = qkv_columns(blocks)

    def gain_rows(rows):
        pairs = [(out[c, rows, :columns], weights[c, rows, :columns]) for c in range(4)]
        sums[0, rows, :] = lane_sums(pairs)

    slabs(0, blocks.shape[1], gain_rows)
    swapped = p.send(sums.at[0], sums.at[1], p.sibling)
    p.arrive(swapped, sums.at[1])
    gain_out[...] = sums[0] + sums[1]
    p.finish()


def exchange(blocks, weights, early):
    depth = blocks.shape[1]
    return pl.pallas_call(
        exchange_kernel,
        out_shape=[
            jax.ShapeDtypeStruct(blocks.shape, blocks.dtype),
            jax.ShapeDtypeStruct((depth, 128), jnp.float32),
        ],
        in_specs=[VMEM, VMEM, ANY],
        out_specs=[VMEM, VMEM],
        scratch_shapes=wires(4) + [pltpu.VMEM((2, depth, 128), jnp.float32)],
        compiler_params=pltpu.CompilerParams(collective_id=5, has_side_effects=True),
        cost_estimate=lasting(8),
        name="exchange_blocks",
    )(blocks, weights, early)


def finish_kernel(
    attn, down, gate_up, tokens, result, attn_sums, ffn_sums, gains,
    query_out, pair_out, out_out, gate_out, up_out, down_out, tokens_out, result_out, gain_out,
):
    width = query_out.shape[1]
    units = gate_out.shape[1]
    query_out[...] = attn[0, :, :width].astype(jnp.float32)
    pair_out[...] = attn[0, :, width : width + 128].astype(jnp.float32)
    out_out[...] = jnp.transpose(attn[0, :, width + 128 :].astype(jnp.float32))
    gate_out[...] = gate_up[0, :, :units].astype(jnp.float32)
    up_out[...] = gate_up[0, :, units:].astype(jnp.float32)
    down_out[...] = jnp.transpose(down[0].astype(jnp.float32))
    tokens_out[...] = tokens[...]
    result_out[...] = result[...]
    gain_out[0:1, :] = jnp.transpose(attn_sums[...])[0:1] / gains[0:1, :]
    gain_out[1:2, :] = jnp.transpose(ffn_sums[...])[0:1] / gains[1:2, :]


def finish(attn, down, gate_up, tokens, result, attn_sums, ffn_sums, gains):
    groups, depth, units = down.shape
    width = attn.shape[2] // 2 - HEAD
    rows, columns = tokens.shape
    part = rows // groups

    def block(c, *shape):
        return pl.BlockSpec((1, *shape), lambda i: (i, 0, 0))

    def wide(count):
        return pl.BlockSpec((depth, count), lambda i: (0, i))

    def tall(count, other):
        return pl.BlockSpec((count, other), lambda i: (i, 0))

    def whole(array):
        return pl.BlockSpec(array.shape, lambda i: (0, 0))

    def f32(*shape):
        return jax.ShapeDtypeStruct(shape, jnp.float32)

    return pl.pallas_call(
        finish_kernel,
        grid=(groups,),
        in_specs=[
            block(0, depth, attn.shape[2]),
            block(0, depth, units),
            block(0, depth, 2 * units),
            tall(part, columns),
            tall(part, columns),
            whole(attn_sums),
            whole(ffn_sums),
            whole(gains),
        ],
        out_specs=[
            wide(width),
            wide(128),
            tall(width, depth),
            wide(units),
            wide(units),
            tall(units, depth),
            tall(part, columns),
            tall(part, columns),
            pl.BlockSpec((2, 128), lambda i: (0, 0)),
        ],
        out_shape=[
            f32(depth, groups * width),
            f32(depth, groups * 128),
            f32(groups * width, depth),
            f32(depth, groups * units),
            f32(depth, groups * units),
            f32(groups * units, depth),
            f32(rows, columns),
            jax.ShapeDtypeStruct(result.shape, result.dtype),
            f32(2, 128),
        ],
        compiler_params=pltpu.CompilerParams(vmem_limit_bytes=VMEM_LIMIT),
        cost_estimate=lasting(12),
        name="finish",
    )(attn, down, gate_up, tokens, result, attn_sums, ffn_sums, gains)


def context_pairs(step):
    return [(i, i ^ step) for i in range(4)]


def ffn_first_kernel(hidden, gate_w, up_w, m, gate, up):
    for j in range(gate_w.shape[1] // 256):
        cut = slice(j * 256, j * 256 + 256)
        gate_part = dot(hidden[...], gate_w[:, cut])
        up_part = dot(hidden[...], up_w[:, cut])
        gate[:, cut] = gate_part.astype(jnp.bfloat16)
        up[:, cut] = up_part.astype(jnp.bfloat16)
        sigmoid = 1.0 / (1.0 + jnp.exp(-gate_part))
        m[:, cut] = (gate_part * sigmoid * up_part).astype(jnp.bfloat16)


def ffn_second_kernel(grad, gate, up, m, gate_w, up_w, down_w, early, slopes, forward, back):
    units = gate_w.shape[1]
    for j in range(units // 256):
        cut = slice(j * 256, j * 256 + 256)
        grad_part = dot(grad[...], down_w[:, cut])
        gate_part = gate[:, cut].astype(jnp.float32)
        up_part = up[:, cut].astype(jnp.float32)
        sigmoid = 1.0 / (1.0 + jnp.exp(-gate_part))
        slope = sigmoid * (1.0 + gate_part * (1.0 - sigmoid))
        slopes[:, cut] = (grad_part * up_part * slope).astype(jnp.bfloat16)
        slopes[:, units + j * 256 : units + j * 256 + 256] = (
            grad_part * gate_part * sigmoid
        ).astype(jnp.bfloat16)
    for j in range(gate_w.shape[0] // 512):
        cut = slice(j * 512, j * 512 + 512)
        forward[:, cut] = dot(m[...], down_w[cut, :], LAST).astype(jnp.bfloat16)
        back[:, cut] = (
            dot(slopes[:, :units], gate_w[cut, :], LAST)
            + dot(slopes[:, units:], up_w[cut, :], LAST)
        ).astype(jnp.bfloat16)


def first_rows_kernel(
    values, gain, weight, up, down, hidden, raw, up_out, down_out, sent, landed, local
):
    step, last = pl.program_id(0), pl.num_programs(0) - 1

    def exchanges(act):
        for i, (source, target) in enumerate(((up, up_out), (down, down_out))):
            act(i, source, target)

    @pl.when(step == 0)
    def start():
        p = Plane(sent, landed, diagonal=True)
        exchanges(lambda i, source, target: Exchange(p, source, target, local.at[i]))

    value = values[...].astype(jnp.float32)
    normed = (value * row_root(value) * gain[...]).astype(jnp.bfloat16)
    hidden[...] = normed
    raw[...] = dot(normed, weight[...])

    @pl.when(step == last)
    def finish():
        p = Plane(sent, landed, entered=True)
        columns = up_out.shape[2]
        for i, (source, target) in enumerate(((up, up_out), (down, down_out))):
            part = source.at[:, pl.ds(0, columns)]
            for j, rank in enumerate((p.at_both, p.at_x, p.at_y)):
                move = p.copy(3 * i + j, part, target.at[rank], p.x)
                move.wait_recv()
                move.wait_send()
            own = source.at[:, pl.ds(pl.multiple_of(p.rank * columns, 128), columns)]
            pltpu.make_async_copy(own, target.at[p.rank], local.at[i]).wait()


def first_rows(values, gain, weight, up, down):
    count, width = values.shape
    columns = weight.shape[1]
    depth, units = up.shape
    moved = jax.ShapeDtypeStruct((4, depth, units // 4), up.dtype)
    return pl.pallas_call(
        first_rows_kernel,
        grid=(count // ROW_TILE,),
        in_specs=[
            pl.BlockSpec((ROW_TILE, width), lambda i: (i, 0)),
            pl.BlockSpec((1, width), lambda i: (0, 0)),
            pl.BlockSpec((width, columns), lambda i: (0, 0)),
            ANY,
            ANY,
        ],
        out_specs=[
            pl.BlockSpec((ROW_TILE, width), lambda i: (i, 0)),
            pl.BlockSpec((ROW_TILE, columns), lambda i: (i, 0)),
            ANY,
            ANY,
        ],
        out_shape=[
            jax.ShapeDtypeStruct((count, width), jnp.bfloat16),
            jax.ShapeDtypeStruct((count, columns), jnp.float32),
            moved,
            moved,
        ],
        scratch_shapes=wires(6) + [pltpu.SemaphoreType.DMA((2,))],
        compiler_params=pltpu.CompilerParams(
            collective_id=6, has_side_effects=True, vmem_limit_bytes=VMEM_LIMIT
        ),
        cost_estimate=lasting(25),
        name="first_rows",
    )(values, gain, weight, up, down)


def attention_weights_kernel(hidden, back, grad, attended, *early_and_out):
    out = early_and_out[-1]
    columns = back.shape[1]
    out[:, :columns] = dot(hidden[...], back[...], FIRST).astype(jnp.bfloat16)
    out[:, columns:] = dot(grad[...], attended[...], FIRST).astype(jnp.bfloat16)


def attention_weights(hidden, back, grad, attended, early):
    count, width = hidden.shape
    first, second = back.shape[1], attended.shape[1]
    tall = pl.BlockSpec((count, 512), lambda i: (0, i))
    return pl.pallas_call(
        attention_weights_kernel,
        grid=(width // 512,),
        in_specs=[
            tall,
            pl.BlockSpec((count, first), lambda i: (0, 0)),
            tall,
            pl.BlockSpec((count, second), lambda i: (0, 0)),
        ]
        + [ANY] * len(early),
        out_specs=pl.BlockSpec((512, first + second), lambda i: (i, 0)),
        out_shape=jax.ShapeDtypeStruct((width, first + second), jnp.bfloat16),
        compiler_params=pltpu.CompilerParams(vmem_limit_bytes=VMEM_LIMIT),
        cost_estimate=lasting(12),
        name="attention_weights",
    )(hidden, back, grad, attended, *early)


ROW_TILE = 256


def row_tiles(kernel, name, rows, weights, extra, widths):
    count = rows[0].shape[0]

    def tile(width):
        return pl.BlockSpec((ROW_TILE, width), lambda i: (i, 0))

    whole = [
        pl.BlockSpec(w.shape, lambda i: (0, 0), pipeline_mode=pl.Buffered(1)) for w in weights
    ]
    flops = 2 * count * sum(w.size for w in weights)
    return pl.pallas_call(
        kernel,
        grid=(count // ROW_TILE,),
        in_specs=[tile(r.shape[1]) for r in rows] + whole + [ANY] * len(extra),
        out_specs=[tile(width) for width in widths],
        out_shape=[jax.ShapeDtypeStruct((count, width), jnp.bfloat16) for width in widths],
        compiler_params=pltpu.CompilerParams(vmem_limit_bytes=56 * 1024 * 1024),
        cost_estimate=pl.CostEstimate(flops=flops, bytes_accessed=flops // 400, transcendentals=0),
        name=name,
    )(*rows, *weights, *extra)


def norm_backward(gradient, normed, inv_root):
    return inv_root * (gradient - normed * jnp.mean(gradient * normed, axis=-1, keepdims=True))


def inverse_root(values):
    return lax.rsqrt(jnp.mean(values * values, axis=-1, keepdims=True) + epsilon)


PLANE = ("context", "tensor")


def gather_rows(values):
    return lax.all_gather(values, PLANE, axis=0, tiled=True)


def scatter_rows(partial):
    return lax.psum_scatter(
        partial.astype(jnp.bfloat16), PLANE, scatter_dimension=0, tiled=True
    ).astype(jnp.float32)


def local(
    tokens,
    cotangent,
    attn_gain,
    w_query,
    w_key,
    w_value,
    w_out,
    ffn_gain,
    w_gate,
    w_up,
    w_down,
    piece_segment,
    piece_parent,
    piece_start,
):
    groups = lax.axis_size("context")
    cores = lax.axis_size("tensor")
    depth = w_query.shape[0]
    kv_count = w_key.shape[1] // HEAD
    sharing = groups // kv_count
    share = tokens.shape[0] // cores
    first_row = lax.axis_index("tensor") * share

    def my_rows(values):
        return lax.dynamic_slice_in_dim(values, first_row, share, 0)

    def blocks(weight):
        return jnp.transpose(weight.reshape(depth, groups, -1), (1, 0, 2))

    def kv_blocks(weight):
        return jnp.repeat(jnp.transpose(weight.reshape(depth, kv_count, HEAD), (1, 0, 2)), sharing, 0)

    def spread(weight_blocks):
        mine = lax.all_to_all(weight_blocks, "context", 0, 0)
        mine = mine.reshape(groups * depth, -1)
        return lax.all_gather(mine, "fsdp", axis=0, tiled=True)

    gains = jnp.stack([attn_gain, ffn_gain], axis=1)
    gains = jnp.broadcast_to(jnp.pad(gains, ((0, 0), (0, 126))), (groups, depth, 128))
    my_packed = jnp.concatenate(
        [blocks(w_query), kv_blocks(w_key), kv_blocks(w_value), blocks(w_out.T), gains], axis=2
    )
    packed = spread(my_packed)
    width = w_query.shape[1] // groups
    qkv_full = packed[:, : width + 2 * HEAD]
    out_full = packed[:, width + 2 * HEAD : 2 * width + 2 * HEAD]
    gains_full = packed[:, 2 * width + 2 * HEAD :].astype(jnp.float32)
    attn_scale, ffn_scale = gains_full[:, 0], gains_full[:, 1]
    square = groups == 4 and cores == 2
    tokens_half, cotangent_half = my_rows(tokens), my_rows(cotangent)
    tables = rope_tables()

    def over_groups(blocks_here):
        return lax.all_gather(
            blocks_here.reshape(groups * depth, -1), "fsdp", axis=0, tiled=True
        )

    down_turned = w_down.T
    if square:
        inputs_full, gate_blocks, ffn_grad, my_ffn_grad = start_plane(
            tokens_half, w_gate, cotangent
        )
        gate_full = over_groups(gate_blocks)
        hidden_first, raw, up_blocks, down_blocks = first_rows(
            inputs_full.reshape(-1, inputs_full.shape[3]),
            attn_scale[None, :],
            qkv_full,
            w_up,
            down_turned,
        )
        up_full, down_full = over_groups(up_blocks), over_groups(down_blocks)
    else:
        gate_full, up_full, down_full = (
            spread(blocks(w)) for w in (w_gate, w_up, down_turned)
        )
        inputs_full = gather_rows(tokens_half).astype(jnp.float32)
        hidden_first = inputs_full * inverse_root(inputs_full) * attn_scale
        hidden_first = hidden_first.astype(jnp.bfloat16)
        raw = dot(hidden_first, qkv_full)
        my_ffn_grad = (residual_scale * cotangent_half.astype(jnp.float32)).astype(jnp.bfloat16)

    segment, starts = piece_segment[0] % 13, piece_start[0]
    places = jnp.where(
        segment == 0,
        starts,
        jnp.where(
            segment <= BRANCHES,
            starts + (segment - 1) * SEG,
            starts + (segment - 1 - BRANCHES) * SEG + (BRANCHES - 1) * SEG,
        ),
    )

    residual_in = tokens_half.astype(jnp.float32)
    grad_result = cotangent_half.astype(jnp.float32)

    attended, *kept = attention_forward(places, starts, raw, tables)
    branch = dot(attended, out_full, LAST).astype(jnp.bfloat16)
    if square:
        ffn_grad_blocks = [
            lax.ppermute(my_ffn_grad, "context", context_pairs(step)) for step in (1, 2, 3)
        ]
        hidden_second, middle, ffn_grad = middle_plane(
            branch, tokens_half, ffn_scale[None, :], ffn_grad, ffn_grad_blocks
        )
    else:
        ffn_grad = gather_rows(my_ffn_grad)
        middle = residual_in + residual_scale * scatter_rows(branch)
        hidden_second = gather_rows((middle * inverse_root(middle) * ffn_scale).astype(jnp.bfloat16))

    units = gate_full.shape[1]
    hidden, gate_proj, up_proj = row_tiles(
        ffn_first_kernel,
        "ffn_first",
        [hidden_second],
        [gate_full, up_full],
        [],
        [units, units, units],
    )
    grad_down = dot(ffn_grad, hidden, FIRST).astype(jnp.bfloat16)
    slopes, ffn_out, grad_second = row_tiles(
        ffn_second_kernel,
        "ffn_second",
        [ffn_grad, gate_proj, up_proj, hidden],
        [gate_full, up_full, down_full],
        [grad_down],
        [2 * units, gate_full.shape[0], gate_full.shape[0]],
    )
    grad_gate_up = dot(hidden_second, slopes, FIRST).astype(jnp.bfloat16)

    def sum_groups(gradient):
        return lax.psum_scatter(gradient, "fsdp", scatter_dimension=0, tiled=True)

    def hand_back(gradient):
        return lax.all_to_all(gradient.reshape(groups, depth, -1), "context", 0, 0)

    def columns(gradient):
        return jnp.transpose(gradient, (1, 0, 2)).reshape(depth, -1).astype(jnp.float32)

    if square:
        attn_grad, grad_middle, ffn_pairs = second_plane(
            grad_second,
            ffn_out,
            middle,
            cotangent_half,
            ffn_scale[None, :],
            [grad_down, grad_gate_up],
        )
        ffn_parts = [ffn_pairs[0]] + [
            lax.ppermute(ffn_pairs[step], "context", context_pairs(step)) for step in (1, 2, 3)
        ]
    else:
        root = inverse_root(middle)
        grad_middle = grad_result + norm_backward(
            scatter_rows(grad_second) * ffn_scale, middle * root, root
        )
        attn_grad = gather_rows((residual_scale * grad_middle).astype(jnp.bfloat16))
        ffn_parts = []
    grad_attended = dot(attn_grad, out_full).astype(jnp.bfloat16)
    grad_down = sum_groups(grad_down)
    grad_gate_up = sum_groups(grad_gate_up)
    back = attention_backward(places, starts, grad_attended, kept, tables, [grad_down])
    grad_down = hand_back(grad_down)
    grad_attn = attention_weights(
        hidden_first, back, attn_grad, attended, [grad_gate_up, grad_down, *ffn_parts[1:]]
    )
    grad_attn = sum_groups(grad_attn)
    grad_gate_up = hand_back(grad_gate_up)
    grad_first = dot(back, qkv_full, LAST).astype(jnp.bfloat16)
    if square:
        grad_tokens, result, ffn_sums = last_plane(
            grad_first,
            tokens_half,
            grad_middle,
            attn_scale[None, :],
            middle,
            ffn_parts,
            grad_gate_up,
            w_gate,
            w_up,
        )
        grad_attn, attn_sums = exchange(
            grad_attn.reshape(groups, depth, -1), my_packed, ffn_sums
        )
        my_gains = jnp.stack([attn_gain, ffn_gain]).astype(jnp.float32)
        query, pair, out, gate, up, down, grad_tokens, result, gain_grads = finish(
            grad_attn, grad_down, grad_gate_up, grad_tokens, result, attn_sums, ffn_sums, my_gains
        )
        key, value = jnp.moveaxis(pair.reshape(depth, groups, 2, HEAD), 2, 0)
        return (
            result,
            grad_tokens,
            gain_grads[0],
            query,
            key.reshape(depth, -1),
            value.reshape(depth, -1),
            out,
            gain_grads[1],
            gate,
            up,
            down,
        )
    else:
        root = inverse_root(residual_in)
        grad_tokens = grad_middle + norm_backward(
            scatter_rows(grad_first) * attn_scale, residual_in * root, root
        )
        grad_tokens = lax.all_gather(grad_tokens, "tensor", axis=0, tiled=True)
        result = (middle + residual_scale * scatter_rows(ffn_out)).astype(jnp.bfloat16)
        grad_attn = hand_back(grad_attn)
        result = lax.all_gather(result, "tensor", axis=0, tiled=True)
    def kv_columns(gradient):
        gradient = gradient.astype(jnp.float32).reshape(kv_count, sharing, depth, HEAD)
        return jnp.transpose(jnp.sum(gradient, axis=1), (1, 0, 2)).reshape(depth, -1)

    grad_query = columns(grad_attn[:, :, :width])
    grad_key = kv_columns(grad_attn[:, :, width : width + HEAD])
    grad_value = kv_columns(grad_attn[:, :, width + HEAD : width + 2 * HEAD])
    grad_gate, grad_up = columns(grad_gate_up[:, :, :units]), columns(grad_gate_up[:, :, units:])

    def against(*pairs):
        return sum(jnp.sum(weight.astype(jnp.float32) * g, axis=1) for weight, g in pairs)

    gain_grads = jnp.stack(
        [
            against((w_query, grad_query), (w_key, grad_key), (w_value, grad_value)),
            against((w_gate, grad_gate), (w_up, grad_up)),
        ]
    )
    gain_grads = lax.psum(gain_grads, "tensor")
    return (
        result,
        grad_tokens,
        gain_grads[0] / attn_gain.astype(jnp.float32),
        grad_query,
        grad_key,
        grad_value,
        columns(grad_attn[:, :, width + 2 * HEAD :]).T,
        gain_grads[1] / ffn_gain.astype(jnp.float32),
        grad_gate,
        grad_up,
        columns(grad_down).T,
    )


ROWS = ("fsdp", "context")


def solution(mesh):
    return jax.shard_map(
        local,
        mesh=mesh,
        in_specs=(
            P(ROWS, None),
            P(ROWS, None),
            P(ROWS),
            P(ROWS, "tensor"),
            P(ROWS, "tensor"),
            P(ROWS, "tensor"),
            P("tensor", ROWS),
            P(ROWS),
            P(ROWS, "tensor"),
            P(ROWS, "tensor"),
            P("tensor", ROWS),
            P("fsdp", None),
            P("fsdp", None),
            P("fsdp", None),
        ),
        out_specs=(
            P(ROWS, None),
            P(ROWS, None),
            P(ROWS),
            P(ROWS, "tensor"),
            P(ROWS, "tensor"),
            P(ROWS, "tensor"),
            P("tensor", ROWS),
            P(ROWS),
            P(ROWS, "tensor"),
            P(ROWS, "tensor"),
            P("tensor", ROWS),
        ),
        check_vma=False,
    )
```

```python
import functools

import jax
import jax.numpy as jnp
from jax import lax
from jax.experimental import pallas as pl
from jax.experimental.pallas import tpu as pltpu
from jax.sharding import PartitionSpec as P

HEAD = 64
SEG = 128
TRUNK = 8 * SEG
BRANCHES = 4
LEAVES = 8
GROUP = TRUNK + (BRANCHES + LEAVES) * SEG
DEPTH = TRUNK + 2 * SEG
TILE = 2 * SEG

epsilon = 1e-05
rope_base = 10000000.0
residual_scale = 0.22
score_scale = 0.015625
masked_score = -1e30

FIRST = (((0,), (0,)), ((), ()))
LAST = (((1,), (1,)), ((), ()))
PLAIN = (((1,), (0,)), ((), ()))


def dot(left_side, right_side, dims=PLAIN):
    return lax.dot_general(left_side, right_side, dims, preferred_element_type=jnp.float32)


def rope_tables():
    frequency = rope_base ** (-(jnp.arange(HEAD // 2).astype(jnp.float32) * 2.0) / HEAD)
    angles = jnp.arange(DEPTH).astype(jnp.float32)[:, None] * frequency[None, :]
    sine = jnp.sin(angles)
    cosine = jnp.cos(angles)
    return (
        jnp.concatenate([cosine] * 4, axis=-1),
        jnp.concatenate([-sine, sine, -sine, sine], axis=-1),
    )


def lanes(values):
    return lax.broadcasted_iota(jnp.int32, values.shape, 1)


def swap_halves(values):
    return jnp.where(
        lanes(values) % HEAD < HEAD // 2,
        pltpu.roll(values, 128 - HEAD // 2, 1),
        pltpu.roll(values, HEAD // 2, 1),
    )


def only_head(values, head):
    return jnp.where(lanes(values) // HEAD == head, values, jnp.zeros_like(values))


def query_tiles(work):
    for j in range(TRUNK // TILE):
        prefix = [(0, j * TILE, False)] if j else []
        work(j * TILE, prefix + [(j * TILE, TILE, True)], False)

    def branch(i, carry):
        row = pl.multiple_of(TRUNK + i * TILE, TILE)
        work(row, [(0, TRUNK, False), (row, TILE, True)], True)
        return carry

    lax.fori_loop(0, BRANCHES * SEG // TILE, branch, 0)

    def leaf(i, carry):
        row = pl.multiple_of(TRUNK + BRANCHES * SEG + i * TILE, TILE)
        parent = pl.multiple_of(TRUNK + i * SEG, SEG)
        work(row, [(0, TRUNK, False), (parent, SEG, False), (row, TILE, True)], True)
        return carry

    lax.fori_loop(0, LEAVES * SEG // TILE, leaf, 0)


def visible_scores(keys, query, own, one_segment):
    scores = dot(keys, query, LAST)
    if not own:
        return scores
    key_at = lax.broadcasted_iota(jnp.int32, scores.shape, 0)
    query_at = lax.broadcasted_iota(jnp.int32, scores.shape, 1)
    seen = key_at <= query_at
    if one_segment:
        seen = seen & (key_at // SEG == query_at // SEG)
    return jnp.where(seen, scores, masked_score)


def turned_over(target, source):
    for first in range(0, source.shape[0], TILE):
        block = source[first : first + TILE, :128].astype(jnp.float32)
        target[:, first : first + TILE] = jnp.transpose(block)[:HEAD].astype(jnp.bfloat16)


def head_pairs(width, work):
    together = min(PAIR, width // HEAD)

    def step(i, carry):
        work([i * together + j for j in range(together)])
        return carry

    lax.fori_loop(0, width // HEAD // together, step, 0)


PAIR = 2


def attention_forward_kernel(
    to_ref, start_ref, raw_ref, cos_ref, sin_ref, out_ref, q_ref, k_ref, v_ref, log_ref,
    held, values_ref, tile_ref,
):
    width = q_ref.shape[1]
    pieces = to_ref.shape[0]
    piece = raw_ref.shape[0] // pieces

    def place(p, carry):
        rows = pl.ds(pl.multiple_of(p * piece, piece), piece)
        to = pl.ds(pl.multiple_of(to_ref[p], piece), piece)
        at = pl.ds(pl.multiple_of(start_ref[p], piece), piece)
        cosine, sine = cos_ref[at, :], sin_ref[at, :]

        def turn(values):
            return values * cosine + swap_halves(values) * sine

        for g in range(width // 128):
            cut = slice(g * 128, g * 128 + 128)
            turned = turn(raw_ref[rows, cut]).astype(jnp.bfloat16)
            q_ref[to, cut] = turned * jnp.bfloat16(score_scale)
        pair = raw_ref[rows, width : width + 128]
        low = lanes(pair) < HEAD
        key = turn(pair)
        key = jnp.where(low, key, pltpu.roll(key, HEAD, 1)).astype(jnp.bfloat16)
        value = jnp.where(low, pltpu.roll(pair, HEAD, 1), pair).astype(jnp.bfloat16)
        for g in range(width // 128):
            cut = slice(g * 128, g * 128 + 128)
            k_ref[to, cut] = key
            v_ref[to, cut] = value
        return carry

    lax.fori_loop(0, pieces, place, 0)
    turned_over(values_ref, v_ref)

    def work(row, parts, one_segment):
        rows = pl.ds(row, TILE)

        def one_head(head):
            query = only_head(q_ref[rows, :], head)
            scores = [
                visible_scores(k_ref[pl.ds(first, count), :], query, own, one_segment)
                for first, count, own in parts
            ]
            largest = functools.reduce(
                jnp.maximum, [jnp.max(s, axis=0, keepdims=True) for s in scores]
            )
            exponent = [jnp.exp(s - largest) for s in scores]
            total = functools.reduce(
                jnp.add, [jnp.sum(e, axis=0, keepdims=True) for e in exponent]
            )
            result = functools.reduce(
                jnp.add,
                [
                    dot(values_ref[:, pl.ds(first, count)], e.astype(jnp.bfloat16))
                    for e, (first, count, own) in zip(exponent, parts)
                ],
            )
            log_ref[head, :, rows] = largest + jnp.log(total)
            tile_ref[pl.ds(pl.multiple_of(head * HEAD, HEAD), HEAD), :] = result * (1.0 / total)

        def heads(together):
            for head in together:
                one_head(head)

        head_pairs(width, heads)
        held[rows, :] = jnp.transpose(tile_ref[...]).astype(jnp.bfloat16)

    query_tiles(work)

    def back(p, carry):
        rows = pl.ds(pl.multiple_of(p * piece, piece), piece)
        to = pl.ds(pl.multiple_of(to_ref[p], piece), piece)
        out_ref[rows, :] = held[to, :]
        return carry

    lax.fori_loop(0, pieces, back, 0)


def attention_backward_kernel(
    to_ref,
    start_ref,
    grad_ref,
    q_ref,
    k_ref,
    v_ref,
    log_ref,
    cos_ref,
    sin_ref,
    *rest,
):
    out_ref, og_ref, dq_ref, dk_ref, dv_ref, keys_ref, tile_ref = rest[-7:]
    width = q_ref.shape[1]
    pieces = to_ref.shape[0]
    piece = grad_ref.shape[0] // pieces

    def place(p, carry):
        rows = pl.ds(pl.multiple_of(p * piece, piece), piece)
        to = pl.ds(pl.multiple_of(to_ref[p], piece), piece)
        og_ref[to, :] = grad_ref[rows, :]
        return carry

    lax.fori_loop(0, pieces, place, 0)
    turned_over(keys_ref, k_ref)
    dk_ref[...] = jnp.zeros_like(dk_ref)
    dv_ref[...] = jnp.zeros_like(dv_ref)

    def work(row, parts, one_segment):
        rows = pl.ds(row, TILE)

        def heads(together):
            queries, out_grads, all_weights, all_grads = [], [], [], []
            for head in together:
                query = only_head(q_ref[rows, :], head)
                out_grad = only_head(og_ref[rows, :], head)
                log_total = log_ref[head, :, rows]
                weights, products = [], []
                for first, count, own in parts:
                    keys = pl.ds(first, count)
                    scores = visible_scores(k_ref[keys, :], query, own, one_segment)
                    weights.append(jnp.exp(scores - log_total))
                    products.append(dot(v_ref[keys, :], out_grad, LAST))
                inner = functools.reduce(
                    jnp.add,
                    [jnp.sum(w * d, axis=0, keepdims=True) for w, d in zip(weights, products)],
                )
                grads = [
                    (w * (d - inner)).astype(jnp.bfloat16) for w, d in zip(weights, products)
                ]
                queries.append(query)
                out_grads.append(out_grad)
                all_weights.append([w.astype(jnp.bfloat16) for w in weights])
                all_grads.append(grads)
                tile_ref[pl.ds(pl.multiple_of(head * HEAD, HEAD), HEAD), :] = functools.reduce(
                    jnp.add,
                    [
                        dot(keys_ref[:, pl.ds(first, count)], g)
                        for (first, count, own), g in zip(parts, grads)
                    ],
                )
            query = jnp.concatenate(queries, axis=0)
            out_grad = jnp.concatenate(out_grads, axis=0)
            for i, (first, count, own) in enumerate(parts):
                keys = pl.ds(first, count)
                weights = jnp.concatenate([w[i] for w in all_weights], axis=1)
                grads = jnp.concatenate([g[i] for g in all_grads], axis=1)
                dv_ref[keys, :] += dot(weights, out_grad)
                dk_ref[keys, :] += dot(grads, query)

        head_pairs(width, heads)
        dq_ref[rows, :] = jnp.transpose(tile_ref[...])

    query_tiles(work)

    def back(p, carry):
        rows = pl.ds(pl.multiple_of(p * piece, piece), piece)
        to = pl.ds(pl.multiple_of(to_ref[p], piece), piece)
        at = pl.ds(pl.multiple_of(start_ref[p], piece), piece)
        cosine, sine = cos_ref[at, :], sin_ref[at, :]

        def turn_back(values):
            return values * cosine - swap_halves(values) * sine

        def over_heads(ref):
            total = functools.reduce(
                jnp.add, [ref[to, g * 128 : g * 128 + 128] for g in range(width // 128)]
            )
            return total + pltpu.roll(total, HEAD, 1)

        for g in range(width // 128):
            cut = slice(g * 128, g * 128 + 128)
            turned = turn_back(score_scale * dq_ref[to, cut])
            out_ref[rows, cut] = turned.astype(jnp.bfloat16)
        key = turn_back(over_heads(dk_ref))
        value = over_heads(dv_ref)
        pair = jnp.where(lanes(key) < HEAD, key, value)
        out_ref[rows, width : width + 128] = pair.astype(jnp.bfloat16)
        return carry

    lax.fori_loop(0, pieces, back, 0)


SMEM = pl.BlockSpec(memory_space=pltpu.SMEM)
VMEM = pl.BlockSpec(memory_space=pltpu.VMEM)
VMEM_LIMIT = 48 * 1024 * 1024


def attention_cost(width, products):
    flops = products * 2 * GROUP * (GROUP * 2 // 5) * width
    return pl.CostEstimate(
        flops=flops, bytes_accessed=16 * GROUP * width, transcendentals=GROUP * GROUP * width // 128
    )


def attention_forward(places, starts, raw, tables):
    width = raw.shape[1] - 2 * HEAD
    rows = raw.shape[0]
    kept = jax.ShapeDtypeStruct((rows, width), jnp.bfloat16)
    return pl.pallas_call(
        attention_forward_kernel,
        out_shape=[kept] * 4 + [jax.ShapeDtypeStruct((width // HEAD, 1, rows), jnp.float32)],
        in_specs=[SMEM, SMEM, VMEM, VMEM, VMEM],
        out_specs=[VMEM] * 5,
        scratch_shapes=[
            pltpu.VMEM((rows, width), jnp.bfloat16),
            pltpu.VMEM((HEAD, rows), jnp.bfloat16),
            pltpu.VMEM((width, TILE), jnp.float32),
        ],
        compiler_params=pltpu.CompilerParams(vmem_limit_bytes=VMEM_LIMIT),
        cost_estimate=attention_cost(width, 4),
        name="attention_forward",
    )(places, starts, raw, *tables)


def attention_backward(places, starts, out_grad, kept, tables, early):
    rows, width = out_grad.shape
    return pl.pallas_call(
        attention_backward_kernel,
        out_shape=jax.ShapeDtypeStruct((rows, width + 2 * HEAD), jnp.bfloat16),
        in_specs=[SMEM, SMEM] + [VMEM] * 7 + [ANY] * len(early),
        out_specs=VMEM,
        scratch_shapes=[
            pltpu.VMEM((rows, width), jnp.bfloat16),
            pltpu.VMEM((rows, width), jnp.float32),
            pltpu.VMEM((rows, width), jnp.float32),
            pltpu.VMEM((rows, width), jnp.float32),
            pltpu.VMEM((HEAD, rows), jnp.bfloat16),
            pltpu.VMEM((width, TILE), jnp.float32),
        ],
        compiler_params=pltpu.CompilerParams(vmem_limit_bytes=VMEM_LIMIT),
        cost_estimate=attention_cost(width, 10),
        name="attention_backward",
    )(places, starts, out_grad, *kept, *tables, *early)


MESH = pl.DeviceIdType.MESH
ANY = pl.BlockSpec(memory_space=pl.ANY)
CHUNKS = 4
SLAB = 16


def lasting(microseconds):
    return pl.CostEstimate(
        flops=0, bytes_accessed=int(microseconds * 3_000_000), transcendentals=0
    )


class Plane:
    def __init__(self, sent, landed, diagonal=False, entered=False):
        self.sent, self.landed = sent, landed
        self.copies = []
        self.rank = lax.axis_index("context")
        self.core = lax.axis_index("tensor")
        self.at_x = self.rank + 1 - 2 * lax.rem(self.rank, 2)
        self.at_y = lax.rem(self.rank + 2, 4)
        self.at_both = 3 - self.rank
        self.x = {"context": self.at_x}
        self.y = {"context": self.at_y}
        self.both = {"context": self.at_both}
        self.sibling = {"tensor": 1 - self.core}
        if entered:
            return
        barrier = pltpu.get_barrier_semaphore()
        partners = [self.x, self.y, self.sibling] + ([self.both] if diagonal else [])
        for partner in partners:
            pl.semaphore_signal(barrier, inc=1, device_id=partner, device_id_type=MESH)
        pl.semaphore_wait(barrier, len(partners))

    def copy(self, number, source, target, partner):
        return pltpu.make_async_remote_copy(
            src_ref=source,
            dst_ref=target,
            send_sem=self.sent.at[number],
            recv_sem=self.landed.at[number],
            device_id=partner,
            device_id_type=MESH,
        )

    def send(self, source, target, partner):
        number = len(self.copies)
        started = self.copy(number, source, target, partner)
        started.start()
        self.copies.append(started)
        return number

    def arrive(self, number, target):
        self.copy(number, target, target, self.sibling).wait_recv()

    def finish(self):
        for started in self.copies:
            started.wait_send()


def chunk(index, rows):
    return pl.ds(index * (rows // CHUNKS), rows // CHUNKS)


class Gather:
    def __init__(self, plane, block, out):
        self.plane, self.block, self.out = plane, block, out
        self.rows = block.shape[0]
        self.to_x, self.to_y, self.across, self.onward = {}, {}, {}, {}

    def start(self, k):
        p, cut = self.plane, chunk(k, self.rows)
        target = self.out.at[p.rank, p.core, cut]
        self.to_x[k] = p.send(self.block.at[cut], target, p.x)
        self.to_y[k] = p.send(self.block.at[cut], target, p.y)
        self.across[0, k] = p.send(self.block.at[cut], target, p.sibling)

    def forward_chunk(self, k):
        p, out = self.plane, self.out
        cut = chunk(k, self.rows)
        from_x, from_y = out.at[p.at_x, p.core, cut], out.at[p.at_y, p.core, cut]
        p.arrive(self.to_x[k], from_x)
        if k < CHUNKS // 2:
            self.onward[k] = p.send(from_x, from_x, p.y)
        self.across[1, k] = p.send(from_x, from_x, p.sibling)
        p.arrive(self.to_y[k], from_y)
        if k >= CHUNKS // 2:
            self.onward[k] = p.send(from_y, from_y, p.x)
        self.across[2, k] = p.send(from_y, from_y, p.sibling)

    def forward_far(self):
        p = self.plane
        for k in range(CHUNKS):
            far = self.out.at[p.at_both, p.core, chunk(k, self.rows)]
            p.arrive(self.onward[k], far)
            self.across[3, k] = p.send(far, far, p.sibling)

    def forward(self):
        for k in range(CHUNKS):
            self.forward_chunk(k)
        self.forward_far()

    def finish(self):
        p = self.plane
        for i, rank in enumerate((p.rank, p.at_x, p.at_y, p.at_both)):
            for k in range(CHUNKS):
                p.arrive(
                    self.across[i, k], self.out.at[rank, 1 - p.core, chunk(k, self.rows)]
                )


GATHER_COPIES = CHUNKS * 8


def add_rows(target, source, first, count):
    def step(i, carry):
        rows = pl.ds(first + i * SLAB, SLAB)
        target[rows, :] = (
            target[rows, :].astype(jnp.float32) + source[rows, :].astype(jnp.float32)
        ).astype(jnp.bfloat16)
        return carry

    lax.fori_loop(0, count // SLAB, step, 0)


class Scatter:
    def __init__(self, plane, partial, held, other, near_x, near_y, far_x, far_y, local):
        p = self.plane = plane
        rows = near_x.shape[0]
        half = rows // 2
        halves = top, low = pl.ds(0, half), pl.ds(half, half)
        order = (p.at_both, p.at_x, p.at_y, p.rank)
        across, kept = {}, []
        for i, h in ((0, 0), (0, 1), (1, 0), (2, 0), (1, 1), (2, 1), (3, 0), (3, 1)):
            source = partial.at[order[i], 1 - p.core, halves[h]]
            across[i, h] = p.send(source, other.at[i, halves[h]], p.sibling)
        for i in range(4):
            kept.append(
                pltpu.make_async_copy(partial.at[order[i], p.core], held.at[i], local.at[i])
            )
            kept[i].start()

        def pair(i, h):
            p.arrive(across[i, h], other.at[i, halves[h]])
            add_rows(held.at[i], other.at[i], h * half, half)

        kept[0].wait()
        pair(0, 0)
        first = p.send(held.at[0, top], far_x, p.x)
        pair(0, 1)
        second = p.send(held.at[0, low], far_y, p.y)
        kept[1].wait()
        pair(1, 0)
        third = p.send(held.at[1, top], near_x.at[top], p.x)
        kept[2].wait()
        pair(2, 0)
        p.arrive(first, far_x)
        add_rows(held.at[2], far_x, 0, half)
        fourth = p.send(held.at[2, top], near_y.at[top], p.y)
        pair(1, 1)
        p.arrive(second, far_y)

        def step(i, carry):
            rows, at = pl.ds(half + i * SLAB, SLAB), pl.ds(i * SLAB, SLAB)
            held[1, rows, :] = (
                held[1, rows, :].astype(jnp.float32) + far_y[at, :].astype(jnp.float32)
            ).astype(jnp.bfloat16)
            return carry

        lax.fori_loop(0, half // SLAB, step, 0)
        fifth = p.send(held.at[1, low], near_x.at[low], p.x)
        pair(2, 1)
        sixth = p.send(held.at[2, low], near_y.at[low], p.y)
        kept[3].wait()
        pair(3, 0)
        pair(3, 1)
        self.halves = halves
        self.from_x, self.from_y = (third, fifth), (fourth, sixth)
        self.parts = (held.at[3], near_x, near_y)

    def ready(self, h):
        _, near_x, near_y = self.parts
        self.plane.arrive(self.from_x[h], near_x.at[self.halves[h]])
        self.plane.arrive(self.from_y[h], near_y.at[self.halves[h]])

    def rows(self, rows):
        return sum(part[rows, :].astype(jnp.float32) for part in self.parts)


SCATTER_COPIES = 8 + 6


def scatter_scratch(share, width):
    kind = jnp.bfloat16
    return [
        pltpu.VMEM((4, share, width), kind),
        pltpu.VMEM((4, share, width), kind),
        pltpu.VMEM((share, width), kind),
        pltpu.VMEM((share, width), kind),
        pltpu.VMEM((share // 2, width), kind),
        pltpu.VMEM((share // 2, width), kind),
        pltpu.SemaphoreType.DMA((4,)),
    ]


def wires(count):
    return [pltpu.SemaphoreType.DMA((count,)), pltpu.SemaphoreType.DMA((count,))]


def row_root(values):
    return lax.rsqrt(jnp.mean(values * values, axis=-1, keepdims=True) + epsilon)


def slabs(first, count, work):
    def step(i, carry):
        work(pl.ds(first + i * SLAB, SLAB))
        return carry

    lax.fori_loop(0, count // SLAB, step, 0)


class Exchange:
    def __init__(self, plane, source, target, local):
        p = plane
        columns = target.shape[2]

        def part(rank):
            return source.at[:, pl.ds(pl.multiple_of(rank * columns, 128), columns)]

        self.plane, self.target, self.moves = p, target, []
        self.mine = pltpu.make_async_copy(part(p.rank), target.at[p.rank], local)
        self.mine.start()
        for partner, rank in ((p.both, p.at_both), (p.x, p.at_x), (p.y, p.at_y)):
            self.moves.append((p.send(part(rank), target.at[p.rank], partner), rank))

    def finish(self):
        for number, rank in self.moves:
            self.plane.arrive(number, self.target.at[rank])
        self.mine.wait()


def start_kernel(block, gate, cotangent, out, gate_out, scaled, my_scaled, sent, landed, local):
    p = Plane(sent, landed, diagonal=True)
    gather = Gather(p, block, out)
    mine = pltpu.make_async_copy(block, out.at[p.rank, p.core], local.at[0])
    for k in range(CHUNKS):
        gather.start(k)
    exchange = Exchange(p, gate, gate_out, local.at[1])
    mine.start()
    share = block.shape[0]

    def scale(rows):
        value = residual_scale * cotangent[rows, :].astype(jnp.float32)
        scaled[rows, :] = value.astype(jnp.bfloat16)

    def keep(rows):
        from_rows = pl.ds(pl.multiple_of(p.core * share + rows.start, SLAB), SLAB)
        my_scaled[rows, :] = scaled[from_rows, :]

    slabs(0, scaled.shape[0], scale)
    slabs(0, share, keep)
    gather.forward()
    gather.finish()
    exchange.finish()
    p.finish()
    mine.wait()


def start_plane(block, gate, cotangent):
    share, width = block.shape
    depth, units = gate.shape
    return pl.pallas_call(
        start_kernel,
        out_shape=[
            jax.ShapeDtypeStruct((4, 2, share, width), block.dtype),
            jax.ShapeDtypeStruct((4, depth, units // 4), gate.dtype),
            jax.ShapeDtypeStruct(cotangent.shape, jnp.bfloat16),
            jax.ShapeDtypeStruct(block.shape, jnp.bfloat16),
        ],
        in_specs=[VMEM, ANY, VMEM],
        out_specs=[ANY, ANY, VMEM, VMEM],
        scratch_shapes=wires(GATHER_COPIES + 3) + [pltpu.SemaphoreType.DMA((2,))],
        compiler_params=pltpu.CompilerParams(
            collective_id=1, has_side_effects=True, vmem_limit_bytes=VMEM_LIMIT
        ),
        cost_estimate=lasting(60),
        name="gather_tokens",
    )(block, gate, cotangent)


def middle_kernel(
    partial,
    residual,
    gain,
    beside,
    from_x,
    from_y,
    from_both,
    out,
    middle,
    beside_out,
    sent,
    landed,
    local,
    hidden,
    held_beside,
    held_blocks,
    *scratch,
):
    p = Plane(sent, landed)
    blocks = ((from_x, p.at_x), (from_y, p.at_y), (from_both, p.at_both))
    loads = [pltpu.make_async_copy(beside, held_beside, local.at[0])]
    for i, (block, rank) in enumerate(blocks):
        loads.append(pltpu.make_async_copy(block, held_blocks.at[i], local.at[i + 1]))
    for started in loads:
        started.start()
    total = Scatter(p, partial, *scratch)
    kept, across = [], []
    loads[0].wait()
    kept.append(pltpu.make_async_copy(held_beside, beside_out.at[p.rank], local.at[0]))
    kept[0].start()
    for i, (block, rank) in enumerate(blocks):
        loads[i + 1].wait()
        place = beside_out.at[rank, p.core]
        kept.append(pltpu.make_async_copy(held_blocks.at[i], place, local.at[i + 1]))
        kept[i + 1].start()
        across.append(p.send(held_blocks.at[i], place, p.sibling))
    share = hidden.shape[0]
    gather = Gather(p, hidden, out)

    def work(rows):
        value = residual[rows, :].astype(jnp.float32) + residual_scale * total.rows(rows)
        middle[rows, :] = value
        hidden[rows, :] = (value * row_root(value) * gain[...]).astype(jnp.bfloat16)

    for k in range(CHUNKS):
        if k % (CHUNKS // 2) == 0:
            total.ready(k // (CHUNKS // 2))
        slabs(k * (share // CHUNKS), share // CHUNKS, work)
        gather.start(k)
    kept.append(pltpu.make_async_copy(hidden, out.at[p.rank, p.core], local.at[4]))
    kept[4].start()
    gather.forward()
    gather.finish()
    for number, rank in zip(across, (p.at_x, p.at_y, p.at_both)):
        p.arrive(number, beside_out.at[rank, 1 - p.core])
    p.finish()
    for started in kept:
        started.wait()


def middle_plane(partial, residual, gain, beside, blocks):
    share, width = residual.shape
    full = jax.ShapeDtypeStruct((4, 2, share, width), jnp.bfloat16)
    out, middle, beside_out = pl.pallas_call(
        middle_kernel,
        out_shape=[full, jax.ShapeDtypeStruct((share, width), jnp.float32), full],
        in_specs=[ANY, VMEM, VMEM] + [ANY] * 4,
        out_specs=[ANY, VMEM, ANY],
        scratch_shapes=wires(GATHER_COPIES + SCATTER_COPIES + 3)
        + [
            pltpu.SemaphoreType.DMA((5,)),
            pltpu.VMEM((share, width), jnp.bfloat16),
            pltpu.VMEM((2, share, width), jnp.bfloat16),
            pltpu.VMEM((3, share, width), jnp.bfloat16),
        ]
        + scatter_scratch(share, width),
        compiler_params=pltpu.CompilerParams(
            collective_id=2, has_side_effects=True, vmem_limit_bytes=VMEM_LIMIT
        ),
        cost_estimate=lasting(100),
        name="middle_rows",
    )(partial.reshape(full.shape), residual, gain, beside.reshape(2, share, width), *blocks)
    return out.reshape(8 * share, width), middle, beside_out.reshape(8 * share, width)


UNITS = ((0, 0), (0, 1), (1, 0), (2, 0), (1, 1), (2, 1), (3, 0), (3, 1))


def second_kernel(
    slopes,
    gate_w,
    up_w,
    middle,
    cotangent,
    gain,
    early,
    grad_middle,
    hidden,
    sent,
    landed,
    loading,
    slopes_in,
    given,
    held,
    other,
    near_x,
    near_y,
    far_x,
    far_y,
):
    p = Plane(sent, landed)
    share, width = near_x.shape
    half = share // 2
    units = gate_w.shape[1]
    order = (p.at_both, p.at_x, p.at_y, p.rank)
    top, low = halves = pl.ds(0, half), pl.ds(half, half)

    def loads(u):
        i, h = UNITS[u]
        for j, core in enumerate((1 - p.core, p.core)):
            row = (order[i] * 2 + core) * share + h * half
            yield pltpu.make_async_copy(
                slopes.at[pl.ds(pl.multiple_of(row, 32), half)],
                slopes_in.at[u % 2, halves[j]],
                loading.at[u % 2, j],
            )

    def compute(u):
        i, h = UNITS[u]
        slot = u % 2

        def step(j, carry):
            cut = pl.ds(pl.multiple_of(j * 1024, 1024), 1024)
            back = dot(slopes_in[slot, :, :units], gate_w[cut, :], LAST) + dot(
                slopes_in[slot, :, units:], up_w[cut, :], LAST
            )
            given[slot, :, cut] = back[:half].astype(jnp.bfloat16)
            held[i, halves[h], cut] = back[half:].astype(jnp.bfloat16)
            return carry

        lax.fori_loop(0, width // 1024, step, 0)

    moves, across = {}, {}

    def settle(u):
        i, h = UNITS[u]
        p.arrive(across[u], other.at[i, halves[h]])
        add_rows(held.at[i], other.at[i], h * half, half)
        if u == 0:
            moves["far_x"] = p.send(held.at[0, top], far_x, p.x)
        elif u == 1:
            moves["far_y"] = p.send(held.at[0, low], far_y, p.y)
        elif u == 2:
            moves["x", 0] = p.send(held.at[1, top], near_x.at[top], p.x)
        elif u == 3:
            p.arrive(moves["far_x"], far_x)
            add_rows(held.at[2], far_x, 0, half)
            moves["y", 0] = p.send(held.at[2, top], near_y.at[top], p.y)
        elif u == 4:
            p.arrive(moves["far_y"], far_y)

            def step(k, carry):
                rows, at = pl.ds(half + k * SLAB, SLAB), pl.ds(k * SLAB, SLAB)
                held[1, rows, :] = (
                    held[1, rows, :].astype(jnp.float32) + far_y[at, :].astype(jnp.float32)
                ).astype(jnp.bfloat16)
                return carry

            lax.fori_loop(0, half // SLAB, step, 0)
            moves["x", 1] = p.send(held.at[1, low], near_x.at[low], p.x)
        elif u == 5:
            moves["y", 1] = p.send(held.at[2, low], near_y.at[low], p.y)

    for started in loads(0):
        started.start()
    for u in range(8):
        for started in loads(u):
            started.wait()
        if u < 7:
            for started in loads(u + 1):
                started.start()
        if u >= 2:
            p.copies[across[u - 2]].wait_send()
        compute(u)
        i, h = UNITS[u]
        across[u] = p.send(given.at[u % 2], other.at[i, halves[h]], p.sibling)
        if u >= 1:
            settle(u - 1)
    settle(7)

    def work(rows):
        value = middle[rows, :]
        root = row_root(value)
        normed = value * root
        total = sum(part[rows, :].astype(jnp.float32) for part in (held.at[3], near_x, near_y))
        slope = total * gain[...]
        mean = jnp.mean(slope * normed, axis=-1, keepdims=True)
        gradient = cotangent[rows, :].astype(jnp.float32) + root * (slope - normed * mean)
        grad_middle[rows, :] = gradient
        hidden[rows, :] = (residual_scale * gradient).astype(jnp.bfloat16)

    for h in range(2):
        p.arrive(moves["x", h], near_x.at[halves[h]])
        p.arrive(moves["y", h], near_y.at[halves[h]])
        slabs(h * half, half, work)
    for u in (6, 7):
        p.copies[across[u]].wait_send()
    for number, started in enumerate(p.copies):
        if number not in across.values():
            started.wait_send()


def second_plane(slopes, gate_w, up_w, middle, cotangent, gain, early):
    share, width = middle.shape
    kind = jnp.bfloat16
    half = share // 2
    quarter = pltpu.VMEM((4, share, width), kind)
    return pl.pallas_call(
        second_kernel,
        out_shape=[
            jax.ShapeDtypeStruct((share, width), jnp.float32),
            jax.ShapeDtypeStruct((share, width), kind),
        ],
        in_specs=[ANY] + [VMEM] * 5 + [ANY],
        out_specs=[VMEM, VMEM],
        scratch_shapes=wires(8 + 6)
        + [
            pltpu.SemaphoreType.DMA((2, 2)),
            pltpu.VMEM((2, share, slopes.shape[1]), kind),
            pltpu.VMEM((2, half, width), kind),
            quarter,
            quarter,
            pltpu.VMEM((share, width), kind),
            pltpu.VMEM((share, width), kind),
            pltpu.VMEM((half, width), kind),
            pltpu.VMEM((half, width), kind),
        ],
        compiler_params=pltpu.CompilerParams(
            collective_id=3, has_side_effects=True, vmem_limit_bytes=VMEM_LIMIT
        ),
        cost_estimate=lasting(60),
        name="second_rows",
    )(slopes, gate_w, up_w, middle, cotangent, gain, early)


def spread_kernel(
    hidden, m, down_w, out, pair_own, pair_x, pair_y, pair_both,
    sent, landed, local, loading, m_in, given, held, theirs,
):
    p = Plane(sent, landed)
    share, width = hidden.shape
    gather = Gather(p, hidden, out)
    for k in range(CHUNKS):
        gather.start(k)
    mine = pltpu.make_async_copy(hidden, out.at[p.rank, p.core], local.at[4])
    mine.start()
    order = (p.rank, p.at_x, p.at_y, p.at_both)
    halves = pl.ds(0, share), pl.ds(share, share)

    def loads(i):
        for j, core in enumerate((1 - p.core, p.core)):
            yield pltpu.make_async_copy(
                m.at[order[i], core], m_in.at[i % 2, halves[j]], loading.at[i % 2, j]
            )

    across = []
    for started in loads(0):
        started.start()
    for i in range(4):
        for started in loads(i):
            started.wait()
        if i < 3:
            for started in loads(i + 1):
                started.start()

        def step(j, carry, i=i):
            cut = pl.ds(pl.multiple_of(j * 512, 512), 512)
            value = dot(m_in[i % 2], down_w[cut, :], LAST)
            given[i, :, cut] = value[:share].astype(jnp.bfloat16)
            held[i, :, cut] = value[share:].astype(jnp.bfloat16)
            return carry

        lax.fori_loop(0, width // 512, step, 0)
        across.append(p.send(given.at[i], theirs.at[i], p.sibling))
        gather.forward_chunk(i)
    kept = []
    for i in range(4):
        p.arrive(across[i], theirs.at[i])
        add_rows(held.at[i], theirs.at[i], 0, share)
        target = (pair_own, pair_x, pair_y, pair_both)[i]
        kept.append(pltpu.make_async_copy(held.at[i], target, local.at[i]))
        kept[i].start()
    gather.forward_far()
    gather.finish()
    p.finish()
    mine.wait()
    for started in kept:
        started.wait()


def spread_plane(hidden, m, down_w):
    share, width = hidden.shape
    units = m.shape[1]
    full = jax.ShapeDtypeStruct((4, 2, share, width), jnp.bfloat16)
    quarter = pltpu.VMEM((4, share, width), jnp.bfloat16)
    out, *pairs = pl.pallas_call(
        spread_kernel,
        out_shape=[full] + [jax.ShapeDtypeStruct((share, width), jnp.bfloat16)] * 4,
        in_specs=[VMEM, ANY, VMEM],
        out_specs=[ANY] * 5,
        scratch_shapes=wires(GATHER_COPIES + 4)
        + [
            pltpu.SemaphoreType.DMA((5,)),
            pltpu.SemaphoreType.DMA((2, 2)),
            pltpu.VMEM((2, 2 * share, units), jnp.bfloat16),
            quarter,
            quarter,
            quarter,
        ],
        compiler_params=pltpu.CompilerParams(
            collective_id=7, has_side_effects=True, vmem_limit_bytes=VMEM_LIMIT
        ),
        cost_estimate=lasting(60),
        name="spread_rows",
    )(hidden, m.reshape(4, 2, share, units), down_w)
    return out.reshape(8 * share, width), pairs


def lane_sums(pairs):
    total = 0.0
    for a, b in pairs:
        product = a.astype(jnp.float32) * b.astype(jnp.float32)
        total += jnp.sum(product, axis=1, keepdims=True)
    return jnp.broadcast_to(total, (total.shape[0], 128))


def last_kernel(
    partial,
    residual,
    grad_middle,
    gain,
    middle,
    ffn_own,
    ffn_x,
    ffn_y,
    ffn_both,
    grads,
    gate,
    up,
    out,
    result_out,
    gain_out,
    sent,
    landed,
    local,
    held,
    result,
    sums,
    *scratch,
):
    p = Plane(sent, landed)
    total = Scatter(p, partial, *scratch)
    share = held.shape[0]

    def finish_result(rows):
        parts = (ffn_own, ffn_x, ffn_y, ffn_both)
        ffn = sum(part[rows, :].astype(jnp.float32) for part in parts)
        result[rows, :] = (middle[rows, :] + residual_scale * ffn).astype(jnp.bfloat16)

    slabs(0, share, finish_result)
    kept = [pltpu.make_async_copy(result, result_out.at[p.core], local.at[0])]
    kept[0].start()
    given = p.send(result, result_out.at[p.core], p.sibling)
    units = gate.shape[1] // 4

    def gain_rows(rows):
        pairs = []
        for c in range(4):
            columns = slice(c * units, c * units + units)
            pairs.append((grads[c, rows, :units], gate[rows, columns]))
            pairs.append((grads[c, rows, units:], up[rows, columns]))
        sums[0, rows, :] = lane_sums(pairs)

    slabs(0, gate.shape[0], gain_rows)
    swapped = p.send(sums.at[0], sums.at[1], p.sibling)

    def work(rows):
        value = residual[rows, :].astype(jnp.float32)
        root = row_root(value)
        normed = value * root
        slope = total.rows(rows) * gain[...]
        mean = jnp.mean(slope * normed, axis=-1, keepdims=True)
        held[rows, :] = grad_middle[rows, :] + root * (slope - normed * mean)

    across = []
    for k in range(CHUNKS):
        cut = chunk(k, share)
        if k % (CHUNKS // 2) == 0:
            total.ready(k // (CHUNKS // 2))
        slabs(k * (share // CHUNKS), share // CHUNKS, work)
        across.append(p.send(held.at[cut], out.at[p.core, cut], p.sibling))
    kept.append(pltpu.make_async_copy(held, out.at[p.core], local.at[1]))
    kept[1].start()
    p.arrive(swapped, sums.at[1])
    gain_out[...] = sums[0] + sums[1]
    p.arrive(given, result_out.at[1 - p.core])
    for k in range(CHUNKS):
        p.arrive(across[k], out.at[1 - p.core, chunk(k, share)])
    p.finish()
    for started in kept:
        started.wait()


def last_plane(partial, residual, grad_middle, gain, middle, ffn_parts, grads, gate, up):
    share, width = residual.shape
    out, result_out, gain_out = pl.pallas_call(
        last_kernel,
        out_shape=[
            jax.ShapeDtypeStruct((2, share, width), jnp.float32),
            jax.ShapeDtypeStruct((2, share, width), jnp.bfloat16),
            jax.ShapeDtypeStruct((gate.shape[0], 128), jnp.float32),
        ],
        in_specs=[ANY] + [VMEM] * 11,
        out_specs=[ANY, ANY, VMEM],
        scratch_shapes=wires(CHUNKS + 2 + SCATTER_COPIES)
        + [
            pltpu.SemaphoreType.DMA((2,)),
            pltpu.VMEM((share, width), jnp.float32),
            pltpu.VMEM((share, width), jnp.bfloat16),
            pltpu.VMEM((2, gate.shape[0], 128), jnp.float32),
        ]
        + scatter_scratch(share, width),
        compiler_params=pltpu.CompilerParams(
            collective_id=4, has_side_effects=True, vmem_limit_bytes=VMEM_LIMIT
        ),
        cost_estimate=lasting(70),
        name="last_rows",
    )(
        partial.reshape(4, 2, share, width),
        residual,
        grad_middle,
        gain,
        middle,
        *ffn_parts,
        grads,
        gate,
        up,
    )
    return out.reshape(2 * share, width), result_out.reshape(2 * share, width), gain_out


def qkv_columns(blocks):
    return blocks.shape[2] // 2 + HEAD


def exchange_kernel(blocks, weights, early, out, gain_out, sent, landed, sums):
    p = Plane(sent, landed, diagonal=True)
    moves = []
    for partner, rank in ((p.both, p.at_both), (p.x, p.at_x), (p.y, p.at_y)):
        moves.append((p.send(blocks.at[rank], out.at[p.rank], partner), out.at[rank]))
    out[p.rank] = blocks[p.rank]
    for number, target in moves:
        p.arrive(number, target)
    columns = qkv_columns(blocks)

    def gain_rows(rows):
        pairs = [(out[c, rows, :columns], weights[c, rows, :columns]) for c in range(4)]
        sums[0, rows, :] = lane_sums(pairs)

    slabs(0, blocks.shape[1], gain_rows)
    swapped = p.send(sums.at[0], sums.at[1], p.sibling)
    p.arrive(swapped, sums.at[1])
    gain_out[...] = sums[0] + sums[1]
    p.finish()


def exchange(blocks, weights, early):
    depth = blocks.shape[1]
    return pl.pallas_call(
        exchange_kernel,
        out_shape=[
            jax.ShapeDtypeStruct(blocks.shape, blocks.dtype),
            jax.ShapeDtypeStruct((depth, 128), jnp.float32),
        ],
        in_specs=[VMEM, VMEM, ANY],
        out_specs=[VMEM, VMEM],
        scratch_shapes=wires(4) + [pltpu.VMEM((2, depth, 128), jnp.float32)],
        compiler_params=pltpu.CompilerParams(collective_id=5, has_side_effects=True),
        cost_estimate=lasting(8),
        name="exchange_blocks",
    )(blocks, weights, early)


def finish_kernel(
    attn, down, gate_up, tokens, result, attn_sums, ffn_sums, gains,
    query_out, pair_out, out_out, gate_out, up_out, down_out, tokens_out, result_out, gain_out,
):
    width = query_out.shape[1]
    units = gate_out.shape[1]
    query_out[...] = attn[0, :, :width].astype(jnp.float32)
    pair_out[...] = attn[0, :, width : width + 128].astype(jnp.float32)
    out_out[...] = jnp.transpose(attn[0, :, width + 128 :].astype(jnp.float32))
    gate_out[...] = gate_up[0, :, :units].astype(jnp.float32)
    up_out[...] = gate_up[0, :, units:].astype(jnp.float32)
    down_out[...] = jnp.transpose(down[0].astype(jnp.float32))
    tokens_out[...] = tokens[...]
    result_out[...] = result[...]
    gain_out[0:1, :] = jnp.transpose(attn_sums[...])[0:1] / gains[0:1, :]
    gain_out[1:2, :] = jnp.transpose(ffn_sums[...])[0:1] / gains[1:2, :]


def finish(attn, down, gate_up, tokens, result, attn_sums, ffn_sums, gains):
    groups, depth, units = down.shape
    width = attn.shape[2] // 2 - HEAD
    rows, columns = tokens.shape
    part = rows // groups

    def block(c, *shape):
        return pl.BlockSpec((1, *shape), lambda i: (i, 0, 0))

    def wide(count):
        return pl.BlockSpec((depth, count), lambda i: (0, i))

    def tall(count, other):
        return pl.BlockSpec((count, other), lambda i: (i, 0))

    def whole(array):
        return pl.BlockSpec(array.shape, lambda i: (0, 0))

    def f32(*shape):
        return jax.ShapeDtypeStruct(shape, jnp.float32)

    return pl.pallas_call(
        finish_kernel,
        grid=(groups,),
        in_specs=[
            block(0, depth, attn.shape[2]),
            block(0, depth, units),
            block(0, depth, 2 * units),
            tall(part, columns),
            tall(part, columns),
            whole(attn_sums),
            whole(ffn_sums),
            whole(gains),
        ],
        out_specs=[
            wide(width),
            wide(128),
            tall(width, depth),
            wide(units),
            wide(units),
            tall(units, depth),
            tall(part, columns),
            tall(part, columns),
            pl.BlockSpec((2, 128), lambda i: (0, 0)),
        ],
        out_shape=[
            f32(depth, groups * width),
            f32(depth, groups * 128),
            f32(groups * width, depth),
            f32(depth, groups * units),
            f32(depth, groups * units),
            f32(groups * units, depth),
            f32(rows, columns),
            jax.ShapeDtypeStruct(result.shape, result.dtype),
            f32(2, 128),
        ],
        compiler_params=pltpu.CompilerParams(vmem_limit_bytes=VMEM_LIMIT),
        cost_estimate=lasting(12),
        name="finish",
    )(attn, down, gate_up, tokens, result, attn_sums, ffn_sums, gains)


def context_pairs(step):
    return [(i, i ^ step) for i in range(4)]


def ffn_first_kernel(hidden, gate_w, up_w, m, gate, up):
    for j in range(gate_w.shape[1] // 256):
        cut = slice(j * 256, j * 256 + 256)
        gate_part = dot(hidden[...], gate_w[:, cut])
        up_part = dot(hidden[...], up_w[:, cut])
        gate[:, cut] = gate_part.astype(jnp.bfloat16)
        up[:, cut] = up_part.astype(jnp.bfloat16)
        sigmoid = 1.0 / (1.0 + jnp.exp(-gate_part))
        m[:, cut] = (gate_part * sigmoid * up_part).astype(jnp.bfloat16)


def ffn_slopes_kernel(grad, gate, up, down_w, early, slopes):
    units = down_w.shape[1]
    for j in range(units // 256):
        cut = slice(j * 256, j * 256 + 256)
        grad_part = dot(grad[...], down_w[:, cut])
        gate_part = gate[:, cut].astype(jnp.float32)
        up_part = up[:, cut].astype(jnp.float32)
        sigmoid = 1.0 / (1.0 + jnp.exp(-gate_part))
        slope = sigmoid * (1.0 + gate_part * (1.0 - sigmoid))
        slopes[:, cut] = (grad_part * up_part * slope).astype(jnp.bfloat16)
        slopes[:, units + j * 256 : units + j * 256 + 256] = (
            grad_part * gate_part * sigmoid
        ).astype(jnp.bfloat16)


def first_rows_kernel(
    values, gain, weight, up, down, hidden, raw, up_out, down_out, sent, landed, local
):
    step, last = pl.program_id(0), pl.num_programs(0) - 1

    def exchanges(act):
        for i, (source, target) in enumerate(((up, up_out), (down, down_out))):
            act(i, source, target)

    @pl.when(step == 0)
    def start():
        p = Plane(sent, landed, diagonal=True)
        exchanges(lambda i, source, target: Exchange(p, source, target, local.at[i]))

    value = values[...].astype(jnp.float32)
    normed = (value * row_root(value) * gain[...]).astype(jnp.bfloat16)
    hidden[...] = normed
    raw[...] = dot(normed, weight[...])

    @pl.when(step == last)
    def finish():
        p = Plane(sent, landed, entered=True)
        columns = up_out.shape[2]
        for i, (source, target) in enumerate(((up, up_out), (down, down_out))):
            part = source.at[:, pl.ds(0, columns)]
            for j, rank in enumerate((p.at_both, p.at_x, p.at_y)):
                move = p.copy(3 * i + j, part, target.at[rank], p.x)
                move.wait_recv()
                move.wait_send()
            own = source.at[:, pl.ds(pl.multiple_of(p.rank * columns, 128), columns)]
            pltpu.make_async_copy(own, target.at[p.rank], local.at[i]).wait()


def first_rows(values, gain, weight, up, down):
    count, width = values.shape
    columns = weight.shape[1]
    depth, units = up.shape
    moved = jax.ShapeDtypeStruct((4, depth, units // 4), up.dtype)
    return pl.pallas_call(
        first_rows_kernel,
        grid=(count // ROW_TILE,),
        in_specs=[
            pl.BlockSpec((ROW_TILE, width), lambda i: (i, 0)),
            pl.BlockSpec((1, width), lambda i: (0, 0)),
            pl.BlockSpec((width, columns), lambda i: (0, 0)),
            ANY,
            ANY,
        ],
        out_specs=[
            pl.BlockSpec((ROW_TILE, width), lambda i: (i, 0)),
            pl.BlockSpec((ROW_TILE, columns), lambda i: (i, 0)),
            ANY,
            ANY,
        ],
        out_shape=[
            jax.ShapeDtypeStruct((count, width), jnp.bfloat16),
            jax.ShapeDtypeStruct((count, columns), jnp.float32),
            moved,
            moved,
        ],
        scratch_shapes=wires(6) + [pltpu.SemaphoreType.DMA((2,))],
        compiler_params=pltpu.CompilerParams(
            collective_id=6, has_side_effects=True, vmem_limit_bytes=VMEM_LIMIT
        ),
        cost_estimate=lasting(25),
        name="first_rows",
    )(values, gain, weight, up, down)


def attention_weights_kernel(hidden, back, grad, attended, weight, moving, *rest):
    out, rows_out, moved, sent, landed, local = rest[-6:]
    step, last = pl.program_id(0), pl.num_programs(0) - 1

    @pl.when(step == 0)
    def start():
        p = Plane(sent, landed, diagonal=True)
        pltpu.make_async_copy(moving.at[p.rank], moved.at[p.rank], local).start()
        for partner, rank in ((p.both, p.at_both), (p.x, p.at_x), (p.y, p.at_y)):
            p.send(moving.at[rank], moved.at[p.rank], partner)

    columns = back.shape[1]
    out[:, :columns] = dot(hidden[...], back[...], FIRST).astype(jnp.bfloat16)
    out[:, columns:] = dot(grad[...], attended[...], FIRST).astype(jnp.bfloat16)
    rows_out[...] = dot(back[...], weight[...], LAST).astype(jnp.bfloat16)

    @pl.when(step == last)
    def finish():
        p = Plane(sent, landed, entered=True)
        for number, rank in enumerate((p.at_both, p.at_x, p.at_y)):
            move = p.copy(number, moving.at[rank], moved.at[rank], p.x)
            move.wait_recv()
            move.wait_send()
        pltpu.make_async_copy(moving.at[p.rank], moved.at[p.rank], local).wait()


def attention_weights(hidden, back, grad, attended, weight, moving, early):
    count, width = hidden.shape
    first, second = back.shape[1], attended.shape[1]
    tall = pl.BlockSpec((count, 256), lambda i: (0, i))
    return pl.pallas_call(
        attention_weights_kernel,
        grid=(width // 256,),
        in_specs=[
            tall,
            pl.BlockSpec((count, first), lambda i: (0, 0)),
            tall,
            pl.BlockSpec((count, second), lambda i: (0, 0)),
            pl.BlockSpec((256, first), lambda i: (i, 0)),
        ]
        + [ANY] * (1 + len(early)),
        out_specs=[pl.BlockSpec((256, first + second), lambda i: (i, 0)), tall, ANY],
        out_shape=[
            jax.ShapeDtypeStruct((width, first + second), jnp.bfloat16),
            jax.ShapeDtypeStruct((count, width), jnp.bfloat16),
            jax.ShapeDtypeStruct(moving.shape, moving.dtype),
        ],
        scratch_shapes=wires(3) + [pltpu.SemaphoreType.DMA],
        compiler_params=pltpu.CompilerParams(
            collective_id=8, has_side_effects=True, vmem_limit_bytes=VMEM_LIMIT
        ),
        cost_estimate=lasting(25),
        name="attention_weights",
    )(hidden, back, grad, attended, weight, moving, *early)


ROW_TILE = 256


def row_tiles(kernel, name, rows, weights, extra, widths):
    count = rows[0].shape[0]

    def tile(width):
        return pl.BlockSpec((ROW_TILE, width), lambda i: (i, 0))

    whole = [
        pl.BlockSpec(w.shape, lambda i: (0, 0), pipeline_mode=pl.Buffered(1)) for w in weights
    ]
    flops = 2 * count * sum(w.size for w in weights)
    return pl.pallas_call(
        kernel,
        grid=(count // ROW_TILE,),
        in_specs=[tile(r.shape[1]) for r in rows] + whole + [ANY] * len(extra),
        out_specs=[tile(width) for width in widths],
        out_shape=[jax.ShapeDtypeStruct((count, width), jnp.bfloat16) for width in widths],
        compiler_params=pltpu.CompilerParams(vmem_limit_bytes=56 * 1024 * 1024),
        cost_estimate=pl.CostEstimate(flops=flops, bytes_accessed=flops // 400, transcendentals=0),
        name=name,
    )(*rows, *weights, *extra)


def norm_backward(gradient, normed, inv_root):
    return inv_root * (gradient - normed * jnp.mean(gradient * normed, axis=-1, keepdims=True))


def inverse_root(values):
    return lax.rsqrt(jnp.mean(values * values, axis=-1, keepdims=True) + epsilon)


PLANE = ("context", "tensor")


def gather_rows(values):
    return lax.all_gather(values, PLANE, axis=0, tiled=True)


def scatter_rows(partial):
    return lax.psum_scatter(
        partial.astype(jnp.bfloat16), PLANE, scatter_dimension=0, tiled=True
    ).astype(jnp.float32)


def local(
    tokens,
    cotangent,
    attn_gain,
    w_query,
    w_key,
    w_value,
    w_out,
    ffn_gain,
    w_gate,
    w_up,
    w_down,
    piece_segment,
    piece_parent,
    piece_start,
):
    groups = lax.axis_size("context")
    cores = lax.axis_size("tensor")
    depth = w_query.shape[0]
    kv_count = w_key.shape[1] // HEAD
    sharing = groups // kv_count
    share = tokens.shape[0] // cores
    first_row = lax.axis_index("tensor") * share

    def my_rows(values):
        return lax.dynamic_slice_in_dim(values, first_row, share, 0)

    def blocks(weight):
        return jnp.transpose(weight.reshape(depth, groups, -1), (1, 0, 2))

    def kv_blocks(weight):
        return jnp.repeat(jnp.transpose(weight.reshape(depth, kv_count, HEAD), (1, 0, 2)), sharing, 0)

    def spread(weight_blocks):
        mine = lax.all_to_all(weight_blocks, "context", 0, 0)
        mine = mine.reshape(groups * depth, -1)
        return lax.all_gather(mine, "fsdp", axis=0, tiled=True)

    gains = jnp.stack([attn_gain, ffn_gain], axis=1)
    gains = jnp.broadcast_to(jnp.pad(gains, ((0, 0), (0, 126))), (groups, depth, 128))
    my_packed = jnp.concatenate(
        [blocks(w_query), kv_blocks(w_key), kv_blocks(w_value), blocks(w_out.T), gains], axis=2
    )
    packed = spread(my_packed)
    width = w_query.shape[1] // groups
    qkv_full = packed[:, : width + 2 * HEAD]
    out_full = packed[:, width + 2 * HEAD : 2 * width + 2 * HEAD]
    gains_full = packed[:, 2 * width + 2 * HEAD :].astype(jnp.float32)
    attn_scale, ffn_scale = gains_full[:, 0], gains_full[:, 1]
    square = groups == 4 and cores == 2
    tokens_half, cotangent_half = my_rows(tokens), my_rows(cotangent)
    tables = rope_tables()

    def over_groups(blocks_here):
        return lax.all_gather(
            blocks_here.reshape(groups * depth, -1), "fsdp", axis=0, tiled=True
        )

    down_turned = w_down.T
    if square:
        inputs_full, gate_blocks, ffn_grad, my_ffn_grad = start_plane(
            tokens_half, w_gate, cotangent
        )
        gate_full = over_groups(gate_blocks)
        hidden_first, raw, up_blocks, down_blocks = first_rows(
            inputs_full.reshape(-1, inputs_full.shape[3]),
            attn_scale[None, :],
            qkv_full,
            w_up,
            down_turned,
        )
        up_full, down_full = over_groups(up_blocks), over_groups(down_blocks)
    else:
        gate_full, up_full, down_full = (
            spread(blocks(w)) for w in (w_gate, w_up, down_turned)
        )
        inputs_full = gather_rows(tokens_half).astype(jnp.float32)
        hidden_first = inputs_full * inverse_root(inputs_full) * attn_scale
        hidden_first = hidden_first.astype(jnp.bfloat16)
        raw = dot(hidden_first, qkv_full)
        my_ffn_grad = (residual_scale * cotangent_half.astype(jnp.float32)).astype(jnp.bfloat16)

    segment, starts = piece_segment[0] % 13, piece_start[0]
    places = jnp.where(
        segment == 0,
        starts,
        jnp.where(
            segment <= BRANCHES,
            starts + (segment - 1) * SEG,
            starts + (segment - 1 - BRANCHES) * SEG + (BRANCHES - 1) * SEG,
        ),
    )

    residual_in = tokens_half.astype(jnp.float32)
    grad_result = cotangent_half.astype(jnp.float32)

    attended, *kept = attention_forward(places, starts, raw, tables)
    branch = dot(attended, out_full, LAST).astype(jnp.bfloat16)
    if square:
        ffn_grad_blocks = [
            lax.ppermute(my_ffn_grad, "context", context_pairs(step)) for step in (1, 2, 3)
        ]
        hidden_second, middle, ffn_grad = middle_plane(
            branch, tokens_half, ffn_scale[None, :], ffn_grad, ffn_grad_blocks
        )
    else:
        ffn_grad = gather_rows(my_ffn_grad)
        middle = residual_in + residual_scale * scatter_rows(branch)
        hidden_second = gather_rows((middle * inverse_root(middle) * ffn_scale).astype(jnp.bfloat16))

    units = gate_full.shape[1]
    hidden, gate_proj, up_proj = row_tiles(
        ffn_first_kernel,
        "ffn_first",
        [hidden_second],
        [gate_full, up_full],
        [],
        [units, units, units],
    )
    grad_down = dot(ffn_grad, hidden, FIRST).astype(jnp.bfloat16)
    (slopes,) = row_tiles(
        ffn_slopes_kernel,
        "ffn_slopes",
        [ffn_grad, gate_proj, up_proj],
        [down_full],
        [grad_down],
        [2 * units],
    )
    grad_gate_up = dot(hidden_second, slopes, FIRST).astype(jnp.bfloat16)

    def sum_groups(gradient):
        return lax.psum_scatter(gradient, "fsdp", scatter_dimension=0, tiled=True)

    def hand_back(gradient):
        return lax.all_to_all(gradient.reshape(groups, depth, -1), "context", 0, 0)

    def columns(gradient):
        return jnp.transpose(gradient, (1, 0, 2)).reshape(depth, -1).astype(jnp.float32)

    if square:
        grad_middle, my_attn_grad = second_plane(
            slopes, gate_full, up_full, middle, cotangent_half, ffn_scale[None, :], grad_gate_up
        )
        attn_grad, ffn_pairs = spread_plane(my_attn_grad, hidden, down_full)
        ffn_parts = [ffn_pairs[0]] + [
            lax.ppermute(ffn_pairs[step], "context", context_pairs(step)) for step in (1, 2, 3)
        ]
    else:
        root = inverse_root(middle)
        ffn_out = dot(hidden, down_full, LAST)
        grad_second = dot(slopes[:, :units], gate_full, LAST)
        grad_second += dot(slopes[:, units:], up_full, LAST)
        grad_middle = grad_result + norm_backward(
            scatter_rows(grad_second) * ffn_scale, middle * root, root
        )
        attn_grad = gather_rows((residual_scale * grad_middle).astype(jnp.bfloat16))
        ffn_parts = []
    grad_attended = dot(attn_grad, out_full).astype(jnp.bfloat16)
    grad_down = sum_groups(grad_down)
    grad_gate_up = sum_groups(grad_gate_up)
    back = attention_backward(places, starts, grad_attended, kept, tables, [grad_down])
    grad_down = hand_back(grad_down)
    if square:
        grad_attn, grad_first, grad_gate_up = attention_weights(
            hidden_first,
            back,
            attn_grad,
            attended,
            qkv_full,
            grad_gate_up.reshape(groups, depth, -1),
            [grad_down, *ffn_parts[1:]],
        )
    else:
        grad_attn = jnp.concatenate(
            [dot(hidden_first, back, FIRST), dot(attn_grad, attended, FIRST)], axis=1
        ).astype(jnp.bfloat16)
        grad_first = dot(back, qkv_full, LAST).astype(jnp.bfloat16)
        grad_gate_up = hand_back(grad_gate_up)
    grad_attn = sum_groups(grad_attn)
    if square:
        grad_tokens, result, ffn_sums = last_plane(
            grad_first,
            tokens_half,
            grad_middle,
            attn_scale[None, :],
            middle,
            ffn_parts,
            grad_gate_up,
            w_gate,
            w_up,
        )
        grad_attn, attn_sums = exchange(
            grad_attn.reshape(groups, depth, -1), my_packed, ffn_sums
        )
        my_gains = jnp.stack([attn_gain, ffn_gain]).astype(jnp.float32)
        query, pair, out, gate, up, down, grad_tokens, result, gain_grads = finish(
            grad_attn, grad_down, grad_gate_up, grad_tokens, result, attn_sums, ffn_sums, my_gains
        )
        key, value = jnp.moveaxis(pair.reshape(depth, groups, 2, HEAD), 2, 0)
        return (
            result,
            grad_tokens,
            gain_grads[0],
            query,
            key.reshape(depth, -1),
            value.reshape(depth, -1),
            out,
            gain_grads[1],
            gate,
            up,
            down,
        )
    else:
        root = inverse_root(residual_in)
        grad_tokens = grad_middle + norm_backward(
            scatter_rows(grad_first) * attn_scale, residual_in * root, root
        )
        grad_tokens = lax.all_gather(grad_tokens, "tensor", axis=0, tiled=True)
        result = (middle + residual_scale * scatter_rows(ffn_out)).astype(jnp.bfloat16)
        grad_attn = hand_back(grad_attn)
        result = lax.all_gather(result, "tensor", axis=0, tiled=True)
    def kv_columns(gradient):
        gradient = gradient.astype(jnp.float32).reshape(kv_count, sharing, depth, HEAD)
        return jnp.transpose(jnp.sum(gradient, axis=1), (1, 0, 2)).reshape(depth, -1)

    grad_query = columns(grad_attn[:, :, :width])
    grad_key = kv_columns(grad_attn[:, :, width : width + HEAD])
    grad_value = kv_columns(grad_attn[:, :, width + HEAD : width + 2 * HEAD])
    grad_gate, grad_up = columns(grad_gate_up[:, :, :units]), columns(grad_gate_up[:, :, units:])

    def against(*pairs):
        return sum(jnp.sum(weight.astype(jnp.float32) * g, axis=1) for weight, g in pairs)

    gain_grads = jnp.stack(
        [
            against((w_query, grad_query), (w_key, grad_key), (w_value, grad_value)),
            against((w_gate, grad_gate), (w_up, grad_up)),
        ]
    )
    gain_grads = lax.psum(gain_grads, "tensor")
    return (
        result,
        grad_tokens,
        gain_grads[0] / attn_gain.astype(jnp.float32),
        grad_query,
        grad_key,
        grad_value,
        columns(grad_attn[:, :, width + 2 * HEAD :]).T,
        gain_grads[1] / ffn_gain.astype(jnp.float32),
        grad_gate,
        grad_up,
        columns(grad_down).T,
    )


ROWS = ("fsdp", "context")


def solution(mesh):
    return jax.shard_map(
        local,
        mesh=mesh,
        in_specs=(
            P(ROWS, None),
            P(ROWS, None),
            P(ROWS),
            P(ROWS, "tensor"),
            P(ROWS, "tensor"),
            P(ROWS, "tensor"),
            P("tensor", ROWS),
            P(ROWS),
            P(ROWS, "tensor"),
            P(ROWS, "tensor"),
            P("tensor", ROWS),
            P("fsdp", None),
            P("fsdp", None),
            P("fsdp", None),
        ),
        out_specs=(
            P(ROWS, None),
            P(ROWS, None),
            P(ROWS),
            P(ROWS, "tensor"),
            P(ROWS, "tensor"),
            P(ROWS, "tensor"),
            P("tensor", ROWS),
            P(ROWS),
            P(ROWS, "tensor"),
            P(ROWS, "tensor"),
            P("tensor", ROWS),
        ),
        check_vma=False,
    )
```

```python
import functools

import jax
import jax.numpy as jnp
import numpy as np
from jax import lax
from jax.experimental import pallas as pl
from jax.experimental.pallas import tpu as pltpu
from jax.sharding import PartitionSpec as P

HEAD = 64
SEG = 128
TRUNK = 8 * SEG
BRANCHES = 4
LEAVES = 8
GROUP = TRUNK + (BRANCHES + LEAVES) * SEG
DEPTH = TRUNK + 2 * SEG
TILE = 2 * SEG

epsilon = 1e-05
rope_base = 10000000.0
residual_scale = 0.22
score_scale = 0.015625
masked_score = -1e30

FIRST = (((0,), (0,)), ((), ()))
LAST = (((1,), (1,)), ((), ()))
PLAIN = (((1,), (0,)), ((), ()))


def dot(left_side, right_side, dims=PLAIN):
    return lax.dot_general(left_side, right_side, dims, preferred_element_type=jnp.float32)


def rope_tables():
    steps = np.arange(HEAD // 2, dtype=np.float32)
    frequency = np.float32(rope_base) ** (-(steps * np.float32(2)) / np.float32(HEAD))
    angles = np.arange(DEPTH, dtype=np.float32)[:, None] * frequency.astype(np.float32)
    angles = angles.astype(np.float64)
    cosine, sine = np.cos(angles).astype(np.float32), np.sin(angles).astype(np.float32)
    return (
        jnp.asarray(np.concatenate([cosine] * 4, axis=-1)),
        jnp.asarray(np.concatenate([-sine, sine, -sine, sine], axis=-1)),
    )


def lanes(values):
    return lax.broadcasted_iota(jnp.int32, values.shape, 1)


def swap_halves(values):
    return jnp.where(
        lanes(values) % HEAD < HEAD // 2,
        pltpu.roll(values, 128 - HEAD // 2, 1),
        pltpu.roll(values, HEAD // 2, 1),
    )


def only_head(values, head):
    return jnp.where(lanes(values) // HEAD == head, values, jnp.zeros_like(values))


def query_tiles(work):
    for j in range(TRUNK // TILE):
        prefix = [(0, j * TILE, False)] if j else []
        work(j * TILE, prefix + [(j * TILE, TILE, True)], False)

    def branch(i, carry):
        row = pl.multiple_of(TRUNK + i * TILE, TILE)
        work(row, [(0, TRUNK, False), (row, TILE, True)], True)
        return carry

    lax.fori_loop(0, BRANCHES * SEG // TILE, branch, 0)

    def leaf(i, carry):
        row = pl.multiple_of(TRUNK + BRANCHES * SEG + i * TILE, TILE)
        parent = pl.multiple_of(TRUNK + i * SEG, SEG)
        work(row, [(0, TRUNK, False), (parent, SEG, False), (row, TILE, True)], True)
        return carry

    lax.fori_loop(0, LEAVES * SEG // TILE, leaf, 0)


def visible_scores(keys, query, own, one_segment):
    scores = dot(keys, query, LAST)
    if not own:
        return scores
    key_at = lax.broadcasted_iota(jnp.int32, scores.shape, 0)
    query_at = lax.broadcasted_iota(jnp.int32, scores.shape, 1)
    seen = key_at <= query_at
    if one_segment:
        seen = seen & (key_at // SEG == query_at // SEG)
    return jnp.where(seen, scores, masked_score)


def turned_over(target, source):
    for first in range(0, source.shape[0], TILE):
        block = source[first : first + TILE, :128].astype(jnp.float32)
        target[:, first : first + TILE] = jnp.transpose(block)[:HEAD].astype(jnp.bfloat16)


def head_pairs(width, work):
    together = min(PAIR, width // HEAD)

    def step(i, carry):
        work([i * together + j for j in range(together)])
        return carry

    lax.fori_loop(0, width // HEAD // together, step, 0)


PAIR = 2


def attention_forward_kernel(
    to_ref, start_ref, raw_ref, cos_ref, sin_ref, out_ref, q_ref, k_ref, v_ref, log_ref,
    held, values_ref, tile_ref,
):
    width = q_ref.shape[1]
    pieces = to_ref.shape[0]
    piece = raw_ref.shape[0] // pieces

    def place(p, carry):
        rows = pl.ds(pl.multiple_of(p * piece, piece), piece)
        to = pl.ds(pl.multiple_of(to_ref[p], piece), piece)
        at = pl.ds(pl.multiple_of(start_ref[p], piece), piece)
        cosine, sine = cos_ref[at, :], sin_ref[at, :]

        def turn(values):
            return values * cosine + swap_halves(values) * sine

        for g in range(width // 128):
            cut = slice(g * 128, g * 128 + 128)
            turned = turn(raw_ref[rows, cut]).astype(jnp.bfloat16)
            q_ref[to, cut] = turned * jnp.bfloat16(score_scale)
        pair = raw_ref[rows, width : width + 128]
        low = lanes(pair) < HEAD
        key = turn(pair)
        key = jnp.where(low, key, pltpu.roll(key, HEAD, 1)).astype(jnp.bfloat16)
        value = jnp.where(low, pltpu.roll(pair, HEAD, 1), pair).astype(jnp.bfloat16)
        for g in range(width // 128):
            cut = slice(g * 128, g * 128 + 128)
            k_ref[to, cut] = key
            v_ref[to, cut] = value
        return carry

    lax.fori_loop(0, pieces, place, 0)
    turned_over(values_ref, v_ref)

    def work(row, parts, one_segment):
        rows = pl.ds(row, TILE)

        def one_head(head):
            query = only_head(q_ref[rows, :], head)
            scores = [
                visible_scores(k_ref[pl.ds(first, count), :], query, own, one_segment)
                for first, count, own in parts
            ]
            largest = functools.reduce(
                jnp.maximum, [jnp.max(s, axis=0, keepdims=True) for s in scores]
            )
            exponent = [jnp.exp(s - largest) for s in scores]
            total = functools.reduce(
                jnp.add, [jnp.sum(e, axis=0, keepdims=True) for e in exponent]
            )
            result = functools.reduce(
                jnp.add,
                [
                    dot(values_ref[:, pl.ds(first, count)], e.astype(jnp.bfloat16))
                    for e, (first, count, own) in zip(exponent, parts)
                ],
            )
            log_ref[head, :, rows] = largest + jnp.log(total)
            tile_ref[pl.ds(pl.multiple_of(head * HEAD, HEAD), HEAD), :] = result * (1.0 / total)

        def heads(together):
            for head in together:
                one_head(head)

        head_pairs(width, heads)
        held[rows, :] = jnp.transpose(tile_ref[...]).astype(jnp.bfloat16)

    query_tiles(work)

    def back(p, carry):
        rows = pl.ds(pl.multiple_of(p * piece, piece), piece)
        to = pl.ds(pl.multiple_of(to_ref[p], piece), piece)
        out_ref[rows, :] = held[to, :]
        return carry

    lax.fori_loop(0, pieces, back, 0)


def attention_backward_kernel(
    to_ref,
    start_ref,
    grad_ref,
    q_ref,
    k_ref,
    v_ref,
    log_ref,
    cos_ref,
    sin_ref,
    *rest,
):
    out_ref, og_ref, dq_ref, dk_ref, dv_ref, keys_ref, tile_ref = rest[-7:]
    width = q_ref.shape[1]
    pieces = to_ref.shape[0]
    piece = grad_ref.shape[0] // pieces

    def place(p, carry):
        rows = pl.ds(pl.multiple_of(p * piece, piece), piece)
        to = pl.ds(pl.multiple_of(to_ref[p], piece), piece)
        og_ref[to, :] = grad_ref[rows, :]
        return carry

    lax.fori_loop(0, pieces, place, 0)
    turned_over(keys_ref, k_ref)
    dk_ref[...] = jnp.zeros_like(dk_ref)
    dv_ref[...] = jnp.zeros_like(dv_ref)

    def work(row, parts, one_segment):
        rows = pl.ds(row, TILE)

        def heads(together):
            queries, out_grads, all_weights, all_grads = [], [], [], []
            for head in together:
                query = only_head(q_ref[rows, :], head)
                out_grad = only_head(og_ref[rows, :], head)
                log_total = log_ref[head, :, rows]
                weights, products = [], []
                for first, count, own in parts:
                    keys = pl.ds(first, count)
                    scores = visible_scores(k_ref[keys, :], query, own, one_segment)
                    weights.append(jnp.exp(scores - log_total))
                    products.append(dot(v_ref[keys, :], out_grad, LAST))
                inner = functools.reduce(
                    jnp.add,
                    [jnp.sum(w * d, axis=0, keepdims=True) for w, d in zip(weights, products)],
                )
                grads = [
                    (w * (d - inner)).astype(jnp.bfloat16) for w, d in zip(weights, products)
                ]
                queries.append(query)
                out_grads.append(out_grad)
                all_weights.append([w.astype(jnp.bfloat16) for w in weights])
                all_grads.append(grads)
                tile_ref[pl.ds(pl.multiple_of(head * HEAD, HEAD), HEAD), :] = functools.reduce(
                    jnp.add,
                    [
                        dot(keys_ref[:, pl.ds(first, count)], g)
                        for (first, count, own), g in zip(parts, grads)
                    ],
                )
            query = jnp.concatenate(queries, axis=0)
            out_grad = jnp.concatenate(out_grads, axis=0)
            for i, (first, count, own) in enumerate(parts):
                keys = pl.ds(first, count)
                weights = jnp.concatenate([w[i] for w in all_weights], axis=1)
                grads = jnp.concatenate([g[i] for g in all_grads], axis=1)
                dv_ref[keys, :] += dot(weights, out_grad)
                dk_ref[keys, :] += dot(grads, query)

        head_pairs(width, heads)
        dq_ref[rows, :] = jnp.transpose(tile_ref[...])

    query_tiles(work)

    def back(p, carry):
        rows = pl.ds(pl.multiple_of(p * piece, piece), piece)
        to = pl.ds(pl.multiple_of(to_ref[p], piece), piece)
        at = pl.ds(pl.multiple_of(start_ref[p], piece), piece)
        cosine, sine = cos_ref[at, :], sin_ref[at, :]

        def turn_back(values):
            return values * cosine - swap_halves(values) * sine

        def over_heads(ref):
            total = functools.reduce(
                jnp.add, [ref[to, g * 128 : g * 128 + 128] for g in range(width // 128)]
            )
            return total + pltpu.roll(total, HEAD, 1)

        for g in range(width // 128):
            cut = slice(g * 128, g * 128 + 128)
            turned = turn_back(score_scale * dq_ref[to, cut])
            out_ref[rows, cut] = turned.astype(jnp.bfloat16)
        key = turn_back(over_heads(dk_ref))
        value = over_heads(dv_ref)
        pair = jnp.where(lanes(key) < HEAD, key, value)
        out_ref[rows, width : width + 128] = pair.astype(jnp.bfloat16)
        return carry

    lax.fori_loop(0, pieces, back, 0)


SMEM = pl.BlockSpec(memory_space=pltpu.SMEM)
VMEM = pl.BlockSpec(memory_space=pltpu.VMEM)
VMEM_LIMIT = 48 * 1024 * 1024


def attention_cost(width, products):
    flops = products * 2 * GROUP * (GROUP * 2 // 5) * width
    return pl.CostEstimate(
        flops=flops, bytes_accessed=16 * GROUP * width, transcendentals=GROUP * GROUP * width // 128
    )


def attention_forward(places, starts, raw, tables):
    width = raw.shape[1] - 2 * HEAD
    rows = raw.shape[0]
    kept = jax.ShapeDtypeStruct((rows, width), jnp.bfloat16)
    return pl.pallas_call(
        attention_forward_kernel,
        out_shape=[kept] * 4 + [jax.ShapeDtypeStruct((width // HEAD, 1, rows), jnp.float32)],
        in_specs=[SMEM, SMEM, VMEM, VMEM, VMEM],
        out_specs=[VMEM] * 5,
        scratch_shapes=[
            pltpu.VMEM((rows, width), jnp.bfloat16),
            pltpu.VMEM((HEAD, rows), jnp.bfloat16),
            pltpu.VMEM((width, TILE), jnp.float32),
        ],
        compiler_params=pltpu.CompilerParams(vmem_limit_bytes=VMEM_LIMIT),
        cost_estimate=attention_cost(width, 4),
        name="attention_forward",
    )(places, starts, raw, *tables)


def attention_backward(places, starts, out_grad, kept, tables, early):
    rows, width = out_grad.shape
    return pl.pallas_call(
        attention_backward_kernel,
        out_shape=jax.ShapeDtypeStruct((rows, width + 2 * HEAD), jnp.bfloat16),
        in_specs=[SMEM, SMEM] + [VMEM] * 7 + [ANY] * len(early),
        out_specs=VMEM,
        scratch_shapes=[
            pltpu.VMEM((rows, width), jnp.bfloat16),
            pltpu.VMEM((rows, width), jnp.float32),
            pltpu.VMEM((rows, width), jnp.float32),
            pltpu.VMEM((rows, width), jnp.float32),
            pltpu.VMEM((HEAD, rows), jnp.bfloat16),
            pltpu.VMEM((width, TILE), jnp.float32),
        ],
        compiler_params=pltpu.CompilerParams(vmem_limit_bytes=VMEM_LIMIT),
        cost_estimate=attention_cost(width, 10),
        name="attention_backward",
    )(places, starts, out_grad, *kept, *tables, *early)


MESH = pl.DeviceIdType.MESH
ANY = pl.BlockSpec(memory_space=pl.ANY)
CHUNKS = 4
SLAB = 16


def lasting(microseconds):
    return pl.CostEstimate(
        flops=0, bytes_accessed=int(microseconds * 3_000_000), transcendentals=0
    )


class Plane:
    def __init__(self, sent, landed, diagonal=False, entered=False):
        self.sent, self.landed = sent, landed
        self.copies = []
        self.rank = lax.axis_index("context")
        self.core = lax.axis_index("tensor")
        self.at_x = self.rank + 1 - 2 * lax.rem(self.rank, 2)
        self.at_y = lax.rem(self.rank + 2, 4)
        self.at_both = 3 - self.rank
        self.x = {"context": self.at_x}
        self.y = {"context": self.at_y}
        self.both = {"context": self.at_both}
        self.sibling = {"tensor": 1 - self.core}
        if entered:
            return
        barrier = pltpu.get_barrier_semaphore()
        partners = [self.x, self.y, self.sibling] + ([self.both] if diagonal else [])
        for partner in partners:
            pl.semaphore_signal(barrier, inc=1, device_id=partner, device_id_type=MESH)
        pl.semaphore_wait(barrier, len(partners))

    def copy(self, number, source, target, partner):
        return pltpu.make_async_remote_copy(
            src_ref=source,
            dst_ref=target,
            send_sem=self.sent.at[number],
            recv_sem=self.landed.at[number],
            device_id=partner,
            device_id_type=MESH,
        )

    def send(self, source, target, partner):
        number = len(self.copies)
        started = self.copy(number, source, target, partner)
        started.start()
        self.copies.append(started)
        return number

    def arrive(self, number, target):
        self.copy(number, target, target, self.sibling).wait_recv()

    def finish(self):
        for started in self.copies:
            started.wait_send()


def chunk(index, rows):
    return pl.ds(index * (rows // CHUNKS), rows // CHUNKS)


class Gather:
    def __init__(self, plane, block, out):
        self.plane, self.block, self.out = plane, block, out
        self.rows = block.shape[0]
        self.to_x, self.to_y, self.across, self.onward = {}, {}, {}, {}

    def start(self, k):
        p, cut = self.plane, chunk(k, self.rows)
        target = self.out.at[p.rank, p.core, cut]
        self.to_x[k] = p.send(self.block.at[cut], target, p.x)
        self.to_y[k] = p.send(self.block.at[cut], target, p.y)
        self.across[0, k] = p.send(self.block.at[cut], target, p.sibling)

    def forward_chunk(self, k):
        p, out = self.plane, self.out
        cut = chunk(k, self.rows)
        from_x, from_y = out.at[p.at_x, p.core, cut], out.at[p.at_y, p.core, cut]
        p.arrive(self.to_x[k], from_x)
        if k < CHUNKS // 2:
            self.onward[k] = p.send(from_x, from_x, p.y)
        self.across[1, k] = p.send(from_x, from_x, p.sibling)
        p.arrive(self.to_y[k], from_y)
        if k >= CHUNKS // 2:
            self.onward[k] = p.send(from_y, from_y, p.x)
        self.across[2, k] = p.send(from_y, from_y, p.sibling)

    def forward_far(self):
        p = self.plane
        for k in range(CHUNKS):
            far = self.out.at[p.at_both, p.core, chunk(k, self.rows)]
            p.arrive(self.onward[k], far)
            self.across[3, k] = p.send(far, far, p.sibling)

    def forward(self):
        for k in range(CHUNKS):
            self.forward_chunk(k)
        self.forward_far()

    def finish(self):
        p = self.plane
        for i, rank in enumerate((p.rank, p.at_x, p.at_y, p.at_both)):
            for k in range(CHUNKS):
                p.arrive(
                    self.across[i, k], self.out.at[rank, 1 - p.core, chunk(k, self.rows)]
                )


GATHER_COPIES = CHUNKS * 8


def add_rows(target, source, first, count):
    def step(i, carry):
        rows = pl.ds(first + i * SLAB, SLAB)
        target[rows, :] = (
            target[rows, :].astype(jnp.float32) + source[rows, :].astype(jnp.float32)
        ).astype(jnp.bfloat16)
        return carry

    lax.fori_loop(0, count // SLAB, step, 0)


class Scatter:
    def __init__(self, plane, partial, held, other, near_x, near_y, far_x, far_y, local):
        p = self.plane = plane
        rows = near_x.shape[0]
        half = rows // 2
        halves = top, low = pl.ds(0, half), pl.ds(half, half)
        order = (p.at_both, p.at_x, p.at_y, p.rank)
        across, kept = {}, []
        for i, h in ((0, 0), (0, 1), (1, 0), (2, 0), (1, 1), (2, 1), (3, 0), (3, 1)):
            source = partial.at[order[i], 1 - p.core, halves[h]]
            across[i, h] = p.send(source, other.at[i, halves[h]], p.sibling)
        for i in range(4):
            kept.append(
                pltpu.make_async_copy(partial.at[order[i], p.core], held.at[i], local.at[i])
            )
            kept[i].start()

        def pair(i, h):
            p.arrive(across[i, h], other.at[i, halves[h]])
            add_rows(held.at[i], other.at[i], h * half, half)

        kept[0].wait()
        pair(0, 0)
        first = p.send(held.at[0, top], far_x, p.x)
        pair(0, 1)
        second = p.send(held.at[0, low], far_y, p.y)
        kept[1].wait()
        pair(1, 0)
        third = p.send(held.at[1, top], near_x.at[top], p.x)
        kept[2].wait()
        pair(2, 0)
        p.arrive(first, far_x)
        add_rows(held.at[2], far_x, 0, half)
        fourth = p.send(held.at[2, top], near_y.at[top], p.y)
        pair(1, 1)
        p.arrive(second, far_y)

        def step(i, carry):
            rows, at = pl.ds(half + i * SLAB, SLAB), pl.ds(i * SLAB, SLAB)
            held[1, rows, :] = (
                held[1, rows, :].astype(jnp.float32) + far_y[at, :].astype(jnp.float32)
            ).astype(jnp.bfloat16)
            return carry

        lax.fori_loop(0, half // SLAB, step, 0)
        fifth = p.send(held.at[1, low], near_x.at[low], p.x)
        pair(2, 1)
        sixth = p.send(held.at[2, low], near_y.at[low], p.y)
        kept[3].wait()
        pair(3, 0)
        pair(3, 1)
        self.halves = halves
        self.from_x, self.from_y = (third, fifth), (fourth, sixth)
        self.parts = (held.at[3], near_x, near_y)

    def ready(self, h):
        _, near_x, near_y = self.parts
        self.plane.arrive(self.from_x[h], near_x.at[self.halves[h]])
        self.plane.arrive(self.from_y[h], near_y.at[self.halves[h]])

    def rows(self, rows):
        return sum(part[rows, :].astype(jnp.float32) for part in self.parts)


SCATTER_COPIES = 8 + 6


def scatter_scratch(share, width):
    kind = jnp.bfloat16
    return [
        pltpu.VMEM((4, share, width), kind),
        pltpu.VMEM((4, share, width), kind),
        pltpu.VMEM((share, width), kind),
        pltpu.VMEM((share, width), kind),
        pltpu.VMEM((share // 2, width), kind),
        pltpu.VMEM((share // 2, width), kind),
        pltpu.SemaphoreType.DMA((4,)),
    ]


def wires(count):
    return [pltpu.SemaphoreType.DMA((count,)), pltpu.SemaphoreType.DMA((count,))]


def row_root(values):
    return lax.rsqrt(jnp.mean(values * values, axis=-1, keepdims=True) + epsilon)


def slabs(first, count, work):
    def step(i, carry):
        work(pl.ds(first + i * SLAB, SLAB))
        return carry

    lax.fori_loop(0, count // SLAB, step, 0)


class Exchange:
    def __init__(self, plane, source, target, local, first=0, columns=None):
        p = plane
        columns = columns or target.shape[2]

        def part(rank):
            return source.at[:, pl.ds(pl.multiple_of(rank * columns, 128), columns)]

        def place(rank):
            return target.at[rank, :, pl.ds(first, columns)]

        self.plane, self.place, self.moves = p, place, []
        self.mine = pltpu.make_async_copy(part(p.rank), place(p.rank), local)
        self.mine.start()
        for partner, rank in ((p.both, p.at_both), (p.x, p.at_x), (p.y, p.at_y)):
            self.moves.append((p.send(part(rank), place(p.rank), partner), rank))

    def finish(self):
        for number, rank in self.moves:
            self.plane.arrive(number, self.place(rank))
        self.mine.wait()


def first_kernel(query, pair, out_turned, gains, packed, gains_out, sent, landed, local, far_sent, far_landed):
    groups = lax.axis_size("fsdp")
    group, rank = lax.axis_index("fsdp"), lax.axis_index("context")
    depth = gains.shape[1]
    others = [(i, j) for i in range(groups) for j in range(4) if i or j]

    def device(i, j):
        return {"fsdp": lax.rem(group + i, groups), "context": lax.rem(rank + j, 4)}

    def place(f, c):
        return gains_out.at[:, pl.ds(pl.multiple_of((f * 4 + c) * depth, 128), depth)]

    barrier = pltpu.get_barrier_semaphore()
    for i, j in others:
        pl.semaphore_signal(barrier, inc=1, device_id=device(i, j), device_id_type=MESH)
    pl.semaphore_wait(barrier, len(others))
    p = Plane(sent, landed, entered=True)
    width = query.shape[1] // 4
    exchanges = [
        Exchange(p, query, packed, local.at[0], 0, width),
        Exchange(p, pair, packed, local.at[1], width, 128),
        Exchange(p, out_turned, packed, local.at[2], width + 128, width),
    ]
    far = []
    for n, (i, j) in enumerate(others):
        far.append(
            pltpu.make_async_remote_copy(
                src_ref=gains,
                dst_ref=place(group, rank),
                send_sem=far_sent.at[n],
                recv_sem=far_landed.at[n],
                device_id=device(i, j),
                device_id_type=MESH,
            )
        )
        far[n].start()
    gains_out[:, pl.ds(pl.multiple_of((group * 4 + rank) * depth, 128), depth)] = gains[...]
    for started in far:
        started.wait()
    for exchange in exchanges:
        exchange.finish()
    p.finish()


def first_exchange(query, pair, out_turned, gains):
    depth, columns = query.shape
    groups = lax.axis_size("fsdp")
    far = groups * 4 - 1
    return pl.pallas_call(
        first_kernel,
        out_shape=[
            jax.ShapeDtypeStruct((4, depth, columns // 2 + 128), query.dtype),
            jax.ShapeDtypeStruct((8, groups * 4 * depth), jnp.float32),
        ],
        in_specs=[ANY, ANY, ANY, VMEM],
        out_specs=[ANY, VMEM],
        scratch_shapes=wires(9) + [pltpu.SemaphoreType.DMA((3,))] + wires(far),
        compiler_params=pltpu.CompilerParams(collective_id=9, has_side_effects=True),
        cost_estimate=lasting(10),
        name="first_exchange",
    )(query, pair, out_turned, gains)


def start_kernel(
    block, up, cotangent, early, out, up_out, scaled, sent, landed, local
):
    p = Plane(sent, landed, diagonal=True)
    gather = Gather(p, block, out)
    mine = pltpu.make_async_copy(block, out.at[p.rank, p.core], local.at[0])
    for k in range(CHUNKS):
        gather.start(k)
    exchanges = [Exchange(p, up, up_out, local.at[1])]
    mine.start()

    def scale(rows):
        value = residual_scale * cotangent[rows, :].astype(jnp.float32)
        scaled[rows, :] = value.astype(jnp.bfloat16)

    slabs(0, scaled.shape[0], scale)
    gather.forward()
    gather.finish()
    for exchange in exchanges:
        exchange.finish()
    p.finish()
    mine.wait()


def start_plane(block, up, cotangent, early):
    share, width = block.shape
    depth, units = up.shape
    return pl.pallas_call(
        start_kernel,
        out_shape=[
            jax.ShapeDtypeStruct((4, 2, share, width), block.dtype),
            jax.ShapeDtypeStruct((4, depth, units // 4), up.dtype),
            jax.ShapeDtypeStruct(cotangent.shape, jnp.bfloat16),
        ],
        in_specs=[VMEM, ANY, VMEM, ANY],
        out_specs=[ANY, ANY, VMEM],
        scratch_shapes=wires(GATHER_COPIES + 3) + [pltpu.SemaphoreType.DMA((2,))],
        compiler_params=pltpu.CompilerParams(
            collective_id=1, has_side_effects=True, vmem_limit_bytes=VMEM_LIMIT
        ),
        cost_estimate=lasting(60),
        name="gather_tokens",
    )(block, up, cotangent, early)


def columns_kernel(weight, early, out, sent, landed, local):
    p = Plane(sent, landed, diagonal=True)
    exchange = Exchange(p, weight, out, local)
    exchange.finish()
    p.finish()


def exchange_columns(weight, early):
    depth, units = weight.shape
    return pl.pallas_call(
        columns_kernel,
        out_shape=jax.ShapeDtypeStruct((4, depth, units // 4), weight.dtype),
        in_specs=[ANY, ANY],
        out_specs=ANY,
        scratch_shapes=wires(3) + [pltpu.SemaphoreType.DMA],
        compiler_params=pltpu.CompilerParams(collective_id=10, has_side_effects=True),
        cost_estimate=lasting(15),
        name="exchange_columns",
    )(weight, early)


def middle_kernel(
    partial,
    residual,
    gain,
    beside,
    from_x,
    from_y,
    from_both,
    out,
    middle,
    beside_out,
    sent,
    landed,
    local,
    hidden,
    held_beside,
    held_blocks,
    *scratch,
):
    p = Plane(sent, landed)
    blocks = ((from_x, p.at_x), (from_y, p.at_y), (from_both, p.at_both))
    loads = [pltpu.make_async_copy(beside, held_beside, local.at[0])]
    for i, (block, rank) in enumerate(blocks):
        loads.append(pltpu.make_async_copy(block, held_blocks.at[i], local.at[i + 1]))
    for started in loads:
        started.start()
    total = Scatter(p, partial, *scratch)
    kept, across = [], []
    loads[0].wait()
    kept.append(pltpu.make_async_copy(held_beside, beside_out.at[p.rank], local.at[0]))
    kept[0].start()
    for i, (block, rank) in enumerate(blocks):
        loads[i + 1].wait()
        place = beside_out.at[rank, p.core]
        kept.append(pltpu.make_async_copy(held_blocks.at[i], place, local.at[i + 1]))
        kept[i + 1].start()
        across.append(p.send(held_blocks.at[i], place, p.sibling))
    share = hidden.shape[0]
    gather = Gather(p, hidden, out)

    def work(rows):
        value = residual[rows, :].astype(jnp.float32) + residual_scale * total.rows(rows)
        middle[rows, :] = value
        hidden[rows, :] = (value * row_root(value) * gain[1:2, :]).astype(jnp.bfloat16)

    for k in range(CHUNKS):
        if k % (CHUNKS // 2) == 0:
            total.ready(k // (CHUNKS // 2))
        slabs(k * (share // CHUNKS), share // CHUNKS, work)
        gather.start(k)
    kept.append(pltpu.make_async_copy(hidden, out.at[p.rank, p.core], local.at[4]))
    kept[4].start()
    gather.forward()
    gather.finish()
    for number, rank in zip(across, (p.at_x, p.at_y, p.at_both)):
        p.arrive(number, beside_out.at[rank, 1 - p.core])
    p.finish()
    for started in kept:
        started.wait()


def middle_plane(partial, residual, gain, beside, blocks):
    share, width = residual.shape
    full = jax.ShapeDtypeStruct((4, 2, share, width), jnp.bfloat16)
    out, middle, beside_out = pl.pallas_call(
        middle_kernel,
        out_shape=[full, jax.ShapeDtypeStruct((share, width), jnp.float32), full],
        in_specs=[ANY, VMEM, VMEM] + [ANY] * 4,
        out_specs=[ANY, VMEM, ANY],
        scratch_shapes=wires(GATHER_COPIES + SCATTER_COPIES + 3)
        + [
            pltpu.SemaphoreType.DMA((5,)),
            pltpu.VMEM((share, width), jnp.bfloat16),
            pltpu.VMEM((2, share, width), jnp.bfloat16),
            pltpu.VMEM((3, share, width), jnp.bfloat16),
        ]
        + scatter_scratch(share, width),
        compiler_params=pltpu.CompilerParams(
            collective_id=2, has_side_effects=True, vmem_limit_bytes=VMEM_LIMIT
        ),
        cost_estimate=lasting(100),
        name="middle_rows",
    )(partial.reshape(full.shape), residual, gain, beside.reshape(2, share, width), *blocks)
    return out.reshape(8 * share, width), middle, beside_out.reshape(8 * share, width)


class WeightTiles:
    def __init__(self, rows, slopes, target, rows_in, tile_out, wires_in):
        self.rows, self.slopes, self.target = rows, slopes, target
        self.rows_in, self.tile_out, self.wires = rows_in, tile_out, wires_in
        self.count = rows.shape[1] // TILE
        self.load(0, 0).start()

    def load(self, d, slot):
        columns = pl.ds(pl.multiple_of(d * TILE, TILE), TILE)
        return pltpu.make_async_copy(
            self.rows.at[:, columns], self.rows_in.at[slot], self.wires.at[0, slot]
        )

    def store(self, d, slot):
        columns = pl.ds(pl.multiple_of(d * TILE, TILE), TILE)
        return pltpu.make_async_copy(
            self.tile_out.at[slot], self.target.at[columns], self.wires.at[1, slot]
        )

    def run(self, first, last):
        def step(d, carry):
            slot = lax.rem(d, 2)
            self.load(d, slot).wait()

            @pl.when(d < self.count - 1)
            def _():
                self.load(d + 1, 1 - slot).start()

            @pl.when(d >= 2)
            def _():
                self.store(d - 2, slot).wait()

            self.tile_out[slot] = dot(self.rows_in[slot], self.slopes[...], FIRST).astype(
                jnp.bfloat16
            )
            self.store(d, slot).start()
            return carry

        lax.fori_loop(first, last, step, 0)

    def finish(self):
        for d in (self.count - 2, self.count - 1):
            self.store(d, d % 2).wait()


def tile_scratch(count, units):
    return [
        pltpu.SemaphoreType.DMA((2, 2)),
        pltpu.VMEM((2, count, TILE), jnp.bfloat16),
        pltpu.VMEM((2, TILE, units), jnp.bfloat16),
    ]


UNITS = ((0, 0), (0, 1), (1, 0), (2, 0), (1, 1), (2, 1), (3, 0), (3, 1))


def second_kernel(
    slopes,
    normed_rows,
    gate_w,
    up_w,
    middle,
    cotangent,
    gain,
    early,
    grad_middle,
    hidden,
    weight_grads,
    sent,
    landed,
    loading,
    tile_wires,
    rows_in,
    tile_out,
    gate_in,
    up_in,
    given,
    held,
    other,
    near_x,
    near_y,
    far_x,
    far_y,
):
    p = Plane(sent, landed)
    share, width = near_x.shape
    half = share // 2
    order = (p.at_both, p.at_x, p.at_y, p.rank)
    top, low = halves = pl.ds(0, half), pl.ds(half, half)

    def places(u):
        i, h = UNITS[u]
        for core in (1 - p.core, p.core):
            row = (order[i] * 2 + core) * share + h * half
            yield pl.ds(pl.multiple_of(row, 32), half)

    units = gate_in.shape[1]

    def loads(u):
        for j, rows in enumerate(places(u)):
            for n, target in enumerate((gate_in, up_in)):
                yield pltpu.make_async_copy(
                    slopes.at[rows, pl.ds(n * units, units)],
                    target.at[rows],
                    loading.at[u, 2 * j + n],
                )

    def compute(u):
        i, h = UNITS[u]
        slot = u % 2
        gate_rows = jnp.concatenate([gate_in[rows, :] for rows in places(u)], axis=0)
        up_rows = jnp.concatenate([up_in[rows, :] for rows in places(u)], axis=0)
        for j in range(width // 1024):
            cut = slice(j * 1024, j * 1024 + 1024)
            back = dot(gate_rows, gate_w[cut, :], LAST) + dot(up_rows, up_w[cut, :], LAST)
            given[slot, :, cut] = back[:half].astype(jnp.bfloat16)
            held[i, halves[h], cut] = back[half:].astype(jnp.bfloat16)

    tiles = WeightTiles(normed_rows, gate_in, weight_grads, rows_in, tile_out, tile_wires)

    moves, across = {}, {}
    moves, across = {}, {}

    def settle(u):
        i, h = UNITS[u]
        p.arrive(across[u], other.at[i, halves[h]])
        add_rows(held.at[i], other.at[i], h * half, half)
        if u == 0:
            moves["far_x"] = p.send(held.at[0, top], far_x, p.x)
        elif u == 1:
            moves["far_y"] = p.send(held.at[0, low], far_y, p.y)
        elif u == 2:
            moves["x", 0] = p.send(held.at[1, top], near_x.at[top], p.x)
        elif u == 3:
            p.arrive(moves["far_x"], far_x)
            add_rows(held.at[2], far_x, 0, half)
            moves["y", 0] = p.send(held.at[2, top], near_y.at[top], p.y)
        elif u == 4:
            p.arrive(moves["far_y"], far_y)

            def step(k, carry):
                rows, at = pl.ds(half + k * SLAB, SLAB), pl.ds(k * SLAB, SLAB)
                held[1, rows, :] = (
                    held[1, rows, :].astype(jnp.float32) + far_y[at, :].astype(jnp.float32)
                ).astype(jnp.bfloat16)
                return carry

            lax.fori_loop(0, half // SLAB, step, 0)
            moves["x", 1] = p.send(held.at[1, low], near_x.at[low], p.x)
        elif u == 5:
            moves["y", 1] = p.send(held.at[2, low], near_y.at[low], p.y)

    for u in range(8):
        for started in loads(u):
            started.start()

    def unit(u):
        if u >= 2:
            p.copies[across[u - 2]].wait_send()
        compute(u)
        i, h = UNITS[u]
        across[u] = p.send(given.at[u % 2], other.at[i, halves[h]], p.sibling)

    def wait_loads(units_here):
        for u in units_here:
            for started in loads(u):
                started.wait()

    wait_loads((0,))
    unit(0)
    wait_loads((1,))
    unit(1)
    settle(0)
    wait_loads((2, 3))
    unit(2)
    settle(1)
    unit(3)
    settle(2)
    wait_loads((4, 5, 6, 7))
    unit(4)
    tiles.run(0, 2)
    settle(3)
    unit(5)
    settle(4)
    unit(6)
    settle(5)
    unit(7)
    settle(6)
    settle(7)
    tiles.run(2, tiles.count)

    def work(rows):
        value = middle[rows, :]
        root = row_root(value)
        normed = value * root
        total = sum(part[rows, :].astype(jnp.float32) for part in (held.at[3], near_x, near_y))
        slope = total * gain[1:2, :]
        mean = jnp.mean(slope * normed, axis=-1, keepdims=True)
        gradient = cotangent[rows, :].astype(jnp.float32) + root * (slope - normed * mean)
        grad_middle[rows, :] = gradient
        hidden[rows, :] = (residual_scale * gradient).astype(jnp.bfloat16)

    for h in range(2):
        p.arrive(moves["x", h], near_x.at[halves[h]])
        p.arrive(moves["y", h], near_y.at[halves[h]])
        slabs(h * half, half, work)
    for u in (6, 7):
        p.copies[across[u]].wait_send()
    tiles.finish()
    for number, started in enumerate(p.copies):
        if number not in across.values():
            started.wait_send()


def second_plane(slopes, normed_rows, gate_w, up_w, middle, cotangent, gain, early):
    share, width = middle.shape
    count, units = slopes.shape[0], slopes.shape[1] // 2
    kind = jnp.bfloat16
    half = share // 2
    quarter = pltpu.VMEM((4, share, width), kind)
    return pl.pallas_call(
        second_kernel,
        out_shape=[
            jax.ShapeDtypeStruct((share, width), jnp.float32),
            jax.ShapeDtypeStruct((share, width), kind),
            jax.ShapeDtypeStruct((width, units), kind),
        ],
        in_specs=[ANY, ANY] + [VMEM] * 5 + [ANY],
        out_specs=[VMEM, VMEM, ANY],
        scratch_shapes=wires(8 + 6)
        + [pltpu.SemaphoreType.DMA((8, 4))]
        + tile_scratch(count, units)
        + [
            pltpu.VMEM((count, units), kind),
            pltpu.VMEM((count, units), kind),
            pltpu.VMEM((2, half, width), kind),
            quarter,
            quarter,
            pltpu.VMEM((share, width), kind),
            pltpu.VMEM((share, width), kind),
            pltpu.VMEM((half, width), kind),
            pltpu.VMEM((half, width), kind),
        ],
        compiler_params=pltpu.CompilerParams(
            collective_id=3, has_side_effects=True, vmem_limit_bytes=60 * 1024 * 1024
        ),
        cost_estimate=lasting(60),
        name="second_rows",
    )(slopes, normed_rows, gate_w, up_w, middle, cotangent, gain, early)


def spread_kernel(
    hidden, m, down_w, normed_rows, slopes, early, out, pair_own, pair_x, pair_y, pair_both,
    weight_grads, sent, landed, local, loading, tile_wires, rows_in, tile_out, up_in,
    m_in, given, held, theirs,
):
    p = Plane(sent, landed)
    share, width = hidden.shape
    gather = Gather(p, hidden, out)
    for k in range(CHUNKS):
        gather.start(k)
    mine = pltpu.make_async_copy(hidden, out.at[p.rank, p.core], local.at[4])
    mine.start()
    order = (p.rank, p.at_x, p.at_y, p.at_both)
    halves = pl.ds(0, share), pl.ds(share, share)

    def loads(i):
        for j, core in enumerate((1 - p.core, p.core)):
            yield pltpu.make_async_copy(
                m.at[order[i], core], m_in.at[i % 2, halves[j]], loading.at[i % 2, j]
            )

    across = []
    units = up_in.shape[1]
    up_load = pltpu.make_async_copy(slopes.at[:, pl.ds(units, units)], up_in, local.at[5])
    up_load.start()
    for started in loads(0):
        started.start()
    tiles = WeightTiles(normed_rows, up_in, weight_grads, rows_in, tile_out, tile_wires)
    for i in range(4):
        for started in loads(i):
            started.wait()
        if i < 3:
            for started in loads(i + 1):
                started.start()

        def step(j, carry, i=i):
            cut = pl.ds(pl.multiple_of(j * 512, 512), 512)
            value = dot(m_in[i % 2], down_w[cut, :], LAST)
            given[i, :, cut] = value[:share].astype(jnp.bfloat16)
            held[i, :, cut] = value[share:].astype(jnp.bfloat16)
            return carry

        lax.fori_loop(0, width // 512, step, 0)
        across.append(p.send(given.at[i], theirs.at[i], p.sibling))
        if i == 0:
            up_load.wait()
        gather.forward_chunk(i)
        tiles.run(i, i + 1)
    kept = []
    for i in range(4):
        p.arrive(across[i], theirs.at[i])
        add_rows(held.at[i], theirs.at[i], 0, share)
        target = (pair_own, pair_x, pair_y, pair_both)[i]
        kept.append(pltpu.make_async_copy(held.at[i], target, local.at[i]))
        kept[i].start()
    gather.forward_far()
    tiles.run(4, tiles.count)
    tiles.finish()
    gather.finish()
    p.finish()
    mine.wait()
    for started in kept:
        started.wait()


def spread_plane(hidden, m, down_w, normed_rows, slopes, early):
    share, width = hidden.shape
    units = m.shape[1]
    full = jax.ShapeDtypeStruct((4, 2, share, width), jnp.bfloat16)
    quarter = pltpu.VMEM((4, share, width), jnp.bfloat16)
    out, *pairs, weight_grads = pl.pallas_call(
        spread_kernel,
        out_shape=[full]
        + [jax.ShapeDtypeStruct((share, width), jnp.bfloat16)] * 4
        + [jax.ShapeDtypeStruct((width, units), jnp.bfloat16)],
        in_specs=[VMEM, ANY, VMEM, ANY, ANY, ANY],
        out_specs=[ANY] * 6,
        scratch_shapes=wires(GATHER_COPIES + 4)
        + [
            pltpu.SemaphoreType.DMA((6,)),
            pltpu.SemaphoreType.DMA((2, 2)),
        ]
        + tile_scratch(8 * share, units)
        + [
            pltpu.VMEM((8 * share, units), jnp.bfloat16),
            pltpu.VMEM((2, 2 * share, units), jnp.bfloat16),
            quarter,
            quarter,
            quarter,
        ],
        compiler_params=pltpu.CompilerParams(
            collective_id=7, has_side_effects=True, vmem_limit_bytes=60 * 1024 * 1024
        ),
        cost_estimate=lasting(60),
        name="spread_rows",
    )(hidden, m.reshape(4, 2, share, units), down_w, normed_rows, slopes, early)
    return out.reshape(8 * share, width), pairs, weight_grads


def lane_sums(pairs):
    total = 0.0
    for a, b in pairs:
        product = a.astype(jnp.float32) * b.astype(jnp.float32)
        total += jnp.sum(product, axis=1, keepdims=True)
    return jnp.broadcast_to(total, (total.shape[0], 128))


def last_kernel(
    partial,
    residual,
    grad_middle,
    gain,
    middle,
    ffn_own,
    ffn_x,
    ffn_y,
    ffn_both,
    ups,
    gates,
    gate,
    up,
    out,
    result_out,
    up_out,
    gain_out,
    sent,
    landed,
    local,
    held,
    result,
    sums,
    *scratch,
):
    p = Plane(sent, landed, diagonal=True)
    moves = []
    for partner, rank in ((p.both, p.at_both), (p.x, p.at_x), (p.y, p.at_y)):
        moves.append((p.send(ups.at[rank], up_out.at[p.rank], partner), up_out.at[rank]))
    up_out[p.rank] = ups[p.rank]
    total = Scatter(p, partial, *scratch)
    share = held.shape[0]

    def finish_result(rows):
        parts = (ffn_own, ffn_x, ffn_y, ffn_both)
        ffn = sum(part[rows, :].astype(jnp.float32) for part in parts)
        result[rows, :] = (middle[rows, :] + residual_scale * ffn).astype(jnp.bfloat16)

    slabs(0, share, finish_result)
    kept = [pltpu.make_async_copy(result, result_out.at[p.core], local.at[0])]
    kept[0].start()
    given = p.send(result, result_out.at[p.core], p.sibling)
    units = gate.shape[1] // 4

    def gain_rows(rows):
        pairs = []
        for c in range(4):
            columns = slice(c * units, c * units + units)
            pairs.append((gates[c, rows, :], gate[rows, columns]))
            pairs.append((up_out[c, rows, :], up[rows, columns]))
        sums[0, rows, :] = lane_sums(pairs)

    for number, target in moves:
        p.arrive(number, target)
    slabs(0, gate.shape[0], gain_rows)
    swapped = p.send(sums.at[0], sums.at[1], p.sibling)

    def work(rows):
        value = residual[rows, :].astype(jnp.float32)
        root = row_root(value)
        normed = value * root
        slope = total.rows(rows) * gain[0:1, :]
        mean = jnp.mean(slope * normed, axis=-1, keepdims=True)
        held[rows, :] = grad_middle[rows, :] + root * (slope - normed * mean)

    across = []
    for k in range(CHUNKS):
        cut = chunk(k, share)
        if k % (CHUNKS // 2) == 0:
            total.ready(k // (CHUNKS // 2))
        slabs(k * (share // CHUNKS), share // CHUNKS, work)
        across.append(p.send(held.at[cut], out.at[p.core, cut], p.sibling))
    kept.append(pltpu.make_async_copy(held, out.at[p.core], local.at[1]))
    kept[1].start()
    p.arrive(swapped, sums.at[1])
    gain_out[...] = sums[0] + sums[1]
    p.arrive(given, result_out.at[1 - p.core])
    for k in range(CHUNKS):
        p.arrive(across[k], out.at[1 - p.core, chunk(k, share)])
    p.finish()
    for started in kept:
        started.wait()


def last_plane(
    partial, residual, grad_middle, gain, middle, ffn_parts, ups, gates, gate, up
):
    share, width = residual.shape
    out, result_out, up_out, gain_out = pl.pallas_call(
        last_kernel,
        out_shape=[
            jax.ShapeDtypeStruct((2, share, width), jnp.float32),
            jax.ShapeDtypeStruct((2, share, width), jnp.bfloat16),
            jax.ShapeDtypeStruct(ups.shape, ups.dtype),
            jax.ShapeDtypeStruct((gate.shape[0], 128), jnp.float32),
        ],
        in_specs=[ANY] + [VMEM] * 12,
        out_specs=[ANY, ANY, VMEM, VMEM],
        scratch_shapes=wires(CHUNKS + 5 + SCATTER_COPIES)
        + [
            pltpu.SemaphoreType.DMA((2,)),
            pltpu.VMEM((share, width), jnp.float32),
            pltpu.VMEM((share, width), jnp.bfloat16),
            pltpu.VMEM((2, gate.shape[0], 128), jnp.float32),
        ]
        + scatter_scratch(share, width),
        compiler_params=pltpu.CompilerParams(
            collective_id=4, has_side_effects=True, vmem_limit_bytes=VMEM_LIMIT
        ),
        cost_estimate=lasting(70),
        name="last_rows",
    )(
        partial.reshape(4, 2, share, width),
        residual,
        grad_middle,
        gain,
        middle,
        *ffn_parts,
        ups,
        gates,
        gate,
        up,
    )
    return (
        out.reshape(2 * share, width),
        result_out.reshape(2 * share, width),
        up_out,
        gain_out,
    )


def exchange_kernel(blocks, query, pair, other_sums, out, gain_out, sent, landed, sums):
    p = Plane(sent, landed, diagonal=True)
    moves = []
    for partner, rank in ((p.both, p.at_both), (p.x, p.at_x), (p.y, p.at_y)):
        moves.append((p.send(blocks.at[rank], out.at[p.rank], partner), out.at[rank]))
    out[p.rank] = blocks[p.rank]
    width = query.shape[1] // 4

    def attention_rows(rows):
        pairs = []
        for c in range(4):
            pairs.append((out[c, rows, :width], query[rows, c * width : c * width + width]))
            pairs.append((out[c, rows, width : width + 128], pair[rows, c * 128 : c * 128 + 128]))
        sums[0, rows, :] = lane_sums(pairs)

    for number, target in moves:
        p.arrive(number, target)
    slabs(0, blocks.shape[1], attention_rows)
    swapped = p.send(sums.at[0], sums.at[1], p.sibling)
    p.arrive(swapped, sums.at[1])
    gain_out[0] = sums[0] + sums[1]
    gain_out[1] = other_sums[...]
    p.finish()


def exchange(blocks, query, pair, other_sums):
    depth = blocks.shape[1]
    return pl.pallas_call(
        exchange_kernel,
        out_shape=[
            jax.ShapeDtypeStruct(blocks.shape, blocks.dtype),
            jax.ShapeDtypeStruct((2, depth, 128), jnp.float32),
        ],
        in_specs=[VMEM] * 4,
        out_specs=[VMEM] * 2,
        scratch_shapes=wires(4) + [pltpu.VMEM((2, depth, 128), jnp.float32)],
        compiler_params=pltpu.CompilerParams(collective_id=5, has_side_effects=True),
        cost_estimate=lasting(8),
        name="exchange_blocks",
    )(blocks, query, pair, other_sums)


def finish_kernel(
    attn, down, gate, up, tokens, result, sums, gains,
    query_out, pair_out, out_out, gate_out, up_out, down_out, tokens_out, result_out, gain_out,
):
    width = query_out.shape[1]
    query_out[...] = attn[0, :, :width].astype(jnp.float32)
    pair_out[...] = attn[0, :, width : width + 128].astype(jnp.float32)
    out_out[...] = jnp.transpose(attn[0, :, width + 128 :].astype(jnp.float32))
    gate_out[...] = gate[0].astype(jnp.float32)
    up_out[...] = up[0].astype(jnp.float32)
    down_out[...] = jnp.transpose(down[0].astype(jnp.float32))
    tokens_out[...] = tokens[...]
    result_out[...] = result[...]
    for i in range(2):
        gain_out[i : i + 1, :] = jnp.transpose(sums[i])[0:1] / gains[i : i + 1, :]


def finish(attn, down, gate, up, tokens, result, sums, gains):
    groups, depth, units = down.shape
    width = attn.shape[2] // 2 - HEAD
    rows, columns = tokens.shape
    part = rows // groups

    def block(*shape):
        return pl.BlockSpec((1, *shape), lambda i: (i, 0, 0))

    def wide(count):
        return pl.BlockSpec((depth, count), lambda i: (0, i))

    def tall(count, other):
        return pl.BlockSpec((count, other), lambda i: (i, 0))

    def f32(*shape):
        return jax.ShapeDtypeStruct(shape, jnp.float32)

    return pl.pallas_call(
        finish_kernel,
        grid=(groups,),
        in_specs=[
            block(depth, attn.shape[2]),
            block(depth, units),
            block(depth, units),
            block(depth, units),
            tall(part, columns),
            tall(part, columns),
            pl.BlockSpec(sums.shape, lambda i: (0, 0, 0)),
            pl.BlockSpec(gains.shape, lambda i: (0, 0)),
        ],
        out_specs=[
            wide(width),
            wide(128),
            tall(width, depth),
            wide(units),
            wide(units),
            tall(units, depth),
            tall(part, columns),
            tall(part, columns),
            pl.BlockSpec((2, 128), lambda i: (0, 0)),
        ],
        out_shape=[
            f32(depth, groups * width),
            f32(depth, groups * 128),
            f32(groups * width, depth),
            f32(depth, groups * units),
            f32(depth, groups * units),
            f32(groups * units, depth),
            f32(rows, columns),
            jax.ShapeDtypeStruct(result.shape, result.dtype),
            f32(2, 128),
        ],
        compiler_params=pltpu.CompilerParams(vmem_limit_bytes=VMEM_LIMIT),
        cost_estimate=lasting(12),
        name="finish",
    )(attn, down, gate, up, tokens, result, sums, gains)


def context_pairs(step):
    return [(i, i ^ step) for i in range(4)]


def ffn_first_kernel(hidden, gate_w, up_w, m, gate, up):
    units = m.shape[1]
    for j in range(units // 256):
        cut = slice(j * 256, j * 256 + 256)
        gate_part = dot(hidden[...], gate_w[:, cut])
        up_part = dot(hidden[...], up_w[:, cut])
        gate[:, cut] = gate_part.astype(jnp.bfloat16)
        up[:, cut] = up_part.astype(jnp.bfloat16)
        sigmoid = 1.0 / (1.0 + jnp.exp(-gate_part))
        m[:, cut] = (gate_part * sigmoid * up_part).astype(jnp.bfloat16)


def ffn_slopes_kernel(grad, gate, up, down_w, early, slopes):
    units = down_w.shape[1]
    for j in range(units // 256):
        cut = slice(j * 256, j * 256 + 256)
        grad_part = dot(grad[...], down_w[:, cut])
        gate_part = gate[:, cut].astype(jnp.float32)
        up_part = up[:, cut].astype(jnp.float32)
        sigmoid = 1.0 / (1.0 + jnp.exp(-gate_part))
        slope = sigmoid * (1.0 + gate_part * (1.0 - sigmoid))
        slopes[:, cut] = (grad_part * up_part * slope).astype(jnp.bfloat16)
        slopes[:, units + j * 256 : units + j * 256 + 256] = (
            grad_part * gate_part * sigmoid
        ).astype(jnp.bfloat16)


def first_rows_kernel(
    values, gains, weight, cotangent, down, hidden, raw, scaled, down_out, sent, landed, local
):
    step, last = pl.program_id(0), pl.num_programs(0) - 1

    @pl.when(step == 0)
    def start():
        Exchange(Plane(sent, landed, diagonal=True), down, down_out, local)

    scaled[...] = (residual_scale * cotangent[...].astype(jnp.float32)).astype(jnp.bfloat16)
    value = values[...].astype(jnp.float32)
    normed = (value * row_root(value) * gains[0:1, :]).astype(jnp.bfloat16)
    hidden[...] = normed
    raw[...] = dot(normed, weight[...])

    @pl.when(step == last)
    def finish():
        p = Plane(sent, landed, entered=True)
        columns = down_out.shape[2]
        part = down.at[:, pl.ds(0, columns)]
        for j, rank in enumerate((p.at_both, p.at_x, p.at_y)):
            move = p.copy(j, part, down_out.at[rank], p.x)
            move.wait_recv()
            move.wait_send()
        own = down.at[:, pl.ds(pl.multiple_of(p.rank * columns, 128), columns)]
        pltpu.make_async_copy(own, down_out.at[p.rank], local).wait()


def first_rows(values, gains, packed, columns, cotangent, down):
    count, width = values.shape
    depth, units = down.shape
    steps = count // ROW_TILE
    part = pl.BlockSpec((cotangent.shape[0] // steps, width), lambda i: (i, 0))
    return pl.pallas_call(
        first_rows_kernel,
        grid=(steps,),
        in_specs=[
            pl.BlockSpec((ROW_TILE, width), lambda i: (i, 0)),
            pl.BlockSpec((8, width), lambda i: (0, 0)),
            pl.BlockSpec((width, columns), lambda i: (0, 0)),
            part,
            ANY,
        ],
        out_specs=[
            pl.BlockSpec((ROW_TILE, width), lambda i: (i, 0)),
            pl.BlockSpec((ROW_TILE, columns), lambda i: (i, 0)),
            part,
            ANY,
        ],
        out_shape=[
            jax.ShapeDtypeStruct((count, width), jnp.bfloat16),
            jax.ShapeDtypeStruct((count, columns), jnp.float32),
            jax.ShapeDtypeStruct(cotangent.shape, jnp.bfloat16),
            jax.ShapeDtypeStruct((4, depth, units // 4), down.dtype),
        ],
        scratch_shapes=wires(3) + [pltpu.SemaphoreType.DMA],
        compiler_params=pltpu.CompilerParams(
            collective_id=6, has_side_effects=True, vmem_limit_bytes=VMEM_LIMIT
        ),
        cost_estimate=lasting(25),
        name="first_rows",
    )(values, gains, packed, cotangent, down)


def attention_weights_kernel(hidden, back, grad, attended, weight, moving, *rest):
    out, rows_out, moved, sent, landed, local = rest[-6:]
    step, last = pl.program_id(0), pl.num_programs(0) - 1

    @pl.when(step == 0)
    def start():
        p = Plane(sent, landed, diagonal=True)
        pltpu.make_async_copy(moving.at[p.rank], moved.at[p.rank], local).start()
        for partner, rank in ((p.both, p.at_both), (p.x, p.at_x), (p.y, p.at_y)):
            p.send(moving.at[rank], moved.at[p.rank], partner)

    columns = back.shape[1]
    out[:, :columns] = dot(hidden[...], back[...], FIRST).astype(jnp.bfloat16)
    out[:, columns:] = dot(grad[...], attended[...], FIRST).astype(jnp.bfloat16)
    rows_out[...] = dot(back[...], weight[...], LAST).astype(jnp.bfloat16)

    @pl.when(step == last)
    def finish():
        p = Plane(sent, landed, entered=True)
        for number, rank in enumerate((p.at_both, p.at_x, p.at_y)):
            move = p.copy(number, moving.at[rank], moved.at[rank], p.x)
            move.wait_recv()
            move.wait_send()
        pltpu.make_async_copy(moving.at[p.rank], moved.at[p.rank], local).wait()


def attention_weights(hidden, back, grad, attended, weight, moving, early):
    count, width = hidden.shape
    first, second = back.shape[1], attended.shape[1]
    tall = pl.BlockSpec((count, 256), lambda i: (0, i))
    return pl.pallas_call(
        attention_weights_kernel,
        grid=(width // 256,),
        in_specs=[
            tall,
            pl.BlockSpec((count, first), lambda i: (0, 0)),
            tall,
            pl.BlockSpec((count, second), lambda i: (0, 0)),
            pl.BlockSpec((256, first), lambda i: (i, 0)),
        ]
        + [ANY] * (1 + len(early)),
        out_specs=[pl.BlockSpec((256, first + second), lambda i: (i, 0)), tall, ANY],
        out_shape=[
            jax.ShapeDtypeStruct((width, first + second), jnp.bfloat16),
            jax.ShapeDtypeStruct((count, width), jnp.bfloat16),
            jax.ShapeDtypeStruct(moving.shape, moving.dtype),
        ],
        scratch_shapes=wires(3) + [pltpu.SemaphoreType.DMA],
        compiler_params=pltpu.CompilerParams(
            collective_id=8, has_side_effects=True, vmem_limit_bytes=VMEM_LIMIT
        ),
        cost_estimate=lasting(25),
        name="attention_weights",
    )(hidden, back, grad, attended, weight, moving, *early)


ROW_TILE = 256


def row_tiles(kernel, name, rows, weights, extra, widths):
    count = rows[0].shape[0]

    def tile(width):
        return pl.BlockSpec((ROW_TILE, width), lambda i: (i, 0))

    whole = [
        pl.BlockSpec(w.shape, lambda i: (0, 0), pipeline_mode=pl.Buffered(1)) for w in weights
    ]
    flops = 2 * count * sum(w.size for w in weights)
    return pl.pallas_call(
        kernel,
        grid=(count // ROW_TILE,),
        in_specs=[tile(r.shape[1]) for r in rows] + whole + [ANY] * len(extra),
        out_specs=[tile(width) for width in widths],
        out_shape=[jax.ShapeDtypeStruct((count, width), jnp.bfloat16) for width in widths],
        compiler_params=pltpu.CompilerParams(vmem_limit_bytes=56 * 1024 * 1024),
        cost_estimate=pl.CostEstimate(flops=flops, bytes_accessed=flops // 400, transcendentals=0),
        name=name,
    )(*rows, *weights, *extra)


def norm_backward(gradient, normed, inv_root):
    return inv_root * (gradient - normed * jnp.mean(gradient * normed, axis=-1, keepdims=True))


def inverse_root(values):
    return lax.rsqrt(jnp.mean(values * values, axis=-1, keepdims=True) + epsilon)


PLANE = ("context", "tensor")


def gather_rows(values):
    return lax.all_gather(values, PLANE, axis=0, tiled=True)


def scatter_rows(partial):
    return lax.psum_scatter(
        partial.astype(jnp.bfloat16), PLANE, scatter_dimension=0, tiled=True
    ).astype(jnp.float32)


def local(
    tokens,
    cotangent,
    attn_gain,
    w_query,
    w_key,
    w_value,
    w_out,
    ffn_gain,
    w_gate,
    w_up,
    w_down,
    piece_segment,
    piece_parent,
    piece_start,
):
    groups = lax.axis_size("context")
    cores = lax.axis_size("tensor")
    depth = w_query.shape[0]
    kv_count = w_key.shape[1] // HEAD
    sharing = groups // kv_count
    share = tokens.shape[0] // cores
    first_row = lax.axis_index("tensor") * share

    def my_rows(values):
        return lax.dynamic_slice_in_dim(values, first_row, share, 0)

    def blocks(weight):
        return jnp.transpose(weight.reshape(depth, groups, -1), (1, 0, 2))

    def kv_blocks(weight):
        return jnp.repeat(jnp.transpose(weight.reshape(depth, kv_count, HEAD), (1, 0, 2)), sharing, 0)

    def spread(weight_blocks):
        mine = lax.all_to_all(weight_blocks, "context", 0, 0)
        mine = mine.reshape(groups * depth, -1)
        return lax.all_gather(mine, "fsdp", axis=0, tiled=True)

    square = groups == 4 and cores == 2
    width = w_query.shape[1] // groups
    columns_qkv = width + 2 * HEAD
    out_turned, down_turned = w_out.T, w_down.T
    tokens_half, cotangent_half = my_rows(tokens), my_rows(cotangent)

    def over_groups(blocks_here):
        return lax.all_gather(
            blocks_here.reshape(groups * depth, -1), "fsdp", axis=0, tiled=True
        )

    if square:
        gains = jnp.pad(jnp.stack([attn_gain, ffn_gain]).astype(jnp.float32), ((0, 6), (0, 0)))
        w_pair = jnp.stack(
            [w_key.reshape(depth, groups, HEAD), w_value.reshape(depth, groups, HEAD)], axis=2
        ).reshape(depth, -1)
        packed, gain_rows = first_exchange(w_query, w_pair, out_turned, gains)
        packed = over_groups(packed)
        gate_blocks = exchange_columns(w_gate, gain_rows)
        inputs_full, up_blocks, ffn_grad = start_plane(
            tokens_half, w_up, cotangent, gate_blocks
        )
        gate_full, up_full = over_groups(gate_blocks), over_groups(up_blocks)
        hidden_first, raw, my_ffn_grad, down_blocks = first_rows(
            inputs_full.reshape(-1, inputs_full.shape[3]),
            gain_rows,
            packed,
            columns_qkv,
            cotangent_half,
            down_turned,
        )
        down_full = over_groups(down_blocks)
        out_full = packed[:, columns_qkv:]
    else:
        gains = jnp.stack([attn_gain, ffn_gain], axis=1)
        gains = jnp.broadcast_to(jnp.pad(gains, ((0, 0), (0, 126))), (groups, depth, 128))
        packed = spread(
            jnp.concatenate(
                [
                    blocks(w_query),
                    kv_blocks(w_key),
                    kv_blocks(w_value),
                    blocks(out_turned),
                    gains,
                ],
                axis=2,
            )
        )
        qkv_full = packed[:, :columns_qkv]
        out_full = packed[:, columns_qkv : columns_qkv + width]
        gains_full = packed[:, columns_qkv + width :].astype(jnp.float32)
        attn_scale, ffn_scale = gains_full[:, 0], gains_full[:, 1]
        gate_full, up_full = spread(blocks(w_gate)), spread(blocks(w_up))
        down_full = spread(blocks(down_turned))
        inputs_full = gather_rows(tokens_half).astype(jnp.float32)
        hidden_first = inputs_full * inverse_root(inputs_full) * attn_scale
        hidden_first = hidden_first.astype(jnp.bfloat16)
        raw = dot(hidden_first, qkv_full)
        my_ffn_grad = (residual_scale * cotangent_half.astype(jnp.float32)).astype(jnp.bfloat16)
    tables = rope_tables()

    segment, starts = piece_segment[0] % 13, piece_start[0]
    places = jnp.where(
        segment == 0,
        starts,
        jnp.where(
            segment <= BRANCHES,
            starts + (segment - 1) * SEG,
            starts + (segment - 1 - BRANCHES) * SEG + (BRANCHES - 1) * SEG,
        ),
    )

    residual_in = tokens_half.astype(jnp.float32)
    grad_result = cotangent_half.astype(jnp.float32)

    attended, *kept = attention_forward(places, starts, raw, tables)
    branch = dot(attended, out_full, LAST).astype(jnp.bfloat16)
    if square:
        ffn_grad_blocks = [
            lax.ppermute(my_ffn_grad, "context", context_pairs(step)) for step in (1, 2, 3)
        ]
        hidden_second, middle, ffn_grad = middle_plane(
            branch, tokens_half, gain_rows, ffn_grad, ffn_grad_blocks
        )
    else:
        ffn_grad = gather_rows(my_ffn_grad)
        middle = residual_in + residual_scale * scatter_rows(branch)
        hidden_second = gather_rows((middle * inverse_root(middle) * ffn_scale).astype(jnp.bfloat16))

    units = down_full.shape[1]
    hidden, gate_proj, up_proj = row_tiles(
        ffn_first_kernel,
        "ffn_first",
        [hidden_second],
        [gate_full, up_full],
        [],
        [units, units, units],
    )
    grad_down = dot(ffn_grad, hidden, FIRST).astype(jnp.bfloat16)
    (slopes,) = row_tiles(
        ffn_slopes_kernel,
        "ffn_slopes",
        [ffn_grad, gate_proj, up_proj],
        [down_full],
        [grad_down],
        [2 * units],
    )
    def sum_groups(gradient):
        return lax.psum_scatter(gradient, "fsdp", scatter_dimension=0, tiled=True)

    def hand_back(gradient):
        return lax.all_to_all(gradient.reshape(groups, depth, -1), "context", 0, 0)

    def columns(gradient):
        return jnp.transpose(gradient, (1, 0, 2)).reshape(depth, -1).astype(jnp.float32)

    if square:
        grad_middle, my_attn_grad, grad_gate = second_plane(
            slopes,
            hidden_second,
            gate_full,
            up_full,
            middle,
            cotangent_half,
            gain_rows,
            grad_down,
        )
        attn_grad, ffn_pairs, grad_up = spread_plane(
            my_attn_grad, hidden, down_full, hidden_second, slopes, grad_gate
        )
        ffn_parts = [ffn_pairs[0]] + [
            lax.ppermute(ffn_pairs[step], "context", context_pairs(step)) for step in (1, 2, 3)
        ]
    else:
        root = inverse_root(middle)
        ffn_out = dot(hidden, down_full, LAST)
        grad_gate = dot(hidden_second, slopes[:, :units], FIRST).astype(jnp.bfloat16)
        grad_up = dot(hidden_second, slopes[:, units:], FIRST).astype(jnp.bfloat16)
        grad_second = dot(slopes[:, :units], gate_full, LAST)
        grad_second += dot(slopes[:, units:], up_full, LAST)
        grad_middle = grad_result + norm_backward(
            scatter_rows(grad_second) * ffn_scale, middle * root, root
        )
        attn_grad = gather_rows((residual_scale * grad_middle).astype(jnp.bfloat16))
        ffn_parts = []
    grad_attended = dot(attn_grad, out_full).astype(jnp.bfloat16)
    grad_down = sum_groups(grad_down)
    grad_gate, grad_up = sum_groups(grad_gate), sum_groups(grad_up)
    back = attention_backward(places, starts, grad_attended, kept, tables, [grad_down])
    grad_down = hand_back(grad_down)
    if square:
        grad_attn, grad_first, grad_gate = attention_weights(
            hidden_first,
            back,
            attn_grad,
            attended,
            packed,
            grad_gate.reshape(groups, depth, -1),
            [grad_down, *ffn_parts[1:]],
        )
    else:
        grad_attn = jnp.concatenate(
            [dot(hidden_first, back, FIRST), dot(attn_grad, attended, FIRST)], axis=1
        ).astype(jnp.bfloat16)
        grad_first = dot(back, qkv_full, LAST).astype(jnp.bfloat16)
        grad_gate, grad_up = hand_back(grad_gate), hand_back(grad_up)
    grad_attn = sum_groups(grad_attn)
    if square:
        grad_tokens, result, grad_up, ffn_sums = last_plane(
            grad_first,
            tokens_half,
            grad_middle,
            gain_rows,
            middle,
            ffn_parts,
            grad_up.reshape(groups, depth, -1),
            grad_gate,
            w_gate,
            w_up,
        )
        grad_attn, sums = exchange(
            grad_attn.reshape(groups, depth, -1), w_query, w_pair, ffn_sums
        )
        my_gains = jnp.stack([attn_gain, ffn_gain]).astype(jnp.float32)
        query, pair, out, gate, up, down, grad_tokens, result, gain_grads = finish(
            grad_attn, grad_down, grad_gate, grad_up, grad_tokens, result, sums, my_gains
        )
        key, value = jnp.moveaxis(pair.reshape(depth, groups, 2, HEAD), 2, 0)
        return (
            result,
            grad_tokens,
            gain_grads[0],
            query,
            key.reshape(depth, -1),
            value.reshape(depth, -1),
            out,
            gain_grads[1],
            gate,
            up,
            down,
        )
    else:
        root = inverse_root(residual_in)
        grad_tokens = grad_middle + norm_backward(
            scatter_rows(grad_first) * attn_scale, residual_in * root, root
        )
        grad_tokens = lax.all_gather(grad_tokens, "tensor", axis=0, tiled=True)
        result = (middle + residual_scale * scatter_rows(ffn_out)).astype(jnp.bfloat16)
        grad_attn = hand_back(grad_attn)
        result = lax.all_gather(result, "tensor", axis=0, tiled=True)
    def kv_columns(gradient):
        gradient = gradient.astype(jnp.float32).reshape(kv_count, sharing, depth, HEAD)
        return jnp.transpose(jnp.sum(gradient, axis=1), (1, 0, 2)).reshape(depth, -1)

    grad_query = columns(grad_attn[:, :, :width])
    grad_key = kv_columns(grad_attn[:, :, width : width + HEAD])
    grad_value = kv_columns(grad_attn[:, :, width + HEAD : width + 2 * HEAD])
    grad_gate, grad_up = columns(grad_gate), columns(grad_up)

    def against(*pairs):
        return sum(jnp.sum(weight.astype(jnp.float32) * g, axis=1) for weight, g in pairs)

    gain_grads = jnp.stack(
        [
            against((w_query, grad_query), (w_key, grad_key), (w_value, grad_value)),
            against((w_gate, grad_gate), (w_up, grad_up)),
        ]
    )
    gain_grads = lax.psum(gain_grads, "tensor")
    return (
        result,
        grad_tokens,
        gain_grads[0] / attn_gain.astype(jnp.float32),
        grad_query,
        grad_key,
        grad_value,
        columns(grad_attn[:, :, width + 2 * HEAD :]).T,
        gain_grads[1] / ffn_gain.astype(jnp.float32),
        grad_gate,
        grad_up,
        columns(grad_down).T,
    )


ROWS = ("fsdp", "context")


def solution(mesh):
    return jax.shard_map(
        local,
        mesh=mesh,
        in_specs=(
            P(ROWS, None),
            P(ROWS, None),
            P(ROWS),
            P(ROWS, "tensor"),
            P(ROWS, "tensor"),
            P(ROWS, "tensor"),
            P("tensor", ROWS),
            P(ROWS),
            P(ROWS, "tensor"),
            P(ROWS, "tensor"),
            P("tensor", ROWS),
            P("fsdp", None),
            P("fsdp", None),
            P("fsdp", None),
        ),
        out_specs=(
            P(ROWS, None),
            P(ROWS, None),
            P(ROWS),
            P(ROWS, "tensor"),
            P(ROWS, "tensor"),
            P(ROWS, "tensor"),
            P("tensor", ROWS),
            P(ROWS),
            P(ROWS, "tensor"),
            P(ROWS, "tensor"),
            P("tensor", ROWS),
        ),
        check_vma=False,
    )
```

```python
import functools

import jax
import jax.numpy as jnp
import numpy as np
from jax import lax
from jax.experimental import pallas as pl
from jax.experimental.pallas import tpu as pltpu
from jax.sharding import PartitionSpec as P

HEAD = 64
SEG = 128
TRUNK = 8 * SEG
BRANCHES = 4
LEAVES = 8
GROUP = TRUNK + (BRANCHES + LEAVES) * SEG
DEPTH = TRUNK + 2 * SEG
TILE = 2 * SEG

epsilon = 1e-05
rope_base = 10000000.0
residual_scale = 0.22
score_scale = 0.015625
masked_score = -1e30

FIRST = (((0,), (0,)), ((), ()))
LAST = (((1,), (1,)), ((), ()))
PLAIN = (((1,), (0,)), ((), ()))


def dot(left_side, right_side, dims=PLAIN):
    return lax.dot_general(left_side, right_side, dims, preferred_element_type=jnp.float32)


def rope_tables():
    steps = np.arange(HEAD // 2, dtype=np.float32)
    frequency = np.float32(rope_base) ** (-(steps * np.float32(2)) / np.float32(HEAD))
    angles = np.arange(DEPTH, dtype=np.float32)[:, None] * frequency.astype(np.float32)
    angles = angles.astype(np.float64)
    cosine, sine = np.cos(angles).astype(np.float32), np.sin(angles).astype(np.float32)
    return (
        jnp.asarray(np.concatenate([cosine] * 4, axis=-1)),
        jnp.asarray(np.concatenate([-sine, sine, -sine, sine], axis=-1)),
    )


def lanes(values):
    return lax.broadcasted_iota(jnp.int32, values.shape, 1)


def swap_halves(values):
    return jnp.where(
        lanes(values) % HEAD < HEAD // 2,
        pltpu.roll(values, 128 - HEAD // 2, 1),
        pltpu.roll(values, HEAD // 2, 1),
    )


def only_head(values, head):
    return jnp.where(lanes(values) // HEAD == head, values, jnp.zeros_like(values))


def query_tiles(work):
    for j in range(TRUNK // TILE):
        prefix = [(0, j * TILE, False)] if j else []
        work(j * TILE, prefix + [(j * TILE, TILE, True)], False)

    def branch(i, carry):
        row = pl.multiple_of(TRUNK + i * TILE, TILE)
        work(row, [(0, TRUNK, False), (row, TILE, True)], True)
        return carry

    lax.fori_loop(0, BRANCHES * SEG // TILE, branch, 0)

    def leaf(i, carry):
        row = pl.multiple_of(TRUNK + BRANCHES * SEG + i * TILE, TILE)
        parent = pl.multiple_of(TRUNK + i * SEG, SEG)
        work(row, [(0, TRUNK, False), (parent, SEG, False), (row, TILE, True)], True)
        return carry

    lax.fori_loop(0, LEAVES * SEG // TILE, leaf, 0)


def visible_scores(keys, query, own, one_segment):
    scores = dot(keys, query, LAST)
    if not own:
        return scores
    key_at = lax.broadcasted_iota(jnp.int32, scores.shape, 0)
    query_at = lax.broadcasted_iota(jnp.int32, scores.shape, 1)
    seen = key_at <= query_at
    if one_segment:
        seen = seen & (key_at // SEG == query_at // SEG)
    return jnp.where(seen, scores, masked_score)


def turned_over(target, source):
    for first in range(0, source.shape[0], TILE):
        block = source[first : first + TILE, :128].astype(jnp.float32)
        target[:, first : first + TILE] = jnp.transpose(block)[:HEAD].astype(jnp.bfloat16)


def head_pairs(width, work):
    together = min(PAIR, width // HEAD)

    def step(i, carry):
        work([i * together + j for j in range(together)])
        return carry

    lax.fori_loop(0, width // HEAD // together, step, 0)


PAIR = 2


def attention_forward_kernel(
    to_ref, start_ref, raw_ref, cos_ref, sin_ref, out_ref, q_ref, k_ref, v_ref, log_ref,
    held, values_ref, tile_ref,
):
    width = q_ref.shape[1]
    pieces = to_ref.shape[0]
    piece = raw_ref.shape[0] // pieces

    def place(p, carry):
        rows = pl.ds(pl.multiple_of(p * piece, piece), piece)
        to = pl.ds(pl.multiple_of(to_ref[p], piece), piece)
        at = pl.ds(pl.multiple_of(start_ref[p], piece), piece)
        cosine, sine = cos_ref[at, :], sin_ref[at, :]

        def turn(values):
            return values * cosine + swap_halves(values) * sine

        for g in range(width // 128):
            cut = slice(g * 128, g * 128 + 128)
            turned = turn(raw_ref[rows, cut]).astype(jnp.bfloat16)
            q_ref[to, cut] = turned * jnp.bfloat16(score_scale)
        pair = raw_ref[rows, width : width + 128]
        low = lanes(pair) < HEAD
        key = turn(pair)
        key = jnp.where(low, key, pltpu.roll(key, HEAD, 1)).astype(jnp.bfloat16)
        value = jnp.where(low, pltpu.roll(pair, HEAD, 1), pair).astype(jnp.bfloat16)
        for g in range(width // 128):
            cut = slice(g * 128, g * 128 + 128)
            k_ref[to, cut] = key
            v_ref[to, cut] = value
        return carry

    lax.fori_loop(0, pieces, place, 0)
    turned_over(values_ref, v_ref)

    def work(row, parts, one_segment):
        rows = pl.ds(row, TILE)

        def one_head(head):
            query = only_head(q_ref[rows, :], head)
            scores = [
                visible_scores(k_ref[pl.ds(first, count), :], query, own, one_segment)
                for first, count, own in parts
            ]
            largest = functools.reduce(
                jnp.maximum, [jnp.max(s, axis=0, keepdims=True) for s in scores]
            )
            exponent = [jnp.exp(s - largest) for s in scores]
            total = functools.reduce(
                jnp.add, [jnp.sum(e, axis=0, keepdims=True) for e in exponent]
            )
            result = functools.reduce(
                jnp.add,
                [
                    dot(values_ref[:, pl.ds(first, count)], e.astype(jnp.bfloat16))
                    for e, (first, count, own) in zip(exponent, parts)
                ],
            )
            log_ref[head, :, rows] = largest + jnp.log(total)
            tile_ref[pl.ds(pl.multiple_of(head * HEAD, HEAD), HEAD), :] = result * (1.0 / total)

        def heads(together):
            for head in together:
                one_head(head)

        head_pairs(width, heads)
        held[rows, :] = jnp.transpose(tile_ref[...]).astype(jnp.bfloat16)

    query_tiles(work)

    def back(p, carry):
        rows = pl.ds(pl.multiple_of(p * piece, piece), piece)
        to = pl.ds(pl.multiple_of(to_ref[p], piece), piece)
        out_ref[rows, :] = held[to, :]
        return carry

    lax.fori_loop(0, pieces, back, 0)


def attention_backward_kernel(
    to_ref,
    start_ref,
    grad_ref,
    q_ref,
    k_ref,
    v_ref,
    log_ref,
    cos_ref,
    sin_ref,
    *rest,
):
    out_ref, og_ref, dq_ref, dk_ref, dv_ref, keys_ref, tile_ref = rest[-7:]
    width = q_ref.shape[1]
    pieces = to_ref.shape[0]
    piece = grad_ref.shape[0] // pieces

    def place(p, carry):
        rows = pl.ds(pl.multiple_of(p * piece, piece), piece)
        to = pl.ds(pl.multiple_of(to_ref[p], piece), piece)
        og_ref[to, :] = grad_ref[rows, :]
        return carry

    lax.fori_loop(0, pieces, place, 0)
    turned_over(keys_ref, k_ref)
    dk_ref[...] = jnp.zeros_like(dk_ref)
    dv_ref[...] = jnp.zeros_like(dv_ref)

    def work(row, parts, one_segment):
        rows = pl.ds(row, TILE)

        def heads(together):
            queries, out_grads, all_weights, all_grads = [], [], [], []
            for head in together:
                query = only_head(q_ref[rows, :], head)
                out_grad = only_head(og_ref[rows, :], head)
                log_total = log_ref[head, :, rows]
                weights, products = [], []
                for first, count, own in parts:
                    keys = pl.ds(first, count)
                    scores = visible_scores(k_ref[keys, :], query, own, one_segment)
                    weights.append(jnp.exp(scores - log_total))
                    products.append(dot(v_ref[keys, :], out_grad, LAST))
                inner = functools.reduce(
                    jnp.add,
                    [jnp.sum(w * d, axis=0, keepdims=True) for w, d in zip(weights, products)],
                )
                grads = [
                    (w * (d - inner)).astype(jnp.bfloat16) for w, d in zip(weights, products)
                ]
                queries.append(query)
                out_grads.append(out_grad)
                all_weights.append([w.astype(jnp.bfloat16) for w in weights])
                all_grads.append(grads)
                tile_ref[pl.ds(pl.multiple_of(head * HEAD, HEAD), HEAD), :] = functools.reduce(
                    jnp.add,
                    [
                        dot(keys_ref[:, pl.ds(first, count)], g)
                        for (first, count, own), g in zip(parts, grads)
                    ],
                )
            query = jnp.concatenate(queries, axis=0)
            out_grad = jnp.concatenate(out_grads, axis=0)
            for i, (first, count, own) in enumerate(parts):
                keys = pl.ds(first, count)
                weights = jnp.concatenate([w[i] for w in all_weights], axis=1)
                grads = jnp.concatenate([g[i] for g in all_grads], axis=1)
                dv_ref[keys, :] += dot(weights, out_grad)
                dk_ref[keys, :] += dot(grads, query)

        head_pairs(width, heads)
        dq_ref[rows, :] = jnp.transpose(tile_ref[...])

    query_tiles(work)

    def back(p, carry):
        rows = pl.ds(pl.multiple_of(p * piece, piece), piece)
        to = pl.ds(pl.multiple_of(to_ref[p], piece), piece)
        at = pl.ds(pl.multiple_of(start_ref[p], piece), piece)
        cosine, sine = cos_ref[at, :], sin_ref[at, :]

        def turn_back(values):
            return values * cosine - swap_halves(values) * sine

        def over_heads(ref):
            total = functools.reduce(
                jnp.add, [ref[to, g * 128 : g * 128 + 128] for g in range(width // 128)]
            )
            return total + pltpu.roll(total, HEAD, 1)

        for g in range(width // 128):
            cut = slice(g * 128, g * 128 + 128)
            turned = turn_back(score_scale * dq_ref[to, cut])
            out_ref[rows, cut] = turned.astype(jnp.bfloat16)
        key = turn_back(over_heads(dk_ref))
        value = over_heads(dv_ref)
        pair = jnp.where(lanes(key) < HEAD, key, value)
        out_ref[rows, width : width + 128] = pair.astype(jnp.bfloat16)
        return carry

    lax.fori_loop(0, pieces, back, 0)


SMEM = pl.BlockSpec(memory_space=pltpu.SMEM)
VMEM = pl.BlockSpec(memory_space=pltpu.VMEM)
VMEM_LIMIT = 60 * 1024 * 1024


def attention_cost(width, products):
    flops = products * 2 * GROUP * (GROUP * 2 // 5) * width
    return pl.CostEstimate(
        flops=flops, bytes_accessed=16 * GROUP * width, transcendentals=GROUP * GROUP * width // 128
    )


def attention_forward(places, starts, raw, tables):
    width = raw.shape[1] - 2 * HEAD
    rows = raw.shape[0]
    kept = jax.ShapeDtypeStruct((rows, width), jnp.bfloat16)
    return pl.pallas_call(
        attention_forward_kernel,
        out_shape=[kept] * 4 + [jax.ShapeDtypeStruct((width // HEAD, 1, rows), jnp.float32)],
        in_specs=[SMEM, SMEM, VMEM, VMEM, VMEM],
        out_specs=[VMEM] * 5,
        scratch_shapes=[
            pltpu.VMEM((rows, width), jnp.bfloat16),
            pltpu.VMEM((HEAD, rows), jnp.bfloat16),
            pltpu.VMEM((width, TILE), jnp.float32),
        ],
        compiler_params=pltpu.CompilerParams(vmem_limit_bytes=VMEM_LIMIT),
        cost_estimate=attention_cost(width, 4),
        name="attention_forward",
    )(places, starts, raw, *tables)


def attention_backward(places, starts, out_grad, kept, tables, early):
    rows, width = out_grad.shape
    return pl.pallas_call(
        attention_backward_kernel,
        out_shape=jax.ShapeDtypeStruct((rows, width + 2 * HEAD), jnp.bfloat16),
        in_specs=[SMEM, SMEM] + [VMEM] * 7 + [ANY] * len(early),
        out_specs=VMEM,
        scratch_shapes=[
            pltpu.VMEM((rows, width), jnp.bfloat16),
            pltpu.VMEM((rows, width), jnp.float32),
            pltpu.VMEM((rows, width), jnp.float32),
            pltpu.VMEM((rows, width), jnp.float32),
            pltpu.VMEM((HEAD, rows), jnp.bfloat16),
            pltpu.VMEM((width, TILE), jnp.float32),
        ],
        compiler_params=pltpu.CompilerParams(vmem_limit_bytes=VMEM_LIMIT),
        cost_estimate=attention_cost(width, 10),
        name="attention_backward",
    )(places, starts, out_grad, *kept, *tables, *early)


MESH = pl.DeviceIdType.MESH
ANY = pl.BlockSpec(memory_space=pl.ANY)
CHUNKS = 4
SLAB = 16


def lasting(microseconds):
    return pl.CostEstimate(
        flops=0, bytes_accessed=int(microseconds * 3_000_000), transcendentals=0
    )


class Plane:
    def __init__(self, sent, landed, diagonal=False, entered=False):
        self.sent, self.landed = sent, landed
        self.copies = []
        self.rank = lax.axis_index("context")
        self.core = lax.axis_index("tensor")
        self.at_x = self.rank + 1 - 2 * lax.rem(self.rank, 2)
        self.at_y = lax.rem(self.rank + 2, 4)
        self.at_both = 3 - self.rank
        self.x = {"context": self.at_x}
        self.y = {"context": self.at_y}
        self.both = {"context": self.at_both}
        self.sibling = {"tensor": 1 - self.core}
        if entered:
            return
        barrier = pltpu.get_barrier_semaphore()
        partners = [self.x, self.y, self.sibling] + ([self.both] if diagonal else [])
        for partner in partners:
            pl.semaphore_signal(barrier, inc=1, device_id=partner, device_id_type=MESH)
        pl.semaphore_wait(barrier, len(partners))

    def copy(self, number, source, target, partner):
        return pltpu.make_async_remote_copy(
            src_ref=source,
            dst_ref=target,
            send_sem=self.sent.at[number],
            recv_sem=self.landed.at[number],
            device_id=partner,
            device_id_type=MESH,
        )

    def send(self, source, target, partner):
        number = len(self.copies)
        started = self.copy(number, source, target, partner)
        started.start()
        self.copies.append(started)
        return number

    def arrive(self, number, target):
        self.copy(number, target, target, self.sibling).wait_recv()

    def finish(self):
        for started in self.copies:
            started.wait_send()


def chunk(index, rows):
    return pl.ds(index * (rows // CHUNKS), rows // CHUNKS)


class Gather:
    def __init__(self, plane, block, out):
        self.plane, self.block, self.out = plane, block, out
        self.rows = block.shape[0]
        self.to_x, self.to_y, self.across, self.onward = {}, {}, {}, {}

    def start(self, k):
        p, cut = self.plane, chunk(k, self.rows)
        target = self.out.at[p.rank, p.core, cut]
        self.to_x[k] = p.send(self.block.at[cut], target, p.x)
        self.to_y[k] = p.send(self.block.at[cut], target, p.y)
        self.across[0, k] = p.send(self.block.at[cut], target, p.sibling)

    def forward_chunk(self, k):
        p, out = self.plane, self.out
        cut = chunk(k, self.rows)
        from_x, from_y = out.at[p.at_x, p.core, cut], out.at[p.at_y, p.core, cut]
        p.arrive(self.to_x[k], from_x)
        if k < CHUNKS // 2:
            self.onward[k] = p.send(from_x, from_x, p.y)
        self.across[1, k] = p.send(from_x, from_x, p.sibling)
        p.arrive(self.to_y[k], from_y)
        if k >= CHUNKS // 2:
            self.onward[k] = p.send(from_y, from_y, p.x)
        self.across[2, k] = p.send(from_y, from_y, p.sibling)

    def forward_far(self):
        p = self.plane
        for k in range(CHUNKS):
            far = self.out.at[p.at_both, p.core, chunk(k, self.rows)]
            p.arrive(self.onward[k], far)
            self.across[3, k] = p.send(far, far, p.sibling)

    def forward(self):
        for k in range(CHUNKS):
            self.forward_chunk(k)
        self.forward_far()

    def finish(self):
        p = self.plane
        for i, rank in enumerate((p.rank, p.at_x, p.at_y, p.at_both)):
            for k in range(CHUNKS):
                p.arrive(
                    self.across[i, k], self.out.at[rank, 1 - p.core, chunk(k, self.rows)]
                )


GATHER_COPIES = CHUNKS * 8


def add_rows(target, source, first, count):
    def step(i, carry):
        rows = pl.ds(first + i * SLAB, SLAB)
        target[rows, :] = (
            target[rows, :].astype(jnp.float32) + source[rows, :].astype(jnp.float32)
        ).astype(jnp.bfloat16)
        return carry

    lax.fori_loop(0, count // SLAB, step, 0)


class Scatter:
    def __init__(
        self, plane, rows_in, weights, columns, given, held, other, near_x, near_y, far_x, far_y
    ):
        p = self.plane = plane
        rows = near_x.shape[0]
        half = rows // 2
        halves = top, low = pl.ds(0, half), pl.ds(half, half)
        order = (p.at_both, p.at_x, p.at_y, p.rank)
        across = {}

        def make(i, h):
            for core, target in ((1 - p.core, given), (p.core, held)):
                value = dot(rows_in[order[i], core, halves[h], :], weights[:, columns], LAST)
                target[i, halves[h], :] = value.astype(jnp.bfloat16)
                if target is given:
                    source = given.at[i, halves[h]]
                    across[i, h] = p.send(source, other.at[i, halves[h]], p.sibling)

        def pair(i, h):
            p.arrive(across[i, h], other.at[i, halves[h]])
            add_rows(held.at[i], other.at[i], h * half, half)

        make(0, 0)
        make(0, 1)
        pair(0, 0)
        first = p.send(held.at[0, top], far_x, p.x)
        make(1, 0)
        pair(0, 1)
        second = p.send(held.at[0, low], far_y, p.y)
        make(2, 0)
        pair(1, 0)
        third = p.send(held.at[1, top], near_x.at[top], p.x)
        make(1, 1)
        make(2, 1)
        make(3, 0)
        make(3, 1)
        pair(2, 0)
        pair(1, 1)
        pair(2, 1)
        p.arrive(first, far_x)
        add_rows(held.at[2], far_x, 0, half)
        fourth = p.send(held.at[2, top], near_y.at[top], p.y)
        p.arrive(second, far_y)

        def step(i, carry):
            rows, at = pl.ds(half + i * SLAB, SLAB), pl.ds(i * SLAB, SLAB)
            held[1, rows, :] = (
                held[1, rows, :].astype(jnp.float32) + far_y[at, :].astype(jnp.float32)
            ).astype(jnp.bfloat16)
            return carry

        lax.fori_loop(0, half // SLAB, step, 0)
        fifth = p.send(held.at[1, low], near_x.at[low], p.x)
        sixth = p.send(held.at[2, low], near_y.at[low], p.y)
        pair(3, 0)
        pair(3, 1)
        self.halves = halves
        self.from_x, self.from_y = (third, fifth), (fourth, sixth)
        self.parts = (held.at[3], near_x, near_y)

    def ready(self, h):
        _, near_x, near_y = self.parts
        self.plane.arrive(self.from_x[h], near_x.at[self.halves[h]])
        self.plane.arrive(self.from_y[h], near_y.at[self.halves[h]])

    def rows(self, rows):
        return sum(part[rows, :].astype(jnp.float32) for part in self.parts)


SCATTER_COPIES = 8 + 6


def scatter_scratch(share, width):
    kind = jnp.bfloat16
    return [
        pltpu.VMEM((4, share, width), kind),
        pltpu.VMEM((4, share, width), kind),
        pltpu.VMEM((4, share, width), kind),
        pltpu.VMEM((share, width), kind),
        pltpu.VMEM((share, width), kind),
        pltpu.VMEM((share // 2, width), kind),
        pltpu.VMEM((share // 2, width), kind),
    ]


def wires(count):
    return [pltpu.SemaphoreType.DMA((count,)), pltpu.SemaphoreType.DMA((count,))]


def row_root(values):
    return lax.rsqrt(jnp.mean(values * values, axis=-1, keepdims=True) + epsilon)


def slabs(first, count, work):
    def step(i, carry):
        work(pl.ds(first + i * SLAB, SLAB))
        return carry

    lax.fori_loop(0, count // SLAB, step, 0)


class Exchange:
    def __init__(self, plane, source, target, local, first=0, columns=None):
        p = plane
        columns = columns or target.shape[2]

        def part(rank):
            return source.at[:, pl.ds(pl.multiple_of(rank * columns, 128), columns)]

        def place(rank):
            return target.at[rank, :, pl.ds(first, columns)]

        self.plane, self.place, self.moves = p, place, []
        self.mine = pltpu.make_async_copy(part(p.rank), place(p.rank), local)
        self.mine.start()
        for partner, rank in ((p.both, p.at_both), (p.x, p.at_x), (p.y, p.at_y)):
            self.moves.append((p.send(part(rank), place(p.rank), partner), rank))

    def finish(self):
        for number, rank in self.moves:
            self.plane.arrive(number, self.place(rank))
        self.mine.wait()


def first_kernel(query, pair, out_turned, gains, packed, gains_out, sent, landed, local, far_sent, far_landed):
    groups = lax.axis_size("fsdp")
    group, rank = lax.axis_index("fsdp"), lax.axis_index("context")
    depth = gains.shape[1]
    others = [(i, j) for i in range(groups) for j in range(4) if i or j]

    def device(i, j):
        return {"fsdp": lax.rem(group + i, groups), "context": lax.rem(rank + j, 4)}

    def place(f, c):
        return gains_out.at[:, pl.ds(pl.multiple_of((f * 4 + c) * depth, 128), depth)]

    barrier = pltpu.get_barrier_semaphore()
    for i, j in others:
        pl.semaphore_signal(barrier, inc=1, device_id=device(i, j), device_id_type=MESH)
    pl.semaphore_wait(barrier, len(others))
    p = Plane(sent, landed, entered=True)
    width = query.shape[1] // 4
    exchanges = [
        Exchange(p, query, packed, local.at[0], 0, width),
        Exchange(p, pair, packed, local.at[1], width, 128),
        Exchange(p, out_turned, packed, local.at[2], width + 128, width),
    ]
    far = []
    for n, (i, j) in enumerate(others):
        far.append(
            pltpu.make_async_remote_copy(
                src_ref=gains,
                dst_ref=place(group, rank),
                send_sem=far_sent.at[n],
                recv_sem=far_landed.at[n],
                device_id=device(i, j),
                device_id_type=MESH,
            )
        )
        far[n].start()
    gains_out[:, pl.ds(pl.multiple_of((group * 4 + rank) * depth, 128), depth)] = gains[...]
    for started in far:
        started.wait()
    for exchange in exchanges:
        exchange.finish()
    p.finish()


def first_exchange(query, pair, out_turned, gains):
    depth, columns = query.shape
    groups = lax.axis_size("fsdp")
    far = groups * 4 - 1
    return pl.pallas_call(
        first_kernel,
        out_shape=[
            jax.ShapeDtypeStruct((4, depth, columns // 2 + 128), query.dtype),
            jax.ShapeDtypeStruct((8, groups * 4 * depth), jnp.float32),
        ],
        in_specs=[ANY, ANY, ANY, VMEM],
        out_specs=[ANY, VMEM],
        scratch_shapes=wires(9) + [pltpu.SemaphoreType.DMA((3,))] + wires(far),
        compiler_params=pltpu.CompilerParams(collective_id=9, has_side_effects=True),
        cost_estimate=lasting(10),
        name="first_exchange",
    )(query, pair, out_turned, gains)


def start_kernel(block, cotangent, early, out, scaled, my_scaled, sent, landed, local):
    p = Plane(sent, landed)
    gather = Gather(p, block, out)
    mine = pltpu.make_async_copy(block, out.at[p.rank, p.core], local)
    for k in range(CHUNKS):
        gather.start(k)
    mine.start()
    share = block.shape[0]

    def scale(rows):
        value = residual_scale * cotangent[rows, :].astype(jnp.float32)
        scaled[rows, :] = value.astype(jnp.bfloat16)

    def keep(rows):
        from_rows = pl.ds(pl.multiple_of(p.core * share + rows.start, SLAB), SLAB)
        my_scaled[rows, :] = scaled[from_rows, :]

    slabs(0, scaled.shape[0], scale)
    slabs(0, share, keep)
    gather.forward()
    gather.finish()
    p.finish()
    mine.wait()


def start_plane(block, cotangent, early):
    share, width = block.shape
    return pl.pallas_call(
        start_kernel,
        out_shape=[
            jax.ShapeDtypeStruct((4, 2, share, width), block.dtype),
            jax.ShapeDtypeStruct(cotangent.shape, jnp.bfloat16),
            jax.ShapeDtypeStruct(block.shape, jnp.bfloat16),
        ],
        in_specs=[VMEM, VMEM, ANY],
        out_specs=[ANY, VMEM, VMEM],
        scratch_shapes=wires(GATHER_COPIES) + [pltpu.SemaphoreType.DMA],
        compiler_params=pltpu.CompilerParams(
            collective_id=1, has_side_effects=True, vmem_limit_bytes=VMEM_LIMIT
        ),
        cost_estimate=lasting(60),
        name="gather_tokens",
    )(block, cotangent, early)


def columns_kernel(gate, up, down, early, both_out, down_out, sent, landed, local):
    p = Plane(sent, landed, diagonal=True)
    units = down_out.shape[2]
    exchanges = [
        Exchange(p, gate, both_out, local.at[0], 0, units),
        Exchange(p, up, both_out, local.at[1], units, units),
        Exchange(p, down, down_out, local.at[2]),
    ]
    for exchange in exchanges:
        exchange.finish()
    p.finish()


def exchange_columns(gate, up, down, early):
    depth, units = gate.shape
    return pl.pallas_call(
        columns_kernel,
        out_shape=[
            jax.ShapeDtypeStruct((4, depth, units // 2), gate.dtype),
            jax.ShapeDtypeStruct((4, depth, units // 4), gate.dtype),
        ],
        in_specs=[ANY] * 4,
        out_specs=[ANY] * 2,
        scratch_shapes=wires(9) + [pltpu.SemaphoreType.DMA((3,))],
        compiler_params=pltpu.CompilerParams(collective_id=10, has_side_effects=True),
        cost_estimate=lasting(30),
        name="exchange_columns",
    )(gate, up, down, early)


def middle_kernel(
    attended,
    weights,
    residual,
    gain,
    beside,
    from_x,
    from_y,
    from_both,
    hidden,
    middle,
    beside_out,
    sent,
    landed,
    local,
    held_beside,
    held_blocks,
    *scratch,
):
    p = Plane(sent, landed)
    blocks = ((from_x, p.at_x), (from_y, p.at_y), (from_both, p.at_both))
    loads = [pltpu.make_async_copy(beside, held_beside, local.at[0])]
    for i, (block, rank) in enumerate(blocks):
        loads.append(pltpu.make_async_copy(block, held_blocks.at[i], local.at[i + 1]))
    for started in loads:
        started.start()
    width = attended.shape[3]
    columns = slice(weights.shape[1] - width, weights.shape[1])
    total = Scatter(p, attended, weights, columns, *scratch)
    kept, across = [], []
    loads[0].wait()
    kept.append(pltpu.make_async_copy(held_beside, beside_out.at[p.rank], local.at[0]))
    kept[0].start()
    for i, (block, rank) in enumerate(blocks):
        loads[i + 1].wait()
        place = beside_out.at[rank, p.core]
        kept.append(pltpu.make_async_copy(held_blocks.at[i], place, local.at[i + 1]))
        kept[i + 1].start()
        across.append(p.send(held_blocks.at[i], place, p.sibling))
    share = hidden.shape[0]

    def work(rows):
        value = residual[rows, :].astype(jnp.float32) + residual_scale * total.rows(rows)
        middle[rows, :] = value
        hidden[rows, :] = (value * row_root(value) * gain[1:2, :]).astype(jnp.bfloat16)

    for h in range(2):
        total.ready(h)
        slabs(h * (share // 2), share // 2, work)
    for number, rank in zip(across, (p.at_x, p.at_y, p.at_both)):
        p.arrive(number, beside_out.at[rank, 1 - p.core])
    p.finish()
    for started in kept:
        started.wait()


def middle_plane(attended, weights, residual, gain, beside, blocks):
    share, width = residual.shape
    full = jax.ShapeDtypeStruct((4, 2, share, width), jnp.bfloat16)
    hidden, middle, beside_out = pl.pallas_call(
        middle_kernel,
        out_shape=[
            jax.ShapeDtypeStruct((share, width), jnp.bfloat16),
            jax.ShapeDtypeStruct((share, width), jnp.float32),
            full,
        ],
        in_specs=[VMEM] * 4 + [ANY] * 4,
        out_specs=[VMEM, VMEM, ANY],
        scratch_shapes=wires(SCATTER_COPIES + 3)
        + [
            pltpu.SemaphoreType.DMA((4,)),
            pltpu.VMEM((2, share, width), jnp.bfloat16),
            pltpu.VMEM((3, share, width), jnp.bfloat16),
        ]
        + scatter_scratch(share, width),
        compiler_params=pltpu.CompilerParams(
            collective_id=2, has_side_effects=True, vmem_limit_bytes=VMEM_LIMIT
        ),
        cost_estimate=lasting(55),
        name="middle_rows",
    )(
        attended.reshape(4, 2, share, -1),
        weights,
        residual,
        gain,
        beside.reshape(2, share, width),
        *blocks,
    )
    return hidden, middle, beside_out.reshape(8 * share, width)


def ffn_rows_kernel(
    block,
    weights_in,
    out,
    m,
    gate,
    up,
    sent,
    landed,
    local,
    loading,
    storing,
    weights,
    rows_in,
    m_held,
    gate_held,
    up_held,
):
    p = Plane(sent, landed)
    gather = Gather(p, block, out)
    for k in range(CHUNKS):
        gather.start(k)
    weights_load = pltpu.make_async_copy(weights_in, weights, local.at[0])
    weights_load.start()
    mine = pltpu.make_async_copy(block, out.at[p.rank, p.core], local.at[1])
    mine.start()
    units = m.shape[3]
    stores = []

    def load(n, rank, core):
        return pltpu.make_async_copy(out.at[rank, core], rows_in.at[n % 2], loading.at[n % 2])

    def compute(n, rank, core, source):
        slot = n % 2
        if n >= 2:
            for started in stores[n - 2]:
                started.wait()

        def step(j, carry):
            cut = pl.ds(pl.multiple_of(j * 256, 256), 256)
            beyond = pl.ds(pl.multiple_of(units + j * 256, 256), 256)
            gate_part = dot(source[...], weights[:, cut])
            up_part = dot(source[...], weights[:, beyond])
            gate_held[slot, :, cut] = gate_part.astype(jnp.bfloat16)
            up_held[slot, :, cut] = up_part.astype(jnp.bfloat16)
            sigmoid = 1.0 / (1.0 + jnp.exp(-gate_part))
            m_held[slot, :, cut] = (gate_part * sigmoid * up_part).astype(jnp.bfloat16)
            return carry

        lax.fori_loop(0, units // 256, step, 0)
        stores.append(
            [
                pltpu.make_async_copy(held.at[slot], target.at[rank, core], storing.at[slot, i])
                for i, (held, target) in enumerate(((m_held, m), (gate_held, gate), (up_held, up)))
            ]
        )
        for started in stores[n]:
            started.start()

    def from_sibling(i, rank):
        for k in range(CHUNKS):
            p.arrive(
                gather.across[i, k], out.at[rank, 1 - p.core, chunk(k, gather.rows)]
            )

    weights_load.wait()
    compute(0, p.rank, p.core, block)
    gather.forward_chunk(0)
    from_sibling(0, p.rank)
    load(1, p.rank, 1 - p.core).start()
    load(1, p.rank, 1 - p.core).wait()
    compute(1, p.rank, 1 - p.core, rows_in.at[1])
    for k in range(1, CHUNKS):
        gather.forward_chunk(k)
    load(2, p.at_x, p.core).start()
    load(3, p.at_y, p.core).start()
    load(2, p.at_x, p.core).wait()
    compute(2, p.at_x, p.core, rows_in.at[0])
    from_sibling(1, p.at_x)
    load(4, p.at_x, 1 - p.core).start()
    load(3, p.at_y, p.core).wait()
    compute(3, p.at_y, p.core, rows_in.at[1])
    from_sibling(2, p.at_y)
    load(5, p.at_y, 1 - p.core).start()
    load(4, p.at_x, 1 - p.core).wait()
    compute(4, p.at_x, 1 - p.core, rows_in.at[0])
    gather.forward_far()
    load(6, p.at_both, p.core).start()
    load(5, p.at_y, 1 - p.core).wait()
    compute(5, p.at_y, 1 - p.core, rows_in.at[1])
    from_sibling(3, p.at_both)
    load(7, p.at_both, 1 - p.core).start()
    load(6, p.at_both, p.core).wait()
    compute(6, p.at_both, p.core, rows_in.at[0])
    load(7, p.at_both, 1 - p.core).wait()
    compute(7, p.at_both, 1 - p.core, rows_in.at[1])
    p.finish()
    mine.wait()
    for n in (6, 7):
        for started in stores[n]:
            started.wait()


def ffn_rows(block, weights):
    share, width = block.shape
    units = weights.shape[1] // 2
    kind = jnp.bfloat16
    full = jax.ShapeDtypeStruct((4, 2, share, width), kind)
    part = jax.ShapeDtypeStruct((4, 2, share, units), kind)
    held = pltpu.VMEM((2, share, units), kind)
    outs = pl.pallas_call(
        ffn_rows_kernel,
        out_shape=[full, part, part, part],
        in_specs=[VMEM, ANY],
        out_specs=[ANY] * 4,
        scratch_shapes=wires(GATHER_COPIES)
        + [
            pltpu.SemaphoreType.DMA((2,)),
            pltpu.SemaphoreType.DMA((2,)),
            pltpu.SemaphoreType.DMA((2, 3)),
            pltpu.VMEM(weights.shape, kind),
            pltpu.VMEM((2, share, width), kind),
            held,
            held,
            held,
        ],
        compiler_params=pltpu.CompilerParams(
            collective_id=11, has_side_effects=True, vmem_limit_bytes=VMEM_LIMIT
        ),
        cost_estimate=lasting(60),
        name="ffn_rows",
    )(block, weights)
    return [array.reshape(8 * share, -1) for array in outs]


class WeightTiles:
    def __init__(self, rows, slopes, target, rows_in, tile_out, wires_in):
        self.rows, self.slopes, self.target = rows, slopes, target
        self.rows_in, self.tile_out, self.wires = rows_in, tile_out, wires_in
        self.count = rows.shape[1] // TILE
        self.load(0, 0).start()

    def load(self, d, slot):
        columns = pl.ds(pl.multiple_of(d * TILE, TILE), TILE)
        return pltpu.make_async_copy(
            self.rows.at[:, columns], self.rows_in.at[slot], self.wires.at[0, slot]
        )

    def store(self, d, slot):
        columns = pl.ds(pl.multiple_of(d * TILE, TILE), TILE)
        return pltpu.make_async_copy(
            self.tile_out.at[slot], self.target.at[columns], self.wires.at[1, slot]
        )

    def run(self, first, last):
        def step(d, carry):
            slot = lax.rem(d, 2)
            self.load(d, slot).wait()

            @pl.when(d < self.count - 1)
            def _():
                self.load(d + 1, 1 - slot).start()

            @pl.when(d >= 2)
            def _():
                self.store(d - 2, slot).wait()

            self.tile_out[slot] = dot(self.rows_in[slot], self.slopes[...], FIRST).astype(
                jnp.bfloat16
            )
            self.store(d, slot).start()
            return carry

        lax.fori_loop(first, last, step, 0)

    def finish(self):
        for d in (self.count - 2, self.count - 1):
            self.store(d, d % 2).wait()


def tile_scratch(count, units):
    return [
        pltpu.SemaphoreType.DMA((2, 2)),
        pltpu.VMEM((2, count, TILE), jnp.bfloat16),
        pltpu.VMEM((2, TILE, units), jnp.bfloat16),
    ]


UNITS = ((0, 0), (0, 1), (1, 0), (2, 0), (1, 1), (2, 1), (3, 0), (3, 1))


def second_kernel(
    slopes,
    normed_rows,
    weights,
    middle,
    cotangent,
    gain,
    early,
    grad_middle,
    hidden,
    weight_grads,
    sent,
    landed,
    loading,
    tile_wires,
    rows_in,
    tile_out,
    gate_in,
    up_in,
    given,
    held,
    other,
    near_x,
    near_y,
    far_x,
    far_y,
):
    p = Plane(sent, landed)
    share, width = near_x.shape
    half = share // 2
    order = (p.at_both, p.at_x, p.at_y, p.rank)
    top, low = halves = pl.ds(0, half), pl.ds(half, half)

    def places(u):
        i, h = UNITS[u]
        for core in (1 - p.core, p.core):
            row = (order[i] * 2 + core) * share + h * half
            yield pl.ds(pl.multiple_of(row, 32), half)

    units = gate_in.shape[1]

    def loads(u):
        for j, rows in enumerate(places(u)):
            for n, target in enumerate((gate_in, up_in)):
                yield pltpu.make_async_copy(
                    slopes.at[rows, pl.ds(n * units, units)],
                    target.at[rows],
                    loading.at[u, 2 * j + n],
                )

    def compute(u):
        i, h = UNITS[u]
        slot = u % 2
        gate_rows = jnp.concatenate([gate_in[rows, :] for rows in places(u)], axis=0)
        up_rows = jnp.concatenate([up_in[rows, :] for rows in places(u)], axis=0)
        for j in range(width // 1024):
            cut = slice(j * 1024, j * 1024 + 1024)
            back = dot(gate_rows, weights[cut, :units], LAST) + dot(
                up_rows, weights[cut, units:], LAST
            )
            given[slot, :, cut] = back[:half].astype(jnp.bfloat16)
            held[i, halves[h], cut] = back[half:].astype(jnp.bfloat16)

    tiles = WeightTiles(normed_rows, gate_in, weight_grads, rows_in, tile_out, tile_wires)

    moves, across = {}, {}
    moves, across = {}, {}

    def settle(u):
        i, h = UNITS[u]
        p.arrive(across[u], other.at[i, halves[h]])
        add_rows(held.at[i], other.at[i], h * half, half)
        if u == 0:
            moves["far_x"] = p.send(held.at[0, top], far_x, p.x)
        elif u == 1:
            moves["far_y"] = p.send(held.at[0, low], far_y, p.y)
        elif u == 2:
            moves["x", 0] = p.send(held.at[1, top], near_x.at[top], p.x)
        elif u == 3:
            p.arrive(moves["far_x"], far_x)
            add_rows(held.at[2], far_x, 0, half)
            moves["y", 0] = p.send(held.at[2, top], near_y.at[top], p.y)
        elif u == 4:
            p.arrive(moves["far_y"], far_y)

            def step(k, carry):
                rows, at = pl.ds(half + k * SLAB, SLAB), pl.ds(k * SLAB, SLAB)
                held[1, rows, :] = (
                    held[1, rows, :].astype(jnp.float32) + far_y[at, :].astype(jnp.float32)
                ).astype(jnp.bfloat16)
                return carry

            lax.fori_loop(0, half // SLAB, step, 0)
            moves["x", 1] = p.send(held.at[1, low], near_x.at[low], p.x)
        elif u == 5:
            moves["y", 1] = p.send(held.at[2, low], near_y.at[low], p.y)

    for u in range(8):
        for started in loads(u):
            started.start()

    def unit(u):
        if u >= 2:
            p.copies[across[u - 2]].wait_send()
        compute(u)
        i, h = UNITS[u]
        across[u] = p.send(given.at[u % 2], other.at[i, halves[h]], p.sibling)

    def wait_loads(units_here):
        for u in units_here:
            for started in loads(u):
                started.wait()

    wait_loads((0,))
    unit(0)
    wait_loads((1,))
    unit(1)
    settle(0)
    wait_loads((2, 3))
    unit(2)
    settle(1)
    unit(3)
    settle(2)
    wait_loads((4, 5, 6, 7))
    unit(4)
    tiles.run(0, 2)
    settle(3)
    unit(5)
    settle(4)
    unit(6)
    settle(5)
    unit(7)
    settle(6)
    settle(7)
    tiles.run(2, tiles.count)

    def work(rows):
        value = middle[rows, :]
        root = row_root(value)
        normed = value * root
        total = sum(part[rows, :].astype(jnp.float32) for part in (held.at[3], near_x, near_y))
        slope = total * gain[1:2, :]
        mean = jnp.mean(slope * normed, axis=-1, keepdims=True)
        gradient = cotangent[rows, :].astype(jnp.float32) + root * (slope - normed * mean)
        grad_middle[rows, :] = gradient
        hidden[rows, :] = (residual_scale * gradient).astype(jnp.bfloat16)

    for h in range(2):
        p.arrive(moves["x", h], near_x.at[halves[h]])
        p.arrive(moves["y", h], near_y.at[halves[h]])
        slabs(h * half, half, work)
    for u in (6, 7):
        p.copies[across[u]].wait_send()
    tiles.finish()
    for number, started in enumerate(p.copies):
        if number not in across.values():
            started.wait_send()


def second_plane(slopes, normed_rows, weights, middle, cotangent, gain, early):
    share, width = middle.shape
    count, units = slopes.shape[0], slopes.shape[1] // 2
    kind = jnp.bfloat16
    half = share // 2
    quarter = pltpu.VMEM((4, share, width), kind)
    return pl.pallas_call(
        second_kernel,
        out_shape=[
            jax.ShapeDtypeStruct((share, width), jnp.float32),
            jax.ShapeDtypeStruct((share, width), kind),
            jax.ShapeDtypeStruct((width, units), kind),
        ],
        in_specs=[ANY, ANY] + [VMEM] * 4 + [ANY],
        out_specs=[VMEM, VMEM, ANY],
        scratch_shapes=wires(8 + 6)
        + [pltpu.SemaphoreType.DMA((8, 4))]
        + tile_scratch(count, units)
        + [
            pltpu.VMEM((count, units), kind),
            pltpu.VMEM((count, units), kind),
            pltpu.VMEM((2, half, width), kind),
            quarter,
            quarter,
            pltpu.VMEM((share, width), kind),
            pltpu.VMEM((share, width), kind),
            pltpu.VMEM((half, width), kind),
            pltpu.VMEM((half, width), kind),
        ],
        compiler_params=pltpu.CompilerParams(
            collective_id=3, has_side_effects=True, vmem_limit_bytes=60 * 1024 * 1024
        ),
        cost_estimate=lasting(60),
        name="second_rows",
    )(slopes, normed_rows, weights, middle, cotangent, gain, early)


def spread_kernel(
    hidden, m, down_w, normed_rows, slopes, early, out, pair_own, pair_x, pair_y, pair_both,
    weight_grads, sent, landed, local, loading, tile_wires, rows_in, tile_out, up_in,
    m_in, given, held, theirs,
):
    p = Plane(sent, landed)
    share, width = hidden.shape
    gather = Gather(p, hidden, out)
    for k in range(CHUNKS):
        gather.start(k)
    mine = pltpu.make_async_copy(hidden, out.at[p.rank, p.core], local.at[4])
    mine.start()
    order = (p.rank, p.at_x, p.at_y, p.at_both)
    halves = pl.ds(0, share), pl.ds(share, share)

    def loads(i):
        for j, core in enumerate((1 - p.core, p.core)):
            yield pltpu.make_async_copy(
                m.at[order[i], core], m_in.at[i % 2, halves[j]], loading.at[i % 2, j]
            )

    across = []
    units = up_in.shape[1]
    up_load = pltpu.make_async_copy(slopes.at[:, pl.ds(units, units)], up_in, local.at[5])
    up_load.start()
    for started in loads(0):
        started.start()
    tiles = WeightTiles(normed_rows, up_in, weight_grads, rows_in, tile_out, tile_wires)
    for i in range(4):
        for started in loads(i):
            started.wait()
        if i < 3:
            for started in loads(i + 1):
                started.start()

        def step(j, carry, i=i):
            cut = pl.ds(pl.multiple_of(j * 512, 512), 512)
            value = dot(m_in[i % 2], down_w[cut, :], LAST)
            given[i, :, cut] = value[:share].astype(jnp.bfloat16)
            held[i, :, cut] = value[share:].astype(jnp.bfloat16)
            return carry

        lax.fori_loop(0, width // 512, step, 0)
        across.append(p.send(given.at[i], theirs.at[i], p.sibling))
        if i == 0:
            up_load.wait()
        gather.forward_chunk(i)
        tiles.run(i, i + 1)
    kept = []
    for i in range(4):
        p.arrive(across[i], theirs.at[i])
        add_rows(held.at[i], theirs.at[i], 0, share)
        target = (pair_own, pair_x, pair_y, pair_both)[i]
        kept.append(pltpu.make_async_copy(held.at[i], target, local.at[i]))
        kept[i].start()
    gather.forward_far()
    tiles.run(4, tiles.count)
    tiles.finish()
    gather.finish()
    p.finish()
    mine.wait()
    for started in kept:
        started.wait()


def spread_plane(hidden, m, down_w, normed_rows, slopes, early):
    share, width = hidden.shape
    units = m.shape[1]
    full = jax.ShapeDtypeStruct((4, 2, share, width), jnp.bfloat16)
    quarter = pltpu.VMEM((4, share, width), jnp.bfloat16)
    out, *pairs, weight_grads = pl.pallas_call(
        spread_kernel,
        out_shape=[full]
        + [jax.ShapeDtypeStruct((share, width), jnp.bfloat16)] * 4
        + [jax.ShapeDtypeStruct((width, units), jnp.bfloat16)],
        in_specs=[VMEM, ANY, VMEM, ANY, ANY, ANY],
        out_specs=[ANY] * 6,
        scratch_shapes=wires(GATHER_COPIES + 4)
        + [
            pltpu.SemaphoreType.DMA((6,)),
            pltpu.SemaphoreType.DMA((2, 2)),
        ]
        + tile_scratch(8 * share, units)
        + [
            pltpu.VMEM((8 * share, units), jnp.bfloat16),
            pltpu.VMEM((2, 2 * share, units), jnp.bfloat16),
            quarter,
            quarter,
            quarter,
        ],
        compiler_params=pltpu.CompilerParams(
            collective_id=7, has_side_effects=True, vmem_limit_bytes=60 * 1024 * 1024
        ),
        cost_estimate=lasting(60),
        name="spread_rows",
    )(hidden, m.reshape(4, 2, share, units), down_w, normed_rows, slopes, early)
    return out.reshape(8 * share, width), pairs, weight_grads


def lane_sums(pairs):
    total = 0.0
    for a, b in pairs:
        product = a.astype(jnp.float32) * b.astype(jnp.float32)
        total += jnp.sum(product, axis=1, keepdims=True)
    return jnp.broadcast_to(total, (total.shape[0], 128))


LATER = 10


def last_kernel(
    back,
    weights,
    gain,
    ups,
    *rest,
):
    later, rest = rest[:LATER], rest[LATER:]
    out, result_out, up_out, gain_out, sent, landed, local, loading, held, result, sums = rest[:11]
    landing, scratch = rest[11 : 11 + LATER], rest[11 + LATER :]
    loads = [
        pltpu.make_async_copy(source, target, loading.at[i])
        for i, (source, target) in enumerate(zip(later, landing))
    ]
    for started in loads:
        started.start()
    middle, ffn_own, ffn_x, ffn_y, ffn_both, gates, gate, up, residual, grad_middle = landing
    p = Plane(sent, landed, diagonal=True)
    moves = []
    for partner, rank in ((p.both, p.at_both), (p.x, p.at_x), (p.y, p.at_y)):
        moves.append((p.send(ups.at[rank], up_out.at[p.rank], partner), up_out.at[rank]))
    up_out[p.rank] = ups[p.rank]
    total = Scatter(p, back, weights, slice(0, back.shape[3]), *scratch)
    share = held.shape[0]

    def finish_result(rows):
        parts = (ffn_own, ffn_x, ffn_y, ffn_both)
        ffn = sum(part[rows, :].astype(jnp.float32) for part in parts)
        result[rows, :] = (middle[rows, :] + residual_scale * ffn).astype(jnp.bfloat16)

    for started in loads:
        started.wait()
    slabs(0, share, finish_result)
    kept = [pltpu.make_async_copy(result, result_out.at[p.core], local.at[0])]
    kept[0].start()
    given = p.send(result, result_out.at[p.core], p.sibling)
    units = gate.shape[1] // 4

    def gain_rows(rows):
        pairs = []
        for c in range(4):
            columns = slice(c * units, c * units + units)
            pairs.append((gates[c, rows, :], gate[rows, columns]))
            pairs.append((up_out[c, rows, :], up[rows, columns]))
        sums[0, rows, :] = lane_sums(pairs)

    for number, target in moves:
        p.arrive(number, target)
    slabs(0, gate.shape[0], gain_rows)
    swapped = p.send(sums.at[0], sums.at[1], p.sibling)

    def work(rows):
        value = residual[rows, :].astype(jnp.float32)
        root = row_root(value)
        normed = value * root
        slope = total.rows(rows) * gain[0:1, :]
        mean = jnp.mean(slope * normed, axis=-1, keepdims=True)
        held[rows, :] = grad_middle[rows, :] + root * (slope - normed * mean)

    across = []
    for k in range(CHUNKS):
        cut = chunk(k, share)
        if k % (CHUNKS // 2) == 0:
            total.ready(k // (CHUNKS // 2))
        slabs(k * (share // CHUNKS), share // CHUNKS, work)
        across.append(p.send(held.at[cut], out.at[p.core, cut], p.sibling))
    kept.append(pltpu.make_async_copy(held, out.at[p.core], local.at[1]))
    kept[1].start()
    p.arrive(swapped, sums.at[1])
    gain_out[...] = sums[0] + sums[1]
    p.arrive(given, result_out.at[1 - p.core])
    for k in range(CHUNKS):
        p.arrive(across[k], out.at[1 - p.core, chunk(k, share)])
    p.finish()
    for started in kept:
        started.wait()


def last_plane(
    back, weights, residual, grad_middle, gain, middle, ffn_parts, ups, gates, gate, up
):
    share, width = residual.shape
    later = [middle, *ffn_parts, gates, gate, up, residual, grad_middle]
    out, result_out, up_out, gain_out = pl.pallas_call(
        last_kernel,
        out_shape=[
            jax.ShapeDtypeStruct((2, share, width), jnp.float32),
            jax.ShapeDtypeStruct((2, share, width), jnp.bfloat16),
            jax.ShapeDtypeStruct(ups.shape, ups.dtype),
            jax.ShapeDtypeStruct((gate.shape[0], 128), jnp.float32),
        ],
        in_specs=[VMEM] * 4 + [ANY] * LATER,
        out_specs=[ANY, ANY, VMEM, VMEM],
        scratch_shapes=wires(CHUNKS + 5 + SCATTER_COPIES)
        + [
            pltpu.SemaphoreType.DMA((2,)),
            pltpu.SemaphoreType.DMA((LATER,)),
            pltpu.VMEM((share, width), jnp.float32),
            pltpu.VMEM((share, width), jnp.bfloat16),
            pltpu.VMEM((2, gate.shape[0], 128), jnp.float32),
        ]
        + [pltpu.VMEM(array.shape, array.dtype) for array in later]
        + scatter_scratch(share, width),
        compiler_params=pltpu.CompilerParams(
            collective_id=4, has_side_effects=True, vmem_limit_bytes=VMEM_LIMIT
        ),
        cost_estimate=lasting(70),
        name="last_rows",
    )(
        back.reshape(4, 2, share, -1),
        weights,
        gain,
        ups,
        *later,
    )
    return (
        out.reshape(2 * share, width),
        result_out.reshape(2 * share, width),
        up_out,
        gain_out,
    )


def exchange_kernel(blocks, query, pair, other_sums, out, gain_out, sent, landed, sums):
    p = Plane(sent, landed, diagonal=True)
    moves = []
    for partner, rank in ((p.both, p.at_both), (p.x, p.at_x), (p.y, p.at_y)):
        moves.append((p.send(blocks.at[rank], out.at[p.rank], partner), out.at[rank]))
    out[p.rank] = blocks[p.rank]
    width = query.shape[1] // 4

    def attention_rows(rows):
        pairs = []
        for c in range(4):
            pairs.append((out[c, rows, :width], query[rows, c * width : c * width + width]))
            pairs.append((out[c, rows, width : width + 128], pair[rows, c * 128 : c * 128 + 128]))
        sums[0, rows, :] = lane_sums(pairs)

    for number, target in moves:
        p.arrive(number, target)
    slabs(0, blocks.shape[1], attention_rows)
    swapped = p.send(sums.at[0], sums.at[1], p.sibling)
    p.arrive(swapped, sums.at[1])
    gain_out[0] = sums[0] + sums[1]
    gain_out[1] = other_sums[...]
    p.finish()


def exchange(blocks, query, pair, other_sums):
    depth = blocks.shape[1]
    return pl.pallas_call(
        exchange_kernel,
        out_shape=[
            jax.ShapeDtypeStruct(blocks.shape, blocks.dtype),
            jax.ShapeDtypeStruct((2, depth, 128), jnp.float32),
        ],
        in_specs=[VMEM] * 4,
        out_specs=[VMEM] * 2,
        scratch_shapes=wires(4) + [pltpu.VMEM((2, depth, 128), jnp.float32)],
        compiler_params=pltpu.CompilerParams(collective_id=5, has_side_effects=True),
        cost_estimate=lasting(8),
        name="exchange_blocks",
    )(blocks, query, pair, other_sums)


def finish_kernel(
    attn, down, gate, up, tokens, result, sums, gains,
    query_out, pair_out, out_out, gate_out, up_out, down_out, tokens_out, result_out, gain_out,
):
    width = query_out.shape[1]
    query_out[...] = attn[0, :, :width].astype(jnp.float32)
    pair_out[...] = attn[0, :, width : width + 128].astype(jnp.float32)
    out_out[...] = jnp.transpose(attn[0, :, width + 128 :].astype(jnp.float32))
    gate_out[...] = gate[0].astype(jnp.float32)
    up_out[...] = up[0].astype(jnp.float32)
    down_out[...] = jnp.transpose(down[0].astype(jnp.float32))
    tokens_out[...] = tokens[...]
    result_out[...] = result[...]
    for i in range(2):
        gain_out[i : i + 1, :] = jnp.transpose(sums[i])[0:1] / gains[i : i + 1, :]


def finish(attn, down, gate, up, tokens, result, sums, gains):
    groups, depth, units = down.shape
    width = attn.shape[2] // 2 - HEAD
    rows, columns = tokens.shape
    part = rows // groups

    def block(*shape):
        return pl.BlockSpec((1, *shape), lambda i: (i, 0, 0))

    def wide(count):
        return pl.BlockSpec((depth, count), lambda i: (0, i))

    def tall(count, other):
        return pl.BlockSpec((count, other), lambda i: (i, 0))

    def f32(*shape):
        return jax.ShapeDtypeStruct(shape, jnp.float32)

    return pl.pallas_call(
        finish_kernel,
        grid=(groups,),
        in_specs=[
            block(depth, attn.shape[2]),
            block(depth, units),
            block(depth, units),
            block(depth, units),
            tall(part, columns),
            tall(part, columns),
            pl.BlockSpec(sums.shape, lambda i: (0, 0, 0)),
            pl.BlockSpec(gains.shape, lambda i: (0, 0)),
        ],
        out_specs=[
            wide(width),
            wide(128),
            tall(width, depth),
            wide(units),
            wide(units),
            tall(units, depth),
            tall(part, columns),
            tall(part, columns),
            pl.BlockSpec((2, 128), lambda i: (0, 0)),
        ],
        out_shape=[
            f32(depth, groups * width),
            f32(depth, groups * 128),
            f32(groups * width, depth),
            f32(depth, groups * units),
            f32(depth, groups * units),
            f32(groups * units, depth),
            f32(rows, columns),
            jax.ShapeDtypeStruct(result.shape, result.dtype),
            f32(2, 128),
        ],
        compiler_params=pltpu.CompilerParams(vmem_limit_bytes=VMEM_LIMIT),
        cost_estimate=lasting(12),
        name="finish",
    )(attn, down, gate, up, tokens, result, sums, gains)


def context_pairs(step):
    return [(i, i ^ step) for i in range(4)]


def ffn_first_kernel(hidden, weights, m, gate, up):
    units = m.shape[1]
    for j in range(units // 256):
        cut = slice(j * 256, j * 256 + 256)
        gate_part = dot(hidden[...], weights[:, cut])
        up_part = dot(hidden[...], weights[:, units + j * 256 : units + j * 256 + 256])
        gate[:, cut] = gate_part.astype(jnp.bfloat16)
        up[:, cut] = up_part.astype(jnp.bfloat16)
        sigmoid = 1.0 / (1.0 + jnp.exp(-gate_part))
        m[:, cut] = (gate_part * sigmoid * up_part).astype(jnp.bfloat16)


def ffn_slopes_kernel(grad, gate, up, down_w, early, slopes):
    units = down_w.shape[1]
    for j in range(units // 256):
        cut = slice(j * 256, j * 256 + 256)
        grad_part = dot(grad[...], down_w[:, cut])
        gate_part = gate[:, cut].astype(jnp.float32)
        up_part = up[:, cut].astype(jnp.float32)
        sigmoid = 1.0 / (1.0 + jnp.exp(-gate_part))
        slope = sigmoid * (1.0 + gate_part * (1.0 - sigmoid))
        slopes[:, cut] = (grad_part * up_part * slope).astype(jnp.bfloat16)
        slopes[:, units + j * 256 : units + j * 256 + 256] = (
            grad_part * gate_part * sigmoid
        ).astype(jnp.bfloat16)


def first_rows_kernel(values, gains, weight, hidden, raw):
    value = values[...].astype(jnp.float32)
    normed = (value * row_root(value) * gains[0:1, :]).astype(jnp.bfloat16)
    hidden[...] = normed
    raw[...] = dot(normed, weight[...])


def first_rows(values, gains, packed, columns):
    count, width = values.shape
    return pl.pallas_call(
        first_rows_kernel,
        grid=(count // ROW_TILE,),
        in_specs=[
            pl.BlockSpec((ROW_TILE, width), lambda i: (i, 0)),
            pl.BlockSpec((8, width), lambda i: (0, 0)),
            pl.BlockSpec((width, columns), lambda i: (0, 0)),
        ],
        out_specs=[
            pl.BlockSpec((ROW_TILE, width), lambda i: (i, 0)),
            pl.BlockSpec((ROW_TILE, columns), lambda i: (i, 0)),
        ],
        out_shape=[
            jax.ShapeDtypeStruct((count, width), jnp.bfloat16),
            jax.ShapeDtypeStruct((count, columns), jnp.float32),
        ],
        compiler_params=pltpu.CompilerParams(vmem_limit_bytes=VMEM_LIMIT),
        cost_estimate=lasting(4),
        name="first_rows",
    )(values, gains, packed)


def attention_weights_kernel(hidden, back, grad, attended, moving, *rest):
    out, moved, sent, landed, local = rest[-5:]
    step, last = pl.program_id(0), pl.num_programs(0) - 1

    @pl.when(step == 0)
    def start():
        p = Plane(sent, landed, diagonal=True)
        pltpu.make_async_copy(moving.at[p.rank], moved.at[p.rank], local).start()
        for partner, rank in ((p.both, p.at_both), (p.x, p.at_x), (p.y, p.at_y)):
            p.send(moving.at[rank], moved.at[p.rank], partner)

    columns = back.shape[1]
    out[:, :columns] = dot(hidden[...], back[...], FIRST).astype(jnp.bfloat16)
    out[:, columns:] = dot(grad[...], attended[...], FIRST).astype(jnp.bfloat16)

    @pl.when(step == last)
    def finish():
        p = Plane(sent, landed, entered=True)
        for number, rank in enumerate((p.at_both, p.at_x, p.at_y)):
            move = p.copy(number, moving.at[rank], moved.at[rank], p.x)
            move.wait_recv()
            move.wait_send()
        pltpu.make_async_copy(moving.at[p.rank], moved.at[p.rank], local).wait()


def attention_weights(hidden, back, grad, attended, moving, early):
    count, width = hidden.shape
    first, second = back.shape[1], attended.shape[1]
    tall = pl.BlockSpec((count, 256), lambda i: (0, i))
    return pl.pallas_call(
        attention_weights_kernel,
        grid=(width // 256,),
        in_specs=[
            tall,
            pl.BlockSpec((count, first), lambda i: (0, 0)),
            tall,
            pl.BlockSpec((count, second), lambda i: (0, 0)),
        ]
        + [ANY] * (1 + len(early)),
        out_specs=[pl.BlockSpec((256, first + second), lambda i: (i, 0)), ANY],
        out_shape=[
            jax.ShapeDtypeStruct((width, first + second), jnp.bfloat16),
            jax.ShapeDtypeStruct(moving.shape, moving.dtype),
        ],
        scratch_shapes=wires(3) + [pltpu.SemaphoreType.DMA],
        compiler_params=pltpu.CompilerParams(
            collective_id=8, has_side_effects=True, vmem_limit_bytes=VMEM_LIMIT
        ),
        cost_estimate=lasting(25),
        name="attention_weights",
    )(hidden, back, grad, attended, moving, *early)


ROW_TILE = 256


def row_tiles(kernel, name, rows, weights, extra, widths):
    count = rows[0].shape[0]

    def tile(width):
        return pl.BlockSpec((ROW_TILE, width), lambda i: (i, 0))

    whole = [
        pl.BlockSpec(w.shape, lambda i: (0, 0), pipeline_mode=pl.Buffered(1)) for w in weights
    ]
    flops = 2 * count * sum(w.size for w in weights)
    return pl.pallas_call(
        kernel,
        grid=(count // ROW_TILE,),
        in_specs=[tile(r.shape[1]) for r in rows] + whole + [ANY] * len(extra),
        out_specs=[tile(width) for width in widths],
        out_shape=[jax.ShapeDtypeStruct((count, width), jnp.bfloat16) for width in widths],
        compiler_params=pltpu.CompilerParams(vmem_limit_bytes=56 * 1024 * 1024),
        cost_estimate=pl.CostEstimate(flops=flops, bytes_accessed=flops // 400, transcendentals=0),
        name=name,
    )(*rows, *weights, *extra)


def norm_backward(gradient, normed, inv_root):
    return inv_root * (gradient - normed * jnp.mean(gradient * normed, axis=-1, keepdims=True))


def inverse_root(values):
    return lax.rsqrt(jnp.mean(values * values, axis=-1, keepdims=True) + epsilon)


PLANE = ("context", "tensor")


def gather_rows(values):
    return lax.all_gather(values, PLANE, axis=0, tiled=True)


def scatter_rows(partial):
    return lax.psum_scatter(
        partial.astype(jnp.bfloat16), PLANE, scatter_dimension=0, tiled=True
    ).astype(jnp.float32)


def local(
    tokens,
    cotangent,
    attn_gain,
    w_query,
    w_key,
    w_value,
    w_out,
    ffn_gain,
    w_gate,
    w_up,
    w_down,
    piece_segment,
    piece_parent,
    piece_start,
):
    groups = lax.axis_size("context")
    cores = lax.axis_size("tensor")
    depth = w_query.shape[0]
    kv_count = w_key.shape[1] // HEAD
    sharing = groups // kv_count
    share = tokens.shape[0] // cores
    first_row = lax.axis_index("tensor") * share

    def my_rows(values):
        return lax.dynamic_slice_in_dim(values, first_row, share, 0)

    def blocks(weight):
        return jnp.transpose(weight.reshape(depth, groups, -1), (1, 0, 2))

    def kv_blocks(weight):
        return jnp.repeat(jnp.transpose(weight.reshape(depth, kv_count, HEAD), (1, 0, 2)), sharing, 0)

    def spread(weight_blocks):
        mine = lax.all_to_all(weight_blocks, "context", 0, 0)
        mine = mine.reshape(groups * depth, -1)
        return lax.all_gather(mine, "fsdp", axis=0, tiled=True)

    square = groups == 4 and cores == 2
    width = w_query.shape[1] // groups
    columns_qkv = width + 2 * HEAD
    out_turned, down_turned = w_out.T, w_down.T
    tokens_half, cotangent_half = my_rows(tokens), my_rows(cotangent)

    def over_groups(blocks_here):
        return lax.all_gather(
            blocks_here.reshape(groups * depth, -1), "fsdp", axis=0, tiled=True
        )

    if square:
        gains = jnp.pad(jnp.stack([attn_gain, ffn_gain]).astype(jnp.float32), ((0, 6), (0, 0)))
        w_pair = jnp.stack(
            [w_key.reshape(depth, groups, HEAD), w_value.reshape(depth, groups, HEAD)], axis=2
        ).reshape(depth, -1)
        packed, gain_rows = first_exchange(w_query, w_pair, out_turned, gains)
        packed = over_groups(packed)
        both_blocks, down_blocks = exchange_columns(w_gate, w_up, down_turned, gain_rows)
        inputs_full, ffn_grad, my_ffn_grad = start_plane(tokens_half, cotangent, down_blocks)
        both_full, down_full = over_groups(both_blocks), over_groups(down_blocks)
        hidden_first, raw = first_rows(
            inputs_full.reshape(-1, inputs_full.shape[3]), gain_rows, packed, columns_qkv
        )
        out_full = packed[:, columns_qkv:]
    else:
        gains = jnp.stack([attn_gain, ffn_gain], axis=1)
        gains = jnp.broadcast_to(jnp.pad(gains, ((0, 0), (0, 126))), (groups, depth, 128))
        packed = spread(
            jnp.concatenate(
                [
                    blocks(w_query),
                    kv_blocks(w_key),
                    kv_blocks(w_value),
                    blocks(out_turned),
                    gains,
                ],
                axis=2,
            )
        )
        qkv_full = packed[:, :columns_qkv]
        out_full = packed[:, columns_qkv : columns_qkv + width]
        gains_full = packed[:, columns_qkv + width :].astype(jnp.float32)
        attn_scale, ffn_scale = gains_full[:, 0], gains_full[:, 1]
        both_full = spread(jnp.concatenate([blocks(w_gate), blocks(w_up)], axis=2))
        down_full = spread(blocks(down_turned))
        inputs_full = gather_rows(tokens_half).astype(jnp.float32)
        hidden_first = inputs_full * inverse_root(inputs_full) * attn_scale
        hidden_first = hidden_first.astype(jnp.bfloat16)
        raw = dot(hidden_first, qkv_full)
        my_ffn_grad = (residual_scale * cotangent_half.astype(jnp.float32)).astype(jnp.bfloat16)
    tables = rope_tables()

    segment, starts = piece_segment[0] % 13, piece_start[0]
    places = jnp.where(
        segment == 0,
        starts,
        jnp.where(
            segment <= BRANCHES,
            starts + (segment - 1) * SEG,
            starts + (segment - 1 - BRANCHES) * SEG + (BRANCHES - 1) * SEG,
        ),
    )

    residual_in = tokens_half.astype(jnp.float32)
    grad_result = cotangent_half.astype(jnp.float32)

    attended, *kept = attention_forward(places, starts, raw, tables)
    if square:
        ffn_grad_blocks = [
            lax.ppermute(my_ffn_grad, "context", context_pairs(step)) for step in (1, 2, 3)
        ]
        hidden_block, middle, ffn_grad = middle_plane(
            attended, packed, tokens_half, gain_rows, ffn_grad, ffn_grad_blocks
        )
    else:
        ffn_grad = gather_rows(my_ffn_grad)
        middle = residual_in + residual_scale * scatter_rows(dot(attended, out_full, LAST))
        hidden_second = gather_rows((middle * inverse_root(middle) * ffn_scale).astype(jnp.bfloat16))

    units = down_full.shape[1]
    if square:
        hidden_second, hidden, gate_proj, up_proj = ffn_rows(hidden_block, both_full)
    else:
        hidden, gate_proj, up_proj = row_tiles(
            ffn_first_kernel,
            "ffn_first",
            [hidden_second],
            [both_full],
            [],
            [units, units, units],
        )
    grad_down = dot(ffn_grad, hidden, FIRST).astype(jnp.bfloat16)
    (slopes,) = row_tiles(
        ffn_slopes_kernel,
        "ffn_slopes",
        [ffn_grad, gate_proj, up_proj],
        [down_full],
        [grad_down],
        [2 * units],
    )
    def sum_groups(gradient):
        return lax.psum_scatter(gradient, "fsdp", scatter_dimension=0, tiled=True)

    def hand_back(gradient):
        return lax.all_to_all(gradient.reshape(groups, depth, -1), "context", 0, 0)

    def columns(gradient):
        return jnp.transpose(gradient, (1, 0, 2)).reshape(depth, -1).astype(jnp.float32)

    if square:
        grad_middle, my_attn_grad, grad_gate = second_plane(
            slopes,
            hidden_second,
            both_full,
            middle,
            cotangent_half,
            gain_rows,
            grad_down,
        )
        attn_grad, ffn_pairs, grad_up = spread_plane(
            my_attn_grad, hidden, down_full, hidden_second, slopes, grad_gate
        )
        ffn_parts = [ffn_pairs[0]] + [
            lax.ppermute(ffn_pairs[step], "context", context_pairs(step)) for step in (1, 2, 3)
        ]
    else:
        root = inverse_root(middle)
        ffn_out = dot(hidden, down_full, LAST)
        grad_gate = dot(hidden_second, slopes[:, :units], FIRST).astype(jnp.bfloat16)
        grad_up = dot(hidden_second, slopes[:, units:], FIRST).astype(jnp.bfloat16)
        grad_second = dot(slopes, both_full, LAST)
        grad_middle = grad_result + norm_backward(
            scatter_rows(grad_second) * ffn_scale, middle * root, root
        )
        attn_grad = gather_rows((residual_scale * grad_middle).astype(jnp.bfloat16))
        ffn_parts = []
    grad_attended = dot(attn_grad, out_full).astype(jnp.bfloat16)
    grad_down = sum_groups(grad_down)
    grad_gate, grad_up = sum_groups(grad_gate), sum_groups(grad_up)
    back = attention_backward(places, starts, grad_attended, kept, tables, [grad_down])
    grad_down = hand_back(grad_down)
    if square:
        grad_attn, grad_gate = attention_weights(
            hidden_first,
            back,
            attn_grad,
            attended,
            grad_gate.reshape(groups, depth, -1),
            [grad_down, *ffn_parts[1:]],
        )
    else:
        grad_attn = jnp.concatenate(
            [dot(hidden_first, back, FIRST), dot(attn_grad, attended, FIRST)], axis=1
        ).astype(jnp.bfloat16)
        grad_first = dot(back, qkv_full, LAST).astype(jnp.bfloat16)
        grad_gate, grad_up = hand_back(grad_gate), hand_back(grad_up)
    grad_attn = sum_groups(grad_attn)
    if square:
        grad_tokens, result, grad_up, ffn_sums = last_plane(
            back,
            packed,
            tokens_half,
            grad_middle,
            gain_rows,
            middle,
            ffn_parts,
            grad_up.reshape(groups, depth, -1),
            grad_gate,
            w_gate,
            w_up,
        )
        grad_attn, sums = exchange(
            grad_attn.reshape(groups, depth, -1), w_query, w_pair, ffn_sums
        )
        my_gains = jnp.stack([attn_gain, ffn_gain]).astype(jnp.float32)
        query, pair, out, gate, up, down, grad_tokens, result, gain_grads = finish(
            grad_attn, grad_down, grad_gate, grad_up, grad_tokens, result, sums, my_gains
        )
        key, value = jnp.moveaxis(pair.reshape(depth, groups, 2, HEAD), 2, 0)
        return (
            result,
            grad_tokens,
            gain_grads[0],
            query,
            key.reshape(depth, -1),
            value.reshape(depth, -1),
            out,
            gain_grads[1],
            gate,
            up,
            down,
        )
    else:
        root = inverse_root(residual_in)
        grad_tokens = grad_middle + norm_backward(
            scatter_rows(grad_first) * attn_scale, residual_in * root, root
        )
        grad_tokens = lax.all_gather(grad_tokens, "tensor", axis=0, tiled=True)
        result = (middle + residual_scale * scatter_rows(ffn_out)).astype(jnp.bfloat16)
        grad_attn = hand_back(grad_attn)
        result = lax.all_gather(result, "tensor", axis=0, tiled=True)
    def kv_columns(gradient):
        gradient = gradient.astype(jnp.float32).reshape(kv_count, sharing, depth, HEAD)
        return jnp.transpose(jnp.sum(gradient, axis=1), (1, 0, 2)).reshape(depth, -1)

    grad_query = columns(grad_attn[:, :, :width])
    grad_key = kv_columns(grad_attn[:, :, width : width + HEAD])
    grad_value = kv_columns(grad_attn[:, :, width + HEAD : width + 2 * HEAD])
    grad_gate, grad_up = columns(grad_gate), columns(grad_up)

    def against(*pairs):
        return sum(jnp.sum(weight.astype(jnp.float32) * g, axis=1) for weight, g in pairs)

    gain_grads = jnp.stack(
        [
            against((w_query, grad_query), (w_key, grad_key), (w_value, grad_value)),
            against((w_gate, grad_gate), (w_up, grad_up)),
        ]
    )
    gain_grads = lax.psum(gain_grads, "tensor")
    return (
        result,
        grad_tokens,
        gain_grads[0] / attn_gain.astype(jnp.float32),
        grad_query,
        grad_key,
        grad_value,
        columns(grad_attn[:, :, width + 2 * HEAD :]).T,
        gain_grads[1] / ffn_gain.astype(jnp.float32),
        grad_gate,
        grad_up,
        columns(grad_down).T,
    )


ROWS = ("fsdp", "context")


def solution(mesh):
    return jax.shard_map(
        local,
        mesh=mesh,
        in_specs=(
            P(ROWS, None),
            P(ROWS, None),
            P(ROWS),
            P(ROWS, "tensor"),
            P(ROWS, "tensor"),
            P(ROWS, "tensor"),
            P("tensor", ROWS),
            P(ROWS),
            P(ROWS, "tensor"),
            P(ROWS, "tensor"),
            P("tensor", ROWS),
            P("fsdp", None),
            P("fsdp", None),
            P("fsdp", None),
        ),
        out_specs=(
            P(ROWS, None),
            P(ROWS, None),
            P(ROWS),
            P(ROWS, "tensor"),
            P(ROWS, "tensor"),
            P(ROWS, "tensor"),
            P("tensor", ROWS),
            P(ROWS),
            P(ROWS, "tensor"),
            P(ROWS, "tensor"),
            P("tensor", ROWS),
        ),
        check_vma=False,
    )
```

```python
import functools

import jax
import jax.numpy as jnp
import numpy as np
from jax import lax
from jax.experimental import pallas as pl
from jax.experimental.pallas import tpu as pltpu
from jax.sharding import PartitionSpec as P

HEAD = 64
SEG = 128
TRUNK = 8 * SEG
BRANCHES = 4
LEAVES = 8
GROUP = TRUNK + (BRANCHES + LEAVES) * SEG
DEPTH = TRUNK + 2 * SEG
TILE = 2 * SEG

epsilon = 1e-05
rope_base = 10000000.0
residual_scale = 0.22
score_scale = 0.015625
masked_score = -1e30

FIRST = (((0,), (0,)), ((), ()))
LAST = (((1,), (1,)), ((), ()))
PLAIN = (((1,), (0,)), ((), ()))


def dot(left_side, right_side, dims=PLAIN):
    return lax.dot_general(left_side, right_side, dims, preferred_element_type=jnp.float32)


def rope_tables():
    steps = np.arange(HEAD // 2, dtype=np.float32)
    frequency = np.float32(rope_base) ** (-(steps * np.float32(2)) / np.float32(HEAD))
    angles = np.arange(DEPTH, dtype=np.float32)[:, None] * frequency.astype(np.float32)
    angles = angles.astype(np.float64)
    cosine, sine = np.cos(angles).astype(np.float32), np.sin(angles).astype(np.float32)
    return (
        jnp.asarray(np.concatenate([cosine] * 4, axis=-1)),
        jnp.asarray(np.concatenate([-sine, sine, -sine, sine], axis=-1)),
    )


def lanes(values):
    return lax.broadcasted_iota(jnp.int32, values.shape, 1)


def swap_halves(values):
    return jnp.where(
        lanes(values) % HEAD < HEAD // 2,
        pltpu.roll(values, 128 - HEAD // 2, 1),
        pltpu.roll(values, HEAD // 2, 1),
    )


def only_head(values, head):
    return jnp.where(lanes(values) // HEAD == head, values, jnp.zeros_like(values))


def query_tiles(work):
    for j in range(TRUNK // TILE):
        prefix = [(0, j * TILE, False)] if j else []
        work(j * TILE, prefix + [(j * TILE, TILE, True)], False)

    def branch(i, carry):
        row = pl.multiple_of(TRUNK + i * TILE, TILE)
        work(row, [(0, TRUNK, False), (row, TILE, True)], True)
        return carry

    lax.fori_loop(0, BRANCHES * SEG // TILE, branch, 0)

    def leaf(i, carry):
        row = pl.multiple_of(TRUNK + BRANCHES * SEG + i * TILE, TILE)
        parent = pl.multiple_of(TRUNK + i * SEG, SEG)
        work(row, [(0, TRUNK, False), (parent, SEG, False), (row, TILE, True)], True)
        return carry

    lax.fori_loop(0, LEAVES * SEG // TILE, leaf, 0)


def visible_scores(keys, query, own, one_segment):
    scores = dot(keys, query, LAST)
    if not own:
        return scores
    key_at = lax.broadcasted_iota(jnp.int32, scores.shape, 0)
    query_at = lax.broadcasted_iota(jnp.int32, scores.shape, 1)
    seen = key_at <= query_at
    if one_segment:
        seen = seen & (key_at // SEG == query_at // SEG)
    return jnp.where(seen, scores, masked_score)


def turned_over(target, source):
    for first in range(0, source.shape[0], TILE):
        block = source[first : first + TILE, :128].astype(jnp.float32)
        target[:, first : first + TILE] = jnp.transpose(block)[:HEAD].astype(jnp.bfloat16)


def head_pairs(width, work):
    together = min(PAIR, width // HEAD)

    def step(i, carry):
        work([i * together + j for j in range(together)])
        return carry

    lax.fori_loop(0, width // HEAD // together, step, 0)


PAIR = 2


def attention_forward_kernel(
    to_ref, start_ref, raw_ref, cos_ref, sin_ref, out_ref, q_ref, k_ref, v_ref, log_ref,
    held, values_ref, tile_ref,
):
    width = q_ref.shape[1]
    pieces = to_ref.shape[0]
    piece = raw_ref.shape[0] // pieces

    def place(p, carry):
        rows = pl.ds(pl.multiple_of(p * piece, piece), piece)
        to = pl.ds(pl.multiple_of(to_ref[p], piece), piece)
        at = pl.ds(pl.multiple_of(start_ref[p], piece), piece)
        cosine, sine = cos_ref[at, :], sin_ref[at, :]

        def turn(values):
            return values * cosine + swap_halves(values) * sine

        for g in range(width // 128):
            cut = slice(g * 128, g * 128 + 128)
            turned = turn(raw_ref[rows, cut]).astype(jnp.bfloat16)
            q_ref[to, cut] = turned * jnp.bfloat16(score_scale)
        pair = raw_ref[rows, width : width + 128]
        low = lanes(pair) < HEAD
        key = turn(pair)
        key = jnp.where(low, key, pltpu.roll(key, HEAD, 1)).astype(jnp.bfloat16)
        value = jnp.where(low, pltpu.roll(pair, HEAD, 1), pair).astype(jnp.bfloat16)
        for g in range(width // 128):
            cut = slice(g * 128, g * 128 + 128)
            k_ref[to, cut] = key
            v_ref[to, cut] = value
        return carry

    lax.fori_loop(0, pieces, place, 0)
    turned_over(values_ref, v_ref)

    def work(row, parts, one_segment):
        rows = pl.ds(row, TILE)

        def one_head(head):
            query = only_head(q_ref[rows, :], head)
            scores = [
                visible_scores(k_ref[pl.ds(first, count), :], query, own, one_segment)
                for first, count, own in parts
            ]
            largest = functools.reduce(
                jnp.maximum, [jnp.max(s, axis=0, keepdims=True) for s in scores]
            )
            exponent = [jnp.exp(s - largest) for s in scores]
            total = functools.reduce(
                jnp.add, [jnp.sum(e, axis=0, keepdims=True) for e in exponent]
            )
            result = functools.reduce(
                jnp.add,
                [
                    dot(values_ref[:, pl.ds(first, count)], e.astype(jnp.bfloat16))
                    for e, (first, count, own) in zip(exponent, parts)
                ],
            )
            log_ref[head, :, rows] = largest + jnp.log(total)
            tile_ref[pl.ds(pl.multiple_of(head * HEAD, HEAD), HEAD), :] = result * (1.0 / total)

        def heads(together):
            for head in together:
                one_head(head)

        head_pairs(width, heads)
        held[rows, :] = jnp.transpose(tile_ref[...]).astype(jnp.bfloat16)

    query_tiles(work)

    def back(p, carry):
        rows = pl.ds(pl.multiple_of(p * piece, piece), piece)
        to = pl.ds(pl.multiple_of(to_ref[p], piece), piece)
        out_ref[rows, :] = held[to, :]
        return carry

    lax.fori_loop(0, pieces, back, 0)


def attention_backward_kernel(
    to_ref,
    start_ref,
    grad_ref,
    q_ref,
    k_ref,
    v_ref,
    log_ref,
    cos_ref,
    sin_ref,
    *rest,
):
    out_ref, og_ref, dq_ref, dk_ref, dv_ref, keys_ref, tile_ref = rest[-7:]
    width = q_ref.shape[1]
    pieces = to_ref.shape[0]
    piece = grad_ref.shape[0] // pieces

    def place(p, carry):
        rows = pl.ds(pl.multiple_of(p * piece, piece), piece)
        to = pl.ds(pl.multiple_of(to_ref[p], piece), piece)
        og_ref[to, :] = grad_ref[rows, :]
        return carry

    lax.fori_loop(0, pieces, place, 0)
    turned_over(keys_ref, k_ref)
    dk_ref[...] = jnp.zeros_like(dk_ref)
    dv_ref[...] = jnp.zeros_like(dv_ref)

    def work(row, parts, one_segment):
        rows = pl.ds(row, TILE)

        def heads(together):
            queries, out_grads, all_weights, all_grads = [], [], [], []
            for head in together:
                query = only_head(q_ref[rows, :], head)
                out_grad = only_head(og_ref[rows, :], head)
                log_total = log_ref[head, :, rows]
                weights, products = [], []
                for first, count, own in parts:
                    keys = pl.ds(first, count)
                    scores = visible_scores(k_ref[keys, :], query, own, one_segment)
                    weights.append(jnp.exp(scores - log_total))
                    products.append(dot(v_ref[keys, :], out_grad, LAST))
                inner = functools.reduce(
                    jnp.add,
                    [jnp.sum(w * d, axis=0, keepdims=True) for w, d in zip(weights, products)],
                )
                grads = [
                    (w * (d - inner)).astype(jnp.bfloat16) for w, d in zip(weights, products)
                ]
                queries.append(query)
                out_grads.append(out_grad)
                all_weights.append([w.astype(jnp.bfloat16) for w in weights])
                all_grads.append(grads)
                tile_ref[pl.ds(pl.multiple_of(head * HEAD, HEAD), HEAD), :] = functools.reduce(
                    jnp.add,
                    [
                        dot(keys_ref[:, pl.ds(first, count)], g)
                        for (first, count, own), g in zip(parts, grads)
                    ],
                )
            query = jnp.concatenate(queries, axis=0)
            out_grad = jnp.concatenate(out_grads, axis=0)
            for i, (first, count, own) in enumerate(parts):
                keys = pl.ds(first, count)
                weights = jnp.concatenate([w[i] for w in all_weights], axis=1)
                grads = jnp.concatenate([g[i] for g in all_grads], axis=1)
                dv_ref[keys, :] += dot(weights, out_grad)
                dk_ref[keys, :] += dot(grads, query)

        head_pairs(width, heads)
        dq_ref[rows, :] = jnp.transpose(tile_ref[...])

    query_tiles(work)

    def back(p, carry):
        rows = pl.ds(pl.multiple_of(p * piece, piece), piece)
        to = pl.ds(pl.multiple_of(to_ref[p], piece), piece)
        at = pl.ds(pl.multiple_of(start_ref[p], piece), piece)
        cosine, sine = cos_ref[at, :], sin_ref[at, :]

        def turn_back(values):
            return values * cosine - swap_halves(values) * sine

        def over_heads(ref):
            total = functools.reduce(
                jnp.add, [ref[to, g * 128 : g * 128 + 128] for g in range(width // 128)]
            )
            return total + pltpu.roll(total, HEAD, 1)

        for g in range(width // 128):
            cut = slice(g * 128, g * 128 + 128)
            turned = turn_back(score_scale * dq_ref[to, cut])
            out_ref[rows, cut] = turned.astype(jnp.bfloat16)
        key = turn_back(over_heads(dk_ref))
        value = over_heads(dv_ref)
        pair = jnp.where(lanes(key) < HEAD, key, value)
        out_ref[rows, width : width + 128] = pair.astype(jnp.bfloat16)
        return carry

    lax.fori_loop(0, pieces, back, 0)


SMEM = pl.BlockSpec(memory_space=pltpu.SMEM)
VMEM = pl.BlockSpec(memory_space=pltpu.VMEM)
VMEM_LIMIT = 60 * 1024 * 1024


def attention_cost(width, products):
    flops = products * 2 * GROUP * (GROUP * 2 // 5) * width
    return pl.CostEstimate(
        flops=flops, bytes_accessed=16 * GROUP * width, transcendentals=GROUP * GROUP * width // 128
    )


def attention_forward(places, starts, raw, tables):
    width = raw.shape[1] - 2 * HEAD
    rows = raw.shape[0]
    kept = jax.ShapeDtypeStruct((rows, width), jnp.bfloat16)
    return pl.pallas_call(
        attention_forward_kernel,
        out_shape=[kept] * 4 + [jax.ShapeDtypeStruct((width // HEAD, 1, rows), jnp.float32)],
        in_specs=[SMEM, SMEM, VMEM, VMEM, VMEM],
        out_specs=[VMEM] * 5,
        scratch_shapes=[
            pltpu.VMEM((rows, width), jnp.bfloat16),
            pltpu.VMEM((HEAD, rows), jnp.bfloat16),
            pltpu.VMEM((width, TILE), jnp.float32),
        ],
        compiler_params=pltpu.CompilerParams(vmem_limit_bytes=VMEM_LIMIT),
        cost_estimate=attention_cost(width, 4),
        name="attention_forward",
    )(places, starts, raw, *tables)


def attention_backward(places, starts, out_grad, kept, tables, early):
    rows, width = out_grad.shape
    return pl.pallas_call(
        attention_backward_kernel,
        out_shape=jax.ShapeDtypeStruct((rows, width + 2 * HEAD), jnp.bfloat16),
        in_specs=[SMEM, SMEM] + [VMEM] * 7 + [ANY] * len(early),
        out_specs=VMEM,
        scratch_shapes=[
            pltpu.VMEM((rows, width), jnp.bfloat16),
            pltpu.VMEM((rows, width), jnp.float32),
            pltpu.VMEM((rows, width), jnp.float32),
            pltpu.VMEM((rows, width), jnp.float32),
            pltpu.VMEM((HEAD, rows), jnp.bfloat16),
            pltpu.VMEM((width, TILE), jnp.float32),
        ],
        compiler_params=pltpu.CompilerParams(vmem_limit_bytes=VMEM_LIMIT),
        cost_estimate=attention_cost(width, 10),
        name="attention_backward",
    )(places, starts, out_grad, *kept, *tables, *early)


MESH = pl.DeviceIdType.MESH
ANY = pl.BlockSpec(memory_space=pl.ANY)
CHUNKS = 4
SLAB = 16


def lasting(microseconds):
    return pl.CostEstimate(
        flops=0, bytes_accessed=int(microseconds * 3_000_000), transcendentals=0
    )


class Plane:
    def __init__(self, sent, landed, diagonal=False, entered=False):
        self.sent, self.landed = sent, landed
        self.copies = []
        self.rank = lax.axis_index("context")
        self.core = lax.axis_index("tensor")
        self.at_x = self.rank + 1 - 2 * lax.rem(self.rank, 2)
        self.at_y = lax.rem(self.rank + 2, 4)
        self.at_both = 3 - self.rank
        self.x = {"context": self.at_x}
        self.y = {"context": self.at_y}
        self.both = {"context": self.at_both}
        self.sibling = {"tensor": 1 - self.core}
        if entered:
            return
        barrier = pltpu.get_barrier_semaphore()
        partners = [self.x, self.y, self.sibling] + ([self.both] if diagonal else [])
        for partner in partners:
            pl.semaphore_signal(barrier, inc=1, device_id=partner, device_id_type=MESH)
        pl.semaphore_wait(barrier, len(partners))

    def copy(self, number, source, target, partner):
        return pltpu.make_async_remote_copy(
            src_ref=source,
            dst_ref=target,
            send_sem=self.sent.at[number],
            recv_sem=self.landed.at[number],
            device_id=partner,
            device_id_type=MESH,
        )

    def send(self, source, target, partner):
        number = len(self.copies)
        started = self.copy(number, source, target, partner)
        started.start()
        self.copies.append(started)
        return number

    def arrive(self, number, target):
        self.copy(number, target, target, self.sibling).wait_recv()

    def finish(self):
        for started in self.copies:
            started.wait_send()


def chunk(index, rows):
    return pl.ds(index * (rows // CHUNKS), rows // CHUNKS)


class Gather:
    def __init__(self, plane, block, out):
        self.plane, self.block, self.out = plane, block, out
        self.rows = block.shape[0]
        self.to_x, self.to_y, self.across, self.onward = {}, {}, {}, {}

    def start(self, k):
        p, cut = self.plane, chunk(k, self.rows)
        target = self.out.at[p.rank, p.core, cut]
        self.to_x[k] = p.send(self.block.at[cut], target, p.x)
        self.to_y[k] = p.send(self.block.at[cut], target, p.y)
        self.across[0, k] = p.send(self.block.at[cut], target, p.sibling)

    def forward_chunk(self, k):
        p, out = self.plane, self.out
        cut = chunk(k, self.rows)
        from_x, from_y = out.at[p.at_x, p.core, cut], out.at[p.at_y, p.core, cut]
        p.arrive(self.to_x[k], from_x)
        if k < CHUNKS // 2:
            self.onward[k] = p.send(from_x, from_x, p.y)
        self.across[1, k] = p.send(from_x, from_x, p.sibling)
        p.arrive(self.to_y[k], from_y)
        if k >= CHUNKS // 2:
            self.onward[k] = p.send(from_y, from_y, p.x)
        self.across[2, k] = p.send(from_y, from_y, p.sibling)

    def forward_far(self):
        p = self.plane
        for k in range(CHUNKS):
            far = self.out.at[p.at_both, p.core, chunk(k, self.rows)]
            p.arrive(self.onward[k], far)
            self.across[3, k] = p.send(far, far, p.sibling)

    def forward(self):
        for k in range(CHUNKS):
            self.forward_chunk(k)
        self.forward_far()

    def finish(self):
        p = self.plane
        for i, rank in enumerate((p.rank, p.at_x, p.at_y, p.at_both)):
            for k in range(CHUNKS):
                p.arrive(
                    self.across[i, k], self.out.at[rank, 1 - p.core, chunk(k, self.rows)]
                )


GATHER_COPIES = CHUNKS * 8


def add_rows(target, source, first, count):
    def step(i, carry):
        rows = pl.ds(first + i * SLAB, SLAB)
        target[rows, :] = (
            target[rows, :].astype(jnp.float32) + source[rows, :].astype(jnp.float32)
        ).astype(jnp.bfloat16)
        return carry

    lax.fori_loop(0, count // SLAB, step, 0)


class Scatter:
    def __init__(
        self, plane, rows_in, weights, columns, given, held, other, near_x, near_y, far_x, far_y
    ):
        p = self.plane = plane
        rows = near_x.shape[0]
        half = rows // 2
        halves = top, low = pl.ds(0, half), pl.ds(half, half)
        order = (p.at_both, p.at_x, p.at_y, p.rank)
        across = {}

        def make(i, h):
            for core, target in ((1 - p.core, given), (p.core, held)):
                value = dot(rows_in[order[i], core, halves[h], :], weights[:, columns], LAST)
                target[i, halves[h], :] = value.astype(jnp.bfloat16)
                if target is given:
                    source = given.at[i, halves[h]]
                    across[i, h] = p.send(source, other.at[i, halves[h]], p.sibling)

        def pair(i, h):
            p.arrive(across[i, h], other.at[i, halves[h]])
            add_rows(held.at[i], other.at[i], h * half, half)

        make(0, 0)
        make(0, 1)
        pair(0, 0)
        first = p.send(held.at[0, top], far_x, p.x)
        make(1, 0)
        pair(0, 1)
        second = p.send(held.at[0, low], far_y, p.y)
        make(2, 0)
        pair(1, 0)
        third = p.send(held.at[1, top], near_x.at[top], p.x)
        make(1, 1)
        make(2, 1)
        make(3, 0)
        make(3, 1)
        pair(2, 0)
        pair(1, 1)
        pair(2, 1)
        p.arrive(first, far_x)
        add_rows(held.at[2], far_x, 0, half)
        fourth = p.send(held.at[2, top], near_y.at[top], p.y)
        p.arrive(second, far_y)

        def step(i, carry):
            rows, at = pl.ds(half + i * SLAB, SLAB), pl.ds(i * SLAB, SLAB)
            held[1, rows, :] = (
                held[1, rows, :].astype(jnp.float32) + far_y[at, :].astype(jnp.float32)
            ).astype(jnp.bfloat16)
            return carry

        lax.fori_loop(0, half // SLAB, step, 0)
        fifth = p.send(held.at[1, low], near_x.at[low], p.x)
        sixth = p.send(held.at[2, low], near_y.at[low], p.y)
        pair(3, 0)
        pair(3, 1)
        self.halves = halves
        self.from_x, self.from_y = (third, fifth), (fourth, sixth)
        self.parts = (held.at[3], near_x, near_y)

    def ready(self, h):
        _, near_x, near_y = self.parts
        self.plane.arrive(self.from_x[h], near_x.at[self.halves[h]])
        self.plane.arrive(self.from_y[h], near_y.at[self.halves[h]])

    def rows(self, rows):
        return sum(part[rows, :].astype(jnp.float32) for part in self.parts)


SCATTER_COPIES = 8 + 6


def scatter_scratch(share, width):
    kind = jnp.bfloat16
    return [
        pltpu.VMEM((4, share, width), kind),
        pltpu.VMEM((4, share, width), kind),
        pltpu.VMEM((4, share, width), kind),
        pltpu.VMEM((share, width), kind),
        pltpu.VMEM((share, width), kind),
        pltpu.VMEM((share // 2, width), kind),
        pltpu.VMEM((share // 2, width), kind),
    ]


def wires(count):
    return [pltpu.SemaphoreType.DMA((count,)), pltpu.SemaphoreType.DMA((count,))]


def row_root(values):
    return lax.rsqrt(jnp.mean(values * values, axis=-1, keepdims=True) + epsilon)


def slabs(first, count, work):
    def step(i, carry):
        work(pl.ds(first + i * SLAB, SLAB))
        return carry

    lax.fori_loop(0, count // SLAB, step, 0)


class Exchange:
    def __init__(self, plane, source, target, local, first=0, columns=None):
        p = plane
        columns = columns or target.shape[2]

        def part(rank):
            return source.at[:, pl.ds(pl.multiple_of(rank * columns, 128), columns)]

        def place(rank):
            return target.at[rank, :, pl.ds(first, columns)]

        self.plane, self.place, self.moves = p, place, []
        self.mine = pltpu.make_async_copy(part(p.rank), place(p.rank), local)
        self.mine.start()
        for partner, rank in ((p.both, p.at_both), (p.x, p.at_x), (p.y, p.at_y)):
            self.moves.append((p.send(part(rank), place(p.rank), partner), rank))

    def finish(self):
        for number, rank in self.moves:
            self.plane.arrive(number, self.place(rank))
        self.mine.wait()


def first_kernel(query, pair, out_turned, gains, packed, gains_out, sent, landed, local, far_sent, far_landed):
    groups = lax.axis_size("fsdp")
    group, rank = lax.axis_index("fsdp"), lax.axis_index("context")
    depth = gains.shape[1]
    others = [(i, j) for i in range(groups) for j in range(4) if i or j]

    def device(i, j):
        return {"fsdp": lax.rem(group + i, groups), "context": lax.rem(rank + j, 4)}

    def place(f, c):
        return gains_out.at[:, pl.ds(pl.multiple_of((f * 4 + c) * depth, 128), depth)]

    barrier = pltpu.get_barrier_semaphore()
    for i, j in others:
        pl.semaphore_signal(barrier, inc=1, device_id=device(i, j), device_id_type=MESH)
    pl.semaphore_wait(barrier, len(others))
    p = Plane(sent, landed, entered=True)
    width = query.shape[1] // 4
    exchanges = [
        Exchange(p, query, packed, local.at[0], 0, width),
        Exchange(p, pair, packed, local.at[1], width, 128),
        Exchange(p, out_turned, packed, local.at[2], width + 128, width),
    ]
    far = []
    for n, (i, j) in enumerate(others):
        far.append(
            pltpu.make_async_remote_copy(
                src_ref=gains,
                dst_ref=place(group, rank),
                send_sem=far_sent.at[n],
                recv_sem=far_landed.at[n],
                device_id=device(i, j),
                device_id_type=MESH,
            )
        )
        far[n].start()
    gains_out[:, pl.ds(pl.multiple_of((group * 4 + rank) * depth, 128), depth)] = gains[...]
    for started in far:
        started.wait()
    for exchange in exchanges:
        exchange.finish()
    p.finish()


def first_exchange(query, pair, out_turned, gains):
    depth, columns = query.shape
    groups = lax.axis_size("fsdp")
    far = groups * 4 - 1
    return pl.pallas_call(
        first_kernel,
        out_shape=[
            jax.ShapeDtypeStruct((4, depth, columns // 2 + 128), query.dtype),
            jax.ShapeDtypeStruct((8, groups * 4 * depth), jnp.float32),
        ],
        in_specs=[VMEM] * 4,
        out_specs=[ANY, VMEM],
        scratch_shapes=wires(9) + [pltpu.SemaphoreType.DMA((3,))] + wires(far),
        compiler_params=pltpu.CompilerParams(collective_id=9, has_side_effects=True),
        cost_estimate=lasting(10),
        name="first_exchange",
    )(query, pair, out_turned, gains)


def start_kernel(tokens, cotangent, early, out, scaled, my_scaled, sent, landed, local):
    p = Plane(sent, landed)
    share = my_scaled.shape[0]
    block = tokens.at[pl.ds(pl.multiple_of(p.core * share, SLAB), share)]
    gather = Gather(p, block, out)
    mine = pltpu.make_async_copy(block, out.at[p.rank, p.core], local)
    for k in range(CHUNKS):
        gather.start(k)
    mine.start()

    def scale(rows):
        value = residual_scale * cotangent[rows, :].astype(jnp.float32)
        scaled[rows, :] = value.astype(jnp.bfloat16)

    def keep(rows):
        from_rows = pl.ds(pl.multiple_of(p.core * share + rows.start, SLAB), SLAB)
        my_scaled[rows, :] = scaled[from_rows, :]

    slabs(0, scaled.shape[0], scale)
    slabs(0, share, keep)
    gather.forward()
    gather.finish()
    p.finish()
    mine.wait()


def start_plane(tokens, cotangent, early):
    share, width = tokens.shape[0] // 2, tokens.shape[1]
    return pl.pallas_call(
        start_kernel,
        out_shape=[
            jax.ShapeDtypeStruct((4, 2, share, width), tokens.dtype),
            jax.ShapeDtypeStruct(cotangent.shape, jnp.bfloat16),
            jax.ShapeDtypeStruct((share, width), jnp.bfloat16),
        ],
        in_specs=[VMEM, VMEM, ANY],
        out_specs=[ANY, VMEM, VMEM],
        scratch_shapes=wires(GATHER_COPIES) + [pltpu.SemaphoreType.DMA],
        compiler_params=pltpu.CompilerParams(
            collective_id=1, has_side_effects=True, vmem_limit_bytes=VMEM_LIMIT
        ),
        cost_estimate=lasting(60),
        name="gather_tokens",
    )(tokens, cotangent, early)


def columns_kernel(gate, up, down, early, both_out, down_out, sent, landed, local):
    p = Plane(sent, landed, diagonal=True)
    units = down_out.shape[2]
    exchanges = [
        Exchange(p, gate, both_out, local.at[0], 0, units),
        Exchange(p, up, both_out, local.at[1], units, units),
        Exchange(p, down, down_out, local.at[2]),
    ]
    for exchange in exchanges:
        exchange.finish()
    p.finish()


def exchange_columns(gate, up, down, early):
    depth, units = gate.shape
    return pl.pallas_call(
        columns_kernel,
        out_shape=[
            jax.ShapeDtypeStruct((4, depth, units // 2), gate.dtype),
            jax.ShapeDtypeStruct((4, depth, units // 4), gate.dtype),
        ],
        in_specs=[VMEM] * 3 + [ANY],
        out_specs=[ANY] * 2,
        scratch_shapes=wires(9) + [pltpu.SemaphoreType.DMA((3,))],
        compiler_params=pltpu.CompilerParams(collective_id=10, has_side_effects=True),
        cost_estimate=lasting(30),
        name="exchange_columns",
    )(gate, up, down, early)


def middle_kernel(
    attended,
    weights,
    gain,
    tokens,
    beside,
    from_x,
    from_y,
    from_both,
    hidden,
    middle,
    beside_out,
    sent,
    landed,
    local,
    residual,
    held_beside,
    held_blocks,
    *scratch,
):
    p = Plane(sent, landed)
    blocks = ((from_x, p.at_x), (from_y, p.at_y), (from_both, p.at_both))
    loads = [pltpu.make_async_copy(beside, held_beside, local.at[0])]
    for i, (block, rank) in enumerate(blocks):
        loads.append(pltpu.make_async_copy(block, held_blocks.at[i], local.at[i + 1]))
    share = hidden.shape[0]
    first = pl.ds(pl.multiple_of(p.core * share, SLAB), share)
    loads.append(pltpu.make_async_copy(tokens.at[first], residual, local.at[4]))
    for started in loads:
        started.start()
    width = attended.shape[3]
    columns = slice(weights.shape[1] - width, weights.shape[1])
    total = Scatter(p, attended, weights, columns, *scratch)
    kept, across = [], []
    loads[0].wait()
    kept.append(pltpu.make_async_copy(held_beside, beside_out.at[p.rank], local.at[0]))
    kept[0].start()
    for i, (block, rank) in enumerate(blocks):
        loads[i + 1].wait()
        place = beside_out.at[rank, p.core]
        kept.append(pltpu.make_async_copy(held_blocks.at[i], place, local.at[i + 1]))
        kept[i + 1].start()
        across.append(p.send(held_blocks.at[i], place, p.sibling))
    loads[4].wait()

    def work(rows):
        value = residual[rows, :].astype(jnp.float32) + residual_scale * total.rows(rows)
        middle[rows, :] = value
        hidden[rows, :] = (value * row_root(value) * gain[1:2, :]).astype(jnp.bfloat16)

    for h in range(2):
        total.ready(h)
        slabs(h * (share // 2), share // 2, work)
    for number, rank in zip(across, (p.at_x, p.at_y, p.at_both)):
        p.arrive(number, beside_out.at[rank, 1 - p.core])
    p.finish()
    for started in kept:
        started.wait()


def middle_plane(attended, weights, tokens, gain, beside, blocks):
    share, width = blocks[0].shape
    full = jax.ShapeDtypeStruct((4, 2, share, width), jnp.bfloat16)
    hidden, middle, beside_out = pl.pallas_call(
        middle_kernel,
        out_shape=[
            jax.ShapeDtypeStruct((share, width), jnp.bfloat16),
            jax.ShapeDtypeStruct((share, width), jnp.float32),
            full,
        ],
        in_specs=[VMEM] * 3 + [ANY] * 5,
        out_specs=[VMEM, VMEM, ANY],
        scratch_shapes=wires(SCATTER_COPIES + 3)
        + [
            pltpu.SemaphoreType.DMA((5,)),
            pltpu.VMEM((share, width), jnp.bfloat16),
            pltpu.VMEM((2, share, width), jnp.bfloat16),
            pltpu.VMEM((3, share, width), jnp.bfloat16),
        ]
        + scatter_scratch(share, width),
        compiler_params=pltpu.CompilerParams(
            collective_id=2, has_side_effects=True, vmem_limit_bytes=VMEM_LIMIT
        ),
        cost_estimate=lasting(55),
        name="middle_rows",
    )(
        attended.reshape(4, 2, share, -1),
        weights,
        gain,
        tokens,
        beside.reshape(2, share, width),
        *blocks,
    )
    return hidden, middle, beside_out.reshape(8 * share, width)


def ffn_rows_kernel(
    block,
    weights_in,
    out,
    m,
    gate,
    up,
    sent,
    landed,
    local,
    loading,
    storing,
    weights,
    rows_in,
    m_held,
    gate_held,
    up_held,
):
    p = Plane(sent, landed)
    gather = Gather(p, block, out)
    for k in range(CHUNKS):
        gather.start(k)
    weights_load = pltpu.make_async_copy(weights_in, weights, local.at[0])
    weights_load.start()
    mine = pltpu.make_async_copy(block, out.at[p.rank, p.core], local.at[1])
    mine.start()
    units = m.shape[3]
    stores = []

    def load(n, rank, core):
        return pltpu.make_async_copy(out.at[rank, core], rows_in.at[n % 2], loading.at[n % 2])

    def compute(n, rank, core, source):
        slot = n % 2
        if n >= 2:
            for started in stores[n - 2]:
                started.wait()

        def step(j, carry):
            cut = pl.ds(pl.multiple_of(j * 256, 256), 256)
            beyond = pl.ds(pl.multiple_of(units + j * 256, 256), 256)
            gate_part = dot(source[...], weights[:, cut])
            up_part = dot(source[...], weights[:, beyond])
            gate_held[slot, :, cut] = gate_part.astype(jnp.bfloat16)
            up_held[slot, :, cut] = up_part.astype(jnp.bfloat16)
            sigmoid = 1.0 / (1.0 + jnp.exp(-gate_part))
            m_held[slot, :, cut] = (gate_part * sigmoid * up_part).astype(jnp.bfloat16)
            return carry

        lax.fori_loop(0, units // 256, step, 0)
        stores.append(
            [
                pltpu.make_async_copy(held.at[slot], target.at[rank, core], storing.at[slot, i])
                for i, (held, target) in enumerate(((m_held, m), (gate_held, gate), (up_held, up)))
            ]
        )
        for started in stores[n]:
            started.start()

    def from_sibling(i, rank):
        for k in range(CHUNKS):
            p.arrive(
                gather.across[i, k], out.at[rank, 1 - p.core, chunk(k, gather.rows)]
            )

    weights_load.wait()
    compute(0, p.rank, p.core, block)
    gather.forward_chunk(0)
    from_sibling(0, p.rank)
    load(1, p.rank, 1 - p.core).start()
    load(1, p.rank, 1 - p.core).wait()
    compute(1, p.rank, 1 - p.core, rows_in.at[1])
    for k in range(1, CHUNKS):
        gather.forward_chunk(k)
    load(2, p.at_x, p.core).start()
    load(3, p.at_y, p.core).start()
    load(2, p.at_x, p.core).wait()
    compute(2, p.at_x, p.core, rows_in.at[0])
    from_sibling(1, p.at_x)
    load(4, p.at_x, 1 - p.core).start()
    load(3, p.at_y, p.core).wait()
    compute(3, p.at_y, p.core, rows_in.at[1])
    from_sibling(2, p.at_y)
    load(5, p.at_y, 1 - p.core).start()
    load(4, p.at_x, 1 - p.core).wait()
    compute(4, p.at_x, 1 - p.core, rows_in.at[0])
    gather.forward_far()
    load(6, p.at_both, p.core).start()
    load(5, p.at_y, 1 - p.core).wait()
    compute(5, p.at_y, 1 - p.core, rows_in.at[1])
    from_sibling(3, p.at_both)
    load(7, p.at_both, 1 - p.core).start()
    load(6, p.at_both, p.core).wait()
    compute(6, p.at_both, p.core, rows_in.at[0])
    load(7, p.at_both, 1 - p.core).wait()
    compute(7, p.at_both, 1 - p.core, rows_in.at[1])
    p.finish()
    mine.wait()
    for n in (6, 7):
        for started in stores[n]:
            started.wait()


def ffn_rows(block, weights):
    share, width = block.shape
    units = weights.shape[1] // 2
    kind = jnp.bfloat16
    full = jax.ShapeDtypeStruct((4, 2, share, width), kind)
    part = jax.ShapeDtypeStruct((4, 2, share, units), kind)
    held = pltpu.VMEM((2, share, units), kind)
    outs = pl.pallas_call(
        ffn_rows_kernel,
        out_shape=[full, part, part, part],
        in_specs=[VMEM, ANY],
        out_specs=[ANY] * 4,
        scratch_shapes=wires(GATHER_COPIES)
        + [
            pltpu.SemaphoreType.DMA((2,)),
            pltpu.SemaphoreType.DMA((2,)),
            pltpu.SemaphoreType.DMA((2, 3)),
            pltpu.VMEM(weights.shape, kind),
            pltpu.VMEM((2, share, width), kind),
            held,
            held,
            held,
        ],
        compiler_params=pltpu.CompilerParams(
            collective_id=11, has_side_effects=True, vmem_limit_bytes=VMEM_LIMIT
        ),
        cost_estimate=lasting(60),
        name="ffn_rows",
    )(block, weights)
    return [array.reshape(8 * share, -1) for array in outs]


class WeightTiles:
    def __init__(self, rows, slopes, target, rows_in, tile_out, wires_in):
        self.rows, self.slopes, self.target = rows, slopes, target
        self.rows_in, self.tile_out, self.wires = rows_in, tile_out, wires_in
        self.count = rows.shape[1] // TILE
        self.load(0, 0).start()

    def load(self, d, slot):
        columns = pl.ds(pl.multiple_of(d * TILE, TILE), TILE)
        return pltpu.make_async_copy(
            self.rows.at[:, columns], self.rows_in.at[slot], self.wires.at[0, slot]
        )

    def store(self, d, slot):
        columns = pl.ds(pl.multiple_of(d * TILE, TILE), TILE)
        return pltpu.make_async_copy(
            self.tile_out.at[slot], self.target.at[columns], self.wires.at[1, slot]
        )

    def run(self, first, last):
        def step(d, carry):
            slot = lax.rem(d, 2)
            self.load(d, slot).wait()

            @pl.when(d < self.count - 1)
            def _():
                self.load(d + 1, 1 - slot).start()

            @pl.when(d >= 2)
            def _():
                self.store(d - 2, slot).wait()

            self.tile_out[slot] = dot(self.rows_in[slot], self.slopes[...], FIRST).astype(
                jnp.bfloat16
            )
            self.store(d, slot).start()
            return carry

        lax.fori_loop(first, last, step, 0)

    def finish(self):
        for d in (self.count - 2, self.count - 1):
            self.store(d, d % 2).wait()


def tile_scratch(count, units):
    return [
        pltpu.SemaphoreType.DMA((2, 2)),
        pltpu.VMEM((2, count, TILE), jnp.bfloat16),
        pltpu.VMEM((2, TILE, units), jnp.bfloat16),
    ]


UNITS = ((0, 0), (0, 1), (1, 0), (2, 0), (1, 1), (2, 1), (3, 0), (3, 1))


def second_kernel(
    slopes,
    normed_rows,
    weights_in,
    middle_in,
    cotangent_in,
    gain,
    early,
    grad_middle,
    hidden,
    weight_grads,
    sent,
    landed,
    loading,
    beside,
    weights,
    middle,
    cotangent,
    tile_wires,
    rows_in,
    tile_out,
    gate_in,
    up_in,
    given,
    held,
    other,
    near_x,
    near_y,
    far_x,
    far_y,
):
    share, width = near_x.shape
    cuts = [slice(j * 512, j * 512 + 512) for j in range(width // 512)]
    weight_loads = [
        pltpu.make_async_copy(weights_in.at[cut], weights.at[cut], beside.at[2 + j])
        for j, cut in enumerate(cuts)
    ]
    for started in weight_loads:
        started.start()
    p = Plane(sent, landed)
    half = share // 2
    order = (p.at_both, p.at_x, p.at_y, p.rank)
    top, low = halves = pl.ds(0, half), pl.ds(half, half)

    def places(u):
        i, h = UNITS[u]
        for core in (1 - p.core, p.core):
            row = (order[i] * 2 + core) * share + h * half
            yield pl.ds(pl.multiple_of(row, 32), half)

    units = gate_in.shape[1]

    def loads(u):
        for j, rows in enumerate(places(u)):
            for n, target in enumerate((gate_in, up_in)):
                yield pltpu.make_async_copy(
                    slopes.at[rows, pl.ds(n * units, units)],
                    target.at[rows],
                    loading.at[u, 2 * j + n],
                )

    def compute(u):
        i, h = UNITS[u]
        slot = u % 2
        gate_rows = jnp.concatenate([gate_in[rows, :] for rows in places(u)], axis=0)
        up_rows = jnp.concatenate([up_in[rows, :] for rows in places(u)], axis=0)
        for j, cut in enumerate(cuts):
            if u == 0:
                weight_loads[j].wait()
            back = dot(gate_rows, weights[cut, :units], LAST) + dot(
                up_rows, weights[cut, units:], LAST
            )
            given[slot, :, cut] = back[:half].astype(jnp.bfloat16)
            held[i, halves[h], cut] = back[half:].astype(jnp.bfloat16)

    first = pl.ds(pl.multiple_of(p.core * share, SLAB), share)
    row_loads = [
        pltpu.make_async_copy(middle_in, middle, beside.at[0]),
        pltpu.make_async_copy(cotangent_in.at[first], cotangent, beside.at[1]),
    ]
    tiles = WeightTiles(normed_rows, gate_in, weight_grads, rows_in, tile_out, tile_wires)

    moves, across = {}, {}
    moves, across = {}, {}

    def settle(u):
        i, h = UNITS[u]
        p.arrive(across[u], other.at[i, halves[h]])
        add_rows(held.at[i], other.at[i], h * half, half)
        if u == 0:
            moves["far_x"] = p.send(held.at[0, top], far_x, p.x)
        elif u == 1:
            moves["far_y"] = p.send(held.at[0, low], far_y, p.y)
        elif u == 2:
            moves["x", 0] = p.send(held.at[1, top], near_x.at[top], p.x)
        elif u == 3:
            p.arrive(moves["far_x"], far_x)
            add_rows(held.at[2], far_x, 0, half)
            moves["y", 0] = p.send(held.at[2, top], near_y.at[top], p.y)
        elif u == 4:
            p.arrive(moves["far_y"], far_y)

            def step(k, carry):
                rows, at = pl.ds(half + k * SLAB, SLAB), pl.ds(k * SLAB, SLAB)
                held[1, rows, :] = (
                    held[1, rows, :].astype(jnp.float32) + far_y[at, :].astype(jnp.float32)
                ).astype(jnp.bfloat16)
                return carry

            lax.fori_loop(0, half // SLAB, step, 0)
            moves["x", 1] = p.send(held.at[1, low], near_x.at[low], p.x)
        elif u == 5:
            moves["y", 1] = p.send(held.at[2, low], near_y.at[low], p.y)

    for u in range(8):
        for started in loads(u):
            started.start()

    def unit(u):
        if u >= 2:
            p.copies[across[u - 2]].wait_send()
        compute(u)
        i, h = UNITS[u]
        across[u] = p.send(given.at[u % 2], other.at[i, halves[h]], p.sibling)

    def wait_loads(units_here):
        for u in units_here:
            for started in loads(u):
                started.wait()

    for started in row_loads:
        started.start()
    wait_loads((0,))
    unit(0)
    wait_loads((1,))
    unit(1)
    settle(0)
    wait_loads((2, 3))
    unit(2)
    settle(1)
    unit(3)
    settle(2)
    wait_loads((4, 5, 6, 7))
    unit(4)
    tiles.run(0, 2)
    settle(3)
    unit(5)
    settle(4)
    unit(6)
    settle(5)
    unit(7)
    settle(6)
    settle(7)
    tiles.run(2, tiles.count)

    def work(rows):
        value = middle[rows, :]
        root = row_root(value)
        normed = value * root
        total = sum(part[rows, :].astype(jnp.float32) for part in (held.at[3], near_x, near_y))
        slope = total * gain[1:2, :]
        mean = jnp.mean(slope * normed, axis=-1, keepdims=True)
        gradient = cotangent[rows, :].astype(jnp.float32) + root * (slope - normed * mean)
        grad_middle[rows, :] = gradient
        hidden[rows, :] = (residual_scale * gradient).astype(jnp.bfloat16)

    for started in row_loads:
        started.wait()
    for h in range(2):
        p.arrive(moves["x", h], near_x.at[halves[h]])
        p.arrive(moves["y", h], near_y.at[halves[h]])
        slabs(h * half, half, work)
    for u in (6, 7):
        p.copies[across[u]].wait_send()
    tiles.finish()
    for number, started in enumerate(p.copies):
        if number not in across.values():
            started.wait_send()


def second_plane(slopes, normed_rows, weights, middle, cotangent, gain, early):
    share, width = middle.shape
    count, units = slopes.shape[0], slopes.shape[1] // 2
    kind = jnp.bfloat16
    half = share // 2
    quarter = pltpu.VMEM((4, share, width), kind)
    return pl.pallas_call(
        second_kernel,
        out_shape=[
            jax.ShapeDtypeStruct((share, width), jnp.float32),
            jax.ShapeDtypeStruct((share, width), kind),
            jax.ShapeDtypeStruct((width, units), kind),
        ],
        in_specs=[ANY] * 5 + [VMEM, ANY],
        out_specs=[VMEM, VMEM, ANY],
        scratch_shapes=wires(8 + 6)
        + [
            pltpu.SemaphoreType.DMA((8, 4)),
            pltpu.SemaphoreType.DMA((2 + width // 512,)),
            pltpu.VMEM(weights.shape, kind),
            pltpu.VMEM((share, width), jnp.float32),
            pltpu.VMEM((share, width), kind),
        ]
        + tile_scratch(count, units)
        + [
            pltpu.VMEM((count, units), kind),
            pltpu.VMEM((count, units), kind),
            pltpu.VMEM((2, half, width), kind),
            quarter,
            quarter,
            pltpu.VMEM((share, width), kind),
            pltpu.VMEM((share, width), kind),
            pltpu.VMEM((half, width), kind),
            pltpu.VMEM((half, width), kind),
        ],
        compiler_params=pltpu.CompilerParams(
            collective_id=3, has_side_effects=True, vmem_limit_bytes=60 * 1024 * 1024
        ),
        cost_estimate=lasting(60),
        name="second_rows",
    )(slopes, normed_rows, weights, middle, cotangent, gain, early)


def spread_kernel(
    hidden, m, down_in, normed_rows, slopes, early, out, pair_own, pair_x, pair_y, pair_both,
    weight_grads, sent, landed, local, loading, tile_wires, rows_in, tile_out, up_in,
    m_in, given, held, theirs, down_w,
):
    p = Plane(sent, landed)
    share, width = hidden.shape
    gather = Gather(p, hidden, out)
    for k in range(CHUNKS):
        gather.start(k)
    mine = pltpu.make_async_copy(hidden, out.at[p.rank, p.core], local.at[4])
    mine.start()
    order = (p.rank, p.at_x, p.at_y, p.at_both)
    halves = pl.ds(0, share), pl.ds(share, share)

    def loads(i):
        for j, core in enumerate((1 - p.core, p.core)):
            yield pltpu.make_async_copy(
                m.at[order[i], core], m_in.at[i % 2, halves[j]], loading.at[i % 2, j]
            )

    across = []
    units = up_in.shape[1]
    up_load = pltpu.make_async_copy(slopes.at[:, pl.ds(units, units)], up_in, local.at[5])
    down_load = pltpu.make_async_copy(down_in, down_w, local.at[6])
    down_load.start()
    up_load.start()
    for started in loads(0):
        started.start()
    down_load.wait()
    tiles = WeightTiles(normed_rows, up_in, weight_grads, rows_in, tile_out, tile_wires)
    for i in range(4):
        for started in loads(i):
            started.wait()
        if i < 3:
            for started in loads(i + 1):
                started.start()

        def step(j, carry, i=i):
            cut = pl.ds(pl.multiple_of(j * 512, 512), 512)
            value = dot(m_in[i % 2], down_w[cut, :], LAST)
            given[i, :, cut] = value[:share].astype(jnp.bfloat16)
            held[i, :, cut] = value[share:].astype(jnp.bfloat16)
            return carry

        lax.fori_loop(0, width // 512, step, 0)
        across.append(p.send(given.at[i], theirs.at[i], p.sibling))
        if i == 0:
            up_load.wait()
        gather.forward_chunk(i)
        tiles.run(i, i + 1)
    kept = []
    for i in range(4):
        p.arrive(across[i], theirs.at[i])
        add_rows(held.at[i], theirs.at[i], 0, share)
        target = (pair_own, pair_x, pair_y, pair_both)[i]
        kept.append(pltpu.make_async_copy(held.at[i], target, local.at[i]))
        kept[i].start()
    gather.forward_far()
    tiles.run(4, tiles.count)
    tiles.finish()
    gather.finish()
    p.finish()
    mine.wait()
    for started in kept:
        started.wait()


def spread_plane(hidden, m, down_w, normed_rows, slopes, early):
    share, width = hidden.shape
    units = m.shape[1]
    full = jax.ShapeDtypeStruct((4, 2, share, width), jnp.bfloat16)
    quarter = pltpu.VMEM((4, share, width), jnp.bfloat16)
    out, *pairs, weight_grads = pl.pallas_call(
        spread_kernel,
        out_shape=[full]
        + [jax.ShapeDtypeStruct((share, width), jnp.bfloat16)] * 4
        + [jax.ShapeDtypeStruct((width, units), jnp.bfloat16)],
        in_specs=[VMEM] + [ANY] * 5,
        out_specs=[ANY] * 6,
        scratch_shapes=wires(GATHER_COPIES + 4)
        + [
            pltpu.SemaphoreType.DMA((7,)),
            pltpu.SemaphoreType.DMA((2, 2)),
        ]
        + tile_scratch(8 * share, units)
        + [
            pltpu.VMEM((8 * share, units), jnp.bfloat16),
            pltpu.VMEM((2, 2 * share, units), jnp.bfloat16),
            quarter,
            quarter,
            quarter,
            pltpu.VMEM(down_w.shape, jnp.bfloat16),
        ],
        compiler_params=pltpu.CompilerParams(
            collective_id=7, has_side_effects=True, vmem_limit_bytes=60 * 1024 * 1024
        ),
        cost_estimate=lasting(60),
        name="spread_rows",
    )(hidden, m.reshape(4, 2, share, units), down_w, normed_rows, slopes, early)
    return out.reshape(8 * share, width), pairs, weight_grads


def lane_sums(pairs):
    total = 0.0
    for a, b in pairs:
        product = a.astype(jnp.float32) * b.astype(jnp.float32)
        total += jnp.sum(product, axis=1, keepdims=True)
    return jnp.broadcast_to(total, (total.shape[0], 128))


LATER = 10


def last_kernel(
    back,
    weights,
    gain,
    ups,
    early,
    *rest,
):
    later, rest = rest[:LATER], rest[LATER:]
    out, result_out, up_out, gain_out, sent, landed, local, loading, held, result, sums = rest[:11]
    landing, scratch = rest[11 : 11 + LATER], rest[11 + LATER :]
    share = landing[8].shape[0]
    first = pl.ds(pl.multiple_of(lax.axis_index("tensor") * share, SLAB), share)
    later = [*later[:8], later[8].at[first], later[9]]
    loads = [
        pltpu.make_async_copy(source, target, loading.at[i])
        for i, (source, target) in enumerate(zip(later, landing))
    ]
    for started in loads:
        started.start()
    middle, ffn_own, ffn_x, ffn_y, ffn_both, gates, gate, up, residual, grad_middle = landing
    p = Plane(sent, landed, diagonal=True)
    total = Scatter(p, back, weights, slice(0, back.shape[3]), *scratch)
    moves = []
    for partner, rank in ((p.both, p.at_both), (p.x, p.at_x), (p.y, p.at_y)):
        moves.append((p.send(ups.at[rank], up_out.at[p.rank], partner), up_out.at[rank]))
    up_out[p.rank] = ups[p.rank]
    share = held.shape[0]

    def finish_result(rows):
        parts = (ffn_own, ffn_x, ffn_y, ffn_both)
        ffn = sum(part[rows, :].astype(jnp.float32) for part in parts)
        result[rows, :] = (middle[rows, :] + residual_scale * ffn).astype(jnp.bfloat16)

    for started in loads:
        started.wait()
    slabs(0, share, finish_result)
    kept = [pltpu.make_async_copy(result, result_out.at[p.core], local.at[0])]
    kept[0].start()
    given = p.send(result, result_out.at[p.core], p.sibling)
    units = gate.shape[1] // 4

    def gate_rows(rows):
        sums[0, rows, :] = lane_sums(
            [(gates[c, rows, :], gate[rows, c * units : c * units + units]) for c in range(4)]
        )

    def up_rows(rows):
        sums[0, rows, :] += lane_sums(
            [(up_out[c, rows, :], up[rows, c * units : c * units + units]) for c in range(4)]
        )

    slabs(0, gate.shape[0], gate_rows)

    def work(rows):
        value = residual[rows, :].astype(jnp.float32)
        root = row_root(value)
        normed = value * root
        slope = total.rows(rows) * gain[0:1, :]
        mean = jnp.mean(slope * normed, axis=-1, keepdims=True)
        held[rows, :] = grad_middle[rows, :] + root * (slope - normed * mean)

    across = []
    for k in range(CHUNKS):
        cut = chunk(k, share)
        if k % (CHUNKS // 2) == 0:
            total.ready(k // (CHUNKS // 2))
        slabs(k * (share // CHUNKS), share // CHUNKS, work)
        across.append(p.send(held.at[cut], out.at[p.core, cut], p.sibling))
    kept.append(pltpu.make_async_copy(held, out.at[p.core], local.at[1]))
    kept[1].start()
    for number, target in moves:
        p.arrive(number, target)
    slabs(0, gate.shape[0], up_rows)
    swapped = p.send(sums.at[0], sums.at[1], p.sibling)
    p.arrive(swapped, sums.at[1])
    gain_out[...] = sums[0] + sums[1]
    p.arrive(given, result_out.at[1 - p.core])
    for k in range(CHUNKS):
        p.arrive(across[k], out.at[1 - p.core, chunk(k, share)])
    p.finish()
    for started in kept:
        started.wait()


def last_plane(
    back, weights, tokens, grad_middle, gain, middle, ffn_parts, ups, gates, gate, up, early
):
    share, width = grad_middle.shape
    later = [middle, *ffn_parts, gates, gate, up, tokens, grad_middle]
    out, result_out, up_out, gain_out = pl.pallas_call(
        last_kernel,
        out_shape=[
            jax.ShapeDtypeStruct((2, share, width), jnp.float32),
            jax.ShapeDtypeStruct((2, share, width), jnp.bfloat16),
            jax.ShapeDtypeStruct(ups.shape, ups.dtype),
            jax.ShapeDtypeStruct((gate.shape[0], 128), jnp.float32),
        ],
        in_specs=[VMEM] * 4 + [ANY] * (1 + LATER),
        out_specs=[ANY, ANY, VMEM, VMEM],
        scratch_shapes=wires(CHUNKS + 5 + SCATTER_COPIES)
        + [
            pltpu.SemaphoreType.DMA((2,)),
            pltpu.SemaphoreType.DMA((LATER,)),
            pltpu.VMEM((share, width), jnp.float32),
            pltpu.VMEM((share, width), jnp.bfloat16),
            pltpu.VMEM((2, gate.shape[0], 128), jnp.float32),
        ]
        + [pltpu.VMEM(array.shape, array.dtype) for array in later[:8]]
        + [pltpu.VMEM((share, width), tokens.dtype), pltpu.VMEM((share, width), jnp.float32)]
        + scatter_scratch(share, width),
        compiler_params=pltpu.CompilerParams(
            collective_id=4, has_side_effects=True, vmem_limit_bytes=VMEM_LIMIT
        ),
        cost_estimate=lasting(70),
        name="last_rows",
    )(
        back.reshape(4, 2, share, -1),
        weights,
        gain,
        ups,
        early,
        *later,
    )
    return (
        out.reshape(2 * share, width),
        result_out.reshape(2 * share, width),
        up_out,
        gain_out,
    )


def exchange_kernel(blocks, query, pair, other_sums, out, gain_out, sent, landed, sums):
    p = Plane(sent, landed, diagonal=True)
    moves = []
    for partner, rank in ((p.both, p.at_both), (p.x, p.at_x), (p.y, p.at_y)):
        moves.append((p.send(blocks.at[rank], out.at[p.rank], partner), out.at[rank]))
    out[p.rank] = blocks[p.rank]
    width = query.shape[1] // 4

    def attention_rows(rows):
        pairs = []
        for c in range(4):
            pairs.append((out[c, rows, :width], query[rows, c * width : c * width + width]))
            pairs.append((out[c, rows, width : width + 128], pair[rows, c * 128 : c * 128 + 128]))
        sums[0, rows, :] = lane_sums(pairs)

    for number, target in moves:
        p.arrive(number, target)
    slabs(0, blocks.shape[1], attention_rows)
    swapped = p.send(sums.at[0], sums.at[1], p.sibling)
    p.arrive(swapped, sums.at[1])
    gain_out[0] = sums[0] + sums[1]
    gain_out[1] = other_sums[...]
    p.finish()


def exchange(blocks, query, pair, other_sums):
    depth = blocks.shape[1]
    return pl.pallas_call(
        exchange_kernel,
        out_shape=[
            jax.ShapeDtypeStruct(blocks.shape, blocks.dtype),
            jax.ShapeDtypeStruct((2, depth, 128), jnp.float32),
        ],
        in_specs=[VMEM] * 4,
        out_specs=[VMEM] * 2,
        scratch_shapes=wires(4) + [pltpu.VMEM((2, depth, 128), jnp.float32)],
        compiler_params=pltpu.CompilerParams(collective_id=5, has_side_effects=True),
        cost_estimate=lasting(8),
        name="exchange_blocks",
    )(blocks, query, pair, other_sums)


def finish_first_kernel(down, gate, down_out, gate_out):
    down_out[...] = jnp.transpose(down[0].astype(jnp.float32))
    gate_out[...] = gate[0].astype(jnp.float32)


def finish_first(down, gate):
    groups, depth, units = down.shape
    block = pl.BlockSpec((1, depth, units), lambda i: (i, 0, 0))
    return pl.pallas_call(
        finish_first_kernel,
        grid=(groups,),
        in_specs=[block, block],
        out_specs=[
            pl.BlockSpec((units, depth), lambda i: (i, 0)),
            pl.BlockSpec((depth, units), lambda i: (0, i)),
        ],
        out_shape=[
            jax.ShapeDtypeStruct((groups * units, depth), jnp.float32),
            jax.ShapeDtypeStruct((depth, groups * units), jnp.float32),
        ],
        compiler_params=pltpu.CompilerParams(vmem_limit_bytes=VMEM_LIMIT),
        cost_estimate=lasting(5),
        name="finish_first",
    )(down, gate)


def finish_kernel(
    attn, up, tokens, result, sums, gains,
    query_out, key_out, value_out, out_out, up_out, tokens_out, result_out, gain_out,
):
    width = query_out.shape[1]
    query_out[...] = attn[0, :, :width].astype(jnp.float32)
    for c in range(key_out.shape[1] // HEAD):

        @pl.when(pl.program_id(0) == c)
        def _(c=c):
            cut = slice(c * HEAD, c * HEAD + HEAD)
            key_out[:, cut] = attn[0, :, width : width + HEAD].astype(jnp.float32)
            value_out[:, cut] = attn[0, :, width + HEAD : width + 2 * HEAD].astype(jnp.float32)

    out_out[...] = jnp.transpose(attn[0, :, width + 128 :].astype(jnp.float32))
    up_out[...] = up[0].astype(jnp.float32)
    tokens_out[...] = tokens[...]
    result_out[...] = result[...]
    for i in range(2):
        gain_out[i : i + 1, :] = jnp.transpose(sums[i])[0:1] / gains[i : i + 1, :]


def finish(attn, up, tokens, result, sums, gains):
    groups, depth, units = up.shape
    width = attn.shape[2] // 2 - HEAD
    rows, columns = tokens.shape
    part = rows // groups

    def block(*shape):
        return pl.BlockSpec((1, *shape), lambda i: (i, 0, 0))

    def wide(count):
        return pl.BlockSpec((depth, count), lambda i: (0, i))

    def tall(count, other):
        return pl.BlockSpec((count, other), lambda i: (i, 0))

    def f32(*shape):
        return jax.ShapeDtypeStruct(shape, jnp.float32)

    return pl.pallas_call(
        finish_kernel,
        grid=(groups,),
        in_specs=[
            block(depth, attn.shape[2]),
            block(depth, units),
            tall(part, columns),
            tall(part, columns),
            pl.BlockSpec(sums.shape, lambda i: (0, 0, 0)),
            pl.BlockSpec(gains.shape, lambda i: (0, 0)),
        ],
        out_specs=[
            wide(width),
            pl.BlockSpec((depth, groups * HEAD), lambda i: (0, 0)),
            pl.BlockSpec((depth, groups * HEAD), lambda i: (0, 0)),
            tall(width, depth),
            wide(units),
            tall(part, columns),
            tall(part, columns),
            pl.BlockSpec((2, 128), lambda i: (0, 0)),
        ],
        out_shape=[
            f32(depth, groups * width),
            f32(depth, groups * HEAD),
            f32(depth, groups * HEAD),
            f32(groups * width, depth),
            f32(depth, groups * units),
            f32(rows, columns),
            jax.ShapeDtypeStruct(result.shape, result.dtype),
            f32(2, 128),
        ],
        compiler_params=pltpu.CompilerParams(vmem_limit_bytes=VMEM_LIMIT),
        cost_estimate=lasting(12),
        name="finish",
    )(attn, up, tokens, result, sums, gains)


def context_pairs(step):
    return [(i, i ^ step) for i in range(4)]


def ffn_first_kernel(hidden, weights, m, gate, up):
    units = m.shape[1]
    for j in range(units // 256):
        cut = slice(j * 256, j * 256 + 256)
        gate_part = dot(hidden[...], weights[:, cut])
        up_part = dot(hidden[...], weights[:, units + j * 256 : units + j * 256 + 256])
        gate[:, cut] = gate_part.astype(jnp.bfloat16)
        up[:, cut] = up_part.astype(jnp.bfloat16)
        sigmoid = 1.0 / (1.0 + jnp.exp(-gate_part))
        m[:, cut] = (gate_part * sigmoid * up_part).astype(jnp.bfloat16)


def ffn_slopes_kernel(grad, gate, up, down_w, early, slopes):
    units = down_w.shape[1]
    for j in range(units // 256):
        cut = slice(j * 256, j * 256 + 256)
        grad_part = dot(grad[...], down_w[:, cut])
        gate_part = gate[:, cut].astype(jnp.float32)
        up_part = up[:, cut].astype(jnp.float32)
        sigmoid = 1.0 / (1.0 + jnp.exp(-gate_part))
        slope = sigmoid * (1.0 + gate_part * (1.0 - sigmoid))
        slopes[:, cut] = (grad_part * up_part * slope).astype(jnp.bfloat16)
        slopes[:, units + j * 256 : units + j * 256 + 256] = (
            grad_part * gate_part * sigmoid
        ).astype(jnp.bfloat16)


def first_rows_kernel(values, gains, weight, hidden, raw):
    value = values[...].astype(jnp.float32)
    normed = (value * row_root(value) * gains[0:1, :]).astype(jnp.bfloat16)
    hidden[...] = normed
    raw[...] = dot(normed, weight[...])


def first_rows(values, gains, packed, columns):
    count, width = values.shape
    return pl.pallas_call(
        first_rows_kernel,
        grid=(count // ROW_TILE,),
        in_specs=[
            pl.BlockSpec((ROW_TILE, width), lambda i: (i, 0)),
            pl.BlockSpec((8, width), lambda i: (0, 0)),
            pl.BlockSpec((width, columns), lambda i: (0, 0)),
        ],
        out_specs=[
            pl.BlockSpec((ROW_TILE, width), lambda i: (i, 0)),
            pl.BlockSpec((ROW_TILE, columns), lambda i: (i, 0)),
        ],
        out_shape=[
            jax.ShapeDtypeStruct((count, width), jnp.bfloat16),
            jax.ShapeDtypeStruct((count, columns), jnp.float32),
        ],
        compiler_params=pltpu.CompilerParams(vmem_limit_bytes=VMEM_LIMIT),
        cost_estimate=lasting(4),
        name="first_rows",
    )(values, gains, packed)


def attention_weights_kernel(hidden, back, grad, attended, moving, *rest):
    out, moved, sent, landed, local = rest[-5:]
    step, last = pl.program_id(0), pl.num_programs(0) - 1

    @pl.when(step == 0)
    def start():
        p = Plane(sent, landed, diagonal=True)
        pltpu.make_async_copy(moving.at[p.rank], moved.at[p.rank], local).start()
        for partner, rank in ((p.both, p.at_both), (p.x, p.at_x), (p.y, p.at_y)):
            p.send(moving.at[rank], moved.at[p.rank], partner)

    columns = back.shape[1]
    out[:, :columns] = dot(hidden[...], back[...], FIRST).astype(jnp.bfloat16)
    out[:, columns:] = dot(grad[...], attended[...], FIRST).astype(jnp.bfloat16)

    @pl.when(step == last)
    def finish():
        p = Plane(sent, landed, entered=True)
        for number, rank in enumerate((p.at_both, p.at_x, p.at_y)):
            move = p.copy(number, moving.at[rank], moved.at[rank], p.x)
            move.wait_recv()
            move.wait_send()
        pltpu.make_async_copy(moving.at[p.rank], moved.at[p.rank], local).wait()


def attention_weights(hidden, back, grad, attended, moving, early):
    count, width = hidden.shape
    first, second = back.shape[1], attended.shape[1]
    tall = pl.BlockSpec((count, 256), lambda i: (0, i))
    return pl.pallas_call(
        attention_weights_kernel,
        grid=(width // 256,),
        in_specs=[
            tall,
            pl.BlockSpec((count, first), lambda i: (0, 0)),
            tall,
            pl.BlockSpec((count, second), lambda i: (0, 0)),
        ]
        + [ANY] * (1 + len(early)),
        out_specs=[pl.BlockSpec((256, first + second), lambda i: (i, 0)), ANY],
        out_shape=[
            jax.ShapeDtypeStruct((width, first + second), jnp.bfloat16),
            jax.ShapeDtypeStruct(moving.shape, moving.dtype),
        ],
        scratch_shapes=wires(3) + [pltpu.SemaphoreType.DMA],
        compiler_params=pltpu.CompilerParams(
            collective_id=8, has_side_effects=True, vmem_limit_bytes=VMEM_LIMIT
        ),
        cost_estimate=lasting(25),
        name="attention_weights",
    )(hidden, back, grad, attended, moving, *early)


ROW_TILE = 256


def row_tiles(kernel, name, rows, weights, extra, widths):
    count = rows[0].shape[0]

    def tile(width):
        return pl.BlockSpec((ROW_TILE, width), lambda i: (i, 0))

    whole = [
        pl.BlockSpec(w.shape, lambda i: (0, 0), pipeline_mode=pl.Buffered(1)) for w in weights
    ]
    flops = 2 * count * sum(w.size for w in weights)
    return pl.pallas_call(
        kernel,
        grid=(count // ROW_TILE,),
        in_specs=[tile(r.shape[1]) for r in rows] + whole + [ANY] * len(extra),
        out_specs=[tile(width) for width in widths],
        out_shape=[jax.ShapeDtypeStruct((count, width), jnp.bfloat16) for width in widths],
        compiler_params=pltpu.CompilerParams(vmem_limit_bytes=56 * 1024 * 1024),
        cost_estimate=pl.CostEstimate(flops=flops, bytes_accessed=flops // 400, transcendentals=0),
        name=name,
    )(*rows, *weights, *extra)


def norm_backward(gradient, normed, inv_root):
    return inv_root * (gradient - normed * jnp.mean(gradient * normed, axis=-1, keepdims=True))


def inverse_root(values):
    return lax.rsqrt(jnp.mean(values * values, axis=-1, keepdims=True) + epsilon)


PLANE = ("context", "tensor")


def gather_rows(values):
    return lax.all_gather(values, PLANE, axis=0, tiled=True)


def scatter_rows(partial):
    return lax.psum_scatter(
        partial.astype(jnp.bfloat16), PLANE, scatter_dimension=0, tiled=True
    ).astype(jnp.float32)


def local(
    tokens,
    cotangent,
    attn_gain,
    w_query,
    w_key,
    w_value,
    w_out,
    ffn_gain,
    w_gate,
    w_up,
    w_down,
    piece_segment,
    piece_parent,
    piece_start,
):
    groups = lax.axis_size("context")
    cores = lax.axis_size("tensor")
    depth = w_query.shape[0]
    kv_count = w_key.shape[1] // HEAD
    sharing = groups // kv_count
    share = tokens.shape[0] // cores
    first_row = lax.axis_index("tensor") * share

    def my_rows(values):
        return lax.dynamic_slice_in_dim(values, first_row, share, 0)

    def blocks(weight):
        return jnp.transpose(weight.reshape(depth, groups, -1), (1, 0, 2))

    def kv_blocks(weight):
        return jnp.repeat(jnp.transpose(weight.reshape(depth, kv_count, HEAD), (1, 0, 2)), sharing, 0)

    def spread(weight_blocks):
        mine = lax.all_to_all(weight_blocks, "context", 0, 0)
        mine = mine.reshape(groups * depth, -1)
        return lax.all_gather(mine, "fsdp", axis=0, tiled=True)

    square = groups == 4 and cores == 2
    width = w_query.shape[1] // groups
    columns_qkv = width + 2 * HEAD
    out_turned, down_turned = w_out.T, w_down.T
    tokens_half, cotangent_half = my_rows(tokens), my_rows(cotangent)

    def over_groups(blocks_here):
        return lax.all_gather(
            blocks_here.reshape(groups * depth, -1), "fsdp", axis=0, tiled=True
        )

    if square:
        gains = jnp.pad(jnp.stack([attn_gain, ffn_gain]).astype(jnp.float32), ((0, 6), (0, 0)))
        w_pair = jnp.stack(
            [w_key.reshape(depth, groups, HEAD), w_value.reshape(depth, groups, HEAD)], axis=2
        ).reshape(depth, -1)
        packed, gain_rows = first_exchange(w_query, w_pair, out_turned, gains)
        packed = over_groups(packed)
        both_blocks, down_blocks = exchange_columns(w_gate, w_up, down_turned, gain_rows)
        inputs_full, ffn_grad, my_ffn_grad = start_plane(tokens, cotangent, down_blocks)
        both_full, down_full = over_groups(both_blocks), over_groups(down_blocks)
        hidden_first, raw = first_rows(
            inputs_full.reshape(-1, inputs_full.shape[3]), gain_rows, packed, columns_qkv
        )
        out_full = packed[:, columns_qkv:]
    else:
        gains = jnp.stack([attn_gain, ffn_gain], axis=1)
        gains = jnp.broadcast_to(jnp.pad(gains, ((0, 0), (0, 126))), (groups, depth, 128))
        packed = spread(
            jnp.concatenate(
                [
                    blocks(w_query),
                    kv_blocks(w_key),
                    kv_blocks(w_value),
                    blocks(out_turned),
                    gains,
                ],
                axis=2,
            )
        )
        qkv_full = packed[:, :columns_qkv]
        out_full = packed[:, columns_qkv : columns_qkv + width]
        gains_full = packed[:, columns_qkv + width :].astype(jnp.float32)
        attn_scale, ffn_scale = gains_full[:, 0], gains_full[:, 1]
        both_full = spread(jnp.concatenate([blocks(w_gate), blocks(w_up)], axis=2))
        down_full = spread(blocks(down_turned))
        inputs_full = gather_rows(tokens_half).astype(jnp.float32)
        hidden_first = inputs_full * inverse_root(inputs_full) * attn_scale
        hidden_first = hidden_first.astype(jnp.bfloat16)
        raw = dot(hidden_first, qkv_full)
        my_ffn_grad = (residual_scale * cotangent_half.astype(jnp.float32)).astype(jnp.bfloat16)
    tables = rope_tables()

    segment, starts = piece_segment[0] % 13, piece_start[0]
    places = jnp.where(
        segment == 0,
        starts,
        jnp.where(
            segment <= BRANCHES,
            starts + (segment - 1) * SEG,
            starts + (segment - 1 - BRANCHES) * SEG + (BRANCHES - 1) * SEG,
        ),
    )

    residual_in = tokens_half.astype(jnp.float32)
    grad_result = cotangent_half.astype(jnp.float32)

    attended, *kept = attention_forward(places, starts, raw, tables)
    if square:
        ffn_grad_blocks = [
            lax.ppermute(my_ffn_grad, "context", context_pairs(step)) for step in (1, 2, 3)
        ]
        hidden_block, middle, ffn_grad = middle_plane(
            attended, packed, tokens, gain_rows, ffn_grad, ffn_grad_blocks
        )
    else:
        ffn_grad = gather_rows(my_ffn_grad)
        middle = residual_in + residual_scale * scatter_rows(dot(attended, out_full, LAST))
        hidden_second = gather_rows((middle * inverse_root(middle) * ffn_scale).astype(jnp.bfloat16))

    units = down_full.shape[1]
    if square:
        hidden_second, hidden, gate_proj, up_proj = ffn_rows(hidden_block, both_full)
    else:
        hidden, gate_proj, up_proj = row_tiles(
            ffn_first_kernel,
            "ffn_first",
            [hidden_second],
            [both_full],
            [],
            [units, units, units],
        )
    grad_down = dot(ffn_grad, hidden, FIRST).astype(jnp.bfloat16)
    (slopes,) = row_tiles(
        ffn_slopes_kernel,
        "ffn_slopes",
        [ffn_grad, gate_proj, up_proj],
        [down_full],
        [grad_down],
        [2 * units],
    )
    def sum_groups(gradient):
        return lax.psum_scatter(gradient, "fsdp", scatter_dimension=0, tiled=True)

    def hand_back(gradient):
        return lax.all_to_all(gradient.reshape(groups, depth, -1), "context", 0, 0)

    def columns(gradient):
        return jnp.transpose(gradient, (1, 0, 2)).reshape(depth, -1).astype(jnp.float32)

    if square:
        grad_middle, my_attn_grad, grad_gate = second_plane(
            slopes,
            hidden_second,
            both_full,
            middle,
            cotangent,
            gain_rows,
            grad_down,
        )
        attn_grad, ffn_pairs, grad_up = spread_plane(
            my_attn_grad, hidden, down_full, hidden_second, slopes, grad_gate
        )
        ffn_parts = [ffn_pairs[0]] + [
            lax.ppermute(ffn_pairs[step], "context", context_pairs(step)) for step in (1, 2, 3)
        ]
    else:
        root = inverse_root(middle)
        ffn_out = dot(hidden, down_full, LAST)
        grad_gate = dot(hidden_second, slopes[:, :units], FIRST).astype(jnp.bfloat16)
        grad_up = dot(hidden_second, slopes[:, units:], FIRST).astype(jnp.bfloat16)
        grad_second = dot(slopes, both_full, LAST)
        grad_middle = grad_result + norm_backward(
            scatter_rows(grad_second) * ffn_scale, middle * root, root
        )
        attn_grad = gather_rows((residual_scale * grad_middle).astype(jnp.bfloat16))
        ffn_parts = []
    grad_attended = dot(attn_grad, out_full).astype(jnp.bfloat16)
    grad_down = sum_groups(grad_down)
    grad_gate, grad_up = sum_groups(grad_gate), sum_groups(grad_up)
    back = attention_backward(places, starts, grad_attended, kept, tables, [grad_down])
    grad_down = hand_back(grad_down)
    if square:
        grad_attn, grad_gate = attention_weights(
            hidden_first,
            back,
            attn_grad,
            attended,
            grad_gate.reshape(groups, depth, -1),
            [grad_down, *ffn_parts[1:]],
        )
    else:
        grad_attn = jnp.concatenate(
            [dot(hidden_first, back, FIRST), dot(attn_grad, attended, FIRST)], axis=1
        ).astype(jnp.bfloat16)
        grad_first = dot(back, qkv_full, LAST).astype(jnp.bfloat16)
        grad_gate, grad_up = hand_back(grad_gate), hand_back(grad_up)
    grad_attn = sum_groups(grad_attn)
    if square:
        down, gate = finish_first(grad_down, grad_gate)
        grad_tokens, result, grad_up, ffn_sums = last_plane(
            back,
            packed,
            tokens,
            grad_middle,
            gain_rows,
            middle,
            ffn_parts,
            grad_up.reshape(groups, depth, -1),
            grad_gate,
            w_gate,
            w_up,
            down,
        )
        grad_attn, sums = exchange(
            grad_attn.reshape(groups, depth, -1), w_query, w_pair, ffn_sums
        )
        my_gains = jnp.stack([attn_gain, ffn_gain]).astype(jnp.float32)
        query, key, value, out, up, grad_tokens, result, gain_grads = finish(
            grad_attn, grad_up, grad_tokens, result, sums, my_gains
        )
        return (
            result,
            grad_tokens,
            gain_grads[0],
            query,
            key,
            value,
            out,
            gain_grads[1],
            gate,
            up,
            down,
        )
    else:
        root = inverse_root(residual_in)
        grad_tokens = grad_middle + norm_backward(
            scatter_rows(grad_first) * attn_scale, residual_in * root, root
        )
        grad_tokens = lax.all_gather(grad_tokens, "tensor", axis=0, tiled=True)
        result = (middle + residual_scale * scatter_rows(ffn_out)).astype(jnp.bfloat16)
        grad_attn = hand_back(grad_attn)
        result = lax.all_gather(result, "tensor", axis=0, tiled=True)
    def kv_columns(gradient):
        gradient = gradient.astype(jnp.float32).reshape(kv_count, sharing, depth, HEAD)
        return jnp.transpose(jnp.sum(gradient, axis=1), (1, 0, 2)).reshape(depth, -1)

    grad_query = columns(grad_attn[:, :, :width])
    grad_key = kv_columns(grad_attn[:, :, width : width + HEAD])
    grad_value = kv_columns(grad_attn[:, :, width + HEAD : width + 2 * HEAD])
    grad_gate, grad_up = columns(grad_gate), columns(grad_up)

    def against(*pairs):
        return sum(jnp.sum(weight.astype(jnp.float32) * g, axis=1) for weight, g in pairs)

    gain_grads = jnp.stack(
        [
            against((w_query, grad_query), (w_key, grad_key), (w_value, grad_value)),
            against((w_gate, grad_gate), (w_up, grad_up)),
        ]
    )
    gain_grads = lax.psum(gain_grads, "tensor")
    return (
        result,
        grad_tokens,
        gain_grads[0] / attn_gain.astype(jnp.float32),
        grad_query,
        grad_key,
        grad_value,
        columns(grad_attn[:, :, width + 2 * HEAD :]).T,
        gain_grads[1] / ffn_gain.astype(jnp.float32),
        grad_gate,
        grad_up,
        columns(grad_down).T,
    )


ROWS = ("fsdp", "context")


def solution(mesh):
    return jax.shard_map(
        local,
        mesh=mesh,
        in_specs=(
            P(ROWS, None),
            P(ROWS, None),
            P(ROWS),
            P(ROWS, "tensor"),
            P(ROWS, "tensor"),
            P(ROWS, "tensor"),
            P("tensor", ROWS),
            P(ROWS),
            P(ROWS, "tensor"),
            P(ROWS, "tensor"),
            P("tensor", ROWS),
            P("fsdp", None),
            P("fsdp", None),
            P("fsdp", None),
        ),
        out_specs=(
            P(ROWS, None),
            P(ROWS, None),
            P(ROWS),
            P(ROWS, "tensor"),
            P(ROWS, "tensor"),
            P(ROWS, "tensor"),
            P("tensor", ROWS),
            P(ROWS),
            P(ROWS, "tensor"),
            P(ROWS, "tensor"),
            P("tensor", ROWS),
        ),
        check_vma=False,
    )
```

```python
import functools

import jax
import jax.numpy as jnp
import numpy as np
from jax import lax
from jax.experimental import pallas as pl
from jax.experimental.pallas import tpu as pltpu
from jax.sharding import PartitionSpec as P

HEAD = 64
SEG = 128
TRUNK = 8 * SEG
BRANCHES = 4
LEAVES = 8
GROUP = TRUNK + (BRANCHES + LEAVES) * SEG
DEPTH = TRUNK + 2 * SEG
TILE = 2 * SEG

epsilon = 1e-05
rope_base = 10000000.0
residual_scale = 0.22
score_scale = 0.015625
masked_score = -1e30

FIRST = (((0,), (0,)), ((), ()))
LAST = (((1,), (1,)), ((), ()))
PLAIN = (((1,), (0,)), ((), ()))


def dot(left_side, right_side, dims=PLAIN):
    return lax.dot_general(left_side, right_side, dims, preferred_element_type=jnp.float32)


def rope_tables():
    steps = np.arange(HEAD // 2, dtype=np.float32)
    frequency = np.float32(rope_base) ** (-(steps * np.float32(2)) / np.float32(HEAD))
    angles = np.arange(DEPTH, dtype=np.float32)[:, None] * frequency.astype(np.float32)
    angles = angles.astype(np.float64)
    cosine, sine = np.cos(angles).astype(np.float32), np.sin(angles).astype(np.float32)
    return (
        jnp.asarray(np.concatenate([cosine] * 4, axis=-1)),
        jnp.asarray(np.concatenate([-sine, sine, -sine, sine], axis=-1)),
    )


def lanes(values):
    return lax.broadcasted_iota(jnp.int32, values.shape, 1)


def swap_halves(values):
    return jnp.where(
        lanes(values) % HEAD < HEAD // 2,
        pltpu.roll(values, 128 - HEAD // 2, 1),
        pltpu.roll(values, HEAD // 2, 1),
    )


def only_head(values, head):
    return jnp.where(lanes(values) // HEAD == head, values, jnp.zeros_like(values))


def query_tiles(work):
    for j in range(TRUNK // TILE):
        prefix = [(0, j * TILE, False)] if j else []
        work(j * TILE, prefix + [(j * TILE, TILE, True)], False)

    def branch(i, carry):
        row = pl.multiple_of(TRUNK + i * TILE, TILE)
        work(row, [(0, TRUNK, False), (row, TILE, True)], True)
        return carry

    lax.fori_loop(0, BRANCHES * SEG // TILE, branch, 0)

    def leaf(i, carry):
        row = pl.multiple_of(TRUNK + BRANCHES * SEG + i * TILE, TILE)
        parent = pl.multiple_of(TRUNK + i * SEG, SEG)
        work(row, [(0, TRUNK, False), (parent, SEG, False), (row, TILE, True)], True)
        return carry

    lax.fori_loop(0, LEAVES * SEG // TILE, leaf, 0)


def visible_scores(keys, query, own, one_segment):
    scores = dot(keys, query, LAST)
    if not own:
        return scores
    key_at = lax.broadcasted_iota(jnp.int32, scores.shape, 0)
    query_at = lax.broadcasted_iota(jnp.int32, scores.shape, 1)
    seen = key_at <= query_at
    if one_segment:
        seen = seen & (key_at // SEG == query_at // SEG)
    return jnp.where(seen, scores, masked_score)


def turned_over(target, source):
    for first in range(0, source.shape[0], TILE):
        block = source[first : first + TILE, :128].astype(jnp.float32)
        target[:, first : first + TILE] = jnp.transpose(block)[:HEAD].astype(jnp.bfloat16)


def head_pairs(width, work):
    together = min(PAIR, width // HEAD)

    def step(i, carry):
        work([i * together + j for j in range(together)])
        return carry

    lax.fori_loop(0, width // HEAD // together, step, 0)


PAIR = 2


def attention_forward_kernel(
    to_ref, start_ref, raw_ref, cos_ref, sin_ref, out_ref, q_ref, k_ref, v_ref, log_ref,
    held, values_ref, tile_ref,
):
    width = q_ref.shape[1]
    pieces = to_ref.shape[0]
    piece = raw_ref.shape[0] // pieces

    def place(p, carry):
        rows = pl.ds(pl.multiple_of(p * piece, piece), piece)
        to = pl.ds(pl.multiple_of(to_ref[p], piece), piece)
        at = pl.ds(pl.multiple_of(start_ref[p], piece), piece)
        cosine, sine = cos_ref[at, :], sin_ref[at, :]

        def turn(values):
            return values * cosine + swap_halves(values) * sine

        for g in range(width // 128):
            cut = slice(g * 128, g * 128 + 128)
            turned = turn(raw_ref[rows, cut]).astype(jnp.bfloat16)
            q_ref[to, cut] = turned * jnp.bfloat16(score_scale)
        pair = raw_ref[rows, width : width + 128]
        low = lanes(pair) < HEAD
        key = turn(pair)
        key = jnp.where(low, key, pltpu.roll(key, HEAD, 1)).astype(jnp.bfloat16)
        value = jnp.where(low, pltpu.roll(pair, HEAD, 1), pair).astype(jnp.bfloat16)
        for g in range(width // 128):
            cut = slice(g * 128, g * 128 + 128)
            k_ref[to, cut] = key
            v_ref[to, cut] = value
        return carry

    lax.fori_loop(0, pieces, place, 0)
    turned_over(values_ref, v_ref)

    def work(row, parts, one_segment):
        rows = pl.ds(row, TILE)

        def one_head(head):
            query = only_head(q_ref[rows, :], head)
            scores = [
                visible_scores(k_ref[pl.ds(first, count), :], query, own, one_segment)
                for first, count, own in parts
            ]
            largest = functools.reduce(
                jnp.maximum, [jnp.max(s, axis=0, keepdims=True) for s in scores]
            )
            exponent = [jnp.exp(s - largest) for s in scores]
            total = functools.reduce(
                jnp.add, [jnp.sum(e, axis=0, keepdims=True) for e in exponent]
            )
            result = functools.reduce(
                jnp.add,
                [
                    dot(values_ref[:, pl.ds(first, count)], e.astype(jnp.bfloat16))
                    for e, (first, count, own) in zip(exponent, parts)
                ],
            )
            log_ref[head, :, rows] = largest + jnp.log(total)
            tile_ref[pl.ds(pl.multiple_of(head * HEAD, HEAD), HEAD), :] = result * (1.0 / total)

        def heads(together):
            for head in together:
                one_head(head)

        head_pairs(width, heads)
        held[rows, :] = jnp.transpose(tile_ref[...]).astype(jnp.bfloat16)

    query_tiles(work)

    def back(p, carry):
        rows = pl.ds(pl.multiple_of(p * piece, piece), piece)
        to = pl.ds(pl.multiple_of(to_ref[p], piece), piece)
        out_ref[rows, :] = held[to, :]
        return carry

    lax.fori_loop(0, pieces, back, 0)


def attention_backward_kernel(
    to_ref,
    start_ref,
    grad_ref,
    q_ref,
    k_ref,
    v_ref,
    log_ref,
    cos_ref,
    sin_ref,
    *rest,
):
    out_ref, og_ref, dq_ref, dk_ref, dv_ref, keys_ref, tile_ref = rest[-7:]
    width = q_ref.shape[1]
    pieces = to_ref.shape[0]
    piece = grad_ref.shape[0] // pieces

    def place(p, carry):
        rows = pl.ds(pl.multiple_of(p * piece, piece), piece)
        to = pl.ds(pl.multiple_of(to_ref[p], piece), piece)
        og_ref[to, :] = grad_ref[rows, :]
        return carry

    lax.fori_loop(0, pieces, place, 0)
    turned_over(keys_ref, k_ref)
    dk_ref[...] = jnp.zeros_like(dk_ref)
    dv_ref[...] = jnp.zeros_like(dv_ref)

    def work(row, parts, one_segment):
        rows = pl.ds(row, TILE)

        def heads(together):
            queries, out_grads, all_weights, all_grads = [], [], [], []
            for head in together:
                query = only_head(q_ref[rows, :], head)
                out_grad = only_head(og_ref[rows, :], head)
                log_total = log_ref[head, :, rows]
                weights, products = [], []
                for first, count, own in parts:
                    keys = pl.ds(first, count)
                    scores = visible_scores(k_ref[keys, :], query, own, one_segment)
                    weights.append(jnp.exp(scores - log_total))
                    products.append(dot(v_ref[keys, :], out_grad, LAST))
                inner = functools.reduce(
                    jnp.add,
                    [jnp.sum(w * d, axis=0, keepdims=True) for w, d in zip(weights, products)],
                )
                grads = [
                    (w * (d - inner)).astype(jnp.bfloat16) for w, d in zip(weights, products)
                ]
                queries.append(query)
                out_grads.append(out_grad)
                all_weights.append([w.astype(jnp.bfloat16) for w in weights])
                all_grads.append(grads)
                tile_ref[pl.ds(pl.multiple_of(head * HEAD, HEAD), HEAD), :] = functools.reduce(
                    jnp.add,
                    [
                        dot(keys_ref[:, pl.ds(first, count)], g)
                        for (first, count, own), g in zip(parts, grads)
                    ],
                )
            query = jnp.concatenate(queries, axis=0)
            out_grad = jnp.concatenate(out_grads, axis=0)
            for i, (first, count, own) in enumerate(parts):
                keys = pl.ds(first, count)
                weights = jnp.concatenate([w[i] for w in all_weights], axis=1)
                grads = jnp.concatenate([g[i] for g in all_grads], axis=1)
                dv_ref[keys, :] += dot(weights, out_grad)
                dk_ref[keys, :] += dot(grads, query)

        head_pairs(width, heads)
        dq_ref[rows, :] = jnp.transpose(tile_ref[...])

    query_tiles(work)

    def back(p, carry):
        rows = pl.ds(pl.multiple_of(p * piece, piece), piece)
        to = pl.ds(pl.multiple_of(to_ref[p], piece), piece)
        at = pl.ds(pl.multiple_of(start_ref[p], piece), piece)
        cosine, sine = cos_ref[at, :], sin_ref[at, :]

        def turn_back(values):
            return values * cosine - swap_halves(values) * sine

        def over_heads(ref):
            total = functools.reduce(
                jnp.add, [ref[to, g * 128 : g * 128 + 128] for g in range(width // 128)]
            )
            return total + pltpu.roll(total, HEAD, 1)

        for g in range(width // 128):
            cut = slice(g * 128, g * 128 + 128)
            turned = turn_back(score_scale * dq_ref[to, cut])
            out_ref[rows, cut] = turned.astype(jnp.bfloat16)
        key = turn_back(over_heads(dk_ref))
        value = over_heads(dv_ref)
        pair = jnp.where(lanes(key) < HEAD, key, value)
        out_ref[rows, width : width + 128] = pair.astype(jnp.bfloat16)
        return carry

    lax.fori_loop(0, pieces, back, 0)


SMEM = pl.BlockSpec(memory_space=pltpu.SMEM)
VMEM = pl.BlockSpec(memory_space=pltpu.VMEM)
VMEM_LIMIT = 60 * 1024 * 1024


def attention_cost(width, products):
    flops = products * 2 * GROUP * (GROUP * 2 // 5) * width
    return pl.CostEstimate(
        flops=flops, bytes_accessed=16 * GROUP * width, transcendentals=GROUP * GROUP * width // 128
    )


def attention_forward(places, starts, raw, tables):
    width = raw.shape[1] - 2 * HEAD
    rows = raw.shape[0]
    kept = jax.ShapeDtypeStruct((rows, width), jnp.bfloat16)
    return pl.pallas_call(
        attention_forward_kernel,
        out_shape=[kept] * 4 + [jax.ShapeDtypeStruct((width // HEAD, 1, rows), jnp.float32)],
        in_specs=[SMEM, SMEM, VMEM, VMEM, VMEM],
        out_specs=[VMEM] * 5,
        scratch_shapes=[
            pltpu.VMEM((rows, width), jnp.bfloat16),
            pltpu.VMEM((HEAD, rows), jnp.bfloat16),
            pltpu.VMEM((width, TILE), jnp.float32),
        ],
        compiler_params=pltpu.CompilerParams(vmem_limit_bytes=VMEM_LIMIT),
        cost_estimate=attention_cost(width, 4),
        name="attention_forward",
    )(places, starts, raw, *tables)


def attention_backward(places, starts, out_grad, kept, tables, early):
    rows, width = out_grad.shape
    return pl.pallas_call(
        attention_backward_kernel,
        out_shape=jax.ShapeDtypeStruct((rows, width + 2 * HEAD), jnp.bfloat16),
        in_specs=[SMEM, SMEM] + [VMEM] * 7 + [ANY] * len(early),
        out_specs=VMEM,
        scratch_shapes=[
            pltpu.VMEM((rows, width), jnp.bfloat16),
            pltpu.VMEM((rows, width), jnp.float32),
            pltpu.VMEM((rows, width), jnp.float32),
            pltpu.VMEM((rows, width), jnp.float32),
            pltpu.VMEM((HEAD, rows), jnp.bfloat16),
            pltpu.VMEM((width, TILE), jnp.float32),
        ],
        compiler_params=pltpu.CompilerParams(vmem_limit_bytes=VMEM_LIMIT),
        cost_estimate=attention_cost(width, 10),
        name="attention_backward",
    )(places, starts, out_grad, *kept, *tables, *early)


MESH = pl.DeviceIdType.MESH
ANY = pl.BlockSpec(memory_space=pl.ANY)
CHUNKS = 4
SLAB = 16


def lasting(microseconds):
    return pl.CostEstimate(
        flops=0, bytes_accessed=int(microseconds * 3_000_000), transcendentals=0
    )


class Plane:
    def __init__(self, sent, landed, diagonal=False, entered=False):
        self.sent, self.landed = sent, landed
        self.copies = []
        self.rank = lax.axis_index("context")
        self.core = lax.axis_index("tensor")
        self.at_x = self.rank + 1 - 2 * lax.rem(self.rank, 2)
        self.at_y = lax.rem(self.rank + 2, 4)
        self.at_both = 3 - self.rank
        self.x = {"context": self.at_x}
        self.y = {"context": self.at_y}
        self.both = {"context": self.at_both}
        self.sibling = {"tensor": 1 - self.core}
        if entered:
            return
        barrier = pltpu.get_barrier_semaphore()
        partners = [self.x, self.y, self.sibling] + ([self.both] if diagonal else [])
        for partner in partners:
            pl.semaphore_signal(barrier, inc=1, device_id=partner, device_id_type=MESH)
        pl.semaphore_wait(barrier, len(partners))

    def copy(self, number, source, target, partner):
        return pltpu.make_async_remote_copy(
            src_ref=source,
            dst_ref=target,
            send_sem=self.sent.at[number],
            recv_sem=self.landed.at[number],
            device_id=partner,
            device_id_type=MESH,
        )

    def send(self, source, target, partner):
        number = len(self.copies)
        started = self.copy(number, source, target, partner)
        started.start()
        self.copies.append(started)
        return number

    def arrive(self, number, target):
        self.copy(number, target, target, self.sibling).wait_recv()

    def finish(self):
        for started in self.copies:
            started.wait_send()


def chunk(index, rows):
    return pl.ds(index * (rows // CHUNKS), rows // CHUNKS)


class Gather:
    def __init__(self, plane, block, out):
        self.plane, self.block, self.out = plane, block, out
        self.rows = block.shape[0]
        self.to_x, self.to_y, self.across, self.onward = {}, {}, {}, {}

    def start(self, k):
        p, cut = self.plane, chunk(k, self.rows)
        target = self.out.at[p.rank, p.core, cut]
        self.to_x[k] = p.send(self.block.at[cut], target, p.x)
        self.to_y[k] = p.send(self.block.at[cut], target, p.y)
        self.across[0, k] = p.send(self.block.at[cut], target, p.sibling)

    def forward_chunk(self, k):
        p, out = self.plane, self.out
        cut = chunk(k, self.rows)
        from_x, from_y = out.at[p.at_x, p.core, cut], out.at[p.at_y, p.core, cut]
        p.arrive(self.to_x[k], from_x)
        if k < CHUNKS // 2:
            self.onward[k] = p.send(from_x, from_x, p.y)
        self.across[1, k] = p.send(from_x, from_x, p.sibling)
        p.arrive(self.to_y[k], from_y)
        if k >= CHUNKS // 2:
            self.onward[k] = p.send(from_y, from_y, p.x)
        self.across[2, k] = p.send(from_y, from_y, p.sibling)

    def forward_far(self):
        p = self.plane
        for k in range(CHUNKS):
            far = self.out.at[p.at_both, p.core, chunk(k, self.rows)]
            p.arrive(self.onward[k], far)
            self.across[3, k] = p.send(far, far, p.sibling)

    def forward(self):
        for k in range(CHUNKS):
            self.forward_chunk(k)
        self.forward_far()

    def finish(self):
        p = self.plane
        for i, rank in enumerate((p.rank, p.at_x, p.at_y, p.at_both)):
            for k in range(CHUNKS):
                p.arrive(
                    self.across[i, k], self.out.at[rank, 1 - p.core, chunk(k, self.rows)]
                )


GATHER_COPIES = CHUNKS * 8


def add_rows(target, source, first, count):
    def step(i, carry):
        rows = pl.ds(first + i * SLAB, SLAB)
        target[rows, :] = (
            target[rows, :].astype(jnp.float32) + source[rows, :].astype(jnp.float32)
        ).astype(jnp.bfloat16)
        return carry

    lax.fori_loop(0, count // SLAB, step, 0)


class Scatter:
    def __init__(
        self, plane, rows_in, weights, columns, given, held, other, near_x, near_y, far_x, far_y
    ):
        p = self.plane = plane
        rows = near_x.shape[0]
        half = rows // 2
        halves = top, low = pl.ds(0, half), pl.ds(half, half)
        order = (p.at_both, p.at_x, p.at_y, p.rank)
        across = {}

        def make(i, h):
            for core, target in ((1 - p.core, given), (p.core, held)):
                value = dot(rows_in[order[i], core, halves[h], :], weights[:, columns], LAST)
                target[i, halves[h], :] = value.astype(jnp.bfloat16)
                if target is given:
                    source = given.at[i, halves[h]]
                    across[i, h] = p.send(source, other.at[i, halves[h]], p.sibling)

        def pair(i, h):
            p.arrive(across[i, h], other.at[i, halves[h]])
            add_rows(held.at[i], other.at[i], h * half, half)

        make(0, 0)
        make(0, 1)
        pair(0, 0)
        first = p.send(held.at[0, top], far_x, p.x)
        make(1, 0)
        pair(0, 1)
        second = p.send(held.at[0, low], far_y, p.y)
        make(2, 0)
        pair(1, 0)
        third = p.send(held.at[1, top], near_x.at[top], p.x)
        make(1, 1)
        make(2, 1)
        make(3, 0)
        make(3, 1)
        pair(2, 0)
        pair(1, 1)
        pair(2, 1)
        p.arrive(first, far_x)
        add_rows(held.at[2], far_x, 0, half)
        fourth = p.send(held.at[2, top], near_y.at[top], p.y)
        p.arrive(second, far_y)

        def step(i, carry):
            rows, at = pl.ds(half + i * SLAB, SLAB), pl.ds(i * SLAB, SLAB)
            held[1, rows, :] = (
                held[1, rows, :].astype(jnp.float32) + far_y[at, :].astype(jnp.float32)
            ).astype(jnp.bfloat16)
            return carry

        lax.fori_loop(0, half // SLAB, step, 0)
        fifth = p.send(held.at[1, low], near_x.at[low], p.x)
        sixth = p.send(held.at[2, low], near_y.at[low], p.y)
        pair(3, 0)
        pair(3, 1)
        self.halves = halves
        self.from_x, self.from_y = (third, fifth), (fourth, sixth)
        self.parts = (held.at[3], near_x, near_y)

    def ready(self, h):
        _, near_x, near_y = self.parts
        self.plane.arrive(self.from_x[h], near_x.at[self.halves[h]])
        self.plane.arrive(self.from_y[h], near_y.at[self.halves[h]])

    def rows(self, rows):
        return sum(part[rows, :].astype(jnp.float32) for part in self.parts)


SCATTER_COPIES = 8 + 6


def scatter_scratch(share, width):
    kind = jnp.bfloat16
    return [
        pltpu.VMEM((4, share, width), kind),
        pltpu.VMEM((4, share, width), kind),
        pltpu.VMEM((4, share, width), kind),
        pltpu.VMEM((share, width), kind),
        pltpu.VMEM((share, width), kind),
        pltpu.VMEM((share // 2, width), kind),
        pltpu.VMEM((share // 2, width), kind),
    ]


def wires(count):
    return [pltpu.SemaphoreType.DMA((count,)), pltpu.SemaphoreType.DMA((count,))]


def row_root(values):
    return lax.rsqrt(jnp.mean(values * values, axis=-1, keepdims=True) + epsilon)


def slabs(first, count, work):
    def step(i, carry):
        work(pl.ds(first + i * SLAB, SLAB))
        return carry

    lax.fori_loop(0, count // SLAB, step, 0)


class Exchange:
    def __init__(self, plane, source, target, local, first=0, columns=None):
        p = plane
        columns = columns or target.shape[2]

        def part(rank):
            return source.at[:, pl.ds(pl.multiple_of(rank * columns, 128), columns)]

        def place(rank):
            return target.at[rank, :, pl.ds(first, columns)]

        self.plane, self.place, self.moves = p, place, []
        self.mine = pltpu.make_async_copy(part(p.rank), place(p.rank), local)
        self.mine.start()
        for partner, rank in ((p.both, p.at_both), (p.x, p.at_x), (p.y, p.at_y)):
            self.moves.append((p.send(part(rank), place(p.rank), partner), rank))

    def finish(self):
        for number, rank in self.moves:
            self.plane.arrive(number, self.place(rank))
        self.mine.wait()


def first_kernel(query, pair, out_turned, gains, packed, gains_out, sent, landed, local, far_sent, far_landed):
    groups = lax.axis_size("fsdp")
    group, rank = lax.axis_index("fsdp"), lax.axis_index("context")
    depth = gains.shape[1]
    others = [(i, j) for i in range(groups) for j in range(4) if i or j]

    def device(i, j):
        return {"fsdp": lax.rem(group + i, groups), "context": lax.rem(rank + j, 4)}

    def place(f, c):
        return gains_out.at[:, pl.ds(pl.multiple_of((f * 4 + c) * depth, 128), depth)]

    barrier = pltpu.get_barrier_semaphore()
    for i, j in others:
        pl.semaphore_signal(barrier, inc=1, device_id=device(i, j), device_id_type=MESH)
    pl.semaphore_wait(barrier, len(others))
    p = Plane(sent, landed, entered=True)
    width = query.shape[1] // 4
    exchanges = [
        Exchange(p, query, packed, local.at[0], 0, width),
        Exchange(p, pair, packed, local.at[1], width, 128),
        Exchange(p, out_turned, packed, local.at[2], width + 128, width),
    ]
    far = []
    for n, (i, j) in enumerate(others):
        far.append(
            pltpu.make_async_remote_copy(
                src_ref=gains,
                dst_ref=place(group, rank),
                send_sem=far_sent.at[n],
                recv_sem=far_landed.at[n],
                device_id=device(i, j),
                device_id_type=MESH,
            )
        )
        far[n].start()
    gains_out[:, pl.ds(pl.multiple_of((group * 4 + rank) * depth, 128), depth)] = gains[...]
    for started in far:
        started.wait()
    for exchange in exchanges:
        exchange.finish()
    p.finish()


def first_exchange(query, pair, out_turned, gains):
    depth, columns = query.shape
    groups = lax.axis_size("fsdp")
    far = groups * 4 - 1
    return pl.pallas_call(
        first_kernel,
        out_shape=[
            jax.ShapeDtypeStruct((4, depth, columns // 2 + 128), query.dtype),
            jax.ShapeDtypeStruct((8, groups * 4 * depth), jnp.float32),
        ],
        in_specs=[VMEM] * 4,
        out_specs=[ANY, VMEM],
        scratch_shapes=wires(9) + [pltpu.SemaphoreType.DMA((3,))] + wires(far),
        compiler_params=pltpu.CompilerParams(collective_id=9, has_side_effects=True),
        cost_estimate=lasting(10),
        name="first_exchange",
    )(query, pair, out_turned, gains)


def start_kernel(tokens, cotangent, early, out, scaled, my_scaled, sent, landed, local):
    p = Plane(sent, landed)
    share = my_scaled.shape[0]
    block = tokens.at[pl.ds(pl.multiple_of(p.core * share, SLAB), share)]
    gather = Gather(p, block, out)
    mine = pltpu.make_async_copy(block, out.at[p.rank, p.core], local)
    for k in range(CHUNKS):
        gather.start(k)
    mine.start()

    def scale(rows):
        value = residual_scale * cotangent[rows, :].astype(jnp.float32)
        scaled[rows, :] = value.astype(jnp.bfloat16)

    def keep(rows):
        from_rows = pl.ds(pl.multiple_of(p.core * share + rows.start, SLAB), SLAB)
        my_scaled[rows, :] = scaled[from_rows, :]

    slabs(0, scaled.shape[0], scale)
    slabs(0, share, keep)
    gather.forward()
    gather.finish()
    p.finish()
    mine.wait()


def start_plane(tokens, cotangent, early):
    share, width = tokens.shape[0] // 2, tokens.shape[1]
    return pl.pallas_call(
        start_kernel,
        out_shape=[
            jax.ShapeDtypeStruct((4, 2, share, width), tokens.dtype),
            jax.ShapeDtypeStruct(cotangent.shape, jnp.bfloat16),
            jax.ShapeDtypeStruct((share, width), jnp.bfloat16),
        ],
        in_specs=[VMEM, VMEM, ANY],
        out_specs=[ANY, VMEM, VMEM],
        scratch_shapes=wires(GATHER_COPIES) + [pltpu.SemaphoreType.DMA],
        compiler_params=pltpu.CompilerParams(
            collective_id=1, has_side_effects=True, vmem_limit_bytes=VMEM_LIMIT
        ),
        cost_estimate=lasting(60),
        name="gather_tokens",
    )(tokens, cotangent, early)


def columns_kernel(gate, up, down, early, both_out, down_out, sent, landed, local):
    p = Plane(sent, landed, diagonal=True)
    units = down_out.shape[2]
    exchanges = [
        Exchange(p, gate, both_out, local.at[0], 0, units),
        Exchange(p, up, both_out, local.at[1], units, units),
        Exchange(p, down, down_out, local.at[2]),
    ]
    for exchange in exchanges:
        exchange.finish()
    p.finish()


def exchange_columns(gate, up, down, early):
    depth, units = gate.shape
    return pl.pallas_call(
        columns_kernel,
        out_shape=[
            jax.ShapeDtypeStruct((4, depth, units // 2), gate.dtype),
            jax.ShapeDtypeStruct((4, depth, units // 4), gate.dtype),
        ],
        in_specs=[VMEM] * 3 + [ANY],
        out_specs=[ANY] * 2,
        scratch_shapes=wires(9) + [pltpu.SemaphoreType.DMA((3,))],
        compiler_params=pltpu.CompilerParams(collective_id=10, has_side_effects=True),
        cost_estimate=lasting(30),
        name="exchange_columns",
    )(gate, up, down, early)


def middle_kernel(
    attended,
    weights,
    gain,
    tokens,
    hidden,
    middle,
    sent,
    landed,
    local,
    residual,
    *scratch,
):
    p = Plane(sent, landed)
    share = hidden.shape[0]
    first = pl.ds(pl.multiple_of(p.core * share, SLAB), share)
    load = pltpu.make_async_copy(tokens.at[first], residual, local)
    load.start()
    width = attended.shape[3]
    columns = slice(weights.shape[1] - width, weights.shape[1])
    total = Scatter(p, attended, weights, columns, *scratch)
    load.wait()

    def work(rows):
        value = residual[rows, :].astype(jnp.float32) + residual_scale * total.rows(rows)
        middle[rows, :] = value
        hidden[rows, :] = (value * row_root(value) * gain[1:2, :]).astype(jnp.bfloat16)

    for h in range(2):
        total.ready(h)
        slabs(h * (share // 2), share // 2, work)
    p.finish()


def middle_plane(attended, weights, tokens, gain):
    share, width = tokens.shape[0] // 2, tokens.shape[1]
    return pl.pallas_call(
        middle_kernel,
        out_shape=[
            jax.ShapeDtypeStruct((share, width), jnp.bfloat16),
            jax.ShapeDtypeStruct((share, width), jnp.float32),
        ],
        in_specs=[VMEM] * 3 + [ANY],
        out_specs=[VMEM, VMEM],
        scratch_shapes=wires(SCATTER_COPIES)
        + [
            pltpu.SemaphoreType.DMA,
            pltpu.VMEM((share, width), jnp.bfloat16),
        ]
        + scatter_scratch(share, width),
        compiler_params=pltpu.CompilerParams(
            collective_id=2, has_side_effects=True, vmem_limit_bytes=VMEM_LIMIT
        ),
        cost_estimate=lasting(55),
        name="middle_rows",
    )(
        attended.reshape(4, 2, share, -1),
        weights,
        gain,
        tokens,
    )


def ffn_rows_kernel(
    block,
    weights_in,
    beside,
    from_x,
    from_y,
    from_both,
    out,
    m,
    gate,
    up,
    beside_out,
    sent,
    landed,
    local,
    loading,
    storing,
    weights,
    rows_in,
    m_held,
    gate_held,
    up_held,
    wires_beside,
    held_beside,
    held_blocks,
):
    p = Plane(sent, landed)
    gather = Gather(p, block, out)
    for k in range(CHUNKS):
        gather.start(k)
    weights_load = pltpu.make_async_copy(weights_in, weights, local.at[0])
    weights_load.start()
    mine = pltpu.make_async_copy(block, out.at[p.rank, p.core], local.at[1])
    mine.start()
    blocks = ((from_x, p.at_x), (from_y, p.at_y), (from_both, p.at_both))
    loads = [pltpu.make_async_copy(beside, held_beside, wires_beside.at[0])]
    for i, (source, rank) in enumerate(blocks):
        loads.append(
            pltpu.make_async_copy(source, held_blocks.at[i], wires_beside.at[i + 1])
        )
    for started in loads:
        started.start()
    units = m.shape[3]
    stores = []

    def load(n, rank, core):
        return pltpu.make_async_copy(out.at[rank, core], rows_in.at[n % 2], loading.at[n % 2])

    def compute(n, rank, core, source):
        slot = n % 2
        if n >= 2:
            for started in stores[n - 2]:
                started.wait()

        def step(j, carry):
            cut = pl.ds(pl.multiple_of(j * 256, 256), 256)
            beyond = pl.ds(pl.multiple_of(units + j * 256, 256), 256)
            gate_part = dot(source[...], weights[:, cut])
            up_part = dot(source[...], weights[:, beyond])
            gate_held[slot, :, cut] = gate_part.astype(jnp.bfloat16)
            up_held[slot, :, cut] = up_part.astype(jnp.bfloat16)
            sigmoid = 1.0 / (1.0 + jnp.exp(-gate_part))
            m_held[slot, :, cut] = (gate_part * sigmoid * up_part).astype(jnp.bfloat16)
            return carry

        lax.fori_loop(0, units // 256, step, 0)
        stores.append(
            [
                pltpu.make_async_copy(held.at[slot], target.at[rank, core], storing.at[slot, i])
                for i, (held, target) in enumerate(((m_held, m), (gate_held, gate), (up_held, up)))
            ]
        )
        for started in stores[n]:
            started.start()

    def from_sibling(i, rank):
        for k in range(CHUNKS):
            p.arrive(
                gather.across[i, k], out.at[rank, 1 - p.core, chunk(k, gather.rows)]
            )

    weights_load.wait()
    compute(0, p.rank, p.core, block)
    kept, shared = [], []
    loads[0].wait()
    kept.append(pltpu.make_async_copy(held_beside, beside_out.at[p.rank], wires_beside.at[0]))
    kept[0].start()
    for i, (source, rank) in enumerate(blocks):
        loads[i + 1].wait()
        place = beside_out.at[rank, p.core]
        kept.append(pltpu.make_async_copy(held_blocks.at[i], place, wires_beside.at[i + 1]))
        kept[i + 1].start()
        shared.append(p.send(held_blocks.at[i], place, p.sibling))
    gather.forward_chunk(0)
    from_sibling(0, p.rank)
    load(1, p.rank, 1 - p.core).start()
    load(1, p.rank, 1 - p.core).wait()
    compute(1, p.rank, 1 - p.core, rows_in.at[1])
    for k in range(1, CHUNKS):
        gather.forward_chunk(k)
    load(2, p.at_x, p.core).start()
    load(3, p.at_y, p.core).start()
    load(2, p.at_x, p.core).wait()
    compute(2, p.at_x, p.core, rows_in.at[0])
    from_sibling(1, p.at_x)
    load(4, p.at_x, 1 - p.core).start()
    load(3, p.at_y, p.core).wait()
    compute(3, p.at_y, p.core, rows_in.at[1])
    from_sibling(2, p.at_y)
    load(5, p.at_y, 1 - p.core).start()
    load(4, p.at_x, 1 - p.core).wait()
    compute(4, p.at_x, 1 - p.core, rows_in.at[0])
    gather.forward_far()
    load(6, p.at_both, p.core).start()
    load(5, p.at_y, 1 - p.core).wait()
    compute(5, p.at_y, 1 - p.core, rows_in.at[1])
    from_sibling(3, p.at_both)
    load(7, p.at_both, 1 - p.core).start()
    load(6, p.at_both, p.core).wait()
    compute(6, p.at_both, p.core, rows_in.at[0])
    load(7, p.at_both, 1 - p.core).wait()
    compute(7, p.at_both, 1 - p.core, rows_in.at[1])
    for number, (source, rank) in zip(shared, blocks):
        p.arrive(number, beside_out.at[rank, 1 - p.core])
    p.finish()
    mine.wait()
    for started in kept:
        started.wait()
    for n in (6, 7):
        for started in stores[n]:
            started.wait()


def ffn_rows(block, weights, beside, blocks):
    share, width = block.shape
    units = weights.shape[1] // 2
    kind = jnp.bfloat16
    full = jax.ShapeDtypeStruct((4, 2, share, width), kind)
    part = jax.ShapeDtypeStruct((4, 2, share, units), kind)
    held = pltpu.VMEM((2, share, units), kind)
    outs = pl.pallas_call(
        ffn_rows_kernel,
        out_shape=[full, part, part, part, full],
        in_specs=[VMEM] + [ANY] * 5,
        out_specs=[ANY] * 5,
        scratch_shapes=wires(GATHER_COPIES + 3)
        + [
            pltpu.SemaphoreType.DMA((2,)),
            pltpu.SemaphoreType.DMA((2,)),
            pltpu.SemaphoreType.DMA((2, 3)),
            pltpu.VMEM(weights.shape, kind),
            pltpu.VMEM((2, share, width), kind),
            held,
            held,
            held,
            pltpu.SemaphoreType.DMA((4,)),
            pltpu.VMEM((2, share, width), kind),
            pltpu.VMEM((3, share, width), kind),
        ],
        compiler_params=pltpu.CompilerParams(
            collective_id=11, has_side_effects=True, vmem_limit_bytes=VMEM_LIMIT
        ),
        cost_estimate=lasting(60),
        name="ffn_rows",
    )(block, weights, beside.reshape(2, share, width), *blocks)
    return [array.reshape(8 * share, -1) for array in outs]


class WeightTiles:
    def __init__(self, rows, slopes, target, rows_in, tile_out, wires_in):
        self.rows, self.slopes, self.target = rows, slopes, target
        self.rows_in, self.tile_out, self.wires = rows_in, tile_out, wires_in
        self.count = rows.shape[1] // TILE
        self.load(0, 0).start()

    def load(self, d, slot):
        columns = pl.ds(pl.multiple_of(d * TILE, TILE), TILE)
        return pltpu.make_async_copy(
            self.rows.at[:, columns], self.rows_in.at[slot], self.wires.at[0, slot]
        )

    def store(self, d, slot):
        columns = pl.ds(pl.multiple_of(d * TILE, TILE), TILE)
        return pltpu.make_async_copy(
            self.tile_out.at[slot], self.target.at[columns], self.wires.at[1, slot]
        )

    def run(self, first, last):
        def step(d, carry):
            slot = lax.rem(d, 2)
            self.load(d, slot).wait()

            @pl.when(d < self.count - 1)
            def _():
                self.load(d + 1, 1 - slot).start()

            @pl.when(d >= 2)
            def _():
                self.store(d - 2, slot).wait()

            self.tile_out[slot] = dot(self.rows_in[slot], self.slopes[...], FIRST).astype(
                jnp.bfloat16
            )
            self.store(d, slot).start()
            return carry

        lax.fori_loop(first, last, step, 0)

    def finish(self):
        for d in (self.count - 2, self.count - 1):
            self.store(d, d % 2).wait()


def tile_scratch(count, units):
    return [
        pltpu.SemaphoreType.DMA((2, 2)),
        pltpu.VMEM((2, count, TILE), jnp.bfloat16),
        pltpu.VMEM((2, TILE, units), jnp.bfloat16),
    ]


UNITS = ((0, 0), (0, 1), (1, 0), (2, 0), (1, 1), (2, 1), (3, 0), (3, 1))


def second_kernel(
    slopes,
    normed_rows,
    weights_in,
    middle_in,
    cotangent_in,
    gain,
    early,
    grad_middle,
    hidden,
    weight_grads,
    sent,
    landed,
    loading,
    beside,
    weights,
    middle,
    cotangent,
    tile_wires,
    rows_in,
    tile_out,
    gate_in,
    up_in,
    given,
    held,
    other,
    near_x,
    near_y,
    far_x,
    far_y,
):
    share, width = near_x.shape
    cuts = [slice(j * 512, j * 512 + 512) for j in range(width // 512)]
    weight_loads = [
        pltpu.make_async_copy(weights_in.at[cut], weights.at[cut], beside.at[2 + j])
        for j, cut in enumerate(cuts)
    ]
    for started in weight_loads:
        started.start()
    p = Plane(sent, landed)
    half = share // 2
    order = (p.at_both, p.at_x, p.at_y, p.rank)
    top, low = halves = pl.ds(0, half), pl.ds(half, half)

    def places(u):
        i, h = UNITS[u]
        for core in (1 - p.core, p.core):
            row = (order[i] * 2 + core) * share + h * half
            yield pl.ds(pl.multiple_of(row, 32), half)

    units = gate_in.shape[1]

    def loads(u):
        for j, rows in enumerate(places(u)):
            for n, target in enumerate((gate_in, up_in)):
                yield pltpu.make_async_copy(
                    slopes.at[rows, pl.ds(n * units, units)],
                    target.at[rows],
                    loading.at[u, 2 * j + n],
                )

    def compute(u):
        i, h = UNITS[u]
        slot = u % 2
        gate_rows = jnp.concatenate([gate_in[rows, :] for rows in places(u)], axis=0)
        up_rows = jnp.concatenate([up_in[rows, :] for rows in places(u)], axis=0)
        for j, cut in enumerate(cuts):
            if u == 0:
                weight_loads[j].wait()
            back = dot(gate_rows, weights[cut, :units], LAST) + dot(
                up_rows, weights[cut, units:], LAST
            )
            given[slot, :, cut] = back[:half].astype(jnp.bfloat16)
            held[i, halves[h], cut] = back[half:].astype(jnp.bfloat16)

    first = pl.ds(pl.multiple_of(p.core * share, SLAB), share)
    row_loads = [
        pltpu.make_async_copy(middle_in, middle, beside.at[0]),
        pltpu.make_async_copy(cotangent_in.at[first], cotangent, beside.at[1]),
    ]
    tiles = WeightTiles(normed_rows, gate_in, weight_grads, rows_in, tile_out, tile_wires)

    moves, across = {}, {}
    moves, across = {}, {}

    def settle(u):
        i, h = UNITS[u]
        p.arrive(across[u], other.at[i, halves[h]])
        add_rows(held.at[i], other.at[i], h * half, half)
        if u == 0:
            moves["far_x"] = p.send(held.at[0, top], far_x, p.x)
        elif u == 1:
            moves["far_y"] = p.send(held.at[0, low], far_y, p.y)
        elif u == 2:
            moves["x", 0] = p.send(held.at[1, top], near_x.at[top], p.x)
        elif u == 3:
            p.arrive(moves["far_x"], far_x)
            add_rows(held.at[2], far_x, 0, half)
            moves["y", 0] = p.send(held.at[2, top], near_y.at[top], p.y)
        elif u == 4:
            p.arrive(moves["far_y"], far_y)

            def step(k, carry):
                rows, at = pl.ds(half + k * SLAB, SLAB), pl.ds(k * SLAB, SLAB)
                held[1, rows, :] = (
                    held[1, rows, :].astype(jnp.float32) + far_y[at, :].astype(jnp.float32)
                ).astype(jnp.bfloat16)
                return carry

            lax.fori_loop(0, half // SLAB, step, 0)
            moves["x", 1] = p.send(held.at[1, low], near_x.at[low], p.x)
        elif u == 5:
            moves["y", 1] = p.send(held.at[2, low], near_y.at[low], p.y)

    for u in range(8):
        for started in loads(u):
            started.start()

    def unit(u):
        if u >= 2:
            p.copies[across[u - 2]].wait_send()
        compute(u)
        i, h = UNITS[u]
        across[u] = p.send(given.at[u % 2], other.at[i, halves[h]], p.sibling)

    def wait_loads(units_here):
        for u in units_here:
            for started in loads(u):
                started.wait()

    for started in row_loads:
        started.start()
    wait_loads((0,))
    unit(0)
    wait_loads((1,))
    unit(1)
    settle(0)
    wait_loads((2, 3))
    unit(2)
    settle(1)
    unit(3)
    settle(2)
    wait_loads((4, 5, 6, 7))
    unit(4)
    tiles.run(0, 2)
    settle(3)
    unit(5)
    settle(4)
    unit(6)
    settle(5)
    unit(7)
    settle(6)
    settle(7)
    tiles.run(2, tiles.count)

    def work(rows):
        value = middle[rows, :]
        root = row_root(value)
        normed = value * root
        total = sum(part[rows, :].astype(jnp.float32) for part in (held.at[3], near_x, near_y))
        slope = total * gain[1:2, :]
        mean = jnp.mean(slope * normed, axis=-1, keepdims=True)
        gradient = cotangent[rows, :].astype(jnp.float32) + root * (slope - normed * mean)
        grad_middle[rows, :] = gradient
        hidden[rows, :] = (residual_scale * gradient).astype(jnp.bfloat16)

    for started in row_loads:
        started.wait()
    for h in range(2):
        p.arrive(moves["x", h], near_x.at[halves[h]])
        p.arrive(moves["y", h], near_y.at[halves[h]])
        slabs(h * half, half, work)
    for u in (6, 7):
        p.copies[across[u]].wait_send()
    tiles.finish()
    for number, started in enumerate(p.copies):
        if number not in across.values():
            started.wait_send()


def second_plane(slopes, normed_rows, weights, middle, cotangent, gain, early):
    share, width = middle.shape
    count, units = slopes.shape[0], slopes.shape[1] // 2
    kind = jnp.bfloat16
    half = share // 2
    quarter = pltpu.VMEM((4, share, width), kind)
    return pl.pallas_call(
        second_kernel,
        out_shape=[
            jax.ShapeDtypeStruct((share, width), jnp.float32),
            jax.ShapeDtypeStruct((share, width), kind),
            jax.ShapeDtypeStruct((width, units), kind),
        ],
        in_specs=[ANY] * 5 + [VMEM, ANY],
        out_specs=[VMEM, VMEM, ANY],
        scratch_shapes=wires(8 + 6)
        + [
            pltpu.SemaphoreType.DMA((8, 4)),
            pltpu.SemaphoreType.DMA((2 + width // 512,)),
            pltpu.VMEM(weights.shape, kind),
            pltpu.VMEM((share, width), jnp.float32),
            pltpu.VMEM((share, width), kind),
        ]
        + tile_scratch(count, units)
        + [
            pltpu.VMEM((count, units), kind),
            pltpu.VMEM((count, units), kind),
            pltpu.VMEM((2, half, width), kind),
            quarter,
            quarter,
            pltpu.VMEM((share, width), kind),
            pltpu.VMEM((share, width), kind),
            pltpu.VMEM((half, width), kind),
            pltpu.VMEM((half, width), kind),
        ],
        compiler_params=pltpu.CompilerParams(
            collective_id=3, has_side_effects=True, vmem_limit_bytes=60 * 1024 * 1024
        ),
        cost_estimate=lasting(60),
        name="second_rows",
    )(slopes, normed_rows, weights, middle, cotangent, gain, early)


def spread_kernel(
    hidden, m, down_in, normed_rows, slopes, early, out, pair_own, pair_x, pair_y, pair_both,
    weight_grads, sent, landed, local, loading, tile_wires, rows_in, tile_out, up_in,
    m_in, given, held, theirs, down_w,
):
    p = Plane(sent, landed)
    share, width = hidden.shape
    gather = Gather(p, hidden, out)
    for k in range(CHUNKS):
        gather.start(k)
    mine = pltpu.make_async_copy(hidden, out.at[p.rank, p.core], local.at[4])
    mine.start()
    order = (p.rank, p.at_x, p.at_y, p.at_both)
    halves = pl.ds(0, share), pl.ds(share, share)

    def loads(i):
        for j, core in enumerate((1 - p.core, p.core)):
            yield pltpu.make_async_copy(
                m.at[order[i], core], m_in.at[i % 2, halves[j]], loading.at[i % 2, j]
            )

    across = []
    units = up_in.shape[1]
    up_load = pltpu.make_async_copy(slopes.at[:, pl.ds(units, units)], up_in, local.at[5])
    down_load = pltpu.make_async_copy(down_in, down_w, local.at[6])
    down_load.start()
    up_load.start()
    for started in loads(0):
        started.start()
    down_load.wait()
    tiles = WeightTiles(normed_rows, up_in, weight_grads, rows_in, tile_out, tile_wires)
    for i in range(4):
        for started in loads(i):
            started.wait()
        if i < 3:
            for started in loads(i + 1):
                started.start()

        def step(j, carry, i=i):
            cut = pl.ds(pl.multiple_of(j * 512, 512), 512)
            value = dot(m_in[i % 2], down_w[cut, :], LAST)
            given[i, :, cut] = value[:share].astype(jnp.bfloat16)
            held[i, :, cut] = value[share:].astype(jnp.bfloat16)
            return carry

        lax.fori_loop(0, width // 512, step, 0)
        across.append(p.send(given.at[i], theirs.at[i], p.sibling))
        if i == 0:
            up_load.wait()
        gather.forward_chunk(i)
        tiles.run(i, i + 1)
    kept = []
    for i in range(4):
        p.arrive(across[i], theirs.at[i])
        add_rows(held.at[i], theirs.at[i], 0, share)
        target = (pair_own, pair_x, pair_y, pair_both)[i]
        kept.append(pltpu.make_async_copy(held.at[i], target, local.at[i]))
        kept[i].start()
    gather.forward_far()
    tiles.run(4, tiles.count)
    tiles.finish()
    gather.finish()
    p.finish()
    mine.wait()
    for started in kept:
        started.wait()


def spread_plane(hidden, m, down_w, normed_rows, slopes, early):
    share, width = hidden.shape
    units = m.shape[1]
    full = jax.ShapeDtypeStruct((4, 2, share, width), jnp.bfloat16)
    quarter = pltpu.VMEM((4, share, width), jnp.bfloat16)
    out, *pairs, weight_grads = pl.pallas_call(
        spread_kernel,
        out_shape=[full]
        + [jax.ShapeDtypeStruct((share, width), jnp.bfloat16)] * 4
        + [jax.ShapeDtypeStruct((width, units), jnp.bfloat16)],
        in_specs=[VMEM] + [ANY] * 5,
        out_specs=[ANY] * 6,
        scratch_shapes=wires(GATHER_COPIES + 4)
        + [
            pltpu.SemaphoreType.DMA((7,)),
            pltpu.SemaphoreType.DMA((2, 2)),
        ]
        + tile_scratch(8 * share, units)
        + [
            pltpu.VMEM((8 * share, units), jnp.bfloat16),
            pltpu.VMEM((2, 2 * share, units), jnp.bfloat16),
            quarter,
            quarter,
            quarter,
            pltpu.VMEM(down_w.shape, jnp.bfloat16),
        ],
        compiler_params=pltpu.CompilerParams(
            collective_id=7, has_side_effects=True, vmem_limit_bytes=60 * 1024 * 1024
        ),
        cost_estimate=lasting(60),
        name="spread_rows",
    )(hidden, m.reshape(4, 2, share, units), down_w, normed_rows, slopes, early)
    return out.reshape(8 * share, width), pairs, weight_grads


def lane_sums(pairs):
    total = 0.0
    for a, b in pairs:
        product = a.astype(jnp.float32) * b.astype(jnp.float32)
        total += jnp.sum(product, axis=1, keepdims=True)
    return jnp.broadcast_to(total, (total.shape[0], 128))


LATER = 10


def last_kernel(
    back,
    weights,
    gain,
    ups,
    early,
    *rest,
):
    later, rest = rest[:LATER], rest[LATER:]
    out, result_out, up_out, gain_out, sent, landed, local, loading, held, result, sums = rest[:11]
    landing, scratch = rest[11 : 11 + LATER], rest[11 + LATER :]
    share = landing[8].shape[0]
    first = pl.ds(pl.multiple_of(lax.axis_index("tensor") * share, SLAB), share)
    later = [*later[:8], later[8].at[first], later[9]]
    loads = [
        pltpu.make_async_copy(source, target, loading.at[i])
        for i, (source, target) in enumerate(zip(later, landing))
    ]
    for started in loads:
        started.start()
    middle, ffn_own, ffn_x, ffn_y, ffn_both, gates, gate, up, residual, grad_middle = landing
    p = Plane(sent, landed, diagonal=True)
    moves = []

    def hand_back(partner, rank):
        moves.append((p.send(ups.at[rank], up_out.at[p.rank], partner), up_out.at[rank]))

    hand_back(p.both, p.at_both)
    total = Scatter(p, back, weights, slice(0, back.shape[3]), *scratch)
    hand_back(p.x, p.at_x)
    hand_back(p.y, p.at_y)
    up_out[p.rank] = ups[p.rank]
    share = held.shape[0]

    def finish_result(rows):
        parts = (ffn_own, ffn_x, ffn_y, ffn_both)
        ffn = sum(part[rows, :].astype(jnp.float32) for part in parts)
        result[rows, :] = (middle[rows, :] + residual_scale * ffn).astype(jnp.bfloat16)

    for started in loads:
        started.wait()
    slabs(0, share, finish_result)
    kept = [pltpu.make_async_copy(result, result_out.at[p.core], local.at[0])]
    kept[0].start()
    given = p.send(result, result_out.at[p.core], p.sibling)
    units = gate.shape[1] // 4

    def gate_rows(rows):
        sums[0, rows, :] = lane_sums(
            [(gates[c, rows, :], gate[rows, c * units : c * units + units]) for c in range(4)]
        )

    def up_rows(rows):
        sums[0, rows, :] += lane_sums(
            [(up_out[c, rows, :], up[rows, c * units : c * units + units]) for c in range(4)]
        )

    slabs(0, gate.shape[0], gate_rows)

    def work(rows):
        value = residual[rows, :].astype(jnp.float32)
        root = row_root(value)
        normed = value * root
        slope = total.rows(rows) * gain[0:1, :]
        mean = jnp.mean(slope * normed, axis=-1, keepdims=True)
        held[rows, :] = grad_middle[rows, :] + root * (slope - normed * mean)

    across = []
    for k in range(CHUNKS):
        cut = chunk(k, share)
        if k % (CHUNKS // 2) == 0:
            total.ready(k // (CHUNKS // 2))
        slabs(k * (share // CHUNKS), share // CHUNKS, work)
        across.append(p.send(held.at[cut], out.at[p.core, cut], p.sibling))
        kept.append(
            pltpu.make_async_copy(held.at[cut], out.at[p.core, cut], local.at[1 + k])
        )
        kept[1 + k].start()
    for number, target in moves:
        p.arrive(number, target)
    slabs(0, gate.shape[0], up_rows)
    swapped = p.send(sums.at[0], sums.at[1], p.sibling)
    p.arrive(swapped, sums.at[1])
    gain_out[...] = sums[0] + sums[1]
    p.arrive(given, result_out.at[1 - p.core])
    for k in range(CHUNKS):
        p.arrive(across[k], out.at[1 - p.core, chunk(k, share)])
    p.finish()
    for started in kept:
        started.wait()


def last_plane(
    back, weights, tokens, grad_middle, gain, middle, ffn_parts, ups, gates, gate, up, early
):
    share, width = grad_middle.shape
    later = [middle, *ffn_parts, gates, gate, up, tokens, grad_middle]
    out, result_out, up_out, gain_out = pl.pallas_call(
        last_kernel,
        out_shape=[
            jax.ShapeDtypeStruct((2, share, width), jnp.float32),
            jax.ShapeDtypeStruct((2, share, width), jnp.bfloat16),
            jax.ShapeDtypeStruct(ups.shape, ups.dtype),
            jax.ShapeDtypeStruct((gate.shape[0], 128), jnp.float32),
        ],
        in_specs=[VMEM] * 4 + [ANY] * (1 + LATER),
        out_specs=[ANY, ANY, VMEM, VMEM],
        scratch_shapes=wires(CHUNKS + 5 + SCATTER_COPIES)
        + [
            pltpu.SemaphoreType.DMA((1 + CHUNKS,)),
            pltpu.SemaphoreType.DMA((LATER,)),
            pltpu.VMEM((share, width), jnp.float32),
            pltpu.VMEM((share, width), jnp.bfloat16),
            pltpu.VMEM((2, gate.shape[0], 128), jnp.float32),
        ]
        + [pltpu.VMEM(array.shape, array.dtype) for array in later[:8]]
        + [pltpu.VMEM((share, width), tokens.dtype), pltpu.VMEM((share, width), jnp.float32)]
        + scatter_scratch(share, width),
        compiler_params=pltpu.CompilerParams(
            collective_id=4, has_side_effects=True, vmem_limit_bytes=VMEM_LIMIT
        ),
        cost_estimate=lasting(70),
        name="last_rows",
    )(
        back.reshape(4, 2, share, -1),
        weights,
        gain,
        ups,
        early,
        *later,
    )
    return (
        out.reshape(2 * share, width),
        result_out.reshape(2 * share, width),
        up_out,
        gain_out,
    )


def exchange_kernel(blocks, query, pair, other_sums, out, gain_out, sent, landed, sums):
    p = Plane(sent, landed, diagonal=True)
    moves = []
    for partner, rank in ((p.both, p.at_both), (p.x, p.at_x), (p.y, p.at_y)):
        moves.append((p.send(blocks.at[rank], out.at[p.rank], partner), out.at[rank]))
    out[p.rank] = blocks[p.rank]
    width = query.shape[1] // 4

    def attention_rows(rows):
        pairs = []
        for c in range(4):
            pairs.append((out[c, rows, :width], query[rows, c * width : c * width + width]))
            pairs.append((out[c, rows, width : width + 128], pair[rows, c * 128 : c * 128 + 128]))
        sums[0, rows, :] = lane_sums(pairs)

    for number, target in moves:
        p.arrive(number, target)
    slabs(0, blocks.shape[1], attention_rows)
    swapped = p.send(sums.at[0], sums.at[1], p.sibling)
    p.arrive(swapped, sums.at[1])
    gain_out[0] = sums[0] + sums[1]
    gain_out[1] = other_sums[...]
    p.finish()


def exchange(blocks, query, pair, other_sums):
    depth = blocks.shape[1]
    return pl.pallas_call(
        exchange_kernel,
        out_shape=[
            jax.ShapeDtypeStruct(blocks.shape, blocks.dtype),
            jax.ShapeDtypeStruct((2, depth, 128), jnp.float32),
        ],
        in_specs=[VMEM] * 4,
        out_specs=[VMEM] * 2,
        scratch_shapes=wires(4) + [pltpu.VMEM((2, depth, 128), jnp.float32)],
        compiler_params=pltpu.CompilerParams(collective_id=5, has_side_effects=True),
        cost_estimate=lasting(8),
        name="exchange_blocks",
    )(blocks, query, pair, other_sums)


def finish_first_kernel(down, gate, down_out, gate_out):
    down_out[...] = jnp.transpose(down[0].astype(jnp.float32))
    gate_out[...] = gate[0].astype(jnp.float32)


def finish_first(down, gate):
    groups, depth, units = down.shape
    block = pl.BlockSpec((1, depth, units), lambda i: (i, 0, 0))
    return pl.pallas_call(
        finish_first_kernel,
        grid=(groups,),
        in_specs=[block, block],
        out_specs=[
            pl.BlockSpec((units, depth), lambda i: (i, 0)),
            pl.BlockSpec((depth, units), lambda i: (0, i)),
        ],
        out_shape=[
            jax.ShapeDtypeStruct((groups * units, depth), jnp.float32),
            jax.ShapeDtypeStruct((depth, groups * units), jnp.float32),
        ],
        compiler_params=pltpu.CompilerParams(vmem_limit_bytes=VMEM_LIMIT),
        cost_estimate=lasting(5),
        name="finish_first",
    )(down, gate)


def finish_kernel(
    attn, up, tokens, result, sums, gains,
    query_out, key_out, value_out, out_out, up_out, tokens_out, result_out, gain_out,
):
    width = query_out.shape[1]
    query_out[...] = attn[0, :, :width].astype(jnp.float32)
    for c in range(key_out.shape[1] // HEAD):

        @pl.when(pl.program_id(0) == c)
        def _(c=c):
            cut = slice(c * HEAD, c * HEAD + HEAD)
            key_out[:, cut] = attn[0, :, width : width + HEAD].astype(jnp.float32)
            value_out[:, cut] = attn[0, :, width + HEAD : width + 2 * HEAD].astype(jnp.float32)

    out_out[...] = jnp.transpose(attn[0, :, width + 128 :].astype(jnp.float32))
    up_out[...] = up[0].astype(jnp.float32)
    tokens_out[...] = tokens[...]
    result_out[...] = result[...]
    for i in range(2):
        gain_out[i : i + 1, :] = jnp.transpose(sums[i])[0:1] / gains[i : i + 1, :]


def finish(attn, up, tokens, result, sums, gains):
    groups, depth, units = up.shape
    width = attn.shape[2] // 2 - HEAD
    rows, columns = tokens.shape
    part = rows // groups

    def block(*shape):
        return pl.BlockSpec((1, *shape), lambda i: (i, 0, 0))

    def wide(count):
        return pl.BlockSpec((depth, count), lambda i: (0, i))

    def tall(count, other):
        return pl.BlockSpec((count, other), lambda i: (i, 0))

    def f32(*shape):
        return jax.ShapeDtypeStruct(shape, jnp.float32)

    return pl.pallas_call(
        finish_kernel,
        grid=(groups,),
        in_specs=[
            block(depth, attn.shape[2]),
            block(depth, units),
            tall(part, columns),
            tall(part, columns),
            pl.BlockSpec(sums.shape, lambda i: (0, 0, 0)),
            pl.BlockSpec(gains.shape, lambda i: (0, 0)),
        ],
        out_specs=[
            wide(width),
            pl.BlockSpec((depth, groups * HEAD), lambda i: (0, 0)),
            pl.BlockSpec((depth, groups * HEAD), lambda i: (0, 0)),
            tall(width, depth),
            wide(units),
            tall(part, columns),
            tall(part, columns),
            pl.BlockSpec((2, 128), lambda i: (0, 0)),
        ],
        out_shape=[
            f32(depth, groups * width),
            f32(depth, groups * HEAD),
            f32(depth, groups * HEAD),
            f32(groups * width, depth),
            f32(depth, groups * units),
            f32(rows, columns),
            jax.ShapeDtypeStruct(result.shape, result.dtype),
            f32(2, 128),
        ],
        compiler_params=pltpu.CompilerParams(vmem_limit_bytes=VMEM_LIMIT),
        cost_estimate=lasting(12),
        name="finish",
    )(attn, up, tokens, result, sums, gains)


def context_pairs(step):
    return [(i, i ^ step) for i in range(4)]


def ffn_first_kernel(hidden, weights, m, gate, up):
    units = m.shape[1]
    for j in range(units // 256):
        cut = slice(j * 256, j * 256 + 256)
        gate_part = dot(hidden[...], weights[:, cut])
        up_part = dot(hidden[...], weights[:, units + j * 256 : units + j * 256 + 256])
        gate[:, cut] = gate_part.astype(jnp.bfloat16)
        up[:, cut] = up_part.astype(jnp.bfloat16)
        sigmoid = 1.0 / (1.0 + jnp.exp(-gate_part))
        m[:, cut] = (gate_part * sigmoid * up_part).astype(jnp.bfloat16)


def ffn_slopes_kernel(grad, gate, up, down_w, early, slopes):
    units = down_w.shape[1]
    for j in range(units // 256):
        cut = slice(j * 256, j * 256 + 256)
        grad_part = dot(grad[...], down_w[:, cut])
        gate_part = gate[:, cut].astype(jnp.float32)
        up_part = up[:, cut].astype(jnp.float32)
        sigmoid = 1.0 / (1.0 + jnp.exp(-gate_part))
        slope = sigmoid * (1.0 + gate_part * (1.0 - sigmoid))
        slopes[:, cut] = (grad_part * up_part * slope).astype(jnp.bfloat16)
        slopes[:, units + j * 256 : units + j * 256 + 256] = (
            grad_part * gate_part * sigmoid
        ).astype(jnp.bfloat16)


def first_rows_kernel(values, gains, weight, hidden, raw):
    value = values[...].astype(jnp.float32)
    normed = (value * row_root(value) * gains[0:1, :]).astype(jnp.bfloat16)
    hidden[...] = normed
    raw[...] = dot(normed, weight[...])


def first_rows(values, gains, packed, columns):
    count, width = values.shape
    return pl.pallas_call(
        first_rows_kernel,
        grid=(count // ROW_TILE,),
        in_specs=[
            pl.BlockSpec((ROW_TILE, width), lambda i: (i, 0)),
            pl.BlockSpec((8, width), lambda i: (0, 0)),
            pl.BlockSpec((width, columns), lambda i: (0, 0)),
        ],
        out_specs=[
            pl.BlockSpec((ROW_TILE, width), lambda i: (i, 0)),
            pl.BlockSpec((ROW_TILE, columns), lambda i: (i, 0)),
        ],
        out_shape=[
            jax.ShapeDtypeStruct((count, width), jnp.bfloat16),
            jax.ShapeDtypeStruct((count, columns), jnp.float32),
        ],
        compiler_params=pltpu.CompilerParams(vmem_limit_bytes=VMEM_LIMIT),
        cost_estimate=lasting(4),
        name="first_rows",
    )(values, gains, packed)


def attention_weights_kernel(hidden, back, grad, attended, moving, *rest):
    out, moved, sent, landed, local = rest[-5:]
    step, last = pl.program_id(0), pl.num_programs(0) - 1

    @pl.when(step == 0)
    def start():
        p = Plane(sent, landed, diagonal=True)
        pltpu.make_async_copy(moving.at[p.rank], moved.at[p.rank], local).start()
        for partner, rank in ((p.both, p.at_both), (p.x, p.at_x), (p.y, p.at_y)):
            p.send(moving.at[rank], moved.at[p.rank], partner)

    columns = back.shape[1]
    out[:, :columns] = dot(hidden[...], back[...], FIRST).astype(jnp.bfloat16)
    out[:, columns:] = dot(grad[...], attended[...], FIRST).astype(jnp.bfloat16)

    @pl.when(step == last)
    def finish():
        p = Plane(sent, landed, entered=True)
        for number, rank in enumerate((p.at_both, p.at_x, p.at_y)):
            move = p.copy(number, moving.at[rank], moved.at[rank], p.x)
            move.wait_recv()
            move.wait_send()
        pltpu.make_async_copy(moving.at[p.rank], moved.at[p.rank], local).wait()


def attention_weights(hidden, back, grad, attended, moving, early):
    count, width = hidden.shape
    first, second = back.shape[1], attended.shape[1]
    tall = pl.BlockSpec((count, 256), lambda i: (0, i))
    return pl.pallas_call(
        attention_weights_kernel,
        grid=(width // 256,),
        in_specs=[
            tall,
            pl.BlockSpec((count, first), lambda i: (0, 0)),
            tall,
            pl.BlockSpec((count, second), lambda i: (0, 0)),
        ]
        + [ANY] * (1 + len(early)),
        out_specs=[pl.BlockSpec((256, first + second), lambda i: (i, 0)), ANY],
        out_shape=[
            jax.ShapeDtypeStruct((width, first + second), jnp.bfloat16),
            jax.ShapeDtypeStruct(moving.shape, moving.dtype),
        ],
        scratch_shapes=wires(3) + [pltpu.SemaphoreType.DMA],
        compiler_params=pltpu.CompilerParams(
            collective_id=8, has_side_effects=True, vmem_limit_bytes=VMEM_LIMIT
        ),
        cost_estimate=lasting(25),
        name="attention_weights",
    )(hidden, back, grad, attended, moving, *early)


ROW_TILE = 256


def row_tiles(kernel, name, rows, weights, extra, widths):
    count = rows[0].shape[0]

    def tile(width):
        return pl.BlockSpec((ROW_TILE, width), lambda i: (i, 0))

    whole = [
        pl.BlockSpec(w.shape, lambda i: (0, 0), pipeline_mode=pl.Buffered(1)) for w in weights
    ]
    flops = 2 * count * sum(w.size for w in weights)
    return pl.pallas_call(
        kernel,
        grid=(count // ROW_TILE,),
        in_specs=[tile(r.shape[1]) for r in rows] + whole + [ANY] * len(extra),
        out_specs=[tile(width) for width in widths],
        out_shape=[jax.ShapeDtypeStruct((count, width), jnp.bfloat16) for width in widths],
        compiler_params=pltpu.CompilerParams(vmem_limit_bytes=56 * 1024 * 1024),
        cost_estimate=pl.CostEstimate(flops=flops, bytes_accessed=flops // 400, transcendentals=0),
        name=name,
    )(*rows, *weights, *extra)


def norm_backward(gradient, normed, inv_root):
    return inv_root * (gradient - normed * jnp.mean(gradient * normed, axis=-1, keepdims=True))


def inverse_root(values):
    return lax.rsqrt(jnp.mean(values * values, axis=-1, keepdims=True) + epsilon)


PLANE = ("context", "tensor")


def gather_rows(values):
    return lax.all_gather(values, PLANE, axis=0, tiled=True)


def scatter_rows(partial):
    return lax.psum_scatter(
        partial.astype(jnp.bfloat16), PLANE, scatter_dimension=0, tiled=True
    ).astype(jnp.float32)


def local(
    tokens,
    cotangent,
    attn_gain,
    w_query,
    w_key,
    w_value,
    w_out,
    ffn_gain,
    w_gate,
    w_up,
    w_down,
    piece_segment,
    piece_parent,
    piece_start,
):
    groups = lax.axis_size("context")
    cores = lax.axis_size("tensor")
    depth = w_query.shape[0]
    kv_count = w_key.shape[1] // HEAD
    sharing = groups // kv_count
    share = tokens.shape[0] // cores
    first_row = lax.axis_index("tensor") * share

    def my_rows(values):
        return lax.dynamic_slice_in_dim(values, first_row, share, 0)

    def blocks(weight):
        return jnp.transpose(weight.reshape(depth, groups, -1), (1, 0, 2))

    def kv_blocks(weight):
        return jnp.repeat(jnp.transpose(weight.reshape(depth, kv_count, HEAD), (1, 0, 2)), sharing, 0)

    def spread(weight_blocks):
        mine = lax.all_to_all(weight_blocks, "context", 0, 0)
        mine = mine.reshape(groups * depth, -1)
        return lax.all_gather(mine, "fsdp", axis=0, tiled=True)

    square = groups == 4 and cores == 2
    width = w_query.shape[1] // groups
    columns_qkv = width + 2 * HEAD
    out_turned, down_turned = w_out.T, w_down.T
    tokens_half, cotangent_half = my_rows(tokens), my_rows(cotangent)

    def over_groups(blocks_here):
        return lax.all_gather(
            blocks_here.reshape(groups * depth, -1), "fsdp", axis=0, tiled=True
        )

    if square:
        gains = jnp.pad(jnp.stack([attn_gain, ffn_gain]).astype(jnp.float32), ((0, 6), (0, 0)))
        w_pair = jnp.stack(
            [w_key.reshape(depth, groups, HEAD), w_value.reshape(depth, groups, HEAD)], axis=2
        ).reshape(depth, -1)
        packed, gain_rows = first_exchange(w_query, w_pair, out_turned, gains)
        packed = over_groups(packed)
        both_blocks, down_blocks = exchange_columns(w_gate, w_up, down_turned, gain_rows)
        inputs_full, ffn_grad, my_ffn_grad = start_plane(tokens, cotangent, down_blocks)
        both_full, down_full = over_groups(both_blocks), over_groups(down_blocks)
        hidden_first, raw = first_rows(
            inputs_full.reshape(-1, inputs_full.shape[3]), gain_rows, packed, columns_qkv
        )
        out_full = packed[:, columns_qkv:]
    else:
        gains = jnp.stack([attn_gain, ffn_gain], axis=1)
        gains = jnp.broadcast_to(jnp.pad(gains, ((0, 0), (0, 126))), (groups, depth, 128))
        packed = spread(
            jnp.concatenate(
                [
                    blocks(w_query),
                    kv_blocks(w_key),
                    kv_blocks(w_value),
                    blocks(out_turned),
                    gains,
                ],
                axis=2,
            )
        )
        qkv_full = packed[:, :columns_qkv]
        out_full = packed[:, columns_qkv : columns_qkv + width]
        gains_full = packed[:, columns_qkv + width :].astype(jnp.float32)
        attn_scale, ffn_scale = gains_full[:, 0], gains_full[:, 1]
        both_full = spread(jnp.concatenate([blocks(w_gate), blocks(w_up)], axis=2))
        down_full = spread(blocks(down_turned))
        inputs_full = gather_rows(tokens_half).astype(jnp.float32)
        hidden_first = inputs_full * inverse_root(inputs_full) * attn_scale
        hidden_first = hidden_first.astype(jnp.bfloat16)
        raw = dot(hidden_first, qkv_full)
        my_ffn_grad = (residual_scale * cotangent_half.astype(jnp.float32)).astype(jnp.bfloat16)
    tables = rope_tables()

    segment, starts = piece_segment[0] % 13, piece_start[0]
    places = jnp.where(
        segment == 0,
        starts,
        jnp.where(
            segment <= BRANCHES,
            starts + (segment - 1) * SEG,
            starts + (segment - 1 - BRANCHES) * SEG + (BRANCHES - 1) * SEG,
        ),
    )

    residual_in = tokens_half.astype(jnp.float32)
    grad_result = cotangent_half.astype(jnp.float32)

    attended, *kept = attention_forward(places, starts, raw, tables)
    if square:
        ffn_grad_blocks = [
            lax.ppermute(my_ffn_grad, "context", context_pairs(step)) for step in (1, 2, 3)
        ]
        hidden_block, middle = middle_plane(attended, packed, tokens, gain_rows)
    else:
        ffn_grad = gather_rows(my_ffn_grad)
        middle = residual_in + residual_scale * scatter_rows(dot(attended, out_full, LAST))
        hidden_second = gather_rows((middle * inverse_root(middle) * ffn_scale).astype(jnp.bfloat16))

    units = down_full.shape[1]
    if square:
        hidden_second, hidden, gate_proj, up_proj, ffn_grad = ffn_rows(
            hidden_block, both_full, ffn_grad, ffn_grad_blocks
        )
    else:
        hidden, gate_proj, up_proj = row_tiles(
            ffn_first_kernel,
            "ffn_first",
            [hidden_second],
            [both_full],
            [],
            [units, units, units],
        )
    grad_down = dot(ffn_grad, hidden, FIRST).astype(jnp.bfloat16)
    (slopes,) = row_tiles(
        ffn_slopes_kernel,
        "ffn_slopes",
        [ffn_grad, gate_proj, up_proj],
        [down_full],
        [grad_down],
        [2 * units],
    )
    def sum_groups(gradient):
        return lax.psum_scatter(gradient, "fsdp", scatter_dimension=0, tiled=True)

    def hand_back(gradient):
        return lax.all_to_all(gradient.reshape(groups, depth, -1), "context", 0, 0)

    def columns(gradient):
        return jnp.transpose(gradient, (1, 0, 2)).reshape(depth, -1).astype(jnp.float32)

    if square:
        grad_middle, my_attn_grad, grad_gate = second_plane(
            slopes,
            hidden_second,
            both_full,
            middle,
            cotangent,
            gain_rows,
            grad_down,
        )
        attn_grad, ffn_pairs, grad_up = spread_plane(
            my_attn_grad, hidden, down_full, hidden_second, slopes, grad_gate
        )
        ffn_parts = [ffn_pairs[0]] + [
            lax.ppermute(ffn_pairs[step], "context", context_pairs(step)) for step in (1, 2, 3)
        ]
    else:
        root = inverse_root(middle)
        ffn_out = dot(hidden, down_full, LAST)
        grad_gate = dot(hidden_second, slopes[:, :units], FIRST).astype(jnp.bfloat16)
        grad_up = dot(hidden_second, slopes[:, units:], FIRST).astype(jnp.bfloat16)
        grad_second = dot(slopes, both_full, LAST)
        grad_middle = grad_result + norm_backward(
            scatter_rows(grad_second) * ffn_scale, middle * root, root
        )
        attn_grad = gather_rows((residual_scale * grad_middle).astype(jnp.bfloat16))
        ffn_parts = []
    grad_attended = dot(attn_grad, out_full).astype(jnp.bfloat16)
    grad_down = sum_groups(grad_down)
    grad_gate, grad_up = sum_groups(grad_gate), sum_groups(grad_up)
    back = attention_backward(places, starts, grad_attended, kept, tables, [grad_down])
    grad_down = hand_back(grad_down)
    if square:
        grad_attn, grad_gate = attention_weights(
            hidden_first,
            back,
            attn_grad,
            attended,
            grad_gate.reshape(groups, depth, -1),
            [grad_down, *ffn_parts[1:]],
        )
    else:
        grad_attn = jnp.concatenate(
            [dot(hidden_first, back, FIRST), dot(attn_grad, attended, FIRST)], axis=1
        ).astype(jnp.bfloat16)
        grad_first = dot(back, qkv_full, LAST).astype(jnp.bfloat16)
        grad_gate, grad_up = hand_back(grad_gate), hand_back(grad_up)
    grad_attn = sum_groups(grad_attn)
    if square:
        down, gate = finish_first(grad_down, grad_gate)
        grad_tokens, result, grad_up, ffn_sums = last_plane(
            back,
            packed,
            tokens,
            grad_middle,
            gain_rows,
            middle,
            ffn_parts,
            grad_up.reshape(groups, depth, -1),
            grad_gate,
            w_gate,
            w_up,
            down,
        )
        grad_attn, sums = exchange(
            grad_attn.reshape(groups, depth, -1), w_query, w_pair, ffn_sums
        )
        my_gains = jnp.stack([attn_gain, ffn_gain]).astype(jnp.float32)
        query, key, value, out, up, grad_tokens, result, gain_grads = finish(
            grad_attn, grad_up, grad_tokens, result, sums, my_gains
        )
        return (
            result,
            grad_tokens,
            gain_grads[0],
            query,
            key,
            value,
            out,
            gain_grads[1],
            gate,
            up,
            down,
        )
    else:
        root = inverse_root(residual_in)
        grad_tokens = grad_middle + norm_backward(
            scatter_rows(grad_first) * attn_scale, residual_in * root, root
        )
        grad_tokens = lax.all_gather(grad_tokens, "tensor", axis=0, tiled=True)
        result = (middle + residual_scale * scatter_rows(ffn_out)).astype(jnp.bfloat16)
        grad_attn = hand_back(grad_attn)
        result = lax.all_gather(result, "tensor", axis=0, tiled=True)
    def kv_columns(gradient):
        gradient = gradient.astype(jnp.float32).reshape(kv_count, sharing, depth, HEAD)
        return jnp.transpose(jnp.sum(gradient, axis=1), (1, 0, 2)).reshape(depth, -1)

    grad_query = columns(grad_attn[:, :, :width])
    grad_key = kv_columns(grad_attn[:, :, width : width + HEAD])
    grad_value = kv_columns(grad_attn[:, :, width + HEAD : width + 2 * HEAD])
    grad_gate, grad_up = columns(grad_gate), columns(grad_up)

    def against(*pairs):
        return sum(jnp.sum(weight.astype(jnp.float32) * g, axis=1) for weight, g in pairs)

    gain_grads = jnp.stack(
        [
            against((w_query, grad_query), (w_key, grad_key), (w_value, grad_value)),
            against((w_gate, grad_gate), (w_up, grad_up)),
        ]
    )
    gain_grads = lax.psum(gain_grads, "tensor")
    return (
        result,
        grad_tokens,
        gain_grads[0] / attn_gain.astype(jnp.float32),
        grad_query,
        grad_key,
        grad_value,
        columns(grad_attn[:, :, width + 2 * HEAD :]).T,
        gain_grads[1] / ffn_gain.astype(jnp.float32),
        grad_gate,
        grad_up,
        columns(grad_down).T,
    )


ROWS = ("fsdp", "context")


def solution(mesh):
    return jax.shard_map(
        local,
        mesh=mesh,
        in_specs=(
            P(ROWS, None),
            P(ROWS, None),
            P(ROWS),
            P(ROWS, "tensor"),
            P(ROWS, "tensor"),
            P(ROWS, "tensor"),
            P("tensor", ROWS),
            P(ROWS),
            P(ROWS, "tensor"),
            P(ROWS, "tensor"),
            P("tensor", ROWS),
            P("fsdp", None),
            P("fsdp", None),
            P("fsdp", None),
        ),
        out_specs=(
            P(ROWS, None),
            P(ROWS, None),
            P(ROWS),
            P(ROWS, "tensor"),
            P(ROWS, "tensor"),
            P(ROWS, "tensor"),
            P("tensor", ROWS),
            P(ROWS),
            P(ROWS, "tensor"),
            P(ROWS, "tensor"),
            P("tensor", ROWS),
        ),
        check_vma=False,
    )
```

```python
import functools

import jax
import jax.numpy as jnp
import numpy as np
from jax import lax
from jax.experimental import pallas as pl
from jax.experimental.pallas import tpu as pltpu
from jax.sharding import PartitionSpec as P

HEAD = 64
SEG = 128
TRUNK = 8 * SEG
BRANCHES = 4
LEAVES = 8
GROUP = TRUNK + (BRANCHES + LEAVES) * SEG
DEPTH = TRUNK + 2 * SEG
TILE = 2 * SEG

epsilon = 1e-05
rope_base = 10000000.0
residual_scale = 0.22
score_scale = 0.015625
masked_score = -1e30

FIRST = (((0,), (0,)), ((), ()))
LAST = (((1,), (1,)), ((), ()))
PLAIN = (((1,), (0,)), ((), ()))


def dot(left_side, right_side, dims=PLAIN):
    return lax.dot_general(left_side, right_side, dims, preferred_element_type=jnp.float32)


def rope_tables():
    steps = np.arange(HEAD // 2, dtype=np.float32)
    frequency = np.float32(rope_base) ** (-(steps * np.float32(2)) / np.float32(HEAD))
    angles = np.arange(DEPTH, dtype=np.float32)[:, None] * frequency.astype(np.float32)
    angles = angles.astype(np.float64)
    cosine, sine = np.cos(angles).astype(np.float32), np.sin(angles).astype(np.float32)
    return (
        jnp.asarray(np.concatenate([cosine] * 4, axis=-1)),
        jnp.asarray(np.concatenate([-sine, sine, -sine, sine], axis=-1)),
    )


def lanes(values):
    return lax.broadcasted_iota(jnp.int32, values.shape, 1)


def swap_halves(values):
    return jnp.where(
        lanes(values) % HEAD < HEAD // 2,
        pltpu.roll(values, 128 - HEAD // 2, 1),
        pltpu.roll(values, HEAD // 2, 1),
    )


def only_head(values, head):
    return jnp.where(lanes(values) // HEAD == head, values, jnp.zeros_like(values))


def query_tiles(work):
    for j in range(TRUNK // TILE):
        prefix = [(0, j * TILE, False)] if j else []
        work(j * TILE, prefix + [(j * TILE, TILE, True)], False)

    def branch(i, carry):
        row = pl.multiple_of(TRUNK + i * TILE, TILE)
        work(row, [(0, TRUNK, False), (row, TILE, True)], True)
        return carry

    lax.fori_loop(0, BRANCHES * SEG // TILE, branch, 0)

    def leaf(i, carry):
        row = pl.multiple_of(TRUNK + BRANCHES * SEG + i * TILE, TILE)
        parent = pl.multiple_of(TRUNK + i * SEG, SEG)
        work(row, [(0, TRUNK, False), (parent, SEG, False), (row, TILE, True)], True)
        return carry

    lax.fori_loop(0, LEAVES * SEG // TILE, leaf, 0)


def visible_scores(keys, query, own, one_segment):
    scores = dot(keys, query, LAST)
    if not own:
        return scores
    key_at = lax.broadcasted_iota(jnp.int32, scores.shape, 0)
    query_at = lax.broadcasted_iota(jnp.int32, scores.shape, 1)
    seen = key_at <= query_at
    if one_segment:
        seen = seen & (key_at // SEG == query_at // SEG)
    return jnp.where(seen, scores, masked_score)


def turned_over(target, source):
    for first in range(0, source.shape[0], TILE):
        block = source[first : first + TILE, :128].astype(jnp.float32)
        target[:, first : first + TILE] = jnp.transpose(block)[:HEAD].astype(jnp.bfloat16)


def head_pairs(width, work):
    together = min(PAIR, width // HEAD)

    def step(i, carry):
        work([i * together + j for j in range(together)])
        return carry

    lax.fori_loop(0, width // HEAD // together, step, 0)


PAIR = 2


def attention_forward_kernel(
    to_ref, start_ref, raw_ref, cos_ref, sin_ref, out_ref, q_ref, k_ref, v_ref, log_ref,
    held, values_ref, tile_ref,
):
    width = q_ref.shape[1]
    pieces = to_ref.shape[0]
    piece = raw_ref.shape[0] // pieces

    def place(p, carry):
        rows = pl.ds(pl.multiple_of(p * piece, piece), piece)
        to = pl.ds(pl.multiple_of(to_ref[p], piece), piece)
        at = pl.ds(pl.multiple_of(start_ref[p], piece), piece)
        cosine, sine = cos_ref[at, :], sin_ref[at, :]

        def turn(values):
            return values * cosine + swap_halves(values) * sine

        for g in range(width // 128):
            cut = slice(g * 128, g * 128 + 128)
            turned = turn(raw_ref[rows, cut]).astype(jnp.bfloat16)
            q_ref[to, cut] = turned * jnp.bfloat16(score_scale)
        pair = raw_ref[rows, width : width + 128]
        low = lanes(pair) < HEAD
        key = turn(pair)
        key = jnp.where(low, key, pltpu.roll(key, HEAD, 1)).astype(jnp.bfloat16)
        value = jnp.where(low, pltpu.roll(pair, HEAD, 1), pair).astype(jnp.bfloat16)
        for g in range(width // 128):
            cut = slice(g * 128, g * 128 + 128)
            k_ref[to, cut] = key
            v_ref[to, cut] = value
        return carry

    lax.fori_loop(0, pieces, place, 0)
    turned_over(values_ref, v_ref)

    def work(row, parts, one_segment):
        rows = pl.ds(row, TILE)

        def one_head(head):
            query = only_head(q_ref[rows, :], head)
            scores = [
                visible_scores(k_ref[pl.ds(first, count), :], query, own, one_segment)
                for first, count, own in parts
            ]
            largest = functools.reduce(
                jnp.maximum, [jnp.max(s, axis=0, keepdims=True) for s in scores]
            )
            exponent = [jnp.exp(s - largest) for s in scores]
            total = functools.reduce(
                jnp.add, [jnp.sum(e, axis=0, keepdims=True) for e in exponent]
            )
            result = functools.reduce(
                jnp.add,
                [
                    dot(values_ref[:, pl.ds(first, count)], e.astype(jnp.bfloat16))
                    for e, (first, count, own) in zip(exponent, parts)
                ],
            )
            log_ref[head, :, rows] = largest + jnp.log(total)
            tile_ref[pl.ds(pl.multiple_of(head * HEAD, HEAD), HEAD), :] = result * (1.0 / total)

        def heads(together):
            for head in together:
                one_head(head)

        head_pairs(width, heads)
        held[rows, :] = jnp.transpose(tile_ref[...]).astype(jnp.bfloat16)

    query_tiles(work)

    def back(p, carry):
        rows = pl.ds(pl.multiple_of(p * piece, piece), piece)
        to = pl.ds(pl.multiple_of(to_ref[p], piece), piece)
        out_ref[rows, :] = held[to, :]
        return carry

    lax.fori_loop(0, pieces, back, 0)


def attention_backward_kernel(
    to_ref,
    start_ref,
    grad_ref,
    q_ref,
    k_ref,
    v_ref,
    log_ref,
    cos_ref,
    sin_ref,
    *rest,
):
    out_ref, og_ref, dq_ref, dk_ref, dv_ref, keys_ref, tile_ref = rest[-7:]
    width = q_ref.shape[1]
    pieces = to_ref.shape[0]
    piece = grad_ref.shape[0] // pieces

    def place(p, carry):
        rows = pl.ds(pl.multiple_of(p * piece, piece), piece)
        to = pl.ds(pl.multiple_of(to_ref[p], piece), piece)
        og_ref[to, :] = grad_ref[rows, :]
        return carry

    lax.fori_loop(0, pieces, place, 0)
    turned_over(keys_ref, k_ref)
    dk_ref[...] = jnp.zeros_like(dk_ref)
    dv_ref[...] = jnp.zeros_like(dv_ref)

    def work(row, parts, one_segment):
        rows = pl.ds(row, TILE)

        def heads(together):
            queries, out_grads, all_weights, all_grads = [], [], [], []
            for head in together:
                query = only_head(q_ref[rows, :], head)
                out_grad = only_head(og_ref[rows, :], head)
                log_total = log_ref[head, :, rows]
                weights, products = [], []
                for first, count, own in parts:
                    keys = pl.ds(first, count)
                    scores = visible_scores(k_ref[keys, :], query, own, one_segment)
                    weights.append(jnp.exp(scores - log_total))
                    products.append(dot(v_ref[keys, :], out_grad, LAST))
                inner = functools.reduce(
                    jnp.add,
                    [jnp.sum(w * d, axis=0, keepdims=True) for w, d in zip(weights, products)],
                )
                grads = [
                    (w * (d - inner)).astype(jnp.bfloat16) for w, d in zip(weights, products)
                ]
                queries.append(query)
                out_grads.append(out_grad)
                all_weights.append([w.astype(jnp.bfloat16) for w in weights])
                all_grads.append(grads)
                tile_ref[pl.ds(pl.multiple_of(head * HEAD, HEAD), HEAD), :] = functools.reduce(
                    jnp.add,
                    [
                        dot(keys_ref[:, pl.ds(first, count)], g)
                        for (first, count, own), g in zip(parts, grads)
                    ],
                )
            query = jnp.concatenate(queries, axis=0)
            out_grad = jnp.concatenate(out_grads, axis=0)
            for i, (first, count, own) in enumerate(parts):
                keys = pl.ds(first, count)
                weights = jnp.concatenate([w[i] for w in all_weights], axis=1)
                grads = jnp.concatenate([g[i] for g in all_grads], axis=1)
                dv_ref[keys, :] += dot(weights, out_grad)
                dk_ref[keys, :] += dot(grads, query)

        head_pairs(width, heads)
        dq_ref[rows, :] = jnp.transpose(tile_ref[...])

    query_tiles(work)

    def back(p, carry):
        rows = pl.ds(pl.multiple_of(p * piece, piece), piece)
        to = pl.ds(pl.multiple_of(to_ref[p], piece), piece)
        at = pl.ds(pl.multiple_of(start_ref[p], piece), piece)
        cosine, sine = cos_ref[at, :], sin_ref[at, :]

        def turn_back(values):
            return values * cosine - swap_halves(values) * sine

        def over_heads(ref):
            total = functools.reduce(
                jnp.add, [ref[to, g * 128 : g * 128 + 128] for g in range(width // 128)]
            )
            return total + pltpu.roll(total, HEAD, 1)

        for g in range(width // 128):
            cut = slice(g * 128, g * 128 + 128)
            turned = turn_back(score_scale * dq_ref[to, cut])
            out_ref[rows, cut] = turned.astype(jnp.bfloat16)
        key = turn_back(over_heads(dk_ref))
        value = over_heads(dv_ref)
        pair = jnp.where(lanes(key) < HEAD, key, value)
        out_ref[rows, width : width + 128] = pair.astype(jnp.bfloat16)
        return carry

    lax.fori_loop(0, pieces, back, 0)


SMEM = pl.BlockSpec(memory_space=pltpu.SMEM)
VMEM = pl.BlockSpec(memory_space=pltpu.VMEM)
VMEM_LIMIT = 60 * 1024 * 1024


def attention_cost(width, products):
    flops = products * 2 * GROUP * (GROUP * 2 // 5) * width
    return pl.CostEstimate(
        flops=flops, bytes_accessed=16 * GROUP * width, transcendentals=GROUP * GROUP * width // 128
    )


def attention_forward(places, starts, raw, tables):
    width = raw.shape[1] - 2 * HEAD
    rows = raw.shape[0]
    kept = jax.ShapeDtypeStruct((rows, width), jnp.bfloat16)
    return pl.pallas_call(
        attention_forward_kernel,
        out_shape=[kept] * 4 + [jax.ShapeDtypeStruct((width // HEAD, 1, rows), jnp.float32)],
        in_specs=[SMEM, SMEM, VMEM, VMEM, VMEM],
        out_specs=[VMEM] * 5,
        scratch_shapes=[
            pltpu.VMEM((rows, width), jnp.bfloat16),
            pltpu.VMEM((HEAD, rows), jnp.bfloat16),
            pltpu.VMEM((width, TILE), jnp.float32),
        ],
        compiler_params=pltpu.CompilerParams(vmem_limit_bytes=VMEM_LIMIT),
        cost_estimate=attention_cost(width, 4),
        name="attention_forward",
    )(places, starts, raw, *tables)


def attention_backward(places, starts, out_grad, kept, tables, early):
    rows, width = out_grad.shape
    return pl.pallas_call(
        attention_backward_kernel,
        out_shape=jax.ShapeDtypeStruct((rows, width + 2 * HEAD), jnp.bfloat16),
        in_specs=[SMEM, SMEM] + [VMEM] * 7 + [ANY] * len(early),
        out_specs=VMEM,
        scratch_shapes=[
            pltpu.VMEM((rows, width), jnp.bfloat16),
            pltpu.VMEM((rows, width), jnp.float32),
            pltpu.VMEM((rows, width), jnp.float32),
            pltpu.VMEM((rows, width), jnp.float32),
            pltpu.VMEM((HEAD, rows), jnp.bfloat16),
            pltpu.VMEM((width, TILE), jnp.float32),
        ],
        compiler_params=pltpu.CompilerParams(vmem_limit_bytes=VMEM_LIMIT),
        cost_estimate=attention_cost(width, 10),
        name="attention_backward",
    )(places, starts, out_grad, *kept, *tables, *early)


MESH = pl.DeviceIdType.MESH
ANY = pl.BlockSpec(memory_space=pl.ANY)
CHUNKS = 4
SLAB = 16


def lasting(microseconds):
    return pl.CostEstimate(
        flops=0, bytes_accessed=int(microseconds * 3_000_000), transcendentals=0
    )


class Plane:
    def __init__(self, sent, landed, diagonal=False, entered=False):
        self.sent, self.landed = sent, landed
        self.copies = []
        self.rank = lax.axis_index("context")
        self.core = lax.axis_index("tensor")
        self.at_x = self.rank + 1 - 2 * lax.rem(self.rank, 2)
        self.at_y = lax.rem(self.rank + 2, 4)
        self.at_both = 3 - self.rank
        self.x = {"context": self.at_x}
        self.y = {"context": self.at_y}
        self.both = {"context": self.at_both}
        self.sibling = {"tensor": 1 - self.core}
        if entered:
            return
        barrier = pltpu.get_barrier_semaphore()
        partners = [self.x, self.y, self.sibling] + ([self.both] if diagonal else [])
        for partner in partners:
            pl.semaphore_signal(barrier, inc=1, device_id=partner, device_id_type=MESH)
        pl.semaphore_wait(barrier, len(partners))

    def copy(self, number, source, target, partner):
        return pltpu.make_async_remote_copy(
            src_ref=source,
            dst_ref=target,
            send_sem=self.sent.at[number],
            recv_sem=self.landed.at[number],
            device_id=partner,
            device_id_type=MESH,
        )

    def send(self, source, target, partner):
        number = len(self.copies)
        started = self.copy(number, source, target, partner)
        started.start()
        self.copies.append(started)
        return number

    def arrive(self, number, target):
        self.copy(number, target, target, self.sibling).wait_recv()

    def finish(self):
        for started in self.copies:
            started.wait_send()


def chunk(index, rows):
    return pl.ds(index * (rows // CHUNKS), rows // CHUNKS)


class Gather:
    def __init__(self, plane, block, out):
        self.plane, self.block, self.out = plane, block, out
        self.rows = block.shape[0]
        self.to_x, self.to_y, self.across, self.onward = {}, {}, {}, {}

    def start(self, k):
        p, cut = self.plane, chunk(k, self.rows)
        target = self.out.at[p.rank, p.core, cut]
        self.to_x[k] = p.send(self.block.at[cut], target, p.x)
        self.to_y[k] = p.send(self.block.at[cut], target, p.y)
        self.across[0, k] = p.send(self.block.at[cut], target, p.sibling)

    def forward_chunk(self, k):
        p, out = self.plane, self.out
        cut = chunk(k, self.rows)
        from_x, from_y = out.at[p.at_x, p.core, cut], out.at[p.at_y, p.core, cut]
        p.arrive(self.to_x[k], from_x)
        if k < CHUNKS // 2:
            self.onward[k] = p.send(from_x, from_x, p.y)
        self.across[1, k] = p.send(from_x, from_x, p.sibling)
        p.arrive(self.to_y[k], from_y)
        if k >= CHUNKS // 2:
            self.onward[k] = p.send(from_y, from_y, p.x)
        self.across[2, k] = p.send(from_y, from_y, p.sibling)

    def forward_far(self):
        p = self.plane
        for k in range(CHUNKS):
            far = self.out.at[p.at_both, p.core, chunk(k, self.rows)]
            p.arrive(self.onward[k], far)
            self.across[3, k] = p.send(far, far, p.sibling)

    def forward(self):
        for k in range(CHUNKS):
            self.forward_chunk(k)
        self.forward_far()

    def finish(self):
        p = self.plane
        for i, rank in enumerate((p.rank, p.at_x, p.at_y, p.at_both)):
            for k in range(CHUNKS):
                p.arrive(
                    self.across[i, k], self.out.at[rank, 1 - p.core, chunk(k, self.rows)]
                )


GATHER_COPIES = CHUNKS * 8


def add_rows(target, source, first, count):
    def step(i, carry):
        rows = pl.ds(first + i * SLAB, SLAB)
        target[rows, :] = (
            target[rows, :].astype(jnp.float32) + source[rows, :].astype(jnp.float32)
        ).astype(jnp.bfloat16)
        return carry

    lax.fori_loop(0, count // SLAB, step, 0)


class Scatter:
    def __init__(
        self, plane, rows_in, weights, columns, given, held, other, near_x, near_y, far_x, far_y
    ):
        p = self.plane = plane
        rows = near_x.shape[0]
        half = rows // 2
        halves = top, low = pl.ds(0, half), pl.ds(half, half)
        order = (p.at_both, p.at_x, p.at_y, p.rank)
        across = {}

        def make(i, h):
            for core, target in ((1 - p.core, given), (p.core, held)):
                value = dot(rows_in[order[i], core, halves[h], :], weights[:, columns], LAST)
                target[i, halves[h], :] = value.astype(jnp.bfloat16)
                if target is given:
                    source = given.at[i, halves[h]]
                    across[i, h] = p.send(source, other.at[i, halves[h]], p.sibling)

        def pair(i, h):
            p.arrive(across[i, h], other.at[i, halves[h]])
            add_rows(held.at[i], other.at[i], h * half, half)

        make(0, 0)
        make(0, 1)
        pair(0, 0)
        first = p.send(held.at[0, top], far_x, p.x)
        make(1, 0)
        pair(0, 1)
        second = p.send(held.at[0, low], far_y, p.y)
        make(2, 0)
        pair(1, 0)
        third = p.send(held.at[1, top], near_x.at[top], p.x)
        make(1, 1)
        make(2, 1)
        make(3, 0)
        make(3, 1)
        pair(2, 0)
        pair(1, 1)
        pair(2, 1)
        p.arrive(first, far_x)
        add_rows(held.at[2], far_x, 0, half)
        fourth = p.send(held.at[2, top], near_y.at[top], p.y)
        p.arrive(second, far_y)

        def step(i, carry):
            rows, at = pl.ds(half + i * SLAB, SLAB), pl.ds(i * SLAB, SLAB)
            held[1, rows, :] = (
                held[1, rows, :].astype(jnp.float32) + far_y[at, :].astype(jnp.float32)
            ).astype(jnp.bfloat16)
            return carry

        lax.fori_loop(0, half // SLAB, step, 0)
        fifth = p.send(held.at[1, low], near_x.at[low], p.x)
        sixth = p.send(held.at[2, low], near_y.at[low], p.y)
        pair(3, 0)
        pair(3, 1)
        self.halves = halves
        self.from_x, self.from_y = (third, fifth), (fourth, sixth)
        self.parts = (held.at[3], near_x, near_y)

    def ready(self, h):
        _, near_x, near_y = self.parts
        self.plane.arrive(self.from_x[h], near_x.at[self.halves[h]])
        self.plane.arrive(self.from_y[h], near_y.at[self.halves[h]])

    def rows(self, rows):
        return sum(part[rows, :].astype(jnp.float32) for part in self.parts)


SCATTER_COPIES = 8 + 6


def scatter_scratch(share, width):
    kind = jnp.bfloat16
    return [
        pltpu.VMEM((4, share, width), kind),
        pltpu.VMEM((4, share, width), kind),
        pltpu.VMEM((4, share, width), kind),
        pltpu.VMEM((share, width), kind),
        pltpu.VMEM((share, width), kind),
        pltpu.VMEM((share // 2, width), kind),
        pltpu.VMEM((share // 2, width), kind),
    ]


def wires(count):
    return [pltpu.SemaphoreType.DMA((count,)), pltpu.SemaphoreType.DMA((count,))]


def row_root(values):
    return lax.rsqrt(jnp.mean(values * values, axis=-1, keepdims=True) + epsilon)


def slabs(first, count, work):
    def step(i, carry):
        work(pl.ds(first + i * SLAB, SLAB))
        return carry

    lax.fori_loop(0, count // SLAB, step, 0)


class Exchange:
    def __init__(self, plane, source, target, local, first=0, columns=None):
        p = plane
        columns = columns or target.shape[2]

        def part(rank):
            return source.at[:, pl.ds(pl.multiple_of(rank * columns, 128), columns)]

        def place(rank):
            return target.at[rank, :, pl.ds(first, columns)]

        self.plane, self.place, self.moves = p, place, []
        self.mine = pltpu.make_async_copy(part(p.rank), place(p.rank), local)
        self.mine.start()
        for partner, rank in ((p.both, p.at_both), (p.x, p.at_x), (p.y, p.at_y)):
            self.moves.append((p.send(part(rank), place(p.rank), partner), rank))

    def finish(self):
        for number, rank in self.moves:
            self.plane.arrive(number, self.place(rank))
        self.mine.wait()


def first_kernel(
    query,
    key,
    value,
    out_weight,
    gains,
    packed,
    gains_out,
    pair,
    sent,
    landed,
    local,
    far_sent,
    far_landed,
    out_turned,
):
    groups = lax.axis_size("fsdp")
    group, rank = lax.axis_index("fsdp"), lax.axis_index("context")
    depth = gains.shape[1]
    others = [(i, j) for i in range(groups) for j in range(4) if i or j]

    def device(i, j):
        return {"fsdp": lax.rem(group + i, groups), "context": lax.rem(rank + j, 4)}

    def place(f, c):
        return gains_out.at[:, pl.ds(pl.multiple_of((f * 4 + c) * depth, 128), depth)]

    barrier = pltpu.get_barrier_semaphore()
    for i, j in others:
        pl.semaphore_signal(barrier, inc=1, device_id=device(i, j), device_id_type=MESH)
    for c in range(pair.shape[1] // 128):
        cut = slice(c // 2 * 128, c // 2 * 128 + 128)
        keys, values = key[:, cut].astype(jnp.float32), value[:, cut].astype(jnp.float32)
        if c % 2:
            keys = pltpu.roll(keys, HEAD, 1)
        else:
            values = pltpu.roll(values, HEAD, 1)
        both = jnp.where(lanes(keys) < HEAD, keys, values)
        pair[:, c * 128 : c * 128 + 128] = both.astype(jnp.bfloat16)
    for first in range(0, out_weight.shape[0], 256):
        block = jnp.transpose(out_weight[first : first + 256, :].astype(jnp.float32))
        out_turned[:, first : first + 256] = block.astype(jnp.bfloat16)
    pl.semaphore_wait(barrier, len(others))
    p = Plane(sent, landed, entered=True)
    width = query.shape[1] // 4
    exchanges = [
        Exchange(p, query, packed, local.at[0], 0, width),
        Exchange(p, pair, packed, local.at[1], width, 128),
        Exchange(p, out_turned, packed, local.at[2], width + 128, width),
    ]
    far = []
    for n, (i, j) in enumerate(others):
        far.append(
            pltpu.make_async_remote_copy(
                src_ref=gains,
                dst_ref=place(group, rank),
                send_sem=far_sent.at[n],
                recv_sem=far_landed.at[n],
                device_id=device(i, j),
                device_id_type=MESH,
            )
        )
        far[n].start()
    gains_out[:, pl.ds(pl.multiple_of((group * 4 + rank) * depth, 128), depth)] = gains[...]
    for started in far:
        started.wait()
    for exchange in exchanges:
        exchange.finish()
    p.finish()


def first_exchange(query, key, value, out_weight, gains):
    depth, columns = query.shape
    groups = lax.axis_size("fsdp")
    far = groups * 4 - 1
    return pl.pallas_call(
        first_kernel,
        out_shape=[
            jax.ShapeDtypeStruct((4, depth, columns // 2 + 128), query.dtype),
            jax.ShapeDtypeStruct((8, groups * 4 * depth), jnp.float32),
            jax.ShapeDtypeStruct((depth, 2 * key.shape[1]), key.dtype),
        ],
        in_specs=[VMEM] * 5,
        out_specs=[ANY, VMEM, VMEM],
        scratch_shapes=wires(9)
        + [pltpu.SemaphoreType.DMA((3,))]
        + wires(far)
        + [pltpu.VMEM((depth, columns), query.dtype)],
        compiler_params=pltpu.CompilerParams(
            collective_id=9, has_side_effects=True, vmem_limit_bytes=VMEM_LIMIT
        ),
        cost_estimate=lasting(10),
        name="first_exchange",
    )(query, key, value, out_weight, gains)


def start_kernel(tokens, cotangent, early, out, scaled, my_scaled, sent, landed, local):
    p = Plane(sent, landed)
    share = my_scaled.shape[0]
    block = tokens.at[pl.ds(pl.multiple_of(p.core * share, SLAB), share)]
    gather = Gather(p, block, out)
    mine = pltpu.make_async_copy(block, out.at[p.rank, p.core], local)
    for k in range(CHUNKS):
        gather.start(k)
    mine.start()

    def scale(rows):
        value = residual_scale * cotangent[rows, :].astype(jnp.float32)
        scaled[rows, :] = value.astype(jnp.bfloat16)

    def keep(rows):
        from_rows = pl.ds(pl.multiple_of(p.core * share + rows.start, SLAB), SLAB)
        my_scaled[rows, :] = scaled[from_rows, :]

    slabs(0, scaled.shape[0], scale)
    slabs(0, share, keep)
    gather.forward()
    gather.finish()
    p.finish()
    mine.wait()


def start_plane(tokens, cotangent, early):
    share, width = tokens.shape[0] // 2, tokens.shape[1]
    return pl.pallas_call(
        start_kernel,
        out_shape=[
            jax.ShapeDtypeStruct((4, 2, share, width), tokens.dtype),
            jax.ShapeDtypeStruct(cotangent.shape, jnp.bfloat16),
            jax.ShapeDtypeStruct((share, width), jnp.bfloat16),
        ],
        in_specs=[VMEM, VMEM, ANY],
        out_specs=[ANY, VMEM, VMEM],
        scratch_shapes=wires(GATHER_COPIES) + [pltpu.SemaphoreType.DMA],
        compiler_params=pltpu.CompilerParams(
            collective_id=1, has_side_effects=True, vmem_limit_bytes=VMEM_LIMIT
        ),
        cost_estimate=lasting(60),
        name="gather_tokens",
    )(tokens, cotangent, early)


def columns_kernel(gate, up, down, early, both_out, down_out, sent, landed, local):
    p = Plane(sent, landed, diagonal=True)
    units = down_out.shape[2]
    exchanges = [
        Exchange(p, gate, both_out, local.at[0], 0, units),
        Exchange(p, up, both_out, local.at[1], units, units),
        Exchange(p, down, down_out, local.at[2]),
    ]
    for exchange in exchanges:
        exchange.finish()
    p.finish()


def exchange_columns(gate, up, down, early):
    depth, units = gate.shape
    return pl.pallas_call(
        columns_kernel,
        out_shape=[
            jax.ShapeDtypeStruct((4, depth, units // 2), gate.dtype),
            jax.ShapeDtypeStruct((4, depth, units // 4), gate.dtype),
        ],
        in_specs=[VMEM] * 3 + [ANY],
        out_specs=[ANY] * 2,
        scratch_shapes=wires(9) + [pltpu.SemaphoreType.DMA((3,))],
        compiler_params=pltpu.CompilerParams(collective_id=10, has_side_effects=True),
        cost_estimate=lasting(30),
        name="exchange_columns",
    )(gate, up, down, early)


def middle_kernel(
    attended,
    weights,
    gain,
    tokens,
    hidden,
    middle,
    sent,
    landed,
    local,
    residual,
    *scratch,
):
    p = Plane(sent, landed)
    share = hidden.shape[0]
    first = pl.ds(pl.multiple_of(p.core * share, SLAB), share)
    load = pltpu.make_async_copy(tokens.at[first], residual, local)
    load.start()
    width = attended.shape[3]
    columns = slice(weights.shape[1] - width, weights.shape[1])
    total = Scatter(p, attended, weights, columns, *scratch)
    load.wait()

    def work(rows):
        value = residual[rows, :].astype(jnp.float32) + residual_scale * total.rows(rows)
        middle[rows, :] = value
        hidden[rows, :] = (value * row_root(value) * gain[1:2, :]).astype(jnp.bfloat16)

    for h in range(2):
        total.ready(h)
        slabs(h * (share // 2), share // 2, work)
    p.finish()


def middle_plane(attended, weights, tokens, gain):
    share, width = tokens.shape[0] // 2, tokens.shape[1]
    return pl.pallas_call(
        middle_kernel,
        out_shape=[
            jax.ShapeDtypeStruct((share, width), jnp.bfloat16),
            jax.ShapeDtypeStruct((share, width), jnp.float32),
        ],
        in_specs=[VMEM] * 3 + [ANY],
        out_specs=[VMEM, VMEM],
        scratch_shapes=wires(SCATTER_COPIES)
        + [
            pltpu.SemaphoreType.DMA,
            pltpu.VMEM((share, width), jnp.bfloat16),
        ]
        + scatter_scratch(share, width),
        compiler_params=pltpu.CompilerParams(
            collective_id=2, has_side_effects=True, vmem_limit_bytes=VMEM_LIMIT
        ),
        cost_estimate=lasting(55),
        name="middle_rows",
    )(
        attended.reshape(4, 2, share, -1),
        weights,
        gain,
        tokens,
    )


def ffn_rows_kernel(
    block,
    weights_in,
    beside,
    from_x,
    from_y,
    from_both,
    out,
    m,
    gate,
    up,
    beside_out,
    sent,
    landed,
    local,
    loading,
    storing,
    weights,
    rows_in,
    m_held,
    gate_held,
    up_held,
    wires_beside,
    held_beside,
    held_blocks,
):
    p = Plane(sent, landed)
    gather = Gather(p, block, out)
    for k in range(CHUNKS):
        gather.start(k)
    weights_load = pltpu.make_async_copy(weights_in, weights, local.at[0])
    weights_load.start()
    mine = pltpu.make_async_copy(block, out.at[p.rank, p.core], local.at[1])
    mine.start()
    blocks = ((from_x, p.at_x), (from_y, p.at_y), (from_both, p.at_both))
    loads = [pltpu.make_async_copy(beside, held_beside, wires_beside.at[0])]
    for i, (source, rank) in enumerate(blocks):
        loads.append(
            pltpu.make_async_copy(source, held_blocks.at[i], wires_beside.at[i + 1])
        )
    for started in loads:
        started.start()
    units = m.shape[3]
    stores = []

    def load(n, rank, core):
        return pltpu.make_async_copy(out.at[rank, core], rows_in.at[n % 2], loading.at[n % 2])

    def compute(n, rank, core, source):
        slot = n % 2
        if n >= 2:
            for started in stores[n - 2]:
                started.wait()

        def step(j, carry):
            cut = pl.ds(pl.multiple_of(j * 256, 256), 256)
            beyond = pl.ds(pl.multiple_of(units + j * 256, 256), 256)
            gate_part = dot(source[...], weights[:, cut])
            up_part = dot(source[...], weights[:, beyond])
            gate_held[slot, :, cut] = gate_part.astype(jnp.bfloat16)
            up_held[slot, :, cut] = up_part.astype(jnp.bfloat16)
            sigmoid = 1.0 / (1.0 + jnp.exp(-gate_part))
            m_held[slot, :, cut] = (gate_part * sigmoid * up_part).astype(jnp.bfloat16)
            return carry

        lax.fori_loop(0, units // 256, step, 0)
        stores.append(
            [
                pltpu.make_async_copy(held.at[slot], target.at[rank, core], storing.at[slot, i])
                for i, (held, target) in enumerate(((m_held, m), (gate_held, gate), (up_held, up)))
            ]
        )
        for started in stores[n]:
            started.start()

    def from_sibling(i, rank):
        for k in range(CHUNKS):
            p.arrive(
                gather.across[i, k], out.at[rank, 1 - p.core, chunk(k, gather.rows)]
            )

    weights_load.wait()
    compute(0, p.rank, p.core, block)
    kept, shared = [], []
    loads[0].wait()
    kept.append(pltpu.make_async_copy(held_beside, beside_out.at[p.rank], wires_beside.at[0]))
    kept[0].start()
    for i, (source, rank) in enumerate(blocks):
        loads[i + 1].wait()
        place = beside_out.at[rank, p.core]
        kept.append(pltpu.make_async_copy(held_blocks.at[i], place, wires_beside.at[i + 1]))
        kept[i + 1].start()
        shared.append(p.send(held_blocks.at[i], place, p.sibling))
    gather.forward_chunk(0)
    from_sibling(0, p.rank)
    load(1, p.rank, 1 - p.core).start()
    load(1, p.rank, 1 - p.core).wait()
    compute(1, p.rank, 1 - p.core, rows_in.at[1])
    for k in range(1, CHUNKS):
        gather.forward_chunk(k)
    load(2, p.at_x, p.core).start()
    load(3, p.at_y, p.core).start()
    load(2, p.at_x, p.core).wait()
    compute(2, p.at_x, p.core, rows_in.at[0])
    from_sibling(1, p.at_x)
    load(4, p.at_x, 1 - p.core).start()
    load(3, p.at_y, p.core).wait()
    compute(3, p.at_y, p.core, rows_in.at[1])
    from_sibling(2, p.at_y)
    load(5, p.at_y, 1 - p.core).start()
    load(4, p.at_x, 1 - p.core).wait()
    compute(4, p.at_x, 1 - p.core, rows_in.at[0])
    gather.forward_far()
    load(6, p.at_both, p.core).start()
    load(5, p.at_y, 1 - p.core).wait()
    compute(5, p.at_y, 1 - p.core, rows_in.at[1])
    from_sibling(3, p.at_both)
    load(7, p.at_both, 1 - p.core).start()
    load(6, p.at_both, p.core).wait()
    compute(6, p.at_both, p.core, rows_in.at[0])
    load(7, p.at_both, 1 - p.core).wait()
    compute(7, p.at_both, 1 - p.core, rows_in.at[1])
    for number, (source, rank) in zip(shared, blocks):
        p.arrive(number, beside_out.at[rank, 1 - p.core])
    p.finish()
    mine.wait()
    for started in kept:
        started.wait()
    for n in (6, 7):
        for started in stores[n]:
            started.wait()


def ffn_rows(block, weights, beside, blocks):
    share, width = block.shape
    units = weights.shape[1] // 2
    kind = jnp.bfloat16
    full = jax.ShapeDtypeStruct((4, 2, share, width), kind)
    part = jax.ShapeDtypeStruct((4, 2, share, units), kind)
    held = pltpu.VMEM((2, share, units), kind)
    outs = pl.pallas_call(
        ffn_rows_kernel,
        out_shape=[full, part, part, part, full],
        in_specs=[VMEM] + [ANY] * 5,
        out_specs=[ANY] * 5,
        scratch_shapes=wires(GATHER_COPIES + 3)
        + [
            pltpu.SemaphoreType.DMA((2,)),
            pltpu.SemaphoreType.DMA((2,)),
            pltpu.SemaphoreType.DMA((2, 3)),
            pltpu.VMEM(weights.shape, kind),
            pltpu.VMEM((2, share, width), kind),
            held,
            held,
            held,
            pltpu.SemaphoreType.DMA((4,)),
            pltpu.VMEM((2, share, width), kind),
            pltpu.VMEM((3, share, width), kind),
        ],
        compiler_params=pltpu.CompilerParams(
            collective_id=11, has_side_effects=True, vmem_limit_bytes=VMEM_LIMIT
        ),
        cost_estimate=lasting(60),
        name="ffn_rows",
    )(block, weights, beside.reshape(2, share, width), *blocks)
    return [array.reshape(8 * share, -1) for array in outs]


class WeightTiles:
    def __init__(self, rows, slopes, target, rows_in, tile_out, wires_in):
        self.rows, self.slopes, self.target = rows, slopes, target
        self.rows_in, self.tile_out, self.wires = rows_in, tile_out, wires_in
        self.count = rows.shape[1] // TILE
        self.load(0, 0).start()

    def load(self, d, slot):
        columns = pl.ds(pl.multiple_of(d * TILE, TILE), TILE)
        return pltpu.make_async_copy(
            self.rows.at[:, columns], self.rows_in.at[slot], self.wires.at[0, slot]
        )

    def store(self, d, slot):
        columns = pl.ds(pl.multiple_of(d * TILE, TILE), TILE)
        return pltpu.make_async_copy(
            self.tile_out.at[slot], self.target.at[columns], self.wires.at[1, slot]
        )

    def run(self, first, last):
        def step(d, carry):
            slot = lax.rem(d, 2)
            self.load(d, slot).wait()

            @pl.when(d < self.count - 1)
            def _():
                self.load(d + 1, 1 - slot).start()

            @pl.when(d >= 2)
            def _():
                self.store(d - 2, slot).wait()

            self.tile_out[slot] = dot(self.rows_in[slot], self.slopes[...], FIRST).astype(
                jnp.bfloat16
            )
            self.store(d, slot).start()
            return carry

        lax.fori_loop(first, last, step, 0)

    def finish(self):
        for d in (self.count - 2, self.count - 1):
            self.store(d, d % 2).wait()


def tile_scratch(count, units):
    return [
        pltpu.SemaphoreType.DMA((2, 2)),
        pltpu.VMEM((2, count, TILE), jnp.bfloat16),
        pltpu.VMEM((2, TILE, units), jnp.bfloat16),
    ]


UNITS = ((0, 0), (0, 1), (1, 0), (2, 0), (1, 1), (2, 1), (3, 0), (3, 1))


def second_kernel(
    slopes,
    normed_rows,
    weights_in,
    middle_in,
    cotangent_in,
    gain,
    early,
    grad_middle,
    hidden,
    weight_grads,
    sent,
    landed,
    loading,
    beside,
    weights,
    middle,
    cotangent,
    tile_wires,
    rows_in,
    tile_out,
    gate_in,
    up_in,
    given,
    held,
    other,
    near_x,
    near_y,
    far_x,
    far_y,
):
    share, width = near_x.shape
    cuts = [slice(j * 512, j * 512 + 512) for j in range(width // 512)]
    weight_loads = [
        pltpu.make_async_copy(weights_in.at[cut], weights.at[cut], beside.at[2 + j])
        for j, cut in enumerate(cuts)
    ]
    for started in weight_loads:
        started.start()
    p = Plane(sent, landed)
    half = share // 2
    order = (p.at_both, p.at_x, p.at_y, p.rank)
    top, low = halves = pl.ds(0, half), pl.ds(half, half)

    def places(u):
        i, h = UNITS[u]
        for core in (1 - p.core, p.core):
            row = (order[i] * 2 + core) * share + h * half
            yield pl.ds(pl.multiple_of(row, 32), half)

    units = gate_in.shape[1]

    def loads(u):
        for j, rows in enumerate(places(u)):
            for n, target in enumerate((gate_in, up_in)):
                yield pltpu.make_async_copy(
                    slopes.at[rows, pl.ds(n * units, units)],
                    target.at[rows],
                    loading.at[u, 2 * j + n],
                )

    def compute(u):
        i, h = UNITS[u]
        slot = u % 2
        gate_rows = jnp.concatenate([gate_in[rows, :] for rows in places(u)], axis=0)
        up_rows = jnp.concatenate([up_in[rows, :] for rows in places(u)], axis=0)
        for j, cut in enumerate(cuts):
            if u == 0:
                weight_loads[j].wait()
            back = dot(gate_rows, weights[cut, :units], LAST) + dot(
                up_rows, weights[cut, units:], LAST
            )
            given[slot, :, cut] = back[:half].astype(jnp.bfloat16)
            held[i, halves[h], cut] = back[half:].astype(jnp.bfloat16)

    first = pl.ds(pl.multiple_of(p.core * share, SLAB), share)
    row_loads = [
        pltpu.make_async_copy(middle_in, middle, beside.at[0]),
        pltpu.make_async_copy(cotangent_in.at[first], cotangent, beside.at[1]),
    ]
    tiles = WeightTiles(normed_rows, gate_in, weight_grads, rows_in, tile_out, tile_wires)

    moves, across = {}, {}
    moves, across = {}, {}

    def settle(u):
        i, h = UNITS[u]
        p.arrive(across[u], other.at[i, halves[h]])
        add_rows(held.at[i], other.at[i], h * half, half)
        if u == 0:
            moves["far_x"] = p.send(held.at[0, top], far_x, p.x)
        elif u == 1:
            moves["far_y"] = p.send(held.at[0, low], far_y, p.y)
        elif u == 2:
            moves["x", 0] = p.send(held.at[1, top], near_x.at[top], p.x)
        elif u == 3:
            p.arrive(moves["far_x"], far_x)
            add_rows(held.at[2], far_x, 0, half)
            moves["y", 0] = p.send(held.at[2, top], near_y.at[top], p.y)
        elif u == 4:
            p.arrive(moves["far_y"], far_y)

            def step(k, carry):
                rows, at = pl.ds(half + k * SLAB, SLAB), pl.ds(k * SLAB, SLAB)
                held[1, rows, :] = (
                    held[1, rows, :].astype(jnp.float32) + far_y[at, :].astype(jnp.float32)
                ).astype(jnp.bfloat16)
                return carry

            lax.fori_loop(0, half // SLAB, step, 0)
            moves["x", 1] = p.send(held.at[1, low], near_x.at[low], p.x)
        elif u == 5:
            moves["y", 1] = p.send(held.at[2, low], near_y.at[low], p.y)

    for u in range(8):
        for started in loads(u):
            started.start()

    def unit(u):
        if u >= 2:
            p.copies[across[u - 2]].wait_send()
        compute(u)
        i, h = UNITS[u]
        across[u] = p.send(given.at[u % 2], other.at[i, halves[h]], p.sibling)

    def wait_loads(units_here):
        for u in units_here:
            for started in loads(u):
                started.wait()

    for started in row_loads:
        started.start()
    wait_loads((0,))
    unit(0)
    wait_loads((1,))
    unit(1)
    settle(0)
    wait_loads((2, 3))
    unit(2)
    settle(1)
    unit(3)
    settle(2)
    wait_loads((4, 5, 6, 7))
    unit(4)
    tiles.run(0, 2)
    settle(3)
    unit(5)
    settle(4)
    unit(6)
    settle(5)
    unit(7)
    settle(6)
    settle(7)
    tiles.run(2, tiles.count)

    def work(rows):
        value = middle[rows, :]
        root = row_root(value)
        normed = value * root
        total = sum(part[rows, :].astype(jnp.float32) for part in (held.at[3], near_x, near_y))
        slope = total * gain[1:2, :]
        mean = jnp.mean(slope * normed, axis=-1, keepdims=True)
        gradient = cotangent[rows, :].astype(jnp.float32) + root * (slope - normed * mean)
        grad_middle[rows, :] = gradient
        hidden[rows, :] = (residual_scale * gradient).astype(jnp.bfloat16)

    for started in row_loads:
        started.wait()
    for h in range(2):
        p.arrive(moves["x", h], near_x.at[halves[h]])
        p.arrive(moves["y", h], near_y.at[halves[h]])
        slabs(h * half, half, work)
    for u in (6, 7):
        p.copies[across[u]].wait_send()
    tiles.finish()
    for number, started in enumerate(p.copies):
        if number not in across.values():
            started.wait_send()


def second_plane(slopes, normed_rows, weights, middle, cotangent, gain, early):
    share, width = middle.shape
    count, units = slopes.shape[0], slopes.shape[1] // 2
    kind = jnp.bfloat16
    half = share // 2
    quarter = pltpu.VMEM((4, share, width), kind)
    return pl.pallas_call(
        second_kernel,
        out_shape=[
            jax.ShapeDtypeStruct((share, width), jnp.float32),
            jax.ShapeDtypeStruct((share, width), kind),
            jax.ShapeDtypeStruct((width, units), kind),
        ],
        in_specs=[ANY] * 5 + [VMEM, ANY],
        out_specs=[VMEM, VMEM, ANY],
        scratch_shapes=wires(8 + 6)
        + [
            pltpu.SemaphoreType.DMA((8, 4)),
            pltpu.SemaphoreType.DMA((2 + width // 512,)),
            pltpu.VMEM(weights.shape, kind),
            pltpu.VMEM((share, width), jnp.float32),
            pltpu.VMEM((share, width), kind),
        ]
        + tile_scratch(count, units)
        + [
            pltpu.VMEM((count, units), kind),
            pltpu.VMEM((count, units), kind),
            pltpu.VMEM((2, half, width), kind),
            quarter,
            quarter,
            pltpu.VMEM((share, width), kind),
            pltpu.VMEM((share, width), kind),
            pltpu.VMEM((half, width), kind),
            pltpu.VMEM((half, width), kind),
        ],
        compiler_params=pltpu.CompilerParams(
            collective_id=3, has_side_effects=True, vmem_limit_bytes=60 * 1024 * 1024
        ),
        cost_estimate=lasting(60),
        name="second_rows",
    )(slopes, normed_rows, weights, middle, cotangent, gain, early)


def spread_kernel(
    hidden, m, down_in, normed_rows, slopes, early, out, pair_own, pair_x, pair_y, pair_both,
    weight_grads, sent, landed, local, loading, tile_wires, rows_in, tile_out, up_in,
    m_in, given, held, theirs, down_w,
):
    p = Plane(sent, landed)
    share, width = hidden.shape
    gather = Gather(p, hidden, out)
    for k in range(CHUNKS):
        gather.start(k)
    mine = pltpu.make_async_copy(hidden, out.at[p.rank, p.core], local.at[4])
    mine.start()
    order = (p.rank, p.at_x, p.at_y, p.at_both)
    halves = pl.ds(0, share), pl.ds(share, share)

    def loads(i):
        for j, core in enumerate((1 - p.core, p.core)):
            yield pltpu.make_async_copy(
                m.at[order[i], core], m_in.at[i % 2, halves[j]], loading.at[i % 2, j]
            )

    across = []
    units = up_in.shape[1]
    up_load = pltpu.make_async_copy(slopes.at[:, pl.ds(units, units)], up_in, local.at[5])
    down_load = pltpu.make_async_copy(down_in, down_w, local.at[6])
    down_load.start()
    up_load.start()
    for started in loads(0):
        started.start()
    down_load.wait()
    tiles = WeightTiles(normed_rows, up_in, weight_grads, rows_in, tile_out, tile_wires)
    for i in range(4):
        for started in loads(i):
            started.wait()
        if i < 3:
            for started in loads(i + 1):
                started.start()

        def step(j, carry, i=i):
            cut = pl.ds(pl.multiple_of(j * 512, 512), 512)
            value = dot(m_in[i % 2], down_w[cut, :], LAST)
            given[i, :, cut] = value[:share].astype(jnp.bfloat16)
            held[i, :, cut] = value[share:].astype(jnp.bfloat16)
            return carry

        lax.fori_loop(0, width // 512, step, 0)
        across.append(p.send(given.at[i], theirs.at[i], p.sibling))
        if i == 0:
            up_load.wait()
        gather.forward_chunk(i)
        tiles.run(i, i + 1)
    kept = []
    for i in range(4):
        p.arrive(across[i], theirs.at[i])
        add_rows(held.at[i], theirs.at[i], 0, share)
        target = (pair_own, pair_x, pair_y, pair_both)[i]
        kept.append(pltpu.make_async_copy(held.at[i], target, local.at[i]))
        kept[i].start()
    gather.forward_far()
    tiles.run(4, tiles.count)
    tiles.finish()
    gather.finish()
    p.finish()
    mine.wait()
    for started in kept:
        started.wait()


def spread_plane(hidden, m, down_w, normed_rows, slopes, early):
    share, width = hidden.shape
    units = m.shape[1]
    full = jax.ShapeDtypeStruct((4, 2, share, width), jnp.bfloat16)
    quarter = pltpu.VMEM((4, share, width), jnp.bfloat16)
    out, *pairs, weight_grads = pl.pallas_call(
        spread_kernel,
        out_shape=[full]
        + [jax.ShapeDtypeStruct((share, width), jnp.bfloat16)] * 4
        + [jax.ShapeDtypeStruct((width, units), jnp.bfloat16)],
        in_specs=[VMEM] + [ANY] * 5,
        out_specs=[ANY] * 6,
        scratch_shapes=wires(GATHER_COPIES + 4)
        + [
            pltpu.SemaphoreType.DMA((7,)),
            pltpu.SemaphoreType.DMA((2, 2)),
        ]
        + tile_scratch(8 * share, units)
        + [
            pltpu.VMEM((8 * share, units), jnp.bfloat16),
            pltpu.VMEM((2, 2 * share, units), jnp.bfloat16),
            quarter,
            quarter,
            quarter,
            pltpu.VMEM(down_w.shape, jnp.bfloat16),
        ],
        compiler_params=pltpu.CompilerParams(
            collective_id=7, has_side_effects=True, vmem_limit_bytes=60 * 1024 * 1024
        ),
        cost_estimate=lasting(60),
        name="spread_rows",
    )(hidden, m.reshape(4, 2, share, units), down_w, normed_rows, slopes, early)
    return out.reshape(8 * share, width), pairs, weight_grads


def lane_sums(pairs):
    total = 0.0
    for a, b in pairs:
        product = a.astype(jnp.float32) * b.astype(jnp.float32)
        total += jnp.sum(product, axis=1, keepdims=True)
    return jnp.broadcast_to(total, (total.shape[0], 128))


LATER = 10


def last_kernel(
    back,
    weights,
    gain,
    ups,
    early,
    *rest,
):
    later, rest = rest[:LATER], rest[LATER:]
    out, result_out, up_out, gain_out, sent, landed, local, loading, held, result, sums = rest[:11]
    landing, scratch = rest[11 : 11 + LATER], rest[11 + LATER :]
    share = landing[8].shape[0]
    first = pl.ds(pl.multiple_of(lax.axis_index("tensor") * share, SLAB), share)
    later = [*later[:8], later[8].at[first], later[9]]
    loads = [
        pltpu.make_async_copy(source, target, loading.at[i])
        for i, (source, target) in enumerate(zip(later, landing))
    ]
    for started in loads:
        started.start()
    middle, ffn_own, ffn_x, ffn_y, ffn_both, gates, gate, up, residual, grad_middle = landing
    p = Plane(sent, landed, diagonal=True)
    moves = []

    def hand_back(partner, rank):
        moves.append((p.send(ups.at[rank], up_out.at[p.rank], partner), up_out.at[rank]))

    hand_back(p.both, p.at_both)
    total = Scatter(p, back, weights, slice(0, back.shape[3]), *scratch)
    hand_back(p.x, p.at_x)
    hand_back(p.y, p.at_y)
    up_out[p.rank] = ups[p.rank]
    share = held.shape[0]

    def finish_result(rows):
        parts = (ffn_own, ffn_x, ffn_y, ffn_both)
        ffn = sum(part[rows, :].astype(jnp.float32) for part in parts)
        result[rows, :] = (middle[rows, :] + residual_scale * ffn).astype(jnp.bfloat16)

    for started in loads:
        started.wait()
    slabs(0, share, finish_result)
    kept = [pltpu.make_async_copy(result, result_out.at[p.core], local.at[0])]
    kept[0].start()
    given = p.send(result, result_out.at[p.core], p.sibling)
    units = gate.shape[1] // 4

    def gate_rows(rows):
        sums[0, rows, :] = lane_sums(
            [(gates[c, rows, :], gate[rows, c * units : c * units + units]) for c in range(4)]
        )

    def up_rows(rows):
        sums[0, rows, :] += lane_sums(
            [(up_out[c, rows, :], up[rows, c * units : c * units + units]) for c in range(4)]
        )

    slabs(0, gate.shape[0], gate_rows)

    def work(rows):
        value = residual[rows, :].astype(jnp.float32)
        root = row_root(value)
        normed = value * root
        slope = total.rows(rows) * gain[0:1, :]
        mean = jnp.mean(slope * normed, axis=-1, keepdims=True)
        held[rows, :] = grad_middle[rows, :] + root * (slope - normed * mean)

    across = []
    for k in range(CHUNKS):
        cut = chunk(k, share)
        if k % (CHUNKS // 2) == 0:
            total.ready(k // (CHUNKS // 2))
        slabs(k * (share // CHUNKS), share // CHUNKS, work)
        across.append(p.send(held.at[cut], out.at[p.core, cut], p.sibling))
        kept.append(
            pltpu.make_async_copy(held.at[cut], out.at[p.core, cut], local.at[1 + k])
        )
        kept[1 + k].start()
    for number, target in moves:
        p.arrive(number, target)
    slabs(0, gate.shape[0], up_rows)
    swapped = p.send(sums.at[0], sums.at[1], p.sibling)
    p.arrive(swapped, sums.at[1])
    gain_out[...] = sums[0] + sums[1]
    p.arrive(given, result_out.at[1 - p.core])
    for k in range(CHUNKS):
        p.arrive(across[k], out.at[1 - p.core, chunk(k, share)])
    p.finish()
    for started in kept:
        started.wait()


def last_plane(
    back, weights, tokens, grad_middle, gain, middle, ffn_parts, ups, gates, gate, up, early
):
    share, width = grad_middle.shape
    later = [middle, *ffn_parts, gates, gate, up, tokens, grad_middle]
    out, result_out, up_out, gain_out = pl.pallas_call(
        last_kernel,
        out_shape=[
            jax.ShapeDtypeStruct((2, share, width), jnp.float32),
            jax.ShapeDtypeStruct((2, share, width), jnp.bfloat16),
            jax.ShapeDtypeStruct(ups.shape, ups.dtype),
            jax.ShapeDtypeStruct((gate.shape[0], 128), jnp.float32),
        ],
        in_specs=[VMEM] * 4 + [ANY] * (1 + LATER),
        out_specs=[ANY, ANY, VMEM, VMEM],
        scratch_shapes=wires(CHUNKS + 5 + SCATTER_COPIES)
        + [
            pltpu.SemaphoreType.DMA((1 + CHUNKS,)),
            pltpu.SemaphoreType.DMA((LATER,)),
            pltpu.VMEM((share, width), jnp.float32),
            pltpu.VMEM((share, width), jnp.bfloat16),
            pltpu.VMEM((2, gate.shape[0], 128), jnp.float32),
        ]
        + [pltpu.VMEM(array.shape, array.dtype) for array in later[:8]]
        + [pltpu.VMEM((share, width), tokens.dtype), pltpu.VMEM((share, width), jnp.float32)]
        + scatter_scratch(share, width),
        compiler_params=pltpu.CompilerParams(
            collective_id=4, has_side_effects=True, vmem_limit_bytes=VMEM_LIMIT
        ),
        cost_estimate=lasting(70),
        name="last_rows",
    )(
        back.reshape(4, 2, share, -1),
        weights,
        gain,
        ups,
        early,
        *later,
    )
    return (
        out.reshape(2 * share, width),
        result_out.reshape(2 * share, width),
        up_out,
        gain_out,
    )


def exchange_kernel(blocks, query, pair, other_sums, out, gain_out, sent, landed, sums):
    p = Plane(sent, landed, diagonal=True)
    moves = []
    for partner, rank in ((p.both, p.at_both), (p.x, p.at_x), (p.y, p.at_y)):
        moves.append((p.send(blocks.at[rank], out.at[p.rank], partner), out.at[rank]))
    out[p.rank] = blocks[p.rank]
    width = query.shape[1] // 4

    def attention_rows(rows):
        pairs = []
        for c in range(4):
            pairs.append((out[c, rows, :width], query[rows, c * width : c * width + width]))
            pairs.append((out[c, rows, width : width + 128], pair[rows, c * 128 : c * 128 + 128]))
        sums[0, rows, :] = lane_sums(pairs)

    for number, target in moves:
        p.arrive(number, target)
    slabs(0, blocks.shape[1], attention_rows)
    swapped = p.send(sums.at[0], sums.at[1], p.sibling)
    p.arrive(swapped, sums.at[1])
    gain_out[0] = sums[0] + sums[1]
    gain_out[1] = other_sums[...]
    p.finish()


def exchange(blocks, query, pair, other_sums):
    depth = blocks.shape[1]
    return pl.pallas_call(
        exchange_kernel,
        out_shape=[
            jax.ShapeDtypeStruct(blocks.shape, blocks.dtype),
            jax.ShapeDtypeStruct((2, depth, 128), jnp.float32),
        ],
        in_specs=[VMEM] * 4,
        out_specs=[VMEM] * 2,
        scratch_shapes=wires(4) + [pltpu.VMEM((2, depth, 128), jnp.float32)],
        compiler_params=pltpu.CompilerParams(collective_id=5, has_side_effects=True),
        cost_estimate=lasting(8),
        name="exchange_blocks",
    )(blocks, query, pair, other_sums)


def finish_first_kernel(down, gate, down_out, gate_out):
    down_out[...] = jnp.transpose(down[0].astype(jnp.float32))
    gate_out[...] = gate[0].astype(jnp.float32)


def finish_first(down, gate):
    groups, depth, units = down.shape
    block = pl.BlockSpec((1, depth, units), lambda i: (i, 0, 0))
    return pl.pallas_call(
        finish_first_kernel,
        grid=(groups,),
        in_specs=[block, block],
        out_specs=[
            pl.BlockSpec((units, depth), lambda i: (i, 0)),
            pl.BlockSpec((depth, units), lambda i: (0, i)),
        ],
        out_shape=[
            jax.ShapeDtypeStruct((groups * units, depth), jnp.float32),
            jax.ShapeDtypeStruct((depth, groups * units), jnp.float32),
        ],
        compiler_params=pltpu.CompilerParams(vmem_limit_bytes=VMEM_LIMIT),
        cost_estimate=lasting(5),
        name="finish_first",
    )(down, gate)


def finish_kernel(
    attn, up, tokens, result, sums, gains,
    query_out, key_out, value_out, out_out, up_out, tokens_out, result_out, gain_out,
):
    width = query_out.shape[1]
    query_out[...] = attn[0, :, :width].astype(jnp.float32)
    for c in range(key_out.shape[1] // HEAD):

        @pl.when(pl.program_id(0) == c)
        def _(c=c):
            cut = slice(c * HEAD, c * HEAD + HEAD)
            key_out[:, cut] = attn[0, :, width : width + HEAD].astype(jnp.float32)
            value_out[:, cut] = attn[0, :, width + HEAD : width + 2 * HEAD].astype(jnp.float32)

    out_out[...] = jnp.transpose(attn[0, :, width + 128 :].astype(jnp.float32))
    up_out[...] = up[0].astype(jnp.float32)
    tokens_out[...] = tokens[...]
    result_out[...] = result[...]
    for i in range(2):
        gain_out[i : i + 1, :] = jnp.transpose(sums[i])[0:1] / gains[i : i + 1, :]


def finish(attn, up, tokens, result, sums, gains):
    groups, depth, units = up.shape
    width = attn.shape[2] // 2 - HEAD
    rows, columns = tokens.shape
    part = rows // groups

    def block(*shape):
        return pl.BlockSpec((1, *shape), lambda i: (i, 0, 0))

    def wide(count):
        return pl.BlockSpec((depth, count), lambda i: (0, i))

    def tall(count, other):
        return pl.BlockSpec((count, other), lambda i: (i, 0))

    def f32(*shape):
        return jax.ShapeDtypeStruct(shape, jnp.float32)

    return pl.pallas_call(
        finish_kernel,
        grid=(groups,),
        in_specs=[
            block(depth, attn.shape[2]),
            block(depth, units),
            tall(part, columns),
            tall(part, columns),
            pl.BlockSpec(sums.shape, lambda i: (0, 0, 0)),
            pl.BlockSpec(gains.shape, lambda i: (0, 0)),
        ],
        out_specs=[
            wide(width),
            pl.BlockSpec((depth, groups * HEAD), lambda i: (0, 0)),
            pl.BlockSpec((depth, groups * HEAD), lambda i: (0, 0)),
            tall(width, depth),
            wide(units),
            tall(part, columns),
            tall(part, columns),
            pl.BlockSpec((2, 128), lambda i: (0, 0)),
        ],
        out_shape=[
            f32(depth, groups * width),
            f32(depth, groups * HEAD),
            f32(depth, groups * HEAD),
            f32(groups * width, depth),
            f32(depth, groups * units),
            f32(rows, columns),
            jax.ShapeDtypeStruct(result.shape, result.dtype),
            f32(2, 128),
        ],
        compiler_params=pltpu.CompilerParams(vmem_limit_bytes=VMEM_LIMIT),
        cost_estimate=lasting(12),
        name="finish",
    )(attn, up, tokens, result, sums, gains)


def context_pairs(step):
    return [(i, i ^ step) for i in range(4)]


def ffn_first_kernel(hidden, weights, m, gate, up):
    units = m.shape[1]
    for j in range(units // 256):
        cut = slice(j * 256, j * 256 + 256)
        gate_part = dot(hidden[...], weights[:, cut])
        up_part = dot(hidden[...], weights[:, units + j * 256 : units + j * 256 + 256])
        gate[:, cut] = gate_part.astype(jnp.bfloat16)
        up[:, cut] = up_part.astype(jnp.bfloat16)
        sigmoid = 1.0 / (1.0 + jnp.exp(-gate_part))
        m[:, cut] = (gate_part * sigmoid * up_part).astype(jnp.bfloat16)


def ffn_slopes_kernel(grad, gate, up, down_w, early, slopes):
    units = down_w.shape[1]
    for j in range(units // 256):
        cut = slice(j * 256, j * 256 + 256)
        grad_part = dot(grad[...], down_w[:, cut])
        gate_part = gate[:, cut].astype(jnp.float32)
        up_part = up[:, cut].astype(jnp.float32)
        sigmoid = 1.0 / (1.0 + jnp.exp(-gate_part))
        slope = sigmoid * (1.0 + gate_part * (1.0 - sigmoid))
        slopes[:, cut] = (grad_part * up_part * slope).astype(jnp.bfloat16)
        slopes[:, units + j * 256 : units + j * 256 + 256] = (
            grad_part * gate_part * sigmoid
        ).astype(jnp.bfloat16)


def first_rows_kernel(values, gains, weight, hidden, raw):
    value = values[...].astype(jnp.float32)
    normed = (value * row_root(value) * gains[0:1, :]).astype(jnp.bfloat16)
    hidden[...] = normed
    raw[...] = dot(normed, weight[...])


def first_rows(values, gains, packed, columns):
    count, width = values.shape
    return pl.pallas_call(
        first_rows_kernel,
        grid=(count // ROW_TILE,),
        in_specs=[
            pl.BlockSpec((ROW_TILE, width), lambda i: (i, 0)),
            pl.BlockSpec((8, width), lambda i: (0, 0)),
            pl.BlockSpec((width, columns), lambda i: (0, 0)),
        ],
        out_specs=[
            pl.BlockSpec((ROW_TILE, width), lambda i: (i, 0)),
            pl.BlockSpec((ROW_TILE, columns), lambda i: (i, 0)),
        ],
        out_shape=[
            jax.ShapeDtypeStruct((count, width), jnp.bfloat16),
            jax.ShapeDtypeStruct((count, columns), jnp.float32),
        ],
        compiler_params=pltpu.CompilerParams(vmem_limit_bytes=VMEM_LIMIT),
        cost_estimate=lasting(4),
        name="first_rows",
    )(values, gains, packed)


def attention_weights_kernel(hidden, back, grad, attended, moving, *rest):
    out, moved, sent, landed, local = rest[-5:]
    step, last = pl.program_id(0), pl.num_programs(0) - 1

    @pl.when(step == 0)
    def start():
        p = Plane(sent, landed, diagonal=True)
        pltpu.make_async_copy(moving.at[p.rank], moved.at[p.rank], local).start()
        for partner, rank in ((p.both, p.at_both), (p.x, p.at_x), (p.y, p.at_y)):
            p.send(moving.at[rank], moved.at[p.rank], partner)

    columns = back.shape[1]
    out[:, :columns] = dot(hidden[...], back[...], FIRST).astype(jnp.bfloat16)
    out[:, columns:] = dot(grad[...], attended[...], FIRST).astype(jnp.bfloat16)

    @pl.when(step == last)
    def finish():
        p = Plane(sent, landed, entered=True)
        for number, rank in enumerate((p.at_both, p.at_x, p.at_y)):
            move = p.copy(number, moving.at[rank], moved.at[rank], p.x)
            move.wait_recv()
            move.wait_send()
        pltpu.make_async_copy(moving.at[p.rank], moved.at[p.rank], local).wait()


def attention_weights(hidden, back, grad, attended, moving, early):
    count, width = hidden.shape
    first, second = back.shape[1], attended.shape[1]
    tall = pl.BlockSpec((count, 256), lambda i: (0, i))
    return pl.pallas_call(
        attention_weights_kernel,
        grid=(width // 256,),
        in_specs=[
            tall,
            pl.BlockSpec((count, first), lambda i: (0, 0)),
            tall,
            pl.BlockSpec((count, second), lambda i: (0, 0)),
        ]
        + [ANY] * (1 + len(early)),
        out_specs=[pl.BlockSpec((256, first + second), lambda i: (i, 0)), ANY],
        out_shape=[
            jax.ShapeDtypeStruct((width, first + second), jnp.bfloat16),
            jax.ShapeDtypeStruct(moving.shape, moving.dtype),
        ],
        scratch_shapes=wires(3) + [pltpu.SemaphoreType.DMA],
        compiler_params=pltpu.CompilerParams(
            collective_id=8, has_side_effects=True, vmem_limit_bytes=VMEM_LIMIT
        ),
        cost_estimate=lasting(25),
        name="attention_weights",
    )(hidden, back, grad, attended, moving, *early)


ROW_TILE = 256


def row_tiles(kernel, name, rows, weights, extra, widths):
    count = rows[0].shape[0]

    def tile(width):
        return pl.BlockSpec((ROW_TILE, width), lambda i: (i, 0))

    whole = [
        pl.BlockSpec(w.shape, lambda i: (0, 0), pipeline_mode=pl.Buffered(1)) for w in weights
    ]
    flops = 2 * count * sum(w.size for w in weights)
    return pl.pallas_call(
        kernel,
        grid=(count // ROW_TILE,),
        in_specs=[tile(r.shape[1]) for r in rows] + whole + [ANY] * len(extra),
        out_specs=[tile(width) for width in widths],
        out_shape=[jax.ShapeDtypeStruct((count, width), jnp.bfloat16) for width in widths],
        compiler_params=pltpu.CompilerParams(vmem_limit_bytes=56 * 1024 * 1024),
        cost_estimate=pl.CostEstimate(flops=flops, bytes_accessed=flops // 400, transcendentals=0),
        name=name,
    )(*rows, *weights, *extra)


def norm_backward(gradient, normed, inv_root):
    return inv_root * (gradient - normed * jnp.mean(gradient * normed, axis=-1, keepdims=True))


def inverse_root(values):
    return lax.rsqrt(jnp.mean(values * values, axis=-1, keepdims=True) + epsilon)


PLANE = ("context", "tensor")


def gather_rows(values):
    return lax.all_gather(values, PLANE, axis=0, tiled=True)


def scatter_rows(partial):
    return lax.psum_scatter(
        partial.astype(jnp.bfloat16), PLANE, scatter_dimension=0, tiled=True
    ).astype(jnp.float32)


def local(
    tokens,
    cotangent,
    attn_gain,
    w_query,
    w_key,
    w_value,
    w_out,
    ffn_gain,
    w_gate,
    w_up,
    w_down,
    piece_segment,
    piece_parent,
    piece_start,
):
    groups = lax.axis_size("context")
    cores = lax.axis_size("tensor")
    depth = w_query.shape[0]
    kv_count = w_key.shape[1] // HEAD
    sharing = groups // kv_count
    share = tokens.shape[0] // cores
    first_row = lax.axis_index("tensor") * share

    def my_rows(values):
        return lax.dynamic_slice_in_dim(values, first_row, share, 0)

    def blocks(weight):
        return jnp.transpose(weight.reshape(depth, groups, -1), (1, 0, 2))

    def kv_blocks(weight):
        return jnp.repeat(jnp.transpose(weight.reshape(depth, kv_count, HEAD), (1, 0, 2)), sharing, 0)

    def spread(weight_blocks):
        mine = lax.all_to_all(weight_blocks, "context", 0, 0)
        mine = mine.reshape(groups * depth, -1)
        return lax.all_gather(mine, "fsdp", axis=0, tiled=True)

    square = groups == 4 and cores == 2
    width = w_query.shape[1] // groups
    columns_qkv = width + 2 * HEAD
    down_turned = w_down.T
    tokens_half, cotangent_half = my_rows(tokens), my_rows(cotangent)

    def over_groups(blocks_here):
        return lax.all_gather(
            blocks_here.reshape(groups * depth, -1), "fsdp", axis=0, tiled=True
        )

    if square:
        gains = jnp.pad(jnp.stack([attn_gain, ffn_gain]).astype(jnp.float32), ((0, 6), (0, 0)))
        packed, gain_rows, w_pair = first_exchange(w_query, w_key, w_value, w_out, gains)
        packed = over_groups(packed)
        both_blocks, down_blocks = exchange_columns(w_gate, w_up, down_turned, gain_rows)
        inputs_full, ffn_grad, my_ffn_grad = start_plane(tokens, cotangent, down_blocks)
        both_full, down_full = over_groups(both_blocks), over_groups(down_blocks)
        hidden_first, raw = first_rows(
            inputs_full.reshape(-1, inputs_full.shape[3]), gain_rows, packed, columns_qkv
        )
        out_full = packed[:, columns_qkv:]
    else:
        gains = jnp.stack([attn_gain, ffn_gain], axis=1)
        gains = jnp.broadcast_to(jnp.pad(gains, ((0, 0), (0, 126))), (groups, depth, 128))
        packed = spread(
            jnp.concatenate(
                [
                    blocks(w_query),
                    kv_blocks(w_key),
                    kv_blocks(w_value),
                    blocks(w_out.T),
                    gains,
                ],
                axis=2,
            )
        )
        qkv_full = packed[:, :columns_qkv]
        out_full = packed[:, columns_qkv : columns_qkv + width]
        gains_full = packed[:, columns_qkv + width :].astype(jnp.float32)
        attn_scale, ffn_scale = gains_full[:, 0], gains_full[:, 1]
        both_full = spread(jnp.concatenate([blocks(w_gate), blocks(w_up)], axis=2))
        down_full = spread(blocks(down_turned))
        inputs_full = gather_rows(tokens_half).astype(jnp.float32)
        hidden_first = inputs_full * inverse_root(inputs_full) * attn_scale
        hidden_first = hidden_first.astype(jnp.bfloat16)
        raw = dot(hidden_first, qkv_full)
        my_ffn_grad = (residual_scale * cotangent_half.astype(jnp.float32)).astype(jnp.bfloat16)
    tables = rope_tables()

    segment, starts = piece_segment[0] % 13, piece_start[0]
    places = jnp.where(
        segment == 0,
        starts,
        jnp.where(
            segment <= BRANCHES,
            starts + (segment - 1) * SEG,
            starts + (segment - 1 - BRANCHES) * SEG + (BRANCHES - 1) * SEG,
        ),
    )

    residual_in = tokens_half.astype(jnp.float32)
    grad_result = cotangent_half.astype(jnp.float32)

    attended, *kept = attention_forward(places, starts, raw, tables)
    if square:
        ffn_grad_blocks = [
            lax.ppermute(my_ffn_grad, "context", context_pairs(step)) for step in (1, 2, 3)
        ]
        hidden_block, middle = middle_plane(attended, packed, tokens, gain_rows)
    else:
        ffn_grad = gather_rows(my_ffn_grad)
        middle = residual_in + residual_scale * scatter_rows(dot(attended, out_full, LAST))
        hidden_second = gather_rows((middle * inverse_root(middle) * ffn_scale).astype(jnp.bfloat16))

    units = down_full.shape[1]
    if square:
        hidden_second, hidden, gate_proj, up_proj, ffn_grad = ffn_rows(
            hidden_block, both_full, ffn_grad, ffn_grad_blocks
        )
    else:
        hidden, gate_proj, up_proj = row_tiles(
            ffn_first_kernel,
            "ffn_first",
            [hidden_second],
            [both_full],
            [],
            [units, units, units],
        )
    grad_down = dot(ffn_grad, hidden, FIRST).astype(jnp.bfloat16)
    (slopes,) = row_tiles(
        ffn_slopes_kernel,
        "ffn_slopes",
        [ffn_grad, gate_proj, up_proj],
        [down_full],
        [grad_down],
        [2 * units],
    )
    def sum_groups(gradient):
        return lax.psum_scatter(gradient, "fsdp", scatter_dimension=0, tiled=True)

    def hand_back(gradient):
        return lax.all_to_all(gradient.reshape(groups, depth, -1), "context", 0, 0)

    def columns(gradient):
        return jnp.transpose(gradient, (1, 0, 2)).reshape(depth, -1).astype(jnp.float32)

    if square:
        grad_middle, my_attn_grad, grad_gate = second_plane(
            slopes,
            hidden_second,
            both_full,
            middle,
            cotangent,
            gain_rows,
            grad_down,
        )
        attn_grad, ffn_pairs, grad_up = spread_plane(
            my_attn_grad, hidden, down_full, hidden_second, slopes, grad_gate
        )
        ffn_parts = [ffn_pairs[0]] + [
            lax.ppermute(ffn_pairs[step], "context", context_pairs(step)) for step in (1, 2, 3)
        ]
    else:
        root = inverse_root(middle)
        ffn_out = dot(hidden, down_full, LAST)
        grad_gate = dot(hidden_second, slopes[:, :units], FIRST).astype(jnp.bfloat16)
        grad_up = dot(hidden_second, slopes[:, units:], FIRST).astype(jnp.bfloat16)
        grad_second = dot(slopes, both_full, LAST)
        grad_middle = grad_result + norm_backward(
            scatter_rows(grad_second) * ffn_scale, middle * root, root
        )
        attn_grad = gather_rows((residual_scale * grad_middle).astype(jnp.bfloat16))
        ffn_parts = []
    grad_attended = dot(attn_grad, out_full).astype(jnp.bfloat16)
    grad_down = sum_groups(grad_down)
    grad_gate, grad_up = sum_groups(grad_gate), sum_groups(grad_up)
    back = attention_backward(places, starts, grad_attended, kept, tables, [grad_down])
    grad_down = hand_back(grad_down)
    if square:
        grad_attn, grad_gate = attention_weights(
            hidden_first,
            back,
            attn_grad,
            attended,
            grad_gate.reshape(groups, depth, -1),
            [grad_down, *ffn_parts[1:]],
        )
    else:
        grad_attn = jnp.concatenate(
            [dot(hidden_first, back, FIRST), dot(attn_grad, attended, FIRST)], axis=1
        ).astype(jnp.bfloat16)
        grad_first = dot(back, qkv_full, LAST).astype(jnp.bfloat16)
        grad_gate, grad_up = hand_back(grad_gate), hand_back(grad_up)
    grad_attn = sum_groups(grad_attn)
    if square:
        down, gate = finish_first(grad_down, grad_gate)
        grad_tokens, result, grad_up, ffn_sums = last_plane(
            back,
            packed,
            tokens,
            grad_middle,
            gain_rows,
            middle,
            ffn_parts,
            grad_up.reshape(groups, depth, -1),
            grad_gate,
            w_gate,
            w_up,
            down,
        )
        grad_attn, sums = exchange(
            grad_attn.reshape(groups, depth, -1), w_query, w_pair, ffn_sums
        )
        my_gains = jnp.stack([attn_gain, ffn_gain]).astype(jnp.float32)
        query, key, value, out, up, grad_tokens, result, gain_grads = finish(
            grad_attn, grad_up, grad_tokens, result, sums, my_gains
        )
        return (
            result,
            grad_tokens,
            gain_grads[0],
            query,
            key,
            value,
            out,
            gain_grads[1],
            gate,
            up,
            down,
        )
    else:
        root = inverse_root(residual_in)
        grad_tokens = grad_middle + norm_backward(
            scatter_rows(grad_first) * attn_scale, residual_in * root, root
        )
        grad_tokens = lax.all_gather(grad_tokens, "tensor", axis=0, tiled=True)
        result = (middle + residual_scale * scatter_rows(ffn_out)).astype(jnp.bfloat16)
        grad_attn = hand_back(grad_attn)
        result = lax.all_gather(result, "tensor", axis=0, tiled=True)
    def kv_columns(gradient):
        gradient = gradient.astype(jnp.float32).reshape(kv_count, sharing, depth, HEAD)
        return jnp.transpose(jnp.sum(gradient, axis=1), (1, 0, 2)).reshape(depth, -1)

    grad_query = columns(grad_attn[:, :, :width])
    grad_key = kv_columns(grad_attn[:, :, width : width + HEAD])
    grad_value = kv_columns(grad_attn[:, :, width + HEAD : width + 2 * HEAD])
    grad_gate, grad_up = columns(grad_gate), columns(grad_up)

    def against(*pairs):
        return sum(jnp.sum(weight.astype(jnp.float32) * g, axis=1) for weight, g in pairs)

    gain_grads = jnp.stack(
        [
            against((w_query, grad_query), (w_key, grad_key), (w_value, grad_value)),
            against((w_gate, grad_gate), (w_up, grad_up)),
        ]
    )
    gain_grads = lax.psum(gain_grads, "tensor")
    return (
        result,
        grad_tokens,
        gain_grads[0] / attn_gain.astype(jnp.float32),
        grad_query,
        grad_key,
        grad_value,
        columns(grad_attn[:, :, width + 2 * HEAD :]).T,
        gain_grads[1] / ffn_gain.astype(jnp.float32),
        grad_gate,
        grad_up,
        columns(grad_down).T,
    )


ROWS = ("fsdp", "context")


def solution(mesh):
    return jax.shard_map(
        local,
        mesh=mesh,
        in_specs=(
            P(ROWS, None),
            P(ROWS, None),
            P(ROWS),
            P(ROWS, "tensor"),
            P(ROWS, "tensor"),
            P(ROWS, "tensor"),
            P("tensor", ROWS),
            P(ROWS),
            P(ROWS, "tensor"),
            P(ROWS, "tensor"),
            P("tensor", ROWS),
            P("fsdp", None),
            P("fsdp", None),
            P("fsdp", None),
        ),
        out_specs=(
            P(ROWS, None),
            P(ROWS, None),
            P(ROWS),
            P(ROWS, "tensor"),
            P(ROWS, "tensor"),
            P(ROWS, "tensor"),
            P("tensor", ROWS),
            P(ROWS),
            P(ROWS, "tensor"),
            P(ROWS, "tensor"),
            P("tensor", ROWS),
        ),
        check_vma=False,
    )
```

```python
import functools

import jax
import jax.numpy as jnp
import numpy as np
from jax import lax
from jax.experimental import pallas as pl
from jax.experimental.pallas import tpu as pltpu
from jax.sharding import PartitionSpec as P

HEAD = 64
SEG = 128
TRUNK = 8 * SEG
BRANCHES = 4
LEAVES = 8
GROUP = TRUNK + (BRANCHES + LEAVES) * SEG
DEPTH = TRUNK + 2 * SEG
TILE = 2 * SEG

epsilon = 1e-05
rope_base = 10000000.0
residual_scale = 0.22
score_scale = 0.015625
masked_score = -1e30

FIRST = (((0,), (0,)), ((), ()))
LAST = (((1,), (1,)), ((), ()))
PLAIN = (((1,), (0,)), ((), ()))


def dot(left_side, right_side, dims=PLAIN):
    return lax.dot_general(left_side, right_side, dims, preferred_element_type=jnp.float32)


def rope_tables():
    steps = np.arange(HEAD // 2, dtype=np.float32)
    frequency = np.float32(rope_base) ** (-(steps * np.float32(2)) / np.float32(HEAD))
    angles = np.arange(DEPTH, dtype=np.float32)[:, None] * frequency.astype(np.float32)
    angles = angles.astype(np.float64)
    cosine, sine = np.cos(angles).astype(np.float32), np.sin(angles).astype(np.float32)
    return (
        jnp.asarray(np.concatenate([cosine] * 4, axis=-1)),
        jnp.asarray(np.concatenate([-sine, sine, -sine, sine], axis=-1)),
    )


def lanes(values):
    return lax.broadcasted_iota(jnp.int32, values.shape, 1)


def swap_halves(values):
    return jnp.where(
        lanes(values) % HEAD < HEAD // 2,
        pltpu.roll(values, 128 - HEAD // 2, 1),
        pltpu.roll(values, HEAD // 2, 1),
    )


def only_head(values, head):
    return jnp.where(lanes(values) // HEAD == head, values, jnp.zeros_like(values))


def query_tiles(work):
    for j in range(TRUNK // TILE):
        prefix = [(0, j * TILE, False)] if j else []
        work(j * TILE, prefix + [(j * TILE, TILE, True)], False)

    def branch(i, carry):
        row = pl.multiple_of(TRUNK + i * TILE, TILE)
        work(row, [(0, TRUNK, False), (row, TILE, True)], True)
        return carry

    lax.fori_loop(0, BRANCHES * SEG // TILE, branch, 0)

    def leaf(i, carry):
        row = pl.multiple_of(TRUNK + BRANCHES * SEG + i * TILE, TILE)
        parent = pl.multiple_of(TRUNK + i * SEG, SEG)
        work(row, [(0, TRUNK, False), (parent, SEG, False), (row, TILE, True)], True)
        return carry

    lax.fori_loop(0, LEAVES * SEG // TILE, leaf, 0)


def visible_scores(keys, query, own, one_segment):
    scores = dot(keys, query, LAST)
    if not own:
        return scores
    key_at = lax.broadcasted_iota(jnp.int32, scores.shape, 0)
    query_at = lax.broadcasted_iota(jnp.int32, scores.shape, 1)
    seen = key_at <= query_at
    if one_segment:
        seen = seen & (key_at // SEG == query_at // SEG)
    return jnp.where(seen, scores, masked_score)


def turned_over(target, source):
    for first in range(0, source.shape[0], TILE):
        block = source[first : first + TILE, :128].astype(jnp.float32)
        target[:, first : first + TILE] = jnp.transpose(block)[:HEAD].astype(jnp.bfloat16)


def head_pairs(width, work):
    together = min(PAIR, width // HEAD)

    def step(i, carry):
        work([i * together + j for j in range(together)])
        return carry

    lax.fori_loop(0, width // HEAD // together, step, 0)


PAIR = 2


def attention_forward_kernel(
    to_ref, start_ref, raw_ref, cos_ref, sin_ref, out_ref, q_ref, k_ref, v_ref, log_ref,
    held, values_ref, tile_ref,
):
    width = q_ref.shape[1]
    pieces = to_ref.shape[0]
    piece = raw_ref.shape[0] // pieces

    def place(p, carry):
        rows = pl.ds(pl.multiple_of(p * piece, piece), piece)
        to = pl.ds(pl.multiple_of(to_ref[p], piece), piece)
        at = pl.ds(pl.multiple_of(start_ref[p], piece), piece)
        cosine, sine = cos_ref[at, :], sin_ref[at, :]

        def turn(values):
            return values * cosine + swap_halves(values) * sine

        for g in range(width // 128):
            cut = slice(g * 128, g * 128 + 128)
            turned = turn(raw_ref[rows, cut]).astype(jnp.bfloat16)
            q_ref[to, cut] = turned * jnp.bfloat16(score_scale)
        pair = raw_ref[rows, width : width + 128]
        low = lanes(pair) < HEAD
        key = turn(pair)
        key = jnp.where(low, key, pltpu.roll(key, HEAD, 1)).astype(jnp.bfloat16)
        value = jnp.where(low, pltpu.roll(pair, HEAD, 1), pair).astype(jnp.bfloat16)
        for g in range(width // 128):
            cut = slice(g * 128, g * 128 + 128)
            k_ref[to, cut] = key
            v_ref[to, cut] = value
        return carry

    lax.fori_loop(0, pieces, place, 0)
    turned_over(values_ref, v_ref)

    def work(row, parts, one_segment):
        rows = pl.ds(row, TILE)

        def one_head(head):
            query = only_head(q_ref[rows, :], head)
            scores = [
                visible_scores(k_ref[pl.ds(first, count), :], query, own, one_segment)
                for first, count, own in parts
            ]
            largest = functools.reduce(
                jnp.maximum, [jnp.max(s, axis=0, keepdims=True) for s in scores]
            )
            exponent = [jnp.exp(s - largest) for s in scores]
            total = functools.reduce(
                jnp.add, [jnp.sum(e, axis=0, keepdims=True) for e in exponent]
            )
            result = functools.reduce(
                jnp.add,
                [
                    dot(values_ref[:, pl.ds(first, count)], e.astype(jnp.bfloat16))
                    for e, (first, count, own) in zip(exponent, parts)
                ],
            )
            log_ref[head, :, rows] = largest + jnp.log(total)
            tile_ref[pl.ds(pl.multiple_of(head * HEAD, HEAD), HEAD), :] = result * (1.0 / total)

        def heads(together):
            for head in together:
                one_head(head)

        head_pairs(width, heads)
        held[rows, :] = jnp.transpose(tile_ref[...]).astype(jnp.bfloat16)

    query_tiles(work)

    def back(p, carry):
        rows = pl.ds(pl.multiple_of(p * piece, piece), piece)
        to = pl.ds(pl.multiple_of(to_ref[p], piece), piece)
        out_ref[rows, :] = held[to, :]
        return carry

    lax.fori_loop(0, pieces, back, 0)


def attention_backward_kernel(
    to_ref,
    start_ref,
    grad_ref,
    q_ref,
    k_ref,
    v_ref,
    log_ref,
    cos_ref,
    sin_ref,
    *rest,
):
    out_ref, og_ref, dq_ref, dk_ref, dv_ref, keys_ref, tile_ref = rest[-7:]
    width = q_ref.shape[1]
    pieces = to_ref.shape[0]
    piece = grad_ref.shape[0] // pieces

    def place(p, carry):
        rows = pl.ds(pl.multiple_of(p * piece, piece), piece)
        to = pl.ds(pl.multiple_of(to_ref[p], piece), piece)
        og_ref[to, :] = grad_ref[rows, :]
        return carry

    lax.fori_loop(0, pieces, place, 0)
    turned_over(keys_ref, k_ref)
    dk_ref[...] = jnp.zeros_like(dk_ref)
    dv_ref[...] = jnp.zeros_like(dv_ref)

    def work(row, parts, one_segment):
        rows = pl.ds(row, TILE)

        def heads(together):
            queries, out_grads, all_weights, all_grads = [], [], [], []
            for head in together:
                query = only_head(q_ref[rows, :], head)
                out_grad = only_head(og_ref[rows, :], head)
                log_total = log_ref[head, :, rows]
                weights, products = [], []
                for first, count, own in parts:
                    keys = pl.ds(first, count)
                    scores = visible_scores(k_ref[keys, :], query, own, one_segment)
                    weights.append(jnp.exp(scores - log_total))
                    products.append(dot(v_ref[keys, :], out_grad, LAST))
                inner = functools.reduce(
                    jnp.add,
                    [jnp.sum(w * d, axis=0, keepdims=True) for w, d in zip(weights, products)],
                )
                grads = [
                    (w * (d - inner)).astype(jnp.bfloat16) for w, d in zip(weights, products)
                ]
                queries.append(query)
                out_grads.append(out_grad)
                all_weights.append([w.astype(jnp.bfloat16) for w in weights])
                all_grads.append(grads)
                tile_ref[pl.ds(pl.multiple_of(head * HEAD, HEAD), HEAD), :] = functools.reduce(
                    jnp.add,
                    [
                        dot(keys_ref[:, pl.ds(first, count)], g)
                        for (first, count, own), g in zip(parts, grads)
                    ],
                )
            query = jnp.concatenate(queries, axis=0)
            out_grad = jnp.concatenate(out_grads, axis=0)
            for i, (first, count, own) in enumerate(parts):
                keys = pl.ds(first, count)
                weights = jnp.concatenate([w[i] for w in all_weights], axis=1)
                grads = jnp.concatenate([g[i] for g in all_grads], axis=1)
                dv_ref[keys, :] += dot(weights, out_grad)
                dk_ref[keys, :] += dot(grads, query)

        head_pairs(width, heads)
        dq_ref[rows, :] = jnp.transpose(tile_ref[...])

    query_tiles(work)

    def back(p, carry):
        rows = pl.ds(pl.multiple_of(p * piece, piece), piece)
        to = pl.ds(pl.multiple_of(to_ref[p], piece), piece)
        at = pl.ds(pl.multiple_of(start_ref[p], piece), piece)
        cosine, sine = cos_ref[at, :], sin_ref[at, :]

        def turn_back(values):
            return values * cosine - swap_halves(values) * sine

        def over_heads(ref):
            total = functools.reduce(
                jnp.add, [ref[to, g * 128 : g * 128 + 128] for g in range(width // 128)]
            )
            return total + pltpu.roll(total, HEAD, 1)

        for g in range(width // 128):
            cut = slice(g * 128, g * 128 + 128)
            turned = turn_back(score_scale * dq_ref[to, cut])
            out_ref[rows, cut] = turned.astype(jnp.bfloat16)
        key = turn_back(over_heads(dk_ref))
        value = over_heads(dv_ref)
        pair = jnp.where(lanes(key) < HEAD, key, value)
        out_ref[rows, width : width + 128] = pair.astype(jnp.bfloat16)
        return carry

    lax.fori_loop(0, pieces, back, 0)


SMEM = pl.BlockSpec(memory_space=pltpu.SMEM)
VMEM = pl.BlockSpec(memory_space=pltpu.VMEM)
VMEM_LIMIT = 60 * 1024 * 1024


def attention_cost(width, products):
    flops = products * 2 * GROUP * (GROUP * 2 // 5) * width
    return pl.CostEstimate(
        flops=flops, bytes_accessed=16 * GROUP * width, transcendentals=GROUP * GROUP * width // 128
    )


def attention_forward(places, starts, raw, tables):
    width = raw.shape[1] - 2 * HEAD
    rows = raw.shape[0]
    kept = jax.ShapeDtypeStruct((rows, width), jnp.bfloat16)
    return pl.pallas_call(
        attention_forward_kernel,
        out_shape=[kept] * 4 + [jax.ShapeDtypeStruct((width // HEAD, 1, rows), jnp.float32)],
        in_specs=[SMEM, SMEM, VMEM, VMEM, VMEM],
        out_specs=[VMEM] * 5,
        scratch_shapes=[
            pltpu.VMEM((rows, width), jnp.bfloat16),
            pltpu.VMEM((HEAD, rows), jnp.bfloat16),
            pltpu.VMEM((width, TILE), jnp.float32),
        ],
        compiler_params=pltpu.CompilerParams(vmem_limit_bytes=VMEM_LIMIT),
        cost_estimate=attention_cost(width, 4),
        name="attention_forward",
    )(places, starts, raw, *tables)


def attention_backward(places, starts, out_grad, kept, tables, early):
    rows, width = out_grad.shape
    return pl.pallas_call(
        attention_backward_kernel,
        out_shape=jax.ShapeDtypeStruct((rows, width + 2 * HEAD), jnp.bfloat16),
        in_specs=[SMEM, SMEM] + [VMEM] * 7 + [ANY] * len(early),
        out_specs=VMEM,
        scratch_shapes=[
            pltpu.VMEM((rows, width), jnp.bfloat16),
            pltpu.VMEM((rows, width), jnp.float32),
            pltpu.VMEM((rows, width), jnp.float32),
            pltpu.VMEM((rows, width), jnp.float32),
            pltpu.VMEM((HEAD, rows), jnp.bfloat16),
            pltpu.VMEM((width, TILE), jnp.float32),
        ],
        compiler_params=pltpu.CompilerParams(vmem_limit_bytes=VMEM_LIMIT),
        cost_estimate=attention_cost(width, 10),
        name="attention_backward",
    )(places, starts, out_grad, *kept, *tables, *early)


MESH = pl.DeviceIdType.MESH
ANY = pl.BlockSpec(memory_space=pl.ANY)
CHUNKS = 4
SLAB = 16


def lasting(microseconds):
    return pl.CostEstimate(
        flops=0, bytes_accessed=int(microseconds * 3_000_000), transcendentals=0
    )


class Plane:
    def __init__(self, sent, landed, diagonal=False, entered=False):
        self.sent, self.landed = sent, landed
        self.copies = []
        self.rank = lax.axis_index("context")
        self.core = lax.axis_index("tensor")
        self.at_x = self.rank + 1 - 2 * lax.rem(self.rank, 2)
        self.at_y = lax.rem(self.rank + 2, 4)
        self.at_both = 3 - self.rank
        self.x = {"context": self.at_x}
        self.y = {"context": self.at_y}
        self.both = {"context": self.at_both}
        self.sibling = {"tensor": 1 - self.core}
        if entered:
            return
        barrier = pltpu.get_barrier_semaphore()
        partners = [self.x, self.y, self.sibling] + ([self.both] if diagonal else [])
        for partner in partners:
            pl.semaphore_signal(barrier, inc=1, device_id=partner, device_id_type=MESH)
        pl.semaphore_wait(barrier, len(partners))

    def copy(self, number, source, target, partner):
        return pltpu.make_async_remote_copy(
            src_ref=source,
            dst_ref=target,
            send_sem=self.sent.at[number],
            recv_sem=self.landed.at[number],
            device_id=partner,
            device_id_type=MESH,
        )

    def send(self, source, target, partner):
        number = len(self.copies)
        started = self.copy(number, source, target, partner)
        started.start()
        self.copies.append(started)
        return number

    def arrive(self, number, target):
        self.copy(number, target, target, self.sibling).wait_recv()

    def finish(self):
        for started in self.copies:
            started.wait_send()


def chunk(index, rows):
    return pl.ds(index * (rows // CHUNKS), rows // CHUNKS)


class Gather:
    def __init__(self, plane, block, out):
        self.plane, self.block, self.out = plane, block, out
        self.rows = block.shape[0]
        self.to_x, self.to_y, self.across, self.onward = {}, {}, {}, {}

    def start(self, k):
        p, cut = self.plane, chunk(k, self.rows)
        target = self.out.at[p.rank, p.core, cut]
        self.to_x[k] = p.send(self.block.at[cut], target, p.x)
        self.to_y[k] = p.send(self.block.at[cut], target, p.y)
        self.across[0, k] = p.send(self.block.at[cut], target, p.sibling)

    def forward_chunk(self, k):
        p, out = self.plane, self.out
        cut = chunk(k, self.rows)
        from_x, from_y = out.at[p.at_x, p.core, cut], out.at[p.at_y, p.core, cut]
        p.arrive(self.to_x[k], from_x)
        if k < CHUNKS // 2:
            self.onward[k] = p.send(from_x, from_x, p.y)
        self.across[1, k] = p.send(from_x, from_x, p.sibling)
        p.arrive(self.to_y[k], from_y)
        if k >= CHUNKS // 2:
            self.onward[k] = p.send(from_y, from_y, p.x)
        self.across[2, k] = p.send(from_y, from_y, p.sibling)

    def forward_far(self):
        p = self.plane
        for k in range(CHUNKS):
            far = self.out.at[p.at_both, p.core, chunk(k, self.rows)]
            p.arrive(self.onward[k], far)
            self.across[3, k] = p.send(far, far, p.sibling)

    def forward(self):
        for k in range(CHUNKS):
            self.forward_chunk(k)
        self.forward_far()

    def finish(self):
        p = self.plane
        for i, rank in enumerate((p.rank, p.at_x, p.at_y, p.at_both)):
            for k in range(CHUNKS):
                p.arrive(
                    self.across[i, k], self.out.at[rank, 1 - p.core, chunk(k, self.rows)]
                )


GATHER_COPIES = CHUNKS * 8


def add_rows(target, source, first, count):
    def step(i, carry):
        rows = pl.ds(first + i * SLAB, SLAB)
        target[rows, :] = (
            target[rows, :].astype(jnp.float32) + source[rows, :].astype(jnp.float32)
        ).astype(jnp.bfloat16)
        return carry

    lax.fori_loop(0, count // SLAB, step, 0)


class Scatter:
    def __init__(
        self, plane, rows_in, weights, columns, given, held, other, near_x, near_y, far_x, far_y
    ):
        p = self.plane = plane
        rows = near_x.shape[0]
        half = rows // 2
        halves = top, low = pl.ds(0, half), pl.ds(half, half)
        order = (p.at_both, p.at_x, p.at_y, p.rank)
        across = {}

        def make(i, h):
            for core, target in ((1 - p.core, given), (p.core, held)):
                value = dot(rows_in[order[i], core, halves[h], :], weights[:, columns], LAST)
                target[i, halves[h], :] = value.astype(jnp.bfloat16)
                if target is given:
                    source = given.at[i, halves[h]]
                    across[i, h] = p.send(source, other.at[i, halves[h]], p.sibling)

        def pair(i, h):
            p.arrive(across[i, h], other.at[i, halves[h]])
            add_rows(held.at[i], other.at[i], h * half, half)

        make(0, 0)
        make(0, 1)
        pair(0, 0)
        first = p.send(held.at[0, top], far_x, p.x)
        make(1, 0)
        pair(0, 1)
        second = p.send(held.at[0, low], far_y, p.y)
        make(2, 0)
        pair(1, 0)
        third = p.send(held.at[1, top], near_x.at[top], p.x)
        make(1, 1)
        make(2, 1)
        make(3, 0)
        make(3, 1)
        pair(2, 0)
        pair(1, 1)
        pair(2, 1)
        p.arrive(first, far_x)
        add_rows(held.at[2], far_x, 0, half)
        fourth = p.send(held.at[2, top], near_y.at[top], p.y)
        p.arrive(second, far_y)

        def step(i, carry):
            rows, at = pl.ds(half + i * SLAB, SLAB), pl.ds(i * SLAB, SLAB)
            held[1, rows, :] = (
                held[1, rows, :].astype(jnp.float32) + far_y[at, :].astype(jnp.float32)
            ).astype(jnp.bfloat16)
            return carry

        lax.fori_loop(0, half // SLAB, step, 0)
        fifth = p.send(held.at[1, low], near_x.at[low], p.x)
        sixth = p.send(held.at[2, low], near_y.at[low], p.y)
        pair(3, 0)
        pair(3, 1)
        self.halves = halves
        self.from_x, self.from_y = (third, fifth), (fourth, sixth)
        self.parts = (held.at[3], near_x, near_y)

    def ready(self, h):
        _, near_x, near_y = self.parts
        self.plane.arrive(self.from_x[h], near_x.at[self.halves[h]])
        self.plane.arrive(self.from_y[h], near_y.at[self.halves[h]])

    def rows(self, rows):
        return sum(part[rows, :].astype(jnp.float32) for part in self.parts)


SCATTER_COPIES = 8 + 6


def scatter_scratch(share, width):
    kind = jnp.bfloat16
    return [
        pltpu.VMEM((4, share, width), kind),
        pltpu.VMEM((4, share, width), kind),
        pltpu.VMEM((4, share, width), kind),
        pltpu.VMEM((share, width), kind),
        pltpu.VMEM((share, width), kind),
        pltpu.VMEM((share // 2, width), kind),
        pltpu.VMEM((share // 2, width), kind),
    ]


def wires(count):
    return [pltpu.SemaphoreType.DMA((count,)), pltpu.SemaphoreType.DMA((count,))]


def row_root(values):
    return lax.rsqrt(jnp.mean(values * values, axis=-1, keepdims=True) + epsilon)


def slabs(first, count, work):
    def step(i, carry):
        work(pl.ds(first + i * SLAB, SLAB))
        return carry

    lax.fori_loop(0, count // SLAB, step, 0)


class Exchange:
    def __init__(self, plane, source, target, local, first=0, columns=None):
        p = plane
        columns = columns or target.shape[2]

        def part(rank):
            return source.at[:, pl.ds(pl.multiple_of(rank * columns, 128), columns)]

        def place(rank):
            return target.at[rank, :, pl.ds(first, columns)]

        self.plane, self.place, self.moves = p, place, []
        self.mine = pltpu.make_async_copy(part(p.rank), place(p.rank), local)
        self.mine.start()
        for partner, rank in ((p.both, p.at_both), (p.x, p.at_x), (p.y, p.at_y)):
            self.moves.append((p.send(part(rank), place(p.rank), partner), rank))

    def finish(self):
        for number, rank in self.moves:
            self.plane.arrive(number, self.place(rank))
        self.mine.wait()


def first_kernel(
    query,
    key,
    value,
    out_weight,
    gains,
    packed,
    gains_out,
    pair,
    sent,
    landed,
    local,
    far_sent,
    far_landed,
    out_turned,
):
    groups = lax.axis_size("fsdp")
    group, rank = lax.axis_index("fsdp"), lax.axis_index("context")
    depth = gains.shape[1]
    others = [(i, j) for i in range(groups) for j in range(4) if i or j]

    def device(i, j):
        return {"fsdp": lax.rem(group + i, groups), "context": lax.rem(rank + j, 4)}

    def place(f, c):
        return gains_out.at[:, pl.ds(pl.multiple_of((f * 4 + c) * depth, 128), depth)]

    barrier = pltpu.get_barrier_semaphore()
    for i, j in others:
        pl.semaphore_signal(barrier, inc=1, device_id=device(i, j), device_id_type=MESH)
    for c in range(pair.shape[1] // 128):
        cut = slice(c // 2 * 128, c // 2 * 128 + 128)
        keys, values = key[:, cut].astype(jnp.float32), value[:, cut].astype(jnp.float32)
        if c % 2:
            keys = pltpu.roll(keys, HEAD, 1)
        else:
            values = pltpu.roll(values, HEAD, 1)
        both = jnp.where(lanes(keys) < HEAD, keys, values)
        pair[:, c * 128 : c * 128 + 128] = both.astype(jnp.bfloat16)
    for first in range(0, out_weight.shape[0], 256):
        block = jnp.transpose(out_weight[first : first + 256, :].astype(jnp.float32))
        out_turned[:, first : first + 256] = block.astype(jnp.bfloat16)
    pl.semaphore_wait(barrier, len(others))
    p = Plane(sent, landed, entered=True)
    width = query.shape[1] // 4
    exchanges = [
        Exchange(p, query, packed, local.at[0], 0, width),
        Exchange(p, pair, packed, local.at[1], width, 128),
        Exchange(p, out_turned, packed, local.at[2], width + 128, width),
    ]
    far = []
    for n, (i, j) in enumerate(others):
        far.append(
            pltpu.make_async_remote_copy(
                src_ref=gains,
                dst_ref=place(group, rank),
                send_sem=far_sent.at[n],
                recv_sem=far_landed.at[n],
                device_id=device(i, j),
                device_id_type=MESH,
            )
        )
        far[n].start()
    gains_out[:, pl.ds(pl.multiple_of((group * 4 + rank) * depth, 128), depth)] = gains[...]
    for started in far:
        started.wait()
    for exchange in exchanges:
        exchange.finish()
    p.finish()


def first_exchange(query, key, value, out_weight, gains):
    depth, columns = query.shape
    groups = lax.axis_size("fsdp")
    far = groups * 4 - 1
    return pl.pallas_call(
        first_kernel,
        out_shape=[
            jax.ShapeDtypeStruct((4, depth, columns // 2 + 128), query.dtype),
            jax.ShapeDtypeStruct((8, groups * 4 * depth), jnp.float32),
            jax.ShapeDtypeStruct((depth, 2 * key.shape[1]), key.dtype),
        ],
        in_specs=[VMEM] * 5,
        out_specs=[ANY, VMEM, VMEM],
        scratch_shapes=wires(9)
        + [pltpu.SemaphoreType.DMA((3,))]
        + wires(far)
        + [pltpu.VMEM((depth, columns), query.dtype)],
        compiler_params=pltpu.CompilerParams(
            collective_id=9, has_side_effects=True, vmem_limit_bytes=VMEM_LIMIT
        ),
        cost_estimate=lasting(10),
        name="first_exchange",
    )(query, key, value, out_weight, gains)


def start_kernel(tokens, cotangent, early, out, scaled, my_scaled, sent, landed, local):
    p = Plane(sent, landed)
    share = my_scaled.shape[0]
    block = tokens.at[pl.ds(pl.multiple_of(p.core * share, SLAB), share)]
    gather = Gather(p, block, out)
    mine = pltpu.make_async_copy(block, out.at[p.rank, p.core], local)
    for k in range(CHUNKS):
        gather.start(k)
    mine.start()

    def scale(rows):
        value = residual_scale * cotangent[rows, :].astype(jnp.float32)
        scaled[rows, :] = value.astype(jnp.bfloat16)

    def keep(rows):
        from_rows = pl.ds(pl.multiple_of(p.core * share + rows.start, SLAB), SLAB)
        my_scaled[rows, :] = scaled[from_rows, :]

    slabs(0, scaled.shape[0], scale)
    slabs(0, share, keep)
    gather.forward()
    gather.finish()
    p.finish()
    mine.wait()


def start_plane(tokens, cotangent, early):
    share, width = tokens.shape[0] // 2, tokens.shape[1]
    return pl.pallas_call(
        start_kernel,
        out_shape=[
            jax.ShapeDtypeStruct((4, 2, share, width), tokens.dtype),
            jax.ShapeDtypeStruct(cotangent.shape, jnp.bfloat16),
            jax.ShapeDtypeStruct((share, width), jnp.bfloat16),
        ],
        in_specs=[VMEM, VMEM, ANY],
        out_specs=[ANY, VMEM, VMEM],
        scratch_shapes=wires(GATHER_COPIES) + [pltpu.SemaphoreType.DMA],
        compiler_params=pltpu.CompilerParams(
            collective_id=1, has_side_effects=True, vmem_limit_bytes=VMEM_LIMIT
        ),
        cost_estimate=lasting(60),
        name="gather_tokens",
    )(tokens, cotangent, early)


def columns_kernel(gate, up, down, early, both_out, down_out, sent, landed, local):
    p = Plane(sent, landed, diagonal=True)
    units = down_out.shape[2]
    exchanges = [
        Exchange(p, gate, both_out, local.at[0], 0, units),
        Exchange(p, up, both_out, local.at[1], units, units),
        Exchange(p, down, down_out, local.at[2]),
    ]
    for exchange in exchanges:
        exchange.finish()
    p.finish()


def exchange_columns(gate, up, down, early):
    depth, units = gate.shape
    return pl.pallas_call(
        columns_kernel,
        out_shape=[
            jax.ShapeDtypeStruct((4, depth, units // 2), gate.dtype),
            jax.ShapeDtypeStruct((4, depth, units // 4), gate.dtype),
        ],
        in_specs=[VMEM] * 3 + [ANY],
        out_specs=[ANY] * 2,
        scratch_shapes=wires(9) + [pltpu.SemaphoreType.DMA((3,))],
        compiler_params=pltpu.CompilerParams(collective_id=10, has_side_effects=True),
        cost_estimate=lasting(30),
        name="exchange_columns",
    )(gate, up, down, early)


def middle_kernel(
    attended,
    weights,
    gain,
    tokens,
    hidden,
    middle,
    sent,
    landed,
    local,
    residual,
    *scratch,
):
    p = Plane(sent, landed)
    share = hidden.shape[0]
    first = pl.ds(pl.multiple_of(p.core * share, SLAB), share)
    load = pltpu.make_async_copy(tokens.at[first], residual, local)
    load.start()
    width = attended.shape[3]
    columns = slice(weights.shape[1] - width, weights.shape[1])
    total = Scatter(p, attended, weights, columns, *scratch)
    load.wait()

    def work(rows):
        value = residual[rows, :].astype(jnp.float32) + residual_scale * total.rows(rows)
        middle[rows, :] = value
        hidden[rows, :] = (value * row_root(value) * gain[1:2, :]).astype(jnp.bfloat16)

    for h in range(2):
        total.ready(h)
        slabs(h * (share // 2), share // 2, work)
    p.finish()


def middle_plane(attended, weights, tokens, gain):
    share, width = tokens.shape[0] // 2, tokens.shape[1]
    return pl.pallas_call(
        middle_kernel,
        out_shape=[
            jax.ShapeDtypeStruct((share, width), jnp.bfloat16),
            jax.ShapeDtypeStruct((share, width), jnp.float32),
        ],
        in_specs=[VMEM] * 3 + [ANY],
        out_specs=[VMEM, VMEM],
        scratch_shapes=wires(SCATTER_COPIES)
        + [
            pltpu.SemaphoreType.DMA,
            pltpu.VMEM((share, width), jnp.bfloat16),
        ]
        + scatter_scratch(share, width),
        compiler_params=pltpu.CompilerParams(
            collective_id=2, has_side_effects=True, vmem_limit_bytes=VMEM_LIMIT
        ),
        cost_estimate=lasting(55),
        name="middle_rows",
    )(
        attended.reshape(4, 2, share, -1),
        weights,
        gain,
        tokens,
    )


def ffn_rows_kernel(
    block,
    weights_in,
    beside,
    from_x,
    from_y,
    from_both,
    out,
    m,
    gate,
    up,
    beside_out,
    sent,
    landed,
    local,
    loading,
    storing,
    weights,
    rows_in,
    m_held,
    gate_held,
    up_held,
    wires_beside,
    held_beside,
    held_blocks,
):
    p = Plane(sent, landed)
    gather = Gather(p, block, out)
    for k in range(CHUNKS):
        gather.start(k)
    weights_load = pltpu.make_async_copy(weights_in, weights, local.at[0])
    weights_load.start()
    mine = pltpu.make_async_copy(block, out.at[p.rank, p.core], local.at[1])
    mine.start()
    blocks = ((from_x, p.at_x), (from_y, p.at_y), (from_both, p.at_both))
    loads = [pltpu.make_async_copy(beside, held_beside, wires_beside.at[0])]
    for i, (source, rank) in enumerate(blocks):
        loads.append(
            pltpu.make_async_copy(source, held_blocks.at[i], wires_beside.at[i + 1])
        )
    for started in loads:
        started.start()
    units = m.shape[3]
    stores = []

    def load(n, rank, core):
        return pltpu.make_async_copy(out.at[rank, core], rows_in.at[n % 2], loading.at[n % 2])

    def compute(n, rank, core, source):
        slot = n % 2
        if n >= 2:
            for started in stores[n - 2]:
                started.wait()

        def step(j, carry):
            cut = pl.ds(pl.multiple_of(j * 256, 256), 256)
            beyond = pl.ds(pl.multiple_of(units + j * 256, 256), 256)
            gate_part = dot(source[...], weights[:, cut])
            up_part = dot(source[...], weights[:, beyond])
            gate_held[slot, :, cut] = gate_part.astype(jnp.bfloat16)
            up_held[slot, :, cut] = up_part.astype(jnp.bfloat16)
            sigmoid = 1.0 / (1.0 + jnp.exp(-gate_part))
            m_held[slot, :, cut] = (gate_part * sigmoid * up_part).astype(jnp.bfloat16)
            return carry

        lax.fori_loop(0, units // 256, step, 0)
        stores.append(
            [
                pltpu.make_async_copy(held.at[slot], target.at[rank, core], storing.at[slot, i])
                for i, (held, target) in enumerate(((m_held, m), (gate_held, gate), (up_held, up)))
            ]
        )
        for started in stores[n]:
            started.start()

    def from_sibling(i, rank):
        for k in range(CHUNKS):
            p.arrive(
                gather.across[i, k], out.at[rank, 1 - p.core, chunk(k, gather.rows)]
            )

    weights_load.wait()
    compute(0, p.rank, p.core, block)
    kept, shared = [], []
    loads[0].wait()
    kept.append(pltpu.make_async_copy(held_beside, beside_out.at[p.rank], wires_beside.at[0]))
    kept[0].start()
    for i, (source, rank) in enumerate(blocks):
        loads[i + 1].wait()
        place = beside_out.at[rank, p.core]
        kept.append(pltpu.make_async_copy(held_blocks.at[i], place, wires_beside.at[i + 1]))
        kept[i + 1].start()
        shared.append(p.send(held_blocks.at[i], place, p.sibling))
    gather.forward_chunk(0)
    from_sibling(0, p.rank)
    load(1, p.rank, 1 - p.core).start()
    load(1, p.rank, 1 - p.core).wait()
    compute(1, p.rank, 1 - p.core, rows_in.at[1])
    for k in range(1, CHUNKS):
        gather.forward_chunk(k)
    load(2, p.at_x, p.core).start()
    load(3, p.at_y, p.core).start()
    load(2, p.at_x, p.core).wait()
    compute(2, p.at_x, p.core, rows_in.at[0])
    from_sibling(1, p.at_x)
    load(4, p.at_x, 1 - p.core).start()
    load(3, p.at_y, p.core).wait()
    compute(3, p.at_y, p.core, rows_in.at[1])
    from_sibling(2, p.at_y)
    load(5, p.at_y, 1 - p.core).start()
    load(4, p.at_x, 1 - p.core).wait()
    compute(4, p.at_x, 1 - p.core, rows_in.at[0])
    gather.forward_far()
    load(6, p.at_both, p.core).start()
    load(5, p.at_y, 1 - p.core).wait()
    compute(5, p.at_y, 1 - p.core, rows_in.at[1])
    from_sibling(3, p.at_both)
    load(7, p.at_both, 1 - p.core).start()
    load(6, p.at_both, p.core).wait()
    compute(6, p.at_both, p.core, rows_in.at[0])
    load(7, p.at_both, 1 - p.core).wait()
    compute(7, p.at_both, 1 - p.core, rows_in.at[1])
    for number, (source, rank) in zip(shared, blocks):
        p.arrive(number, beside_out.at[rank, 1 - p.core])
    p.finish()
    mine.wait()
    for started in kept:
        started.wait()
    for n in (6, 7):
        for started in stores[n]:
            started.wait()


def ffn_rows(block, weights, beside, blocks):
    share, width = block.shape
    units = weights.shape[1] // 2
    kind = jnp.bfloat16
    full = jax.ShapeDtypeStruct((4, 2, share, width), kind)
    part = jax.ShapeDtypeStruct((4, 2, share, units), kind)
    held = pltpu.VMEM((2, share, units), kind)
    outs = pl.pallas_call(
        ffn_rows_kernel,
        out_shape=[full, part, part, part, full],
        in_specs=[VMEM] + [ANY] * 5,
        out_specs=[ANY] * 5,
        scratch_shapes=wires(GATHER_COPIES + 3)
        + [
            pltpu.SemaphoreType.DMA((2,)),
            pltpu.SemaphoreType.DMA((2,)),
            pltpu.SemaphoreType.DMA((2, 3)),
            pltpu.VMEM(weights.shape, kind),
            pltpu.VMEM((2, share, width), kind),
            held,
            held,
            held,
            pltpu.SemaphoreType.DMA((4,)),
            pltpu.VMEM((2, share, width), kind),
            pltpu.VMEM((3, share, width), kind),
        ],
        compiler_params=pltpu.CompilerParams(
            collective_id=11, has_side_effects=True, vmem_limit_bytes=VMEM_LIMIT
        ),
        cost_estimate=lasting(60),
        name="ffn_rows",
    )(block, weights, beside.reshape(2, share, width), *blocks)
    return [array.reshape(8 * share, -1) for array in outs]


class WeightTiles:
    def __init__(self, rows, slopes, target, rows_in, tile_out, wires_in):
        self.rows, self.slopes, self.target = rows, slopes, target
        self.rows_in, self.tile_out, self.wires = rows_in, tile_out, wires_in
        self.count = rows.shape[1] // TILE
        self.load(0, 0).start()

    def load(self, d, slot):
        columns = pl.ds(pl.multiple_of(d * TILE, TILE), TILE)
        return pltpu.make_async_copy(
            self.rows.at[:, columns], self.rows_in.at[slot], self.wires.at[0, slot]
        )

    def store(self, d, slot):
        columns = pl.ds(pl.multiple_of(d * TILE, TILE), TILE)
        return pltpu.make_async_copy(
            self.tile_out.at[slot], self.target.at[columns], self.wires.at[1, slot]
        )

    def run(self, first, last):
        def step(d, carry):
            slot = lax.rem(d, 2)
            self.load(d, slot).wait()

            @pl.when(d < self.count - 1)
            def _():
                self.load(d + 1, 1 - slot).start()

            @pl.when(d >= 2)
            def _():
                self.store(d - 2, slot).wait()

            self.tile_out[slot] = dot(self.rows_in[slot], self.slopes[...], FIRST).astype(
                jnp.bfloat16
            )
            self.store(d, slot).start()
            return carry

        lax.fori_loop(first, last, step, 0)

    def finish(self):
        for d in (self.count - 2, self.count - 1):
            self.store(d, d % 2).wait()


def tile_scratch(count, units):
    return [
        pltpu.SemaphoreType.DMA((2, 2)),
        pltpu.VMEM((2, count, TILE), jnp.bfloat16),
        pltpu.VMEM((2, TILE, units), jnp.bfloat16),
    ]


UNITS = ((0, 0), (0, 1), (1, 0), (2, 0), (1, 1), (2, 1), (3, 0), (3, 1))


def second_kernel(
    slopes,
    normed_rows,
    weights_in,
    middle_in,
    cotangent_in,
    gain,
    early,
    grad_middle,
    hidden,
    weight_grads,
    sent,
    landed,
    loading,
    beside,
    weights,
    middle,
    cotangent,
    tile_wires,
    rows_in,
    tile_out,
    gate_in,
    up_in,
    given,
    held,
    other,
    near_x,
    near_y,
    far_x,
    far_y,
):
    share, width = near_x.shape
    cuts = [slice(j * 512, j * 512 + 512) for j in range(width // 512)]
    weight_loads = [
        pltpu.make_async_copy(weights_in.at[cut], weights.at[cut], beside.at[2 + j])
        for j, cut in enumerate(cuts)
    ]
    for started in weight_loads:
        started.start()
    p = Plane(sent, landed)
    half = share // 2
    order = (p.at_both, p.at_x, p.at_y, p.rank)
    top, low = halves = pl.ds(0, half), pl.ds(half, half)

    def places(u):
        i, h = UNITS[u]
        for core in (1 - p.core, p.core):
            row = (order[i] * 2 + core) * share + h * half
            yield pl.ds(pl.multiple_of(row, 32), half)

    units = gate_in.shape[1]

    def loads(u):
        for j, rows in enumerate(places(u)):
            for n, target in enumerate((gate_in, up_in)):
                yield pltpu.make_async_copy(
                    slopes.at[rows, pl.ds(n * units, units)],
                    target.at[rows],
                    loading.at[u, 2 * j + n],
                )

    def compute(u):
        i, h = UNITS[u]
        slot = u % 2
        gate_rows = jnp.concatenate([gate_in[rows, :] for rows in places(u)], axis=0)
        up_rows = jnp.concatenate([up_in[rows, :] for rows in places(u)], axis=0)
        for j, cut in enumerate(cuts):
            if u == 0:
                weight_loads[j].wait()
            back = dot(gate_rows, weights[cut, :units], LAST) + dot(
                up_rows, weights[cut, units:], LAST
            )
            given[slot, :, cut] = back[:half].astype(jnp.bfloat16)
            held[i, halves[h], cut] = back[half:].astype(jnp.bfloat16)

    first = pl.ds(pl.multiple_of(p.core * share, SLAB), share)
    row_loads = [
        pltpu.make_async_copy(middle_in, middle, beside.at[0]),
        pltpu.make_async_copy(cotangent_in.at[first], cotangent, beside.at[1]),
    ]
    tiles = WeightTiles(normed_rows, gate_in, weight_grads, rows_in, tile_out, tile_wires)

    moves, across = {}, {}
    moves, across = {}, {}

    def settle(u):
        i, h = UNITS[u]
        p.arrive(across[u], other.at[i, halves[h]])
        add_rows(held.at[i], other.at[i], h * half, half)
        if u == 0:
            moves["far_x"] = p.send(held.at[0, top], far_x, p.x)
        elif u == 1:
            moves["far_y"] = p.send(held.at[0, low], far_y, p.y)
        elif u == 2:
            moves["x", 0] = p.send(held.at[1, top], near_x.at[top], p.x)
        elif u == 3:
            p.arrive(moves["far_x"], far_x)
            add_rows(held.at[2], far_x, 0, half)
            moves["y", 0] = p.send(held.at[2, top], near_y.at[top], p.y)
        elif u == 4:
            p.arrive(moves["far_y"], far_y)

            def step(k, carry):
                rows, at = pl.ds(half + k * SLAB, SLAB), pl.ds(k * SLAB, SLAB)
                held[1, rows, :] = (
                    held[1, rows, :].astype(jnp.float32) + far_y[at, :].astype(jnp.float32)
                ).astype(jnp.bfloat16)
                return carry

            lax.fori_loop(0, half // SLAB, step, 0)
            moves["x", 1] = p.send(held.at[1, low], near_x.at[low], p.x)
        elif u == 5:
            moves["y", 1] = p.send(held.at[2, low], near_y.at[low], p.y)

    for u in range(8):
        for started in loads(u):
            started.start()

    def unit(u):
        if u >= 2:
            p.copies[across[u - 2]].wait_send()
        compute(u)
        i, h = UNITS[u]
        across[u] = p.send(given.at[u % 2], other.at[i, halves[h]], p.sibling)

    def wait_loads(units_here):
        for u in units_here:
            for started in loads(u):
                started.wait()

    for started in row_loads:
        started.start()
    wait_loads((0,))
    unit(0)
    settle(0)
    wait_loads((1,))
    unit(1)
    settle(1)
    wait_loads((2, 3))
    unit(2)
    unit(3)
    settle(2)
    settle(3)
    wait_loads((4, 5, 6, 7))
    unit(4)
    unit(5)
    settle(4)
    unit(6)
    settle(5)
    unit(7)
    settle(6)
    settle(7)
    tiles.run(0, tiles.count)

    def work(rows):
        value = middle[rows, :]
        root = row_root(value)
        normed = value * root
        total = sum(part[rows, :].astype(jnp.float32) for part in (held.at[3], near_x, near_y))
        slope = total * gain[1:2, :]
        mean = jnp.mean(slope * normed, axis=-1, keepdims=True)
        gradient = cotangent[rows, :].astype(jnp.float32) + root * (slope - normed * mean)
        grad_middle[rows, :] = gradient
        hidden[rows, :] = (residual_scale * gradient).astype(jnp.bfloat16)

    for started in row_loads:
        started.wait()
    for h in range(2):
        p.arrive(moves["x", h], near_x.at[halves[h]])
        p.arrive(moves["y", h], near_y.at[halves[h]])
        slabs(h * half, half, work)
    for u in (6, 7):
        p.copies[across[u]].wait_send()
    tiles.finish()
    for number, started in enumerate(p.copies):
        if number not in across.values():
            started.wait_send()


def second_plane(slopes, normed_rows, weights, middle, cotangent, gain, early):
    share, width = middle.shape
    count, units = slopes.shape[0], slopes.shape[1] // 2
    kind = jnp.bfloat16
    half = share // 2
    quarter = pltpu.VMEM((4, share, width), kind)
    return pl.pallas_call(
        second_kernel,
        out_shape=[
            jax.ShapeDtypeStruct((share, width), jnp.float32),
            jax.ShapeDtypeStruct((share, width), kind),
            jax.ShapeDtypeStruct((width, units), kind),
        ],
        in_specs=[ANY] * 5 + [VMEM, ANY],
        out_specs=[VMEM, VMEM, ANY],
        scratch_shapes=wires(8 + 6)
        + [
            pltpu.SemaphoreType.DMA((8, 4)),
            pltpu.SemaphoreType.DMA((2 + width // 512,)),
            pltpu.VMEM(weights.shape, kind),
            pltpu.VMEM((share, width), jnp.float32),
            pltpu.VMEM((share, width), kind),
        ]
        + tile_scratch(count, units)
        + [
            pltpu.VMEM((count, units), kind),
            pltpu.VMEM((count, units), kind),
            pltpu.VMEM((2, half, width), kind),
            quarter,
            quarter,
            pltpu.VMEM((share, width), kind),
            pltpu.VMEM((share, width), kind),
            pltpu.VMEM((half, width), kind),
            pltpu.VMEM((half, width), kind),
        ],
        compiler_params=pltpu.CompilerParams(
            collective_id=3, has_side_effects=True, vmem_limit_bytes=60 * 1024 * 1024
        ),
        cost_estimate=lasting(60),
        name="second_rows",
    )(slopes, normed_rows, weights, middle, cotangent, gain, early)


def spread_kernel(
    hidden, m, down_in, normed_rows, slopes, early, out, pair_own, pair_x, pair_y, pair_both,
    weight_grads, sent, landed, local, loading, tile_wires, rows_in, tile_out, up_in,
    m_in, given, held, theirs, down_w,
):
    p = Plane(sent, landed)
    share, width = hidden.shape
    gather = Gather(p, hidden, out)
    for k in range(CHUNKS):
        gather.start(k)
    mine = pltpu.make_async_copy(hidden, out.at[p.rank, p.core], local.at[4])
    mine.start()
    order = (p.rank, p.at_x, p.at_y, p.at_both)
    halves = pl.ds(0, share), pl.ds(share, share)

    def loads(i):
        for j, core in enumerate((1 - p.core, p.core)):
            yield pltpu.make_async_copy(
                m.at[order[i], core], m_in.at[i % 2, halves[j]], loading.at[i % 2, j]
            )

    across = []
    units = up_in.shape[1]
    up_load = pltpu.make_async_copy(slopes.at[:, pl.ds(units, units)], up_in, local.at[5])
    down_load = pltpu.make_async_copy(down_in, down_w, local.at[6])
    down_load.start()
    up_load.start()
    for started in loads(0):
        started.start()
    down_load.wait()
    tiles = WeightTiles(normed_rows, up_in, weight_grads, rows_in, tile_out, tile_wires)
    for i in range(4):
        for started in loads(i):
            started.wait()
        if i < 3:
            for started in loads(i + 1):
                started.start()

        def step(j, carry, i=i):
            cut = pl.ds(pl.multiple_of(j * 512, 512), 512)
            value = dot(m_in[i % 2], down_w[cut, :], LAST)
            given[i, :, cut] = value[:share].astype(jnp.bfloat16)
            held[i, :, cut] = value[share:].astype(jnp.bfloat16)
            return carry

        lax.fori_loop(0, width // 512, step, 0)
        across.append(p.send(given.at[i], theirs.at[i], p.sibling))
        if i == 0:
            up_load.wait()
        gather.forward_chunk(i)
        tiles.run(i, i + 1)
    kept = []
    for i in range(4):
        p.arrive(across[i], theirs.at[i])
        add_rows(held.at[i], theirs.at[i], 0, share)
        target = (pair_own, pair_x, pair_y, pair_both)[i]
        kept.append(pltpu.make_async_copy(held.at[i], target, local.at[i]))
        kept[i].start()
    gather.forward_far()
    tiles.run(4, tiles.count)
    tiles.finish()
    gather.finish()
    p.finish()
    mine.wait()
    for started in kept:
        started.wait()


def spread_plane(hidden, m, down_w, normed_rows, slopes, early):
    share, width = hidden.shape
    units = m.shape[1]
    full = jax.ShapeDtypeStruct((4, 2, share, width), jnp.bfloat16)
    quarter = pltpu.VMEM((4, share, width), jnp.bfloat16)
    out, *pairs, weight_grads = pl.pallas_call(
        spread_kernel,
        out_shape=[full]
        + [jax.ShapeDtypeStruct((share, width), jnp.bfloat16)] * 4
        + [jax.ShapeDtypeStruct((width, units), jnp.bfloat16)],
        in_specs=[VMEM] + [ANY] * 5,
        out_specs=[ANY] * 6,
        scratch_shapes=wires(GATHER_COPIES + 4)
        + [
            pltpu.SemaphoreType.DMA((7,)),
            pltpu.SemaphoreType.DMA((2, 2)),
        ]
        + tile_scratch(8 * share, units)
        + [
            pltpu.VMEM((8 * share, units), jnp.bfloat16),
            pltpu.VMEM((2, 2 * share, units), jnp.bfloat16),
            quarter,
            quarter,
            quarter,
            pltpu.VMEM(down_w.shape, jnp.bfloat16),
        ],
        compiler_params=pltpu.CompilerParams(
            collective_id=7, has_side_effects=True, vmem_limit_bytes=60 * 1024 * 1024
        ),
        cost_estimate=lasting(60),
        name="spread_rows",
    )(hidden, m.reshape(4, 2, share, units), down_w, normed_rows, slopes, early)
    return out.reshape(8 * share, width), pairs, weight_grads


def lane_sums(pairs):
    total = 0.0
    for a, b in pairs:
        product = a.astype(jnp.float32) * b.astype(jnp.float32)
        total += jnp.sum(product, axis=1, keepdims=True)
    return jnp.broadcast_to(total, (total.shape[0], 128))


LATER = 10


def last_kernel(
    back,
    weights,
    gain,
    ups,
    early,
    *rest,
):
    later, rest = rest[:LATER], rest[LATER:]
    out, result_out, up_out, gain_out, sent, landed, local, loading, held, result, sums = rest[:11]
    landing, scratch = rest[11 : 11 + LATER], rest[11 + LATER :]
    share = landing[8].shape[0]
    first = pl.ds(pl.multiple_of(lax.axis_index("tensor") * share, SLAB), share)
    later = [*later[:8], later[8].at[first], later[9]]
    loads = [
        pltpu.make_async_copy(source, target, loading.at[i])
        for i, (source, target) in enumerate(zip(later, landing))
    ]
    for started in loads:
        started.start()
    middle, ffn_own, ffn_x, ffn_y, ffn_both, gates, gate, up, residual, grad_middle = landing
    p = Plane(sent, landed, diagonal=True)
    moves = []

    def hand_back(partner, rank):
        moves.append((p.send(ups.at[rank], up_out.at[p.rank], partner), up_out.at[rank]))

    hand_back(p.both, p.at_both)
    total = Scatter(p, back, weights, slice(0, back.shape[3]), *scratch)
    hand_back(p.x, p.at_x)
    hand_back(p.y, p.at_y)
    up_out[p.rank] = ups[p.rank]
    share = held.shape[0]

    def finish_result(rows):
        parts = (ffn_own, ffn_x, ffn_y, ffn_both)
        ffn = sum(part[rows, :].astype(jnp.float32) for part in parts)
        result[rows, :] = (middle[rows, :] + residual_scale * ffn).astype(jnp.bfloat16)

    for started in loads:
        started.wait()
    slabs(0, share, finish_result)
    kept = [pltpu.make_async_copy(result, result_out.at[p.core], local.at[0])]
    kept[0].start()
    given = p.send(result, result_out.at[p.core], p.sibling)
    units = gate.shape[1] // 4

    def gate_rows(rows):
        sums[0, rows, :] = lane_sums(
            [(gates[c, rows, :], gate[rows, c * units : c * units + units]) for c in range(4)]
        )

    def up_rows(rows):
        sums[0, rows, :] += lane_sums(
            [(up_out[c, rows, :], up[rows, c * units : c * units + units]) for c in range(4)]
        )

    slabs(0, gate.shape[0], gate_rows)

    def work(rows):
        value = residual[rows, :].astype(jnp.float32)
        root = row_root(value)
        normed = value * root
        slope = total.rows(rows) * gain[0:1, :]
        mean = jnp.mean(slope * normed, axis=-1, keepdims=True)
        held[rows, :] = grad_middle[rows, :] + root * (slope - normed * mean)

    across = []
    for k in range(CHUNKS):
        cut = chunk(k, share)
        if k % (CHUNKS // 2) == 0:
            total.ready(k // (CHUNKS // 2))
        slabs(k * (share // CHUNKS), share // CHUNKS, work)
        across.append(p.send(held.at[cut], out.at[p.core, cut], p.sibling))
        kept.append(
            pltpu.make_async_copy(held.at[cut], out.at[p.core, cut], local.at[1 + k])
        )
        kept[1 + k].start()
    for number, target in moves:
        p.arrive(number, target)
    slabs(0, gate.shape[0], up_rows)
    swapped = p.send(sums.at[0], sums.at[1], p.sibling)
    p.arrive(swapped, sums.at[1])
    gain_out[...] = sums[0] + sums[1]
    p.arrive(given, result_out.at[1 - p.core])
    for k in range(CHUNKS):
        p.arrive(across[k], out.at[1 - p.core, chunk(k, share)])
    p.finish()
    for started in kept:
        started.wait()


def last_plane(
    back, weights, tokens, grad_middle, gain, middle, ffn_parts, ups, gates, gate, up, early
):
    share, width = grad_middle.shape
    later = [middle, *ffn_parts, gates, gate, up, tokens, grad_middle]
    out, result_out, up_out, gain_out = pl.pallas_call(
        last_kernel,
        out_shape=[
            jax.ShapeDtypeStruct((2, share, width), jnp.float32),
            jax.ShapeDtypeStruct((2, share, width), jnp.bfloat16),
            jax.ShapeDtypeStruct(ups.shape, ups.dtype),
            jax.ShapeDtypeStruct((gate.shape[0], 128), jnp.float32),
        ],
        in_specs=[VMEM] * 4 + [ANY] * (1 + LATER),
        out_specs=[ANY, ANY, VMEM, VMEM],
        scratch_shapes=wires(CHUNKS + 5 + SCATTER_COPIES)
        + [
            pltpu.SemaphoreType.DMA((1 + CHUNKS,)),
            pltpu.SemaphoreType.DMA((LATER,)),
            pltpu.VMEM((share, width), jnp.float32),
            pltpu.VMEM((share, width), jnp.bfloat16),
            pltpu.VMEM((2, gate.shape[0], 128), jnp.float32),
        ]
        + [pltpu.VMEM(array.shape, array.dtype) for array in later[:8]]
        + [pltpu.VMEM((share, width), tokens.dtype), pltpu.VMEM((share, width), jnp.float32)]
        + scatter_scratch(share, width),
        compiler_params=pltpu.CompilerParams(
            collective_id=4, has_side_effects=True, vmem_limit_bytes=VMEM_LIMIT
        ),
        cost_estimate=lasting(70),
        name="last_rows",
    )(
        back.reshape(4, 2, share, -1),
        weights,
        gain,
        ups,
        early,
        *later,
    )
    return (
        out.reshape(2 * share, width),
        result_out.reshape(2 * share, width),
        up_out,
        gain_out,
    )


def exchange_kernel(blocks, query, pair, other_sums, out, gain_out, sent, landed, sums):
    p = Plane(sent, landed, diagonal=True)
    moves = []
    for partner, rank in ((p.both, p.at_both), (p.x, p.at_x), (p.y, p.at_y)):
        moves.append((p.send(blocks.at[rank], out.at[p.rank], partner), out.at[rank]))
    out[p.rank] = blocks[p.rank]
    width = query.shape[1] // 4

    def attention_rows(rows):
        pairs = []
        for c in range(4):
            pairs.append((out[c, rows, :width], query[rows, c * width : c * width + width]))
            pairs.append((out[c, rows, width : width + 128], pair[rows, c * 128 : c * 128 + 128]))
        sums[0, rows, :] = lane_sums(pairs)

    for number, target in moves:
        p.arrive(number, target)
    slabs(0, blocks.shape[1], attention_rows)
    swapped = p.send(sums.at[0], sums.at[1], p.sibling)
    p.arrive(swapped, sums.at[1])
    gain_out[0] = sums[0] + sums[1]
    gain_out[1] = other_sums[...]
    p.finish()


def exchange(blocks, query, pair, other_sums):
    depth = blocks.shape[1]
    return pl.pallas_call(
        exchange_kernel,
        out_shape=[
            jax.ShapeDtypeStruct(blocks.shape, blocks.dtype),
            jax.ShapeDtypeStruct((2, depth, 128), jnp.float32),
        ],
        in_specs=[VMEM] * 4,
        out_specs=[VMEM] * 2,
        scratch_shapes=wires(4) + [pltpu.VMEM((2, depth, 128), jnp.float32)],
        compiler_params=pltpu.CompilerParams(collective_id=5, has_side_effects=True),
        cost_estimate=lasting(8),
        name="exchange_blocks",
    )(blocks, query, pair, other_sums)


def finish_first_kernel(down, gate, down_out, gate_out):
    down_out[...] = jnp.transpose(down[0].astype(jnp.float32))
    gate_out[...] = gate[0].astype(jnp.float32)


def finish_first(down, gate):
    groups, depth, units = down.shape
    block = pl.BlockSpec((1, depth, units), lambda i: (i, 0, 0))
    return pl.pallas_call(
        finish_first_kernel,
        grid=(groups,),
        in_specs=[block, block],
        out_specs=[
            pl.BlockSpec((units, depth), lambda i: (i, 0)),
            pl.BlockSpec((depth, units), lambda i: (0, i)),
        ],
        out_shape=[
            jax.ShapeDtypeStruct((groups * units, depth), jnp.float32),
            jax.ShapeDtypeStruct((depth, groups * units), jnp.float32),
        ],
        compiler_params=pltpu.CompilerParams(vmem_limit_bytes=VMEM_LIMIT),
        cost_estimate=lasting(5),
        name="finish_first",
    )(down, gate)


def finish_kernel(
    attn, up, tokens, result, sums, gains,
    query_out, key_out, value_out, out_out, up_out, tokens_out, result_out, gain_out,
):
    width = query_out.shape[1]
    query_out[...] = attn[0, :, :width].astype(jnp.float32)
    for c in range(key_out.shape[1] // HEAD):

        @pl.when(pl.program_id(0) == c)
        def _(c=c):
            cut = slice(c * HEAD, c * HEAD + HEAD)
            key_out[:, cut] = attn[0, :, width : width + HEAD].astype(jnp.float32)
            value_out[:, cut] = attn[0, :, width + HEAD : width + 2 * HEAD].astype(jnp.float32)

    out_out[...] = jnp.transpose(attn[0, :, width + 128 :].astype(jnp.float32))
    up_out[...] = up[0].astype(jnp.float32)
    tokens_out[...] = tokens[...]
    result_out[...] = result[...]
    for i in range(2):
        gain_out[i : i + 1, :] = jnp.transpose(sums[i])[0:1] / gains[i : i + 1, :]


def finish(attn, up, tokens, result, sums, gains):
    groups, depth, units = up.shape
    width = attn.shape[2] // 2 - HEAD
    rows, columns = tokens.shape
    part = rows // groups

    def block(*shape):
        return pl.BlockSpec((1, *shape), lambda i: (i, 0, 0))

    def wide(count):
        return pl.BlockSpec((depth, count), lambda i: (0, i))

    def tall(count, other):
        return pl.BlockSpec((count, other), lambda i: (i, 0))

    def f32(*shape):
        return jax.ShapeDtypeStruct(shape, jnp.float32)

    return pl.pallas_call(
        finish_kernel,
        grid=(groups,),
        in_specs=[
            block(depth, attn.shape[2]),
            block(depth, units),
            tall(part, columns),
            tall(part, columns),
            pl.BlockSpec(sums.shape, lambda i: (0, 0, 0)),
            pl.BlockSpec(gains.shape, lambda i: (0, 0)),
        ],
        out_specs=[
            wide(width),
            pl.BlockSpec((depth, groups * HEAD), lambda i: (0, 0)),
            pl.BlockSpec((depth, groups * HEAD), lambda i: (0, 0)),
            tall(width, depth),
            wide(units),
            tall(part, columns),
            tall(part, columns),
            pl.BlockSpec((2, 128), lambda i: (0, 0)),
        ],
        out_shape=[
            f32(depth, groups * width),
            f32(depth, groups * HEAD),
            f32(depth, groups * HEAD),
            f32(groups * width, depth),
            f32(depth, groups * units),
            f32(rows, columns),
            jax.ShapeDtypeStruct(result.shape, result.dtype),
            f32(2, 128),
        ],
        compiler_params=pltpu.CompilerParams(vmem_limit_bytes=VMEM_LIMIT),
        cost_estimate=lasting(12),
        name="finish",
    )(attn, up, tokens, result, sums, gains)


def context_pairs(step):
    return [(i, i ^ step) for i in range(4)]


def ffn_first_kernel(hidden, weights, m, gate, up):
    units = m.shape[1]
    for j in range(units // 256):
        cut = slice(j * 256, j * 256 + 256)
        gate_part = dot(hidden[...], weights[:, cut])
        up_part = dot(hidden[...], weights[:, units + j * 256 : units + j * 256 + 256])
        gate[:, cut] = gate_part.astype(jnp.bfloat16)
        up[:, cut] = up_part.astype(jnp.bfloat16)
        sigmoid = 1.0 / (1.0 + jnp.exp(-gate_part))
        m[:, cut] = (gate_part * sigmoid * up_part).astype(jnp.bfloat16)


def ffn_slopes_kernel(grad, gate, up, down_w, early, slopes):
    units = down_w.shape[1]
    for j in range(units // 256):
        cut = slice(j * 256, j * 256 + 256)
        grad_part = dot(grad[...], down_w[:, cut])
        gate_part = gate[:, cut].astype(jnp.float32)
        up_part = up[:, cut].astype(jnp.float32)
        sigmoid = 1.0 / (1.0 + jnp.exp(-gate_part))
        slope = sigmoid * (1.0 + gate_part * (1.0 - sigmoid))
        slopes[:, cut] = (grad_part * up_part * slope).astype(jnp.bfloat16)
        slopes[:, units + j * 256 : units + j * 256 + 256] = (
            grad_part * gate_part * sigmoid
        ).astype(jnp.bfloat16)


def first_rows_kernel(values, gains, weight, hidden, raw):
    value = values[...].astype(jnp.float32)
    normed = (value * row_root(value) * gains[0:1, :]).astype(jnp.bfloat16)
    hidden[...] = normed
    raw[...] = dot(normed, weight[...])


def first_rows(values, gains, packed, columns):
    count, width = values.shape
    return pl.pallas_call(
        first_rows_kernel,
        grid=(count // ROW_TILE,),
        in_specs=[
            pl.BlockSpec((ROW_TILE, width), lambda i: (i, 0)),
            pl.BlockSpec((8, width), lambda i: (0, 0)),
            pl.BlockSpec((width, columns), lambda i: (0, 0)),
        ],
        out_specs=[
            pl.BlockSpec((ROW_TILE, width), lambda i: (i, 0)),
            pl.BlockSpec((ROW_TILE, columns), lambda i: (i, 0)),
        ],
        out_shape=[
            jax.ShapeDtypeStruct((count, width), jnp.bfloat16),
            jax.ShapeDtypeStruct((count, columns), jnp.float32),
        ],
        compiler_params=pltpu.CompilerParams(vmem_limit_bytes=VMEM_LIMIT),
        cost_estimate=lasting(4),
        name="first_rows",
    )(values, gains, packed)


def attention_weights_kernel(hidden, back, grad, attended, moving, *rest):
    out, moved, sent, landed, local = rest[-5:]
    step, last = pl.program_id(0), pl.num_programs(0) - 1

    @pl.when(step == 0)
    def start():
        p = Plane(sent, landed, diagonal=True)
        pltpu.make_async_copy(moving.at[p.rank], moved.at[p.rank], local).start()
        for partner, rank in ((p.both, p.at_both), (p.x, p.at_x), (p.y, p.at_y)):
            p.send(moving.at[rank], moved.at[p.rank], partner)

    columns = back.shape[1]
    out[:, :columns] = dot(hidden[...], back[...], FIRST).astype(jnp.bfloat16)
    out[:, columns:] = dot(grad[...], attended[...], FIRST).astype(jnp.bfloat16)

    @pl.when(step == last)
    def finish():
        p = Plane(sent, landed, entered=True)
        for number, rank in enumerate((p.at_both, p.at_x, p.at_y)):
            move = p.copy(number, moving.at[rank], moved.at[rank], p.x)
            move.wait_recv()
            move.wait_send()
        pltpu.make_async_copy(moving.at[p.rank], moved.at[p.rank], local).wait()


def attention_weights(hidden, back, grad, attended, moving, early):
    count, width = hidden.shape
    first, second = back.shape[1], attended.shape[1]
    tall = pl.BlockSpec((count, 256), lambda i: (0, i))
    return pl.pallas_call(
        attention_weights_kernel,
        grid=(width // 256,),
        in_specs=[
            tall,
            pl.BlockSpec((count, first), lambda i: (0, 0)),
            tall,
            pl.BlockSpec((count, second), lambda i: (0, 0)),
        ]
        + [ANY] * (1 + len(early)),
        out_specs=[pl.BlockSpec((256, first + second), lambda i: (i, 0)), ANY],
        out_shape=[
            jax.ShapeDtypeStruct((width, first + second), jnp.bfloat16),
            jax.ShapeDtypeStruct(moving.shape, moving.dtype),
        ],
        scratch_shapes=wires(3) + [pltpu.SemaphoreType.DMA],
        compiler_params=pltpu.CompilerParams(
            collective_id=8, has_side_effects=True, vmem_limit_bytes=VMEM_LIMIT
        ),
        cost_estimate=lasting(25),
        name="attention_weights",
    )(hidden, back, grad, attended, moving, *early)


ROW_TILE = 256


def row_tiles(kernel, name, rows, weights, extra, widths):
    count = rows[0].shape[0]

    def tile(width):
        return pl.BlockSpec((ROW_TILE, width), lambda i: (i, 0))

    whole = [
        pl.BlockSpec(w.shape, lambda i: (0, 0), pipeline_mode=pl.Buffered(1)) for w in weights
    ]
    flops = 2 * count * sum(w.size for w in weights)
    return pl.pallas_call(
        kernel,
        grid=(count // ROW_TILE,),
        in_specs=[tile(r.shape[1]) for r in rows] + whole + [ANY] * len(extra),
        out_specs=[tile(width) for width in widths],
        out_shape=[jax.ShapeDtypeStruct((count, width), jnp.bfloat16) for width in widths],
        compiler_params=pltpu.CompilerParams(vmem_limit_bytes=56 * 1024 * 1024),
        cost_estimate=pl.CostEstimate(flops=flops, bytes_accessed=flops // 400, transcendentals=0),
        name=name,
    )(*rows, *weights, *extra)


def norm_backward(gradient, normed, inv_root):
    return inv_root * (gradient - normed * jnp.mean(gradient * normed, axis=-1, keepdims=True))


def inverse_root(values):
    return lax.rsqrt(jnp.mean(values * values, axis=-1, keepdims=True) + epsilon)


PLANE = ("context", "tensor")


def gather_rows(values):
    return lax.all_gather(values, PLANE, axis=0, tiled=True)


def scatter_rows(partial):
    return lax.psum_scatter(
        partial.astype(jnp.bfloat16), PLANE, scatter_dimension=0, tiled=True
    ).astype(jnp.float32)


def local(
    tokens,
    cotangent,
    attn_gain,
    w_query,
    w_key,
    w_value,
    w_out,
    ffn_gain,
    w_gate,
    w_up,
    w_down,
    piece_segment,
    piece_parent,
    piece_start,
):
    groups = lax.axis_size("context")
    cores = lax.axis_size("tensor")
    depth = w_query.shape[0]
    kv_count = w_key.shape[1] // HEAD
    sharing = groups // kv_count
    share = tokens.shape[0] // cores
    first_row = lax.axis_index("tensor") * share

    def my_rows(values):
        return lax.dynamic_slice_in_dim(values, first_row, share, 0)

    def blocks(weight):
        return jnp.transpose(weight.reshape(depth, groups, -1), (1, 0, 2))

    def kv_blocks(weight):
        return jnp.repeat(jnp.transpose(weight.reshape(depth, kv_count, HEAD), (1, 0, 2)), sharing, 0)

    def spread(weight_blocks):
        mine = lax.all_to_all(weight_blocks, "context", 0, 0)
        mine = mine.reshape(groups * depth, -1)
        return lax.all_gather(mine, "fsdp", axis=0, tiled=True)

    square = groups == 4 and cores == 2
    width = w_query.shape[1] // groups
    columns_qkv = width + 2 * HEAD
    down_turned = w_down.T
    tokens_half, cotangent_half = my_rows(tokens), my_rows(cotangent)

    def over_groups(blocks_here):
        return lax.all_gather(
            blocks_here.reshape(groups * depth, -1), "fsdp", axis=0, tiled=True
        )

    if square:
        gains = jnp.pad(jnp.stack([attn_gain, ffn_gain]).astype(jnp.float32), ((0, 6), (0, 0)))
        packed, gain_rows, w_pair = first_exchange(w_query, w_key, w_value, w_out, gains)
        packed = over_groups(packed)
        both_blocks, down_blocks = exchange_columns(w_gate, w_up, down_turned, gain_rows)
        inputs_full, ffn_grad, my_ffn_grad = start_plane(tokens, cotangent, down_blocks)
        both_full, down_full = over_groups(both_blocks), over_groups(down_blocks)
        hidden_first, raw = first_rows(
            inputs_full.reshape(-1, inputs_full.shape[3]), gain_rows, packed, columns_qkv
        )
        out_full = packed[:, columns_qkv:]
    else:
        gains = jnp.stack([attn_gain, ffn_gain], axis=1)
        gains = jnp.broadcast_to(jnp.pad(gains, ((0, 0), (0, 126))), (groups, depth, 128))
        packed = spread(
            jnp.concatenate(
                [
                    blocks(w_query),
                    kv_blocks(w_key),
                    kv_blocks(w_value),
                    blocks(w_out.T),
                    gains,
                ],
                axis=2,
            )
        )
        qkv_full = packed[:, :columns_qkv]
        out_full = packed[:, columns_qkv : columns_qkv + width]
        gains_full = packed[:, columns_qkv + width :].astype(jnp.float32)
        attn_scale, ffn_scale = gains_full[:, 0], gains_full[:, 1]
        both_full = spread(jnp.concatenate([blocks(w_gate), blocks(w_up)], axis=2))
        down_full = spread(blocks(down_turned))
        inputs_full = gather_rows(tokens_half).astype(jnp.float32)
        hidden_first = inputs_full * inverse_root(inputs_full) * attn_scale
        hidden_first = hidden_first.astype(jnp.bfloat16)
        raw = dot(hidden_first, qkv_full)
        my_ffn_grad = (residual_scale * cotangent_half.astype(jnp.float32)).astype(jnp.bfloat16)
    tables = rope_tables()

    segment, starts = piece_segment[0] % 13, piece_start[0]
    places = jnp.where(
        segment == 0,
        starts,
        jnp.where(
            segment <= BRANCHES,
            starts + (segment - 1) * SEG,
            starts + (segment - 1 - BRANCHES) * SEG + (BRANCHES - 1) * SEG,
        ),
    )

    residual_in = tokens_half.astype(jnp.float32)
    grad_result = cotangent_half.astype(jnp.float32)

    attended, *kept = attention_forward(places, starts, raw, tables)
    if square:
        ffn_grad_blocks = [
            lax.ppermute(my_ffn_grad, "context", context_pairs(step)) for step in (1, 2, 3)
        ]
        hidden_block, middle = middle_plane(attended, packed, tokens, gain_rows)
    else:
        ffn_grad = gather_rows(my_ffn_grad)
        middle = residual_in + residual_scale * scatter_rows(dot(attended, out_full, LAST))
        hidden_second = gather_rows((middle * inverse_root(middle) * ffn_scale).astype(jnp.bfloat16))

    units = down_full.shape[1]
    if square:
        hidden_second, hidden, gate_proj, up_proj, ffn_grad = ffn_rows(
            hidden_block, both_full, ffn_grad, ffn_grad_blocks
        )
    else:
        hidden, gate_proj, up_proj = row_tiles(
            ffn_first_kernel,
            "ffn_first",
            [hidden_second],
            [both_full],
            [],
            [units, units, units],
        )
    grad_down = dot(ffn_grad, hidden, FIRST).astype(jnp.bfloat16)
    (slopes,) = row_tiles(
        ffn_slopes_kernel,
        "ffn_slopes",
        [ffn_grad, gate_proj, up_proj],
        [down_full],
        [grad_down],
        [2 * units],
    )
    def sum_groups(gradient):
        return lax.psum_scatter(gradient, "fsdp", scatter_dimension=0, tiled=True)

    def hand_back(gradient):
        return lax.all_to_all(gradient.reshape(groups, depth, -1), "context", 0, 0)

    def columns(gradient):
        return jnp.transpose(gradient, (1, 0, 2)).reshape(depth, -1).astype(jnp.float32)

    if square:
        grad_middle, my_attn_grad, grad_gate = second_plane(
            slopes,
            hidden_second,
            both_full,
            middle,
            cotangent,
            gain_rows,
            grad_down,
        )
        attn_grad, ffn_pairs, grad_up = spread_plane(
            my_attn_grad, hidden, down_full, hidden_second, slopes, grad_gate
        )
        ffn_parts = [ffn_pairs[0]] + [
            lax.ppermute(ffn_pairs[step], "context", context_pairs(step)) for step in (1, 2, 3)
        ]
    else:
        root = inverse_root(middle)
        ffn_out = dot(hidden, down_full, LAST)
        grad_gate = dot(hidden_second, slopes[:, :units], FIRST).astype(jnp.bfloat16)
        grad_up = dot(hidden_second, slopes[:, units:], FIRST).astype(jnp.bfloat16)
        grad_second = dot(slopes, both_full, LAST)
        grad_middle = grad_result + norm_backward(
            scatter_rows(grad_second) * ffn_scale, middle * root, root
        )
        attn_grad = gather_rows((residual_scale * grad_middle).astype(jnp.bfloat16))
        ffn_parts = []
    grad_attended = dot(attn_grad, out_full).astype(jnp.bfloat16)
    grad_down = sum_groups(grad_down)
    grad_gate, grad_up = sum_groups(grad_gate), sum_groups(grad_up)
    back = attention_backward(places, starts, grad_attended, kept, tables, [grad_down])
    grad_down = hand_back(grad_down)
    if square:
        grad_attn, grad_gate = attention_weights(
            hidden_first,
            back,
            attn_grad,
            attended,
            grad_gate.reshape(groups, depth, -1),
            [grad_down, *ffn_parts[1:]],
        )
    else:
        grad_attn = jnp.concatenate(
            [dot(hidden_first, back, FIRST), dot(attn_grad, attended, FIRST)], axis=1
        ).astype(jnp.bfloat16)
        grad_first = dot(back, qkv_full, LAST).astype(jnp.bfloat16)
        grad_gate, grad_up = hand_back(grad_gate), hand_back(grad_up)
    grad_attn = sum_groups(grad_attn)
    if square:
        down, gate = finish_first(grad_down, grad_gate)
        grad_tokens, result, grad_up, ffn_sums = last_plane(
            back,
            packed,
            tokens,
            grad_middle,
            gain_rows,
            middle,
            ffn_parts,
            grad_up.reshape(groups, depth, -1),
            grad_gate,
            w_gate,
            w_up,
            down,
        )
        grad_attn, sums = exchange(
            grad_attn.reshape(groups, depth, -1), w_query, w_pair, ffn_sums
        )
        my_gains = jnp.stack([attn_gain, ffn_gain]).astype(jnp.float32)
        query, key, value, out, up, grad_tokens, result, gain_grads = finish(
            grad_attn, grad_up, grad_tokens, result, sums, my_gains
        )
        return (
            result,
            grad_tokens,
            gain_grads[0],
            query,
            key,
            value,
            out,
            gain_grads[1],
            gate,
            up,
            down,
        )
    else:
        root = inverse_root(residual_in)
        grad_tokens = grad_middle + norm_backward(
            scatter_rows(grad_first) * attn_scale, residual_in * root, root
        )
        grad_tokens = lax.all_gather(grad_tokens, "tensor", axis=0, tiled=True)
        result = (middle + residual_scale * scatter_rows(ffn_out)).astype(jnp.bfloat16)
        grad_attn = hand_back(grad_attn)
        result = lax.all_gather(result, "tensor", axis=0, tiled=True)
    def kv_columns(gradient):
        gradient = gradient.astype(jnp.float32).reshape(kv_count, sharing, depth, HEAD)
        return jnp.transpose(jnp.sum(gradient, axis=1), (1, 0, 2)).reshape(depth, -1)

    grad_query = columns(grad_attn[:, :, :width])
    grad_key = kv_columns(grad_attn[:, :, width : width + HEAD])
    grad_value = kv_columns(grad_attn[:, :, width + HEAD : width + 2 * HEAD])
    grad_gate, grad_up = columns(grad_gate), columns(grad_up)

    def against(*pairs):
        return sum(jnp.sum(weight.astype(jnp.float32) * g, axis=1) for weight, g in pairs)

    gain_grads = jnp.stack(
        [
            against((w_query, grad_query), (w_key, grad_key), (w_value, grad_value)),
            against((w_gate, grad_gate), (w_up, grad_up)),
        ]
    )
    gain_grads = lax.psum(gain_grads, "tensor")
    return (
        result,
        grad_tokens,
        gain_grads[0] / attn_gain.astype(jnp.float32),
        grad_query,
        grad_key,
        grad_value,
        columns(grad_attn[:, :, width + 2 * HEAD :]).T,
        gain_grads[1] / ffn_gain.astype(jnp.float32),
        grad_gate,
        grad_up,
        columns(grad_down).T,
    )


ROWS = ("fsdp", "context")


def solution(mesh):
    return jax.shard_map(
        local,
        mesh=mesh,
        in_specs=(
            P(ROWS, None),
            P(ROWS, None),
            P(ROWS),
            P(ROWS, "tensor"),
            P(ROWS, "tensor"),
            P(ROWS, "tensor"),
            P("tensor", ROWS),
            P(ROWS),
            P(ROWS, "tensor"),
            P(ROWS, "tensor"),
            P("tensor", ROWS),
            P("fsdp", None),
            P("fsdp", None),
            P("fsdp", None),
        ),
        out_specs=(
            P(ROWS, None),
            P(ROWS, None),
            P(ROWS),
            P(ROWS, "tensor"),
            P(ROWS, "tensor"),
            P(ROWS, "tensor"),
            P("tensor", ROWS),
            P(ROWS),
            P(ROWS, "tensor"),
            P(ROWS, "tensor"),
            P("tensor", ROWS),
        ),
        check_vma=False,
    )
```
